32 devices in a mesh: groups: 2 (over y), ctx: 4 (over z), heads: 2 (over x), rep: 2 (over core).
Axes of the slice: x: 2, y: 2, z: 4, core: 2. Of those that a mesh axis runs over, the one named last changes fastest.
Arguments:
- query_rows: bfloat16 [8192, 1024], P(('groups', 'ctx', 'rep'), 'heads'), parts along dimension 0, may hold values from -6 to 6
- key_rows: bfloat16 [8192, 256], P(('groups', 'ctx', 'rep'), 'heads'), parts along dimension 0, may hold values from -6 to 6
- value_rows: bfloat16 [8192, 256], P(('groups', 'ctx', 'rep'), 'heads'), parts along dimension 0, may hold values from -6 to 6
- attn_out: bfloat16 [8192, 1024], P(('groups', 'ctx', 'rep'), 'heads'), parts along dimension 0, may hold values from -6 to 6
- out_grads: bfloat16 [8192, 1024], P(('groups', 'ctx', 'rep'), 'heads'), parts along dimension 0, may hold values from -36 to 36
- log_sums: float32 [8, 8192], P('heads', ('groups', 'ctx', 'rep')), parts along dimension 1, may hold values from 5.5 to 7.5
- window_offsets: int32 [64, 2], P('groups'), parts along dimension 0, may hold values from 1 to 3, as said below
- summary_ids: int32 [16], P('groups'), parts along dimension 0, may hold values from 0 to 31, as said below
Outputs:
- query_grads: bfloat16 [8192, 1024], P(('groups', 'ctx', 'rep'), 'heads'), parts along dimension 0
- key_grads: bfloat16 [8192, 256], P(('groups', 'ctx', 'rep'), 'heads'), parts along dimension 0
- value_grads: bfloat16 [8192, 256], P(('groups', 'ctx', 'rep'), 'heads'), parts along dimension 0
The draws below stay inside these ranges and needn't reach their ends.
There are 2 independent parts, one for each index of `groups`. The reference program is written for one: setup_inputs(seed, part) draws one part's arguments, and reference() takes and returns one part's arrays. A program takes and returns all parts, laid end to end along the dimension named above; each array names one. Nothing has to cross between parts.
Inputs may be any that keep to these rules, and one draw needn't show every extreme that they name: `window_offsets`: each row holds two different distances, the smaller first; some row holds 1 and 3. `summary_ids`: 8 different block numbers in no particular order; block 0 and block 31 are always among them.
All inputs are finite; a program needn't handle non-finite values.
Results may differ from the reference program's by a relative error of at most 0.0049.
Values may be sent and summed in bfloat16 or wider, within the bound.
No kernel may reach another device: no remote copies, remote signals or barrier semaphores. Data moves between devices by JAX's collectives and lax.ppermute only.
A program may use at most 64 MiB of HBM per device.

```python
import jax
import jax.numpy as jnp
from jax import lax

HEAD_DIM = 128
GROUP = 4
BLOCK = 128
REACH = 3
SUMMARY = 8
HEADS = 8
KV_HEADS = 2
BLOCKS = 32
SEQ = 4096


def draw_window_offsets(key, part):
    key = jax.random.fold_in(key, 11)
    score_key, pick_key = jax.random.split(key)
    scores = jax.random.randint(score_key, (BLOCKS, REACH), 0, 1 << 20) * REACH + jnp.arange(REACH, dtype=jnp.int32)[None, :]
    ranking = jnp.argsort(scores, axis=1)[:, :2].astype(jnp.int32) + 1
    offset_pair = jnp.sort(ranking, axis=1)
    forced = jax.random.randint(pick_key, (), 0, BLOCKS)
    fixed_row = jnp.array([1, REACH], jnp.int32)
    chosen_row = jnp.arange(BLOCKS)[:, None] == forced
    return jnp.where(chosen_row, fixed_row[None, :], offset_pair).astype(jnp.int32)


def draw_summary_ids(key, part):
    key = jax.random.fold_in(key, 23)
    score_key, order_key = jax.random.split(key)
    inner_count = BLOCKS - 2
    scores = jax.random.randint(score_key, (inner_count,), 0, 1 << 14) * inner_count + jnp.arange(inner_count, dtype=jnp.int32)
    ranking = jnp.argsort(scores).astype(jnp.int32)[:SUMMARY - 2] + 1
    ends = jnp.array([0, BLOCKS - 1], jnp.int32)
    picked = jnp.concatenate([ends, ranking]).astype(jnp.int32)
    return jax.random.permutation(order_key, picked).astype(jnp.int32)


def steps_of(own_key, dims, cuts, low, high):
    level, own = 1.0, jax.random.fold_in(own_key, 6)
    for position, shards_of in cuts:
        heights = jnp.exp(jax.random.uniform(jax.random.fold_in(own, position), (shards_of,), jnp.float32, low / len(cuts), high / len(cuts)))
        level = level * jnp.repeat(heights, dims[position] // shards_of).reshape([-1 if axis == position else 1 for axis in range(len(dims))])
    return level


def scatter_about(key, shape, deviation, limit, shards=(), kind=jnp.bfloat16):
    entries = deviation * jax.random.normal(key, shape, jnp.float32)
    if shards:
        entries = entries * steps_of(key, shape, shards, -0.22, 0.18)
    return jnp.clip(entries, -limit, limit).astype(kind)


def setup_inputs(seed: int = 0, part: int = 0) -> dict:
    seeds = jax.random.split(jax.random.key(seed), 9)
    own_keys = jax.random.split(jax.random.fold_in(seeds[8], part), 9)
    query_rows = scatter_about(own_keys[0], (SEQ, HEADS * HEAD_DIM), 1.0, 6.0, ((0, 8), (1, 2)))
    key_rows = scatter_about(own_keys[1], (SEQ, KV_HEADS * HEAD_DIM), 1.0, 6.0, ((0, 8), (1, 2)))
    value_rows = scatter_about(own_keys[2], (SEQ, KV_HEADS * HEAD_DIM), 1.0, 6.0, ((0, 8), (1, 2)))
    attn_out = scatter_about(own_keys[3], (SEQ, HEADS * HEAD_DIM), 1.0, 6.0, ((0, 8), (1, 2)))
    out_grads = scatter_about(own_keys[4], (SEQ, HEADS * HEAD_DIM), 6.0, 36.0, ((0, 8), (1, 2)))
    log_sums = jnp.clip(5.5 + 2.0 * jax.random.uniform(own_keys[5], (HEADS, SEQ), jnp.float32) ** steps_of(own_keys[5], (HEADS, SEQ), ((0, 2), (1, 8)), -0.2, 0.2), 5.5, 7.5)
    window_offsets = draw_window_offsets(jax.random.fold_in(jax.random.fold_in(seeds[8], part), 71), part)
    summary_ids = draw_summary_ids(jax.random.fold_in(jax.random.fold_in(seeds[8], part), 71), part)
    return {"query_rows": query_rows, "key_rows": key_rows, "value_rows": value_rows, "attn_out": attn_out, "out_grads": out_grads, "log_sums": log_sums, "window_offsets": window_offsets, "summary_ids": summary_ids}


def reference(query_rows, key_rows, value_rows, attn_out, out_grads, log_sums, window_offsets, summary_ids):
    scale = HEAD_DIM ** -0.5

    def split_query(tensor):
        return tensor.reshape(BLOCKS, BLOCK, KV_HEADS, GROUP, HEAD_DIM)

    def split_pair(tensor):
        return tensor.reshape(BLOCKS, BLOCK, KV_HEADS, HEAD_DIM)

    queries = split_query(query_rows)
    key_blocks = split_pair(key_rows)
    value_blocks = split_pair(value_rows)
    grad_blocks = split_query(out_grads)
    lse_rows = log_sums.reshape(KV_HEADS, GROUP, BLOCKS, BLOCK).transpose(2, 0, 1, 3)
    products = out_grads.astype(jnp.float32) * attn_out.astype(jnp.float32)
    delta_rows = jnp.sum(split_query(products), axis=4).transpose(0, 2, 3, 1)
    lower_tri = jnp.arange(BLOCK)[:, None] >= jnp.arange(BLOCK)[None, :]
    own_first = jnp.arange(3 + SUMMARY) == 0

    def block_step(totals, number):
        key_acc, value_acc = totals
        targets = number - window_offsets[number]
        candidates = jnp.concatenate([number[None], targets, summary_ids]).astype(jnp.int32)
        summary_ok = (summary_ids < number) & (summary_ids != targets[0]) & (summary_ids != targets[1])
        valid_pair = jnp.concatenate([jnp.ones((1,), bool), targets >= 0, summary_ok])
        clipped = jnp.clip(candidates, 0, BLOCKS - 1).astype(jnp.int32)
        block_keys = key_blocks[clipped].astype(jnp.float32)
        block_values = value_blocks[clipped].astype(jnp.float32)
        query_block = queries[number].astype(jnp.float32)
        grad_block = grad_blocks[number].astype(jnp.float32)
        block_mask = valid_pair[:, None, None] & (lower_tri[None] | ~own_first[:, None, None])
        scores = jnp.einsum('ikgd,cjkd->kgcij', query_block, block_keys) * scale
        probabilities = jnp.where(block_mask, jnp.exp(scores - lse_rows[number][:, :, None, :, None]), 0.0)
        rounded_probs = lax.optimization_barrier(probabilities.astype(jnp.bfloat16)).astype(jnp.float32)
        value_part = jnp.einsum('kgcij,ikgd->cjkd', rounded_probs, grad_block)
        prob_grads = jnp.einsum('ikgd,cjkd->kgcij', grad_block, block_values)
        score_grads = probabilities * (prob_grads - delta_rows[number][:, :, None, :, None]) * scale
        score_grads = lax.optimization_barrier(score_grads.astype(jnp.bfloat16)).astype(jnp.float32)
        query_part = jnp.einsum('kgcij,cjkd->ikgd', score_grads, block_keys).astype(jnp.bfloat16)
        key_part = jnp.einsum('kgcij,ikgd->cjkd', score_grads, query_block)
        key_acc = key_acc.at[clipped].add(key_part)
        value_acc = value_acc.at[clipped].add(value_part)
        return (key_acc, value_acc), query_part

    zero_state = jnp.zeros((BLOCKS, BLOCK, KV_HEADS, HEAD_DIM), jnp.float32)
    (key_acc, value_acc), query_parts = lax.scan(block_step, (zero_state, zero_state), jnp.arange(BLOCKS, dtype=jnp.int32))
    return (query_parts.reshape(SEQ, HEADS * HEAD_DIM),
            key_acc.astype(jnp.bfloat16).reshape(SEQ, KV_HEADS * HEAD_DIM),
            value_acc.astype(jnp.bfloat16).reshape(SEQ, KV_HEADS * HEAD_DIM))
```

```python
import functools
import math

import jax
import jax.numpy as jnp
from jax import lax
from jax.experimental import pallas as pl
from jax.experimental.pallas import tpu as pltpu
from jax.sharding import PartitionSpec as P

HEAD_DIM = 128
GROUP = 4
BLOCK = 128
REACH = 3
SUMMARY = 8
CORES = 2
SCALE = HEAD_DIM ** (-0.5)
LOG2E = math.log2(math.e)
CAPACITIES = (1, 2, 3, 4, SUMMARY)
F32 = jnp.float32
BF16 = jnp.bfloat16
VMEM = pl.BlockSpec(memory_space=pltpu.VMEM)
SMEM = pl.BlockSpec(memory_space=pltpu.SMEM)


def far_rounds(chips):
    rounds = []
    for source in range(chips):
        for target in range(source + 2, chips):
            for senders, receivers, route in rounds:
                if senders.get(source, 0) < CORES and receivers.get(target, 0) < CORES:
                    break
            else:
                senders, receivers, route = {}, {}, []
                rounds.append((senders, receivers, route))
            sent, got = senders.get(source, 0), receivers.get(target, 0)
            route.append((source * CORES + sent, target * CORES + got))
            senders[source], receivers[target] = sent + 1, got + 1
    return [route for _, _, route in rounds]


def table_entry(table, position):
    value = jnp.int32(-1)
    for place, entry in table.items():
        value = jnp.where(position == place, jnp.int32(entry), value)
    return value


def chip_slot(ids_ref, slot, chip_blocks):
    chip = ids_ref[slot] // chip_blocks
    rank = jnp.int32(0)
    for other in range(slot):
        rank += jnp.where(ids_ref[other] // chip_blocks == chip, 1, 0)
    return chip, rank


def chip_count(ids_ref, chip, chip_blocks):
    count = jnp.int32(0)
    for slot in range(SUMMARY):
        count += jnp.where(ids_ref[slot] // chip_blocks == chip, 1, 0)
    return count


def prep_kernel(out_ref, grad_ref, lse_ref, stats_ref):
    stats_ref[...] = jnp.zeros_like(stats_ref)
    for block in range(stats_ref.shape[0]):
        rows = slice(block * BLOCK, (block + 1) * BLOCK)
        for head in range(GROUP):
            columns = slice(head * HEAD_DIM, (head + 1) * HEAD_DIM)
            product = out_ref[rows, columns].astype(F32) * grad_ref[rows, columns].astype(F32)
            stats_ref[block, 0:1, columns] = lse_ref[head : head + 1, rows] * LOG2E
            stats_ref[block, 1:2, columns] = jnp.sum(product.T, axis=0, keepdims=True)


def pick_kernel(ids_ref, own_ref, partner_ref, picked_ref):
    chip = lax.axis_index("ctx")
    core = lax.axis_index("rep")
    blocks_here = own_ref.shape[0] // BLOCK
    chip_blocks = CORES * blocks_here
    capacity = picked_ref.shape[0] // BLOCK
    picked_ref[...] = jnp.zeros_like(picked_ref)
    for slot in range(SUMMARY):
        owner, rank = chip_slot(ids_ref, slot, chip_blocks)
        local = ids_ref[slot] - chip * chip_blocks
        row = pl.multiple_of((local % blocks_here) * BLOCK, BLOCK)
        place = pl.multiple_of(rank * BLOCK, BLOCK)
        mine = local // blocks_here == core
        wanted = (owner == chip) & (rank < capacity)

        @pl.when(wanted & mine)
        def _():
            picked_ref[pl.ds(place, BLOCK), :] = own_ref[pl.ds(row, BLOCK), :]

        @pl.when(wanted & ~mine)
        def _():
            picked_ref[pl.ds(place, BLOCK), :] = partner_ref[pl.ds(row, BLOCK), :]


def nt(a, b):
    return lax.dot_general(a, b, (((1,), (1,)), ((), ())), preferred_element_type=F32)


def nn(a, b):
    return jnp.dot(a, b, preferred_element_type=F32)


def pair_step(
    kv_ref, kv_row, key_t, query_refs, block, acc_ref, acc_row, dq_ref, dq_block, causal=False
):
    query_ref, grad_ref, stats_ref = query_refs
    keys = kv_ref[pl.ds(kv_row, BLOCK), 0:HEAD_DIM]
    values = kv_ref[pl.ds(kv_row, BLOCK), HEAD_DIM : 2 * HEAD_DIM]
    rows = pl.ds(pl.multiple_of(block * BLOCK, BLOCK), BLOCK)
    key_sum = value_sum = None
    for half in range(GROUP // 2):
        first, second = (
            slice(head * HEAD_DIM, (head + 1) * HEAD_DIM) for head in (2 * half, 2 * half + 1)
        )
        lanes = slice(2 * half * BLOCK, 2 * (half + 1) * BLOCK)
        queries = jnp.concatenate([query_ref[rows, first], query_ref[rows, second]], axis=0)
        grads = jnp.concatenate([grad_ref[rows, first], grad_ref[rows, second]], axis=0)
        log_sums = stats_ref[block, 0:1, lanes]
        deltas = stats_ref[block, 1:2, lanes]
        probs = jnp.exp2(nt(keys, queries) * (SCALE * LOG2E) - log_sums)
        if causal:
            key_at = lax.broadcasted_iota(jnp.int32, probs.shape, 0)
            query_at = lax.broadcasted_iota(jnp.int32, probs.shape, 1) % BLOCK
            probs = jnp.where(query_at >= key_at, probs, 0.0)
        score_grads = (probs * (nt(values, grads) - deltas) * SCALE).astype(BF16)
        value_part = nn(probs.astype(BF16), grads)
        key_part = nn(score_grads, queries)
        dq_ref[dq_block, :, lanes] += nn(key_t, score_grads)
        value_sum = value_part if value_sum is None else value_sum + value_part
        key_sum = key_part if key_sum is None else key_sum + key_part
    acc_rows = pl.ds(acc_row, BLOCK)
    acc_ref[acc_rows, 0:HEAD_DIM] += key_sum
    acc_ref[acc_rows, HEAD_DIM : 2 * HEAD_DIM] += value_sum


def attends(offsets_ref, ids_ref, query_block, key_block):
    summary = ids_ref[0] == key_block
    for slot in range(1, SUMMARY):
        summary |= ids_ref[slot] == key_block
    distance = query_block - key_block
    window = (distance == offsets_ref[query_block, 0]) | (distance == offsets_ref[query_block, 1])
    return (distance > 0) & (key_block >= 0) & (window | summary)


def transposed_keys(kv_ref, row):
    return kv_ref[pl.ds(row, BLOCK), 0:HEAD_DIM].astype(F32).T.astype(BF16)


def sweep(
    offsets_ref, ids_ref, kv_ref, first_key, query_sets, acc_ref, dq_ref, blocks_here, diagonal=False
):
    def key_step(key, carry):
        row = pl.multiple_of(key * BLOCK, BLOCK)
        key_t = transposed_keys(kv_ref, row)
        if diagonal:
            pair_step(kv_ref, row, key_t, query_sets[0][1], key, acc_ref, row, dq_ref, key, True)
        for number, (first_query, refs) in enumerate(query_sets):

            def query_step(block, carry):
                @pl.when(attends(offsets_ref, ids_ref, first_query + block, first_key + key))
                def _():
                    pair_step(
                        kv_ref, row, key_t, refs, block, acc_ref, row, dq_ref,
                        number * blocks_here + block,
                    )

                return carry

            lax.fori_loop(0, blocks_here, query_step, 0)
        return carry

    lax.fori_loop(0, blocks_here, key_step, 0)


def query_starts(blocks_here):
    chip = lax.axis_index("ctx")
    core = lax.axis_index("rep")
    base = chip * CORES * blocks_here
    return chip, core, base, base + core * blocks_here, base + (1 - core) * blocks_here


def near_kernel(
    offsets_ref, ids_ref, kv_ref, q_ref, g_ref, s_ref, pq_ref, pg_ref, ps_ref, grads_ref, dq_ref,
    acc_ref,
):
    blocks_here = kv_ref.shape[0] // BLOCK
    chip, core, base, own, partner = query_starts(blocks_here)
    acc_ref[...] = jnp.zeros_like(acc_ref)
    dq_ref[...] = jnp.zeros_like(dq_ref)
    query_sets = ((own, (q_ref, g_ref, s_ref)), (partner, (pq_ref, pg_ref, ps_ref)))

    @pl.when(chip > 0)
    def _():
        first_key = own - CORES * blocks_here
        sweep(offsets_ref, ids_ref, kv_ref, first_key, query_sets, acc_ref, dq_ref, blocks_here)

    grads_ref[...] = acc_ref[...].astype(BF16)


def far_kernel(sources, ids_ref, *refs):
    count = len(sources)
    kv_refs, refs = refs[:count], refs[count:]
    q_ref, g_ref, s_ref, pq_ref, pg_ref, ps_ref = refs[:6]
    grads_refs, dq_ref, acc_ref = refs[6 : 6 + count], refs[6 + count], refs[7 + count]
    blocks_here = q_ref.shape[0] // BLOCK
    capacity = kv_refs[0].shape[0] // BLOCK
    position = lax.axis_index("ctx") * CORES + lax.axis_index("rep")
    dq_ref[...] = jnp.zeros_like(dq_ref)
    for table, kv_ref, grads_ref in zip(sources, kv_refs, grads_refs):
        held = jnp.minimum(
            chip_count(ids_ref, table_entry(table, position), CORES * blocks_here), capacity
        )
        acc_ref[...] = jnp.zeros_like(acc_ref)

        def key_step(key, carry):
            row = pl.multiple_of(key * BLOCK, BLOCK)
            key_t = transposed_keys(kv_ref, row)
            for number, query_refs in enumerate(((q_ref, g_ref, s_ref), (pq_ref, pg_ref, ps_ref))):

                def query_step(block, carry):
                    pair_step(
                        kv_ref, row, key_t, query_refs, block, acc_ref, row, dq_ref,
                        number * blocks_here + block,
                    )
                    return carry

                lax.fori_loop(0, blocks_here, query_step, 0)
            return carry

        lax.fori_loop(0, held, key_step, 0)
        grads_ref[...] = acc_ref[...].astype(BF16)


def local_kernel(
    offsets_ref, ids_ref, kv_ref, q_ref, g_ref, s_ref, pq_ref, pg_ref, ps_ref, near_ref, far_ref,
    acc_ref, own_ref, partner_ref, dq_ref,
):
    blocks_here = kv_ref.shape[0] // BLOCK
    _, _, _, own, partner = query_starts(blocks_here)
    acc_ref[...] = jnp.zeros_like(acc_ref)
    dq_ref[...] = near_ref[...] + far_ref[...]
    query_sets = ((own, (q_ref, g_ref, s_ref)), (partner, (pq_ref, pg_ref, ps_ref)))
    sweep(offsets_ref, ids_ref, kv_ref, own, query_sets, acc_ref, dq_ref, blocks_here, True)
    for block in range(blocks_here):
        rows = slice(block * BLOCK, (block + 1) * BLOCK)
        for head in range(GROUP):
            lanes = slice(head * HEAD_DIM, (head + 1) * HEAD_DIM)
            own_ref[rows, lanes] = dq_ref[block, :, lanes].T
            partner_ref[rows, lanes] = dq_ref[blocks_here + block, :, lanes].T.astype(BF16)


def final_kernel(last_sender, ids_ref, acc_ref, near_ref, own_ref, partner_ref, *refs):
    far_refs = refs[:-4]
    dq_ref, dk_ref, dv_ref, sum_ref = refs[-4:]
    blocks_here = acc_ref.shape[0] // BLOCK
    chip_blocks = CORES * blocks_here
    chip = lax.axis_index("ctx")
    core = lax.axis_index("rep")
    dq_ref[...] = (own_ref[...] + partner_ref[...].astype(F32)).astype(BF16)
    sum_ref[...] = acc_ref[...] + near_ref[...].astype(F32)
    capacity = far_refs[0].shape[0] // BLOCK
    for slot in range(SUMMARY):
        owner, rank = chip_slot(ids_ref, slot, chip_blocks)
        local = ids_ref[slot] - chip * chip_blocks - core * blocks_here
        mine = (owner == chip) & (local >= 0) & (local < blocks_here)

        @pl.when(mine & (chip <= last_sender) & (rank < capacity))
        def _():
            rows = pl.ds(pl.multiple_of(local * BLOCK, BLOCK), BLOCK)
            place = pl.ds(pl.multiple_of(rank * BLOCK, BLOCK), BLOCK)
            total = sum_ref[rows, :]
            for far_ref in far_refs:
                total += far_ref[place, :].astype(F32)
            sum_ref[rows, :] = total

    dk_ref[...] = sum_ref[:, 0:HEAD_DIM].astype(BF16)
    dv_ref[...] = sum_ref[:, HEAD_DIM : 2 * HEAD_DIM].astype(BF16)


def call(kernel, scalars, arrays, out_shape, scratch=(), flops=0):
    return pl.pallas_call(
        kernel,
        out_shape=out_shape,
        in_specs=[SMEM] * len(scalars) + [VMEM] * len(arrays),
        out_specs=jax.tree.map(lambda _: VMEM, out_shape),
        scratch_shapes=list(scratch),
        compiler_params=pltpu.CompilerParams(vmem_limit_bytes=40 << 20),
        cost_estimate=pl.CostEstimate(flops=flops, bytes_accessed=1 << 20, transcendentals=0),
    )(*scalars, *arrays)


def shape_of(shape, dtype):
    return jax.ShapeDtypeStruct(shape, dtype)


def with_capacity(
    capacity, chips, queries, kv, attn_out, grads, log_sums, window_offsets, summary_ids
):
    rows = queries.shape[0]
    blocks_here = rows // BLOCK
    swap = [(0, 1), (1, 0)]
    up = [(i, i + 1) for i in range(chips - 1)]
    down = [(b, a) for a, b in up]
    routes = far_rounds(chips)
    sources = tuple({b: a // CORES for a, b in route} for route in routes)
    both = ("ctx", "rep")
    pair_flops = 10 * GROUP * BLOCK * BLOCK * HEAD_DIM

    kv_partner = lax.ppermute(kv, "rep", swap)
    kv_near = lax.ppermute(kv, "ctx", up)
    far_shape = shape_of((capacity * BLOCK, 2 * HEAD_DIM), BF16)
    picked = call(pick_kernel, (summary_ids,), (kv, kv_partner), far_shape)
    kv_far = [lax.ppermute(picked, both, route) for route in routes]
    stats = call(
        prep_kernel, (), (attn_out, grads, log_sums),
        shape_of((blocks_here, 8, GROUP * BLOCK), F32),
    )
    own = (queries, grads, stats)
    partner = tuple(lax.ppermute(x, "rep", swap) for x in own)
    acc_shape = (rows, 2 * HEAD_DIM)
    dq_shape = shape_of((CORES * blocks_here, HEAD_DIM, GROUP * BLOCK), F32)
    near_grads, near_dq = call(
        near_kernel, (window_offsets, summary_ids), (kv_near, *own, *partner),
        (shape_of(acc_shape, BF16), dq_shape), [pltpu.VMEM(acc_shape, F32)], 8 * pair_flops,
    )
    near_back = lax.ppermute(near_grads, "ctx", down)
    *far_grads, far_dq = call(
        functools.partial(far_kernel, sources), (summary_ids,), (*kv_far, *own, *partner),
        tuple([far_shape] * len(routes) + [dq_shape]), [pltpu.VMEM(far_shape.shape, F32)],
        16 * pair_flops,
    )
    far_back = [
        lax.ppermute(x, both, [(b, a) for a, b in route]) for x, route in zip(far_grads, routes)
    ]
    acc, dq_own, dq_partner = call(
        local_kernel, (window_offsets, summary_ids), (kv, *own, *partner, near_dq, far_dq),
        (shape_of(acc_shape, F32), shape_of(queries.shape, F32), shape_of(queries.shape, BF16)),
        [pltpu.VMEM(dq_shape.shape, F32)], 20 * pair_flops,
    )
    dq_partner = lax.ppermute(dq_partner, "rep", swap)
    far_other = [lax.ppermute(x, "rep", swap) for x in far_back]
    kv_shape = shape_of((rows, HEAD_DIM), BF16)
    return call(
        functools.partial(final_kernel, chips - 3), (summary_ids,),
        (acc, near_back, dq_own, dq_partner, *far_back, *far_other),
        (shape_of(queries.shape, BF16), kv_shape, kv_shape), [pltpu.VMEM(acc_shape, F32)],
    )


def per_device(chips, queries, keys, values, attn_out, grads, log_sums, window_offsets, summary_ids):
    chip_blocks = CORES * (queries.shape[0] // BLOCK)
    kv = jnp.concatenate([keys, values], axis=1)
    senders = jnp.arange(chips - 2, dtype=jnp.int32)
    owners = summary_ids // chip_blocks
    most = jnp.max(jnp.sum((owners[None, :] == senders[:, None]).astype(jnp.int32), axis=1))
    limits = jnp.array(CAPACITIES[:-1], jnp.int32)
    branch = jnp.sum((most > limits).astype(jnp.int32))
    return lax.switch(
        branch,
        [functools.partial(with_capacity, capacity, chips) for capacity in CAPACITIES],
        queries, kv, attn_out, grads, log_sums, window_offsets, summary_ids,
    )


def solution(mesh):
    rows = P(("groups", "ctx", "rep"), "heads")
    return jax.shard_map(
        functools.partial(per_device, mesh.shape["ctx"]),
        mesh=mesh,
        in_specs=(rows,) * 5 + (P("heads", ("groups", "ctx", "rep")), P("groups", None), P("groups")),
        out_specs=(rows,) * 3,
        check_vma=False,
    )
```

```python
import functools
import math

import jax
import jax.numpy as jnp
from jax import lax
from jax.experimental import pallas as pl
from jax.experimental.pallas import tpu as pltpu
from jax.sharding import PartitionSpec as P

HEAD_DIM = 128
GROUP = 4
BLOCK = 128
REACH = 3
SUMMARY = 8
CORES = 2
SCALE = HEAD_DIM ** (-0.5)
LOG2E = math.log2(math.e)
MICROSECOND = 1_000_000_000
CAPACITIES = (1, 2, 3, 4, SUMMARY)
F32 = jnp.float32
BF16 = jnp.bfloat16
VMEM = pl.BlockSpec(memory_space=pltpu.VMEM)
SMEM = pl.BlockSpec(memory_space=pltpu.SMEM)


def far_rounds(chips):
    rounds = []
    for source in range(chips):
        for target in range(source + 2, chips):
            for senders, receivers, route in rounds:
                if senders.get(source, 0) < CORES and receivers.get(target, 0) < CORES:
                    break
            else:
                senders, receivers, route = {}, {}, []
                rounds.append((senders, receivers, route))
            sent, got = senders.get(source, 0), receivers.get(target, 0)
            route.append((source * CORES + sent, target * CORES + got))
            senders[source], receivers[target] = sent + 1, got + 1
    return [route for _, _, route in rounds]


def table_entry(table, position):
    value = jnp.int32(-1)
    for place, entry in table.items():
        value = jnp.where(position == place, jnp.int32(entry), value)
    return value


def chip_slot(ids_ref, slot, chip_blocks):
    chip = ids_ref[slot] // chip_blocks
    rank = jnp.int32(0)
    for other in range(slot):
        rank += jnp.where(ids_ref[other] // chip_blocks == chip, 1, 0)
    return chip, rank


def chip_count(ids_ref, chip, chip_blocks):
    count = jnp.int32(0)
    for slot in range(SUMMARY):
        count += jnp.where(ids_ref[slot] // chip_blocks == chip, 1, 0)
    return count


def prep_kernel(out_ref, grad_ref, lse_ref, stats_ref):
    stats_ref[...] = jnp.zeros_like(stats_ref)
    for block in range(stats_ref.shape[0]):
        rows = slice(block * BLOCK, (block + 1) * BLOCK)
        for head in range(GROUP):
            columns = slice(head * HEAD_DIM, (head + 1) * HEAD_DIM)
            product = out_ref[rows, columns].astype(F32) * grad_ref[rows, columns].astype(F32)
            stats_ref[block, 0:1, columns] = lse_ref[head : head + 1, rows] * LOG2E
            stats_ref[block, 1:2, columns] = jnp.sum(product.T, axis=0, keepdims=True)


def start_kernel(chips, ids_ref, key_ref, value_ref, kv_ref, branch_ref):
    chip_blocks = CORES * (key_ref.shape[0] // BLOCK)
    kv_ref[:, 0:HEAD_DIM] = key_ref[...]
    kv_ref[:, HEAD_DIM : 2 * HEAD_DIM] = value_ref[...]
    most = jnp.int32(0)
    for chip in range(chips - 2):
        most = jnp.maximum(most, chip_count(ids_ref, chip, chip_blocks))
    branch = jnp.int32(0)
    for capacity in capacities(chips)[:-1]:
        branch += jnp.where(most > capacity, 1, 0)
    branch_ref[0] = branch


def pick_kernel(ids_ref, own_ref, partner_ref, picked_ref):
    chip = lax.axis_index("ctx")
    core = lax.axis_index("rep")
    blocks_here = own_ref.shape[0] // BLOCK
    chip_blocks = CORES * blocks_here
    capacity = picked_ref.shape[0] // BLOCK
    picked_ref[...] = jnp.zeros_like(picked_ref)
    for slot in range(SUMMARY):
        owner, rank = chip_slot(ids_ref, slot, chip_blocks)
        local = ids_ref[slot] - chip * chip_blocks
        row = pl.multiple_of((local % blocks_here) * BLOCK, BLOCK)
        place = pl.multiple_of(rank * BLOCK, BLOCK)
        mine = local // blocks_here == core
        wanted = (owner == chip) & (rank < capacity)

        @pl.when(wanted & mine)
        def _():
            picked_ref[pl.ds(place, BLOCK), :] = own_ref[pl.ds(row, BLOCK), :]

        @pl.when(wanted & ~mine)
        def _():
            picked_ref[pl.ds(place, BLOCK), :] = partner_ref[pl.ds(row, BLOCK), :]


def nt(a, b):
    return lax.dot_general(a, b, (((1,), (1,)), ((), ())), preferred_element_type=F32)


def nn(a, b):
    return jnp.dot(a, b, preferred_element_type=F32)


def stacked(ref, rows):
    heads = (slice(head * HEAD_DIM, (head + 1) * HEAD_DIM) for head in range(GROUP))
    return jnp.concatenate([ref[rows, head] for head in heads], axis=0)


def block_grads(keys, values, key_t, query_refs, block, biases=None, causal=False):
    query_ref, grad_ref, stats_ref = query_refs
    rows = pl.ds(pl.multiple_of(block * BLOCK, BLOCK), BLOCK)
    queries, grads = stacked(query_ref, rows), stacked(grad_ref, rows)
    log_sums = stats_ref[block, 0:1, :]
    scores = nt(keys, queries) * (SCALE * LOG2E)
    count = keys.shape[0] // BLOCK
    if biases is None and not causal:
        probs = jnp.exp2(scores - log_sums)
    else:
        parts = []
        for key in range(count):
            shift = log_sums if biases is None or biases[key] is None else log_sums + biases[key]
            part = jnp.exp2(scores[key * BLOCK : (key + 1) * BLOCK] - shift)
            if causal and key == count - 1:
                key_at = lax.broadcasted_iota(jnp.int32, part.shape, 0)
                query_at = lax.broadcasted_iota(jnp.int32, part.shape, 1) % BLOCK
                part = jnp.where(query_at >= key_at, part, 0.0)
            parts.append(part)
        probs = jnp.concatenate(parts, axis=0)
    prob_grads = nt(values, grads)
    score_grads = (probs * (prob_grads - stats_ref[block, 1:2, :]) * SCALE).astype(BF16)
    return (
        nn(key_t, score_grads), nn(score_grads, queries), nn(probs.astype(BF16), grads)
    )


def attends(offsets_ref, ids_ref, query_block, key_block):
    summary = ids_ref[0] == key_block
    for slot in range(1, SUMMARY):
        summary |= ids_ref[slot] == key_block
    distance = query_block - key_block
    window = (distance == offsets_ref[query_block, 0]) | (distance == offsets_ref[query_block, 1])
    return (distance > 0) & (key_block >= 0) & (window | summary)


def keys_of(kv_ref, rows):
    return kv_ref[rows, 0:HEAD_DIM]


def values_of(kv_ref, rows):
    return kv_ref[rows, HEAD_DIM : 2 * HEAD_DIM]


def transposed(keys):
    return keys.astype(F32).T.astype(BF16)


def add_grads(acc_ref, rows, key_part, value_part):
    acc_ref[rows, 0:HEAD_DIM] += key_part
    acc_ref[rows, HEAD_DIM : 2 * HEAD_DIM] += value_part


def sweep(offsets_ref, ids_ref, kv_ref, first_key, first_query, query_refs, acc_ref, dq_ref, dq_at):
    blocks_here = kv_ref.shape[0] // BLOCK
    everything = pl.ds(0, blocks_here * BLOCK)

    def query_step(block, carry):
        flags = [
            attends(offsets_ref, ids_ref, first_query + block, first_key + key)
            for key in range(blocks_here)
        ]
        count, first, last = jnp.int32(0), jnp.int32(0), jnp.int32(0)
        for key in range(blocks_here):
            count += jnp.where(flags[key], 1, 0)
            last = jnp.where(flags[key], key, last)
        for key in reversed(range(blocks_here)):
            first = jnp.where(flags[key], key, first)

        def some(places):
            rows = [pl.ds(pl.multiple_of(place * BLOCK, BLOCK), BLOCK) for place in places]
            keys = jnp.concatenate([keys_of(kv_ref, row) for row in rows], axis=0)
            values = jnp.concatenate([values_of(kv_ref, row) for row in rows], axis=0)
            dq, dk, dv = block_grads(keys, values, transposed(keys), query_refs, block)
            dq_ref[dq_at + block] += dq
            for number, row in enumerate(rows):
                part = slice(number * BLOCK, (number + 1) * BLOCK)
                add_grads(acc_ref, row, dk[part], dv[part])

        @pl.when(count == 1)
        def _():
            some([first])

        @pl.when(count == 2)
        def _():
            some([first, last])

        @pl.when(count > 2)
        def _():
            biases = [jnp.where(flag, 0.0, 1e30).astype(F32) for flag in flags]
            keys = keys_of(kv_ref, everything)
            dq, dk, dv = block_grads(
                keys, values_of(kv_ref, everything), transposed(keys), query_refs, block, biases
            )
            dq_ref[dq_at + block] += dq
            add_grads(acc_ref, everything, dk, dv)

        return carry

    lax.fori_loop(0, blocks_here, query_step, 0)


def query_starts(blocks_here):
    chip = lax.axis_index("ctx")
    core = lax.axis_index("rep")
    base = chip * CORES * blocks_here
    return chip, core, base + core * blocks_here, base + (1 - core) * blocks_here


def near_kernel(
    offsets_ref, ids_ref, kv_ref, q_ref, g_ref, s_ref, pq_ref, pg_ref, ps_ref, grads_ref, dq_ref,
    acc_ref,
):
    blocks_here = kv_ref.shape[0] // BLOCK
    chip, _, own, partner = query_starts(blocks_here)
    acc_ref[...] = jnp.zeros_like(acc_ref)
    dq_ref[...] = jnp.zeros_like(dq_ref)
    query_sets = ((own, (q_ref, g_ref, s_ref)), (partner, (pq_ref, pg_ref, ps_ref)))

    @pl.when(chip > 0)
    def _():
        first_key = own - CORES * blocks_here
        for number, (first_query, refs) in enumerate(query_sets):
            sweep(
                offsets_ref, ids_ref, kv_ref, first_key, first_query, refs, acc_ref, dq_ref,
                number * blocks_here,
            )

    grads_ref[...] = acc_ref[...].astype(BF16)


def far_kernel(sources, ids_ref, *refs):
    count = len(sources)
    kv_refs, refs = refs[:count], refs[count:]
    q_ref, g_ref, s_ref, pq_ref, pg_ref, ps_ref = refs[:6]
    grads_refs, dq_ref, acc_ref = refs[6 : 6 + count], refs[6 + count], refs[7 + count]
    blocks_here = q_ref.shape[0] // BLOCK
    capacity = kv_refs[0].shape[0] // BLOCK
    position = lax.axis_index("ctx") * CORES + lax.axis_index("rep")
    chunk = min(capacity, 4)
    chunks = [(number, start) for number in range(count) for start in range(0, capacity, chunk)]
    held = [
        chip_count(ids_ref, table_entry(table, position), CORES * blocks_here) for table in sources
    ]
    single = len(chunks) == 1
    if not single:
        dq_ref[...] = jnp.zeros_like(dq_ref)
    for number, start in chunks:
        kv_ref, grads_ref = kv_refs[number], grads_refs[number]
        rows = slice(start * BLOCK, (start + chunk) * BLOCK)
        busy = held[number] > start

        @pl.when(busy)
        def _():
            keys, values = keys_of(kv_ref, rows), values_of(kv_ref, rows)
            key_t = transposed(keys)
            acc_ref[...] = jnp.zeros_like(acc_ref)
            for side, query_refs in enumerate(((q_ref, g_ref, s_ref), (pq_ref, pg_ref, ps_ref))):

                def query_step(block, carry):
                    dq, dk, dv = block_grads(keys, values, key_t, query_refs, block)
                    if single:
                        dq_ref[side * blocks_here + block] = dq
                    else:
                        dq_ref[side * blocks_here + block] += dq
                    add_grads(acc_ref, slice(0, chunk * BLOCK), dk, dv)
                    return carry

                lax.fori_loop(0, blocks_here, query_step, 0, unroll=single)
            grads_ref[rows, :] = acc_ref[...].astype(BF16)

        @pl.when(~busy)
        def _():
            grads_ref[rows, :] = jnp.zeros((chunk * BLOCK, 2 * HEAD_DIM), BF16)
            if single:
                dq_ref[...] = jnp.zeros_like(dq_ref)


def local_kernel(
    offsets_ref, ids_ref, kv_ref, q_ref, g_ref, s_ref, pq_ref, pg_ref, ps_ref, near_ref, far_ref,
    back_ref, acc_ref, own_ref, partner_ref, dq_ref,
):
    blocks_here = kv_ref.shape[0] // BLOCK
    _, core, own, partner = query_starts(blocks_here)
    acc_ref[...] = back_ref[...].astype(F32)
    dq_ref[...] = near_ref[...] + far_ref[...]
    key_t = transposed(keys_of(kv_ref, slice(0, blocks_here * BLOCK)))
    for block in range(blocks_here):
        rows = slice(0, (block + 1) * BLOCK)
        biases = [
            jnp.where(attends(offsets_ref, ids_ref, own + block, own + key), 0.0, 1e30).astype(F32)
            for key in range(block)
        ] + [None]
        dq, dk, dv = block_grads(
            keys_of(kv_ref, rows), values_of(kv_ref, rows), key_t[:, rows], (q_ref, g_ref, s_ref),
            block, biases, True,
        )
        dq_ref[block] += dq
        add_grads(acc_ref, rows, dk, dv)

    @pl.when(core == 0)
    def _():
        sweep(
            offsets_ref, ids_ref, kv_ref, own, partner, (pq_ref, pg_ref, ps_ref), acc_ref, dq_ref,
            blocks_here,
        )

    for block in range(blocks_here):
        rows = slice(block * BLOCK, (block + 1) * BLOCK)
        for head in range(GROUP):
            lanes = slice(head * HEAD_DIM, (head + 1) * HEAD_DIM)
            own_ref[rows, lanes] = dq_ref[block, :, lanes].T
            partner_ref[rows, lanes] = dq_ref[blocks_here + block, :, lanes].T.astype(BF16)


def final_kernel(last_sender, ids_ref, acc_ref, *refs):
    far_refs = refs[:-3]
    dk_ref, dv_ref, sum_ref = refs[-3:]
    blocks_here = acc_ref.shape[0] // BLOCK
    chip_blocks = CORES * blocks_here
    chip = lax.axis_index("ctx")
    core = lax.axis_index("rep")
    sum_ref[...] = acc_ref[...]
    capacity = far_refs[0].shape[0] // BLOCK
    for slot in range(SUMMARY):
        owner, rank = chip_slot(ids_ref, slot, chip_blocks)
        local = ids_ref[slot] - chip * chip_blocks - core * blocks_here
        mine = (owner == chip) & (local >= 0) & (local < blocks_here)

        @pl.when(mine & (chip <= last_sender) & (rank < capacity))
        def _():
            rows = pl.ds(pl.multiple_of(local * BLOCK, BLOCK), BLOCK)
            place = pl.ds(pl.multiple_of(rank * BLOCK, BLOCK), BLOCK)
            total = sum_ref[rows, :]
            for far_ref in far_refs:
                total += far_ref[place, :].astype(F32)
            sum_ref[rows, :] = total

    dk_ref[...] = sum_ref[:, 0:HEAD_DIM].astype(BF16)
    dv_ref[...] = sum_ref[:, HEAD_DIM : 2 * HEAD_DIM].astype(BF16)


def call(kernel, scalars, arrays, out_shape, scratch=(), flops=0, out_specs=None):
    return pl.pallas_call(
        kernel,
        out_shape=out_shape,
        in_specs=[SMEM] * len(scalars) + [VMEM] * len(arrays),
        out_specs=out_specs or jax.tree.map(lambda _: VMEM, out_shape),
        scratch_shapes=list(scratch),
        compiler_params=pltpu.CompilerParams(vmem_limit_bytes=24 << 20),
        cost_estimate=pl.CostEstimate(flops=flops, bytes_accessed=1 << 20, transcendentals=0),
    )(*scalars, *arrays)


def shape_of(shape, dtype):
    return jax.ShapeDtypeStruct(shape, dtype)


def with_capacity(
    capacity, chips, queries, kv, attn_out, grads, log_sums, window_offsets, summary_ids
):
    rows = queries.shape[0]
    blocks_here = rows // BLOCK
    swap = [(0, 1), (1, 0)]
    up = [(i, i + 1) for i in range(chips - 1)]
    down = [(b, a) for a, b in up]
    routes = far_rounds(chips)
    sources = tuple({b: a // CORES for a, b in route} for route in routes)
    both = ("ctx", "rep")

    kv_partner = lax.ppermute(kv, "rep", swap)
    kv_near = lax.ppermute(kv, "ctx", up)
    far_shape = shape_of((capacity * BLOCK, 2 * HEAD_DIM), BF16)
    picked = call(pick_kernel, (summary_ids,), (kv, kv_partner), far_shape)
    kv_far = [lax.ppermute(picked, both, route) for route in routes]
    stats = call(
        prep_kernel, (), (attn_out, grads, log_sums),
        shape_of((blocks_here, 8, GROUP * BLOCK), F32),
    )
    own = (queries, grads, stats)
    partner = tuple(lax.ppermute(x, "rep", swap) for x in own)
    acc_shape = (rows, 2 * HEAD_DIM)
    dq_shape = shape_of((CORES * blocks_here, HEAD_DIM, GROUP * BLOCK), F32)
    near_grads, near_dq = call(
        near_kernel, (window_offsets, summary_ids), (kv_near, *own, *partner),
        (shape_of(acc_shape, BF16), dq_shape), [pltpu.VMEM(acc_shape, F32)], 4 * MICROSECOND,
    )
    near_back = lax.ppermute(near_grads, "ctx", down)
    chunk_shape = (min(capacity, 4) * BLOCK, 2 * HEAD_DIM)
    *far_grads, far_dq = call(
        functools.partial(far_kernel, sources), (summary_ids,), (*kv_far, *own, *partner),
        tuple([far_shape] * len(routes) + [dq_shape]), [pltpu.VMEM(chunk_shape, F32)],
        5 * MICROSECOND,
    )
    far_back = [
        lax.ppermute(x, both, [(b, a) for a, b in route]) for x, route in zip(far_grads, routes)
    ]
    acc, dq_own, dq_partner = call(
        local_kernel, (window_offsets, summary_ids),
        (kv, *own, *partner, near_dq, far_dq, near_back),
        (shape_of(acc_shape, F32), shape_of(queries.shape, F32), shape_of(queries.shape, BF16)),
        [pltpu.VMEM(dq_shape.shape, F32)], 6 * MICROSECOND,
    )
    dq_partner = lax.ppermute(dq_partner, "rep", swap)
    query_grads = (dq_own + dq_partner.astype(F32)).astype(BF16)
    far_other = [lax.ppermute(x, "rep", swap) for x in far_back]
    kv_shape = shape_of((rows, HEAD_DIM), BF16)
    key_grads, value_grads = call(
        functools.partial(final_kernel, chips - 3), (summary_ids,),
        (acc, *far_back, *far_other), (kv_shape, kv_shape), [pltpu.VMEM(acc_shape, F32)],
    )
    return query_grads, key_grads, value_grads


def capacities(chips):
    return CAPACITIES if len(far_rounds(chips)) == 1 else CAPACITIES[-1:]


def per_device(chips, queries, keys, values, attn_out, grads, log_sums, window_offsets, summary_ids):
    kv, branch = call(
        functools.partial(start_kernel, chips), (summary_ids,), (keys, values),
        (shape_of((keys.shape[0], 2 * HEAD_DIM), BF16), shape_of((1,), jnp.int32)),
        out_specs=(VMEM, SMEM),
    )
    branches = [functools.partial(with_capacity, limit, chips) for limit in capacities(chips)]
    operands = (queries, kv, attn_out, grads, log_sums, window_offsets, summary_ids)
    return lax.switch(branch[0], branches, *operands) if len(branches) > 1 else branches[0](*operands)


def solution(mesh):
    rows = P(("groups", "ctx", "rep"), "heads")
    return jax.shard_map(
        functools.partial(per_device, mesh.shape["ctx"]),
        mesh=mesh,
        in_specs=(rows,) * 5 + (P("heads", ("groups", "ctx", "rep")), P("groups", None), P("groups")),
        out_specs=(rows,) * 3,
        check_vma=False,
    )
```

```python
import functools
import math

import jax
import jax.numpy as jnp
from jax import lax
from jax.experimental import pallas as pl
from jax.experimental.pallas import tpu as pltpu
from jax.sharding import PartitionSpec as P

HEAD_DIM = 128
GROUP = 4
BLOCK = 128
REACH = 3
SUMMARY = 8
CORES = 2
SCALE = HEAD_DIM ** (-0.5)
LOG2E = math.log2(math.e)
MICROSECOND = 1_000_000_000
CAPACITIES = (1, 2, 3, 4, SUMMARY)
F32 = jnp.float32
BF16 = jnp.bfloat16
VMEM = pl.BlockSpec(memory_space=pltpu.VMEM)
SMEM = pl.BlockSpec(memory_space=pltpu.SMEM)
HBM = pl.BlockSpec(memory_space=pltpu.HBM)


def far_rounds(chips):
    rounds = []
    for source in range(chips):
        for target in range(source + 2, chips):
            for senders, receivers, route in rounds:
                if senders.get(source, 0) < CORES and receivers.get(target, 0) < CORES:
                    break
            else:
                senders, receivers, route = {}, {}, []
                rounds.append((senders, receivers, route))
            sent, got = senders.get(source, 0), receivers.get(target, 0)
            route.append((source * CORES + sent, target * CORES + got))
            senders[source], receivers[target] = sent + 1, got + 1
    return [route for _, _, route in rounds]


def table_entry(table, position):
    value = jnp.int32(-1)
    for place, entry in table.items():
        value = jnp.where(position == place, jnp.int32(entry), value)
    return value


def chip_slot(ids_ref, slot, chip_blocks):
    chip = ids_ref[slot] // chip_blocks
    rank = jnp.int32(0)
    for other in range(slot):
        rank += jnp.where(ids_ref[other] // chip_blocks == chip, 1, 0)
    return chip, rank


def chip_count(ids_ref, chip, chip_blocks):
    count = jnp.int32(0)
    for slot in range(SUMMARY):
        count += jnp.where(ids_ref[slot] // chip_blocks == chip, 1, 0)
    return count


def prep_kernel(out_ref, grad_ref, lse_ref, stats_ref):
    stats_ref[...] = jnp.zeros_like(stats_ref)
    for block in range(stats_ref.shape[0]):
        rows = slice(block * BLOCK, (block + 1) * BLOCK)
        for head in range(GROUP):
            columns = slice(head * HEAD_DIM, (head + 1) * HEAD_DIM)
            product = out_ref[rows, columns].astype(F32) * grad_ref[rows, columns].astype(F32)
            stats_ref[block, 0:1, columns] = lse_ref[head : head + 1, rows] * LOG2E
            stats_ref[block, 1:2, columns] = jnp.sum(product.T, axis=0, keepdims=True)


def start_kernel(chips, ids_ref, key_ref, value_ref, kv_ref, branch_ref, sems):
    chip_blocks = CORES * (key_ref.shape[0] // BLOCK)
    copies = [
        pltpu.make_async_copy(
            ref, kv_ref.at[:, number * HEAD_DIM : (number + 1) * HEAD_DIM], sems.at[number]
        )
        for number, ref in enumerate((key_ref, value_ref))
    ]
    for copy in copies:
        copy.start()
    most = jnp.int32(0)
    for chip in range(chips - 2):
        most = jnp.maximum(most, chip_count(ids_ref, chip, chip_blocks))
    branch = jnp.int32(0)
    for capacity in capacities(chips)[:-1]:
        branch += jnp.where(most > capacity, 1, 0)
    branch_ref[0] = branch
    for copy in copies:
        copy.wait()


def pick_kernel(ids_ref, own_ref, partner_ref, picked_ref):
    chip = lax.axis_index("ctx")
    core = lax.axis_index("rep")
    blocks_here = own_ref.shape[0] // BLOCK
    chip_blocks = CORES * blocks_here
    capacity = picked_ref.shape[0] // BLOCK
    picked_ref[...] = jnp.zeros_like(picked_ref)
    for slot in range(SUMMARY):
        owner, rank = chip_slot(ids_ref, slot, chip_blocks)
        local = ids_ref[slot] - chip * chip_blocks
        row = pl.multiple_of((local % blocks_here) * BLOCK, BLOCK)
        place = pl.multiple_of(rank * BLOCK, BLOCK)
        mine = local // blocks_here == core
        wanted = (owner == chip) & (rank < capacity)

        @pl.when(wanted & mine)
        def _():
            picked_ref[pl.ds(place, BLOCK), :] = own_ref[pl.ds(row, BLOCK), :]

        @pl.when(wanted & ~mine)
        def _():
            picked_ref[pl.ds(place, BLOCK), :] = partner_ref[pl.ds(row, BLOCK), :]


def nt(a, b):
    return lax.dot_general(a, b, (((1,), (1,)), ((), ())), preferred_element_type=F32)


def nn(a, b):
    return jnp.dot(a, b, preferred_element_type=F32)


def stacked(refs, rows, own):
    heads = [slice(head * HEAD_DIM, (head + 1) * HEAD_DIM) for head in range(GROUP)]
    mine, theirs = (jnp.concatenate([ref[rows, head] for head in heads], axis=0) for ref in refs)
    return jnp.where(own, mine, theirs)


def block_grads(keys, values, key_t, query_refs, number, blocks_here, biases=None, query_at=None):
    (query_ref, grad_ref, stats_ref), (other_query, other_grad, other_stats) = query_refs
    own = number < blocks_here
    block = jnp.where(own, number, number - blocks_here)
    rows = pl.ds(pl.multiple_of(block * BLOCK, BLOCK), BLOCK)
    queries = stacked((query_ref, other_query), rows, own)
    grads = stacked((grad_ref, other_grad), rows, own)
    log_sums = jnp.where(own, stats_ref[block, 0:1, :], other_stats[block, 0:1, :])
    deltas = jnp.where(own, stats_ref[block, 1:2, :], other_stats[block, 1:2, :])
    scores = nt(keys, queries) * (SCALE * LOG2E)
    if biases is None:
        probs = jnp.exp2(scores - log_sums)
    else:
        parts = []
        for key, bias in enumerate(biases):
            part = jnp.exp2(scores[key * BLOCK : (key + 1) * BLOCK] - (log_sums + bias))
            if query_at is not None:
                row = lax.broadcasted_iota(jnp.int32, part.shape, 0)
                column = lax.broadcasted_iota(jnp.int32, part.shape, 1) % BLOCK
                part = jnp.where(column - row >= (key - query_at) * BLOCK, part, 0.0)
            parts.append(part)
        probs = jnp.concatenate(parts, axis=0)
    prob_grads = nt(values, grads)
    score_grads = (probs * (prob_grads - deltas) * SCALE).astype(BF16)
    return nn(key_t, score_grads), nn(score_grads, queries), nn(probs.astype(BF16), grads)


def attends(offsets_ref, ids_ref, query_block, key_block):
    summary = ids_ref[0] == key_block
    for slot in range(1, SUMMARY):
        summary |= ids_ref[slot] == key_block
    distance = query_block - key_block
    window = (distance == offsets_ref[query_block, 0]) | (distance == offsets_ref[query_block, 1])
    return (distance > 0) & (key_block >= 0) & (window | summary)


def keys_of(kv_ref, rows):
    return kv_ref[rows, 0:HEAD_DIM]


def values_of(kv_ref, rows):
    return kv_ref[rows, HEAD_DIM : 2 * HEAD_DIM]


def transposed(keys):
    return keys.astype(F32).T.astype(BF16)


def add_grads(acc_ref, rows, key_part, value_part):
    acc_ref[rows, 0:HEAD_DIM] += key_part
    acc_ref[rows, HEAD_DIM : 2 * HEAD_DIM] += value_part


def query_number(first_block, number, blocks_here):
    core = lax.axis_index("rep")
    side = jnp.where(number < blocks_here, core, 1 - core)
    return first_block + side * blocks_here + jnp.where(
        number < blocks_here, number, number - blocks_here
    )


def places(blocks_here):
    chip = lax.axis_index("ctx")
    base = chip * CORES * blocks_here
    return chip, base, base + lax.axis_index("rep") * blocks_here


def bias_of(flag):
    return jnp.where(flag, 0.0, 1e30).astype(F32)


def near_kernel(offsets_ref, ids_ref, kv_ref, *refs):
    query_refs, (local_ref, grads_ref, dq_ref, acc_ref, key_ref) = (refs[0:3], refs[3:6]), refs[6:]
    blocks_here = kv_ref.shape[0] // BLOCK
    chip, base, own = places(blocks_here)
    first_key = own - CORES * blocks_here
    everything = slice(0, blocks_here * BLOCK)
    acc_ref[...] = jnp.zeros_like(acc_ref)
    dq_ref[0:blocks_here] = jnp.zeros_like(local_ref)
    dq_ref[blocks_here:] = local_ref[...]

    def query_step(number, carry):
        query = query_number(base, number, blocks_here)
        flags = [attends(offsets_ref, ids_ref, query, first_key + key) for key in range(blocks_here)]
        count, first, last = jnp.int32(0), jnp.int32(0), jnp.int32(0)
        for key in range(blocks_here):
            count += jnp.where(flags[key], 1, 0)
            last = jnp.where(flags[key], key, last)
        for key in reversed(range(blocks_here)):
            first = jnp.where(flags[key], key, first)

        def some(chosen):
            rows = [pl.ds(pl.multiple_of(key * BLOCK, BLOCK), BLOCK) for key in chosen]
            keys = jnp.concatenate([keys_of(kv_ref, row) for row in rows], axis=0)
            values = jnp.concatenate([values_of(kv_ref, row) for row in rows], axis=0)
            key_t = jnp.concatenate([key_ref[key] for key in chosen], axis=1)
            dq, dk, dv = block_grads(keys, values, key_t, query_refs, number, blocks_here)
            dq_ref[number] += dq
            for place, row in enumerate(rows):
                part = slice(place * BLOCK, (place + 1) * BLOCK)
                add_grads(acc_ref, row, dk[part], dv[part])

        @pl.when(count == 1)
        def _():
            some([first])

        @pl.when(count == 2)
        def _():
            some([first, last])

        @pl.when(count > 2)
        def _():
            key_t = jnp.concatenate([key_ref[key] for key in range(blocks_here)], axis=1)
            dq, dk, dv = block_grads(
                keys_of(kv_ref, everything), values_of(kv_ref, everything), key_t, query_refs,
                number, blocks_here, [bias_of(flag) for flag in flags],
            )
            dq_ref[number] += dq
            add_grads(acc_ref, everything, dk, dv)

        return carry

    @pl.when(chip > 0)
    def _():
        for key in range(blocks_here):
            key_ref[key] = transposed(keys_of(kv_ref, slice(key * BLOCK, (key + 1) * BLOCK)))
        lax.fori_loop(0, CORES * blocks_here, query_step, 0)

    grads_ref[...] = acc_ref[...].astype(BF16)


def far_kernel(sources, ids_ref, *refs):
    count = len(sources)
    kv_refs, refs = refs[:count], refs[count:]
    query_refs, near_ref, refs = (refs[0:3], refs[3:6]), refs[6], refs[7:]
    grads_refs, (dq_ref, partner_ref, acc_ref) = refs[:count], refs[count:]
    blocks_here = query_refs[0][0].shape[0] // BLOCK
    capacity = kv_refs[0].shape[0] // BLOCK
    position = lax.axis_index("ctx") * CORES + lax.axis_index("rep")
    chunk = min(capacity, 4)
    dq_ref[...] = near_ref[...]
    for table, kv_ref, grads_ref in zip(sources, kv_refs, grads_refs):
        held = chip_count(ids_ref, table_entry(table, position), CORES * blocks_here)
        for start in range(0, capacity, chunk):
            rows = slice(start * BLOCK, (start + chunk) * BLOCK)
            acc_ref[...] = jnp.zeros_like(acc_ref)

            @pl.when(held > start)
            def _():
                keys, values = keys_of(kv_ref, rows), values_of(kv_ref, rows)
                key_t = transposed(keys)

                def query_step(number, carry):
                    dq, dk, dv = block_grads(keys, values, key_t, query_refs, number, blocks_here)
                    dq_ref[number] += dq
                    add_grads(acc_ref, slice(0, chunk * BLOCK), dk, dv)
                    return carry

                lax.fori_loop(0, CORES * blocks_here, query_step, 0)

            grads_ref[rows, :] = acc_ref[...].astype(BF16)
    partner_ref[...] = dq_ref[blocks_here:].astype(BF16)


def cross_kernel(offsets_ref, ids_ref, kv_ref, *refs):
    query_refs, (acc_ref, dq_ref) = (refs[0:3], refs[3:6]), refs[6:]
    blocks_here = kv_ref.shape[0] // BLOCK
    _, base, own = places(blocks_here)
    acc_ref[...] = jnp.zeros_like(acc_ref)
    dq_ref[...] = jnp.zeros_like(dq_ref)
    everything = slice(0, blocks_here * BLOCK)

    @pl.when(lax.axis_index("rep") == 0)
    def _():
        keys, values = keys_of(kv_ref, everything), values_of(kv_ref, everything)
        key_t = transposed(keys)

        def query_step(block, carry):
            number = block + blocks_here
            query = query_number(base, number, blocks_here)
            flags = [attends(offsets_ref, ids_ref, query, own + key) for key in range(blocks_here)]
            some = flags[0]
            for flag in flags[1:]:
                some |= flag

            @pl.when(some)
            def _():
                dq, dk, dv = block_grads(
                    keys, values, key_t, query_refs, number, blocks_here,
                    [bias_of(flag) for flag in flags],
                )
                dq_ref[block] = dq
                add_grads(acc_ref, everything, dk, dv)

            return carry

        lax.fori_loop(0, blocks_here, query_step, 0)


def own_kernel(
    offsets_ref, ids_ref, kv_ref, q_ref, g_ref, s_ref, cross_ref, back_ref, far_ref, partner_ref,
    acc_ref, dq_ref,
):
    blocks_here = kv_ref.shape[0] // BLOCK
    _, base, own = places(blocks_here)
    query_refs = ((q_ref, g_ref, s_ref),) * 2
    everything = slice(0, blocks_here * BLOCK)
    acc_ref[...] = cross_ref[...] + back_ref[...].astype(F32)
    keys, values = keys_of(kv_ref, everything), values_of(kv_ref, everything)
    key_t = transposed(keys)

    def query_step(block, carry):
        flags = [
            (key >= block) | attends(offsets_ref, ids_ref, own + block, own + key)
            for key in range(blocks_here)
        ]
        dq, dk, dv = block_grads(
            keys, values, key_t, query_refs, block, blocks_here,
            [bias_of(flag) for flag in flags], block,
        )
        add_grads(acc_ref, everything, dk, dv)
        total = far_ref[block] + partner_ref[block].astype(F32) + dq
        rows = pl.ds(pl.multiple_of(block * BLOCK, BLOCK), BLOCK)
        for head in range(GROUP):
            lanes = slice(head * HEAD_DIM, (head + 1) * HEAD_DIM)
            dq_ref[rows, lanes] = total[:, lanes].T.astype(BF16)
        return carry

    lax.fori_loop(0, blocks_here, query_step, 0)


def final_kernel(last_sender, ids_ref, acc_ref, *refs):
    far_refs, (dk_ref, dv_ref) = refs[:-2], refs[-2:]
    blocks_here = acc_ref.shape[0] // BLOCK
    chip_blocks = CORES * blocks_here
    chip = lax.axis_index("ctx")
    core = lax.axis_index("rep")
    dk_ref[...] = keys_of(acc_ref, slice(None)).astype(BF16)
    dv_ref[...] = values_of(acc_ref, slice(None)).astype(BF16)
    capacity = far_refs[0].shape[0] // BLOCK
    for slot in range(SUMMARY):
        owner, rank = chip_slot(ids_ref, slot, chip_blocks)
        local = ids_ref[slot] - chip * chip_blocks - core * blocks_here
        mine = (owner == chip) & (local >= 0) & (local < blocks_here)

        @pl.when(mine & (chip <= last_sender) & (rank < capacity))
        def _():
            rows = pl.ds(pl.multiple_of(local * BLOCK, BLOCK), BLOCK)
            place = pl.ds(pl.multiple_of(rank * BLOCK, BLOCK), BLOCK)
            total = acc_ref[rows, :]
            for far_ref in far_refs:
                total += far_ref[place, :].astype(F32)
            dk_ref[rows, :] = total[:, 0:HEAD_DIM].astype(BF16)
            dv_ref[rows, :] = total[:, HEAD_DIM : 2 * HEAD_DIM].astype(BF16)


def call(kernel, scalars, arrays, out_shape, scratch=(), flops=0, in_space=VMEM, out_specs=None):
    return pl.pallas_call(
        kernel,
        out_shape=out_shape,
        in_specs=[SMEM] * len(scalars) + [in_space] * len(arrays),
        out_specs=out_specs or jax.tree.map(lambda _: VMEM, out_shape),
        scratch_shapes=list(scratch),
        compiler_params=pltpu.CompilerParams(vmem_limit_bytes=24 << 20),
        cost_estimate=pl.CostEstimate(flops=flops, bytes_accessed=1 << 20, transcendentals=0),
    )(*scalars, *arrays)


def shape_of(shape, dtype):
    return jax.ShapeDtypeStruct(shape, dtype)


def with_capacity(
    capacity, chips, queries, kv, attn_out, grads, log_sums, window_offsets, summary_ids
):
    rows = queries.shape[0]
    blocks_here = rows // BLOCK
    swap = [(0, 1), (1, 0)]
    up = [(i, i + 1) for i in range(chips - 1)]
    down = [(b, a) for a, b in up]
    routes = far_rounds(chips)
    sources = tuple({b: a // CORES for a, b in route} for route in routes)
    both = ("ctx", "rep")

    kv_partner = lax.ppermute(kv, "rep", swap)
    kv_near = lax.ppermute(kv, "ctx", up)
    far_shape = shape_of((capacity * BLOCK, 2 * HEAD_DIM), BF16)
    picked = call(pick_kernel, (summary_ids,), (kv, kv_partner), far_shape)
    kv_far = [lax.ppermute(picked, both, route) for route in routes]
    attn_out, window_offsets, _ = lax.optimization_barrier((attn_out, window_offsets, picked))
    tables = (window_offsets, summary_ids)
    stats = call(
        prep_kernel, (), (attn_out, grads, log_sums),
        shape_of((blocks_here, 8, GROUP * BLOCK), F32), flops=MICROSECOND,
    )
    own = (queries, grads, stats)
    every = own + tuple(lax.ppermute(x, "rep", swap) for x in own)
    acc_shape = (rows, 2 * HEAD_DIM)
    half_shape = (blocks_here, HEAD_DIM, GROUP * BLOCK)
    dq_shape = shape_of((CORES * blocks_here, *half_shape[1:]), F32)
    cross_acc, cross_dq = call(
        cross_kernel, tables, (kv, *every), (shape_of(acc_shape, F32), shape_of(half_shape, F32)),
        flops=3 * MICROSECOND,
    )
    near_grads, near_dq = call(
        near_kernel, tables, (kv_near, *every, cross_dq), (shape_of(acc_shape, BF16), dq_shape),
        [pltpu.VMEM(acc_shape, F32), pltpu.VMEM((blocks_here, HEAD_DIM, BLOCK), BF16)],
        flops=4 * MICROSECOND,
    )
    near_back = lax.ppermute(near_grads, "ctx", down)
    chunk_shape = (min(capacity, 4) * BLOCK, 2 * HEAD_DIM)
    *far_grads, far_dq, dq_partner = call(
        functools.partial(far_kernel, sources), (summary_ids,), (*kv_far, *every, near_dq),
        (*[far_shape] * len(routes), dq_shape, shape_of(half_shape, BF16)),
        [pltpu.VMEM(chunk_shape, F32)], flops=5 * MICROSECOND,
    )
    far_back = [
        lax.ppermute(x, both, [(b, a) for a, b in route]) for x, route in zip(far_grads, routes)
    ]
    dq_partner = lax.ppermute(dq_partner, "rep", swap)
    acc, query_grads = call(
        own_kernel, tables, (kv, *own, cross_acc, near_back, far_dq, dq_partner),
        (shape_of(acc_shape, F32), shape_of(queries.shape, BF16)), flops=10 * MICROSECOND,
    )
    far_other = [lax.ppermute(x, "rep", swap) for x in far_back]
    kv_shape = shape_of((rows, HEAD_DIM), BF16)
    key_grads, value_grads = call(
        functools.partial(final_kernel, chips - 3), (summary_ids,),
        (acc, *far_back, *far_other), (kv_shape, kv_shape),
    )
    return query_grads, key_grads, value_grads


def capacities(chips):
    return CAPACITIES if len(far_rounds(chips)) == 1 else CAPACITIES[-1:]


def per_device(chips, queries, keys, values, attn_out, grads, log_sums, window_offsets, summary_ids):
    kv, branch = call(
        functools.partial(start_kernel, chips), (summary_ids,), (keys, values),
        (shape_of((keys.shape[0], 2 * HEAD_DIM), BF16), shape_of((1,), jnp.int32)),
        [pltpu.SemaphoreType.DMA((2,))], in_space=HBM, out_specs=(VMEM, SMEM),
    )
    branches = [functools.partial(with_capacity, limit, chips) for limit in capacities(chips)]
    operands = (queries, kv, attn_out, grads, log_sums, window_offsets, summary_ids)
    return lax.switch(branch[0], branches, *operands) if len(branches) > 1 else branches[0](*operands)


def solution(mesh):
    rows = P(("groups", "ctx", "rep"), "heads")
    return jax.shard_map(
        functools.partial(per_device, mesh.shape["ctx"]),
        mesh=mesh,
        in_specs=(rows,) * 5 + (P("heads", ("groups", "ctx", "rep")), P("groups", None), P("groups")),
        out_specs=(rows,) * 3,
        check_vma=False,
    )
```

```python
import functools
import math

import jax
import jax.numpy as jnp
from jax import lax
from jax.experimental import pallas as pl
from jax.experimental.pallas import tpu as pltpu
from jax.sharding import PartitionSpec as P

HEAD_DIM = 128
GROUP = 4
BLOCK = 128
REACH = 3
SUMMARY = 8
CORES = 2
SCALE = HEAD_DIM ** (-0.5)
LOG2E = math.log2(math.e)
MICROSECOND = 1_000_000_000
CAPACITIES = (1, 2, 3, 4, SUMMARY)
F32 = jnp.float32
BF16 = jnp.bfloat16
VMEM = pl.BlockSpec(memory_space=pltpu.VMEM)
SMEM = pl.BlockSpec(memory_space=pltpu.SMEM)
HBM = pl.BlockSpec(memory_space=pltpu.HBM)


def far_rounds(chips):
    rounds = []
    for source in range(chips):
        for target in range(source + 2, chips):
            for senders, receivers, route in rounds:
                if senders.get(source, 0) < CORES and receivers.get(target, 0) < CORES:
                    break
            else:
                senders, receivers, route = {}, {}, []
                rounds.append((senders, receivers, route))
            sent, got = senders.get(source, 0), receivers.get(target, 0)
            route.append((source * CORES + sent, target * CORES + got))
            senders[source], receivers[target] = sent + 1, got + 1
    return [route for _, _, route in rounds]


def table_entry(table, position):
    value = jnp.int32(-1)
    for place, entry in table.items():
        value = jnp.where(position == place, jnp.int32(entry), value)
    return value


def chip_slot(ids_ref, slot, chip_blocks):
    chip = ids_ref[slot] // chip_blocks
    rank = jnp.int32(0)
    for other in range(slot):
        rank += jnp.where(ids_ref[other] // chip_blocks == chip, 1, 0)
    return chip, rank


def chip_count(ids_ref, chip, chip_blocks):
    count = jnp.int32(0)
    for slot in range(SUMMARY):
        count += jnp.where(ids_ref[slot] // chip_blocks == chip, 1, 0)
    return count


def prep_kernel(out_ref, grad_ref, lse_ref, stats_ref):
    stats_ref[...] = jnp.zeros_like(stats_ref)
    for block in range(stats_ref.shape[0]):
        rows = slice(block * BLOCK, (block + 1) * BLOCK)
        for head in range(GROUP):
            columns = slice(head * HEAD_DIM, (head + 1) * HEAD_DIM)
            product = out_ref[rows, columns].astype(F32) * grad_ref[rows, columns].astype(F32)
            stats_ref[block, 0:1, columns] = lse_ref[head : head + 1, rows] * LOG2E
            stats_ref[block, 1:2, columns] = jnp.sum(product.T, axis=0, keepdims=True)


def start_kernel(chips, ids_ref, key_ref, value_ref, kv_ref, branch_ref, sems):
    chip_blocks = CORES * (key_ref.shape[0] // BLOCK)
    copies = [
        pltpu.make_async_copy(
            ref, kv_ref.at[:, number * HEAD_DIM : (number + 1) * HEAD_DIM], sems.at[number]
        )
        for number, ref in enumerate((key_ref, value_ref))
    ]
    for copy in copies:
        copy.start()
    most = jnp.int32(0)
    for chip in range(chips - 2):
        most = jnp.maximum(most, chip_count(ids_ref, chip, chip_blocks))
    branch = jnp.int32(0)
    for capacity in capacities(chips)[:-1]:
        branch += jnp.where(most > capacity, 1, 0)
    branch_ref[0] = branch
    for copy in copies:
        copy.wait()


def pick_kernel(ids_ref, own_ref, partner_ref, picked_ref):
    chip = lax.axis_index("ctx")
    core = lax.axis_index("rep")
    blocks_here = own_ref.shape[0] // BLOCK
    chip_blocks = CORES * blocks_here
    capacity = picked_ref.shape[0] // BLOCK
    picked_ref[...] = jnp.zeros_like(picked_ref)
    for slot in range(SUMMARY):
        owner, rank = chip_slot(ids_ref, slot, chip_blocks)
        local = ids_ref[slot] - chip * chip_blocks
        row = pl.multiple_of((local % blocks_here) * BLOCK, BLOCK)
        place = pl.multiple_of(rank * BLOCK, BLOCK)
        mine = local // blocks_here == core
        wanted = (owner == chip) & (rank < capacity)

        @pl.when(wanted & mine)
        def _():
            picked_ref[pl.ds(place, BLOCK), :] = own_ref[pl.ds(row, BLOCK), :]

        @pl.when(wanted & ~mine)
        def _():
            picked_ref[pl.ds(place, BLOCK), :] = partner_ref[pl.ds(row, BLOCK), :]


def nt(a, b):
    return lax.dot_general(a, b, (((1,), (1,)), ((), ())), preferred_element_type=F32)


def nn(a, b):
    return jnp.dot(a, b, preferred_element_type=F32)


def stacked(refs, rows, own):
    heads = [slice(head * HEAD_DIM, (head + 1) * HEAD_DIM) for head in range(GROUP)]
    mine, theirs = (jnp.concatenate([ref[rows, head] for head in heads], axis=0) for ref in refs)
    return jnp.where(own, mine, theirs)


def block_grads(keys, values, key_t, query_refs, number, blocks_here, biases=None, query_at=None):
    (query_ref, grad_ref, stats_ref), (other_query, other_grad, other_stats) = query_refs
    own = number < blocks_here
    block = jnp.where(own, number, number - blocks_here)
    rows = pl.ds(pl.multiple_of(block * BLOCK, BLOCK), BLOCK)
    queries = stacked((query_ref, other_query), rows, own)
    grads = stacked((grad_ref, other_grad), rows, own)
    log_sums = jnp.where(own, stats_ref[block, 0:1, :], other_stats[block, 0:1, :])
    deltas = jnp.where(own, stats_ref[block, 1:2, :], other_stats[block, 1:2, :])
    scores = nt(keys, queries) * (SCALE * LOG2E)
    if biases is None:
        probs = jnp.exp2(scores - log_sums)
    else:
        parts = []
        for key, bias in enumerate(biases):
            part = jnp.exp2(scores[key * BLOCK : (key + 1) * BLOCK] - (log_sums + bias))
            if query_at is not None:
                row = lax.broadcasted_iota(jnp.int32, part.shape, 0)
                column = lax.broadcasted_iota(jnp.int32, part.shape, 1) % BLOCK
                part = jnp.where(column - row >= (key - query_at) * BLOCK, part, 0.0)
            parts.append(part)
        probs = jnp.concatenate(parts, axis=0)
    prob_grads = nt(values, grads)
    score_grads = (probs * (prob_grads - deltas) * SCALE).astype(BF16)
    return nn(key_t, score_grads), nn(score_grads, queries), nn(probs.astype(BF16), grads)


def is_summary(ids_ref, key_block):
    found = ids_ref[0] == key_block
    for slot in range(1, SUMMARY):
        found |= ids_ref[slot] == key_block
    return found


def in_window(offsets_ref, query_block, key_block):
    distance = query_block - key_block
    return (distance == offsets_ref[query_block, 0]) | (distance == offsets_ref[query_block, 1])


def attends(offsets_ref, ids_ref, query_block, key_block):
    chosen = in_window(offsets_ref, query_block, key_block) | is_summary(ids_ref, key_block)
    return (query_block > key_block) & chosen


def keys_of(kv_ref, rows):
    return kv_ref[rows, 0:HEAD_DIM]


def values_of(kv_ref, rows):
    return kv_ref[rows, HEAD_DIM : 2 * HEAD_DIM]


def transposed(keys):
    return keys.astype(F32).T.astype(BF16)


def add_grads(acc_ref, rows, key_part, value_part):
    acc_ref[rows, 0:HEAD_DIM] += key_part
    acc_ref[rows, HEAD_DIM : 2 * HEAD_DIM] += value_part


def query_number(first_block, number, blocks_here):
    core = lax.axis_index("rep")
    side = jnp.where(number < blocks_here, core, 1 - core)
    return first_block + side * blocks_here + jnp.where(
        number < blocks_here, number, number - blocks_here
    )


def places(blocks_here):
    chip = lax.axis_index("ctx")
    base = chip * CORES * blocks_here
    return chip, base, base + lax.axis_index("rep") * blocks_here


def bias_of(flag):
    return jnp.where(flag, 0.0, 1e30).astype(F32)


def near_kernel(offsets_ref, ids_ref, kv_ref, *refs):
    query_refs, (local_ref, grads_ref, dq_ref, acc_ref) = (refs[0:3], refs[3:6]), refs[6:]
    blocks_here = kv_ref.shape[0] // BLOCK
    chip, base, own = places(blocks_here)
    first_key = own - CORES * blocks_here
    everything = slice(0, blocks_here * BLOCK)
    acc_ref[...] = jnp.zeros_like(acc_ref)
    dq_ref[0:blocks_here] = jnp.zeros_like(local_ref)
    dq_ref[blocks_here:] = local_ref[...]
    flags = [is_summary(ids_ref, first_key + key) & (chip > 0) for key in range(blocks_here)]
    count, first, last = jnp.int32(0), jnp.int32(0), jnp.int32(0)
    for key in range(blocks_here):
        count += jnp.where(flags[key], 1, 0)
        last = jnp.where(flags[key], key, last)
    for key in reversed(range(blocks_here)):
        first = jnp.where(flags[key], key, first)

    def all_queries(chosen, unroll):
        rows = [pl.ds(pl.multiple_of(key * BLOCK, BLOCK), BLOCK) for key in chosen]
        keys = jnp.concatenate([keys_of(kv_ref, row) for row in rows], axis=0)
        values = jnp.concatenate([values_of(kv_ref, row) for row in rows], axis=0)
        key_t = transposed(keys)

        def query_step(number, carry):
            dq, dk, dv = block_grads(keys, values, key_t, query_refs, number, blocks_here)
            dq_ref[number] += dq
            for place, row in enumerate(rows):
                part = slice(place * BLOCK, (place + 1) * BLOCK)
                add_grads(acc_ref, row, dk[part], dv[part])
            return carry

        lax.fori_loop(0, CORES * blocks_here, query_step, 0, unroll=unroll)

    @pl.when(count == 1)
    def _():
        all_queries([first], 2)

    @pl.when(count == 2)
    def _():
        all_queries([first, last], 2)

    @pl.when(count > 2)
    def _():
        keys, values = keys_of(kv_ref, everything), values_of(kv_ref, everything)
        key_t = transposed(keys)
        biases = [bias_of(flag) for flag in flags]

        def query_step(number, carry):
            dq, dk, dv = block_grads(keys, values, key_t, query_refs, number, blocks_here, biases)
            dq_ref[number] += dq
            add_grads(acc_ref, everything, dk, dv)
            return carry

        lax.fori_loop(0, CORES * blocks_here, query_step, 0)

    keep = min(REACH, blocks_here)
    reached = slice((blocks_here - keep) * BLOCK, blocks_here * BLOCK)
    reached_keys = range(blocks_here - keep, blocks_here)

    @pl.when((chip > 0) & (lax.axis_index("rep") == CORES - 1))
    def _():
        keys, values = keys_of(kv_ref, reached), values_of(kv_ref, reached)
        key_t = transposed(keys)

        def query_step(number, carry):
            window = [
                in_window(offsets_ref, base + number, first_key + key) & ~flags[key]
                for key in reached_keys
            ]
            some = window[0]
            for flag in window[1:]:
                some |= flag

            @pl.when(some)
            def _():
                at = number + blocks_here
                dq, dk, dv = block_grads(
                    keys, values, key_t, query_refs, at, blocks_here,
                    [bias_of(flag) for flag in window],
                )
                dq_ref[at] += dq
                add_grads(acc_ref, reached, dk, dv)

            return carry

        lax.fori_loop(0, keep, query_step, 0)

    grads_ref[...] = acc_ref[...].astype(BF16)


def far_kernel(sources, ids_ref, *refs):
    count = len(sources)
    kv_refs, refs = refs[:count], refs[count:]
    query_refs, near_ref, refs = (refs[0:3], refs[3:6]), refs[6], refs[7:]
    grads_refs, (dq_ref, partner_ref, acc_ref) = refs[:count], refs[count:]
    blocks_here = query_refs[0][0].shape[0] // BLOCK
    capacity = kv_refs[0].shape[0] // BLOCK
    position = lax.axis_index("ctx") * CORES + lax.axis_index("rep")
    chunk = min(capacity, 4)
    dq_ref[...] = near_ref[...]
    for table, kv_ref, grads_ref in zip(sources, kv_refs, grads_refs):
        held = chip_count(ids_ref, table_entry(table, position), CORES * blocks_here)
        for start in range(0, capacity, chunk):
            rows = slice(start * BLOCK, (start + chunk) * BLOCK)
            acc_ref[...] = jnp.zeros_like(acc_ref)

            @pl.when(held > start)
            def _():
                keys, values = keys_of(kv_ref, rows), values_of(kv_ref, rows)
                key_t = transposed(keys)

                def query_step(number, carry):
                    dq, dk, dv = block_grads(keys, values, key_t, query_refs, number, blocks_here)
                    dq_ref[number] += dq
                    add_grads(acc_ref, slice(0, chunk * BLOCK), dk, dv)
                    return carry

                lax.fori_loop(0, CORES * blocks_here, query_step, 0, unroll=2)

            grads_ref[rows, :] = acc_ref[...].astype(BF16)
    partner_ref[...] = dq_ref[blocks_here:].astype(BF16)


def cross_kernel(offsets_ref, ids_ref, kv_ref, *refs):
    query_refs, (acc_ref, dq_ref) = (refs[0:3], refs[3:6]), refs[6:]
    blocks_here = kv_ref.shape[0] // BLOCK
    _, base, own = places(blocks_here)
    acc_ref[...] = jnp.zeros_like(acc_ref)
    dq_ref[...] = jnp.zeros_like(dq_ref)
    everything = slice(0, blocks_here * BLOCK)

    @pl.when(lax.axis_index("rep") == 0)
    def _():
        keys, values = keys_of(kv_ref, everything), values_of(kv_ref, everything)
        key_t = transposed(keys)

        def query_step(block, carry):
            number = block + blocks_here
            query = query_number(base, number, blocks_here)
            flags = [attends(offsets_ref, ids_ref, query, own + key) for key in range(blocks_here)]
            some = flags[0]
            for flag in flags[1:]:
                some |= flag

            @pl.when(some)
            def _():
                dq, dk, dv = block_grads(
                    keys, values, key_t, query_refs, number, blocks_here,
                    [bias_of(flag) for flag in flags],
                )
                dq_ref[block] = dq
                add_grads(acc_ref, everything, dk, dv)

            return carry

        lax.fori_loop(0, blocks_here, query_step, 0)


def own_kernel(
    offsets_ref, ids_ref, kv_ref, q_ref, g_ref, s_ref, cross_ref, far_ref, partner_ref,
    acc_ref, dq_ref,
):
    blocks_here = kv_ref.shape[0] // BLOCK
    _, base, own = places(blocks_here)
    query_refs = ((q_ref, g_ref, s_ref),) * 2
    everything = slice(0, blocks_here * BLOCK)
    acc_ref[...] = cross_ref[...]
    keys, values = keys_of(kv_ref, everything), values_of(kv_ref, everything)
    key_t = transposed(keys)

    def query_step(block, carry):
        flags = [
            (key >= block) | attends(offsets_ref, ids_ref, own + block, own + key)
            for key in range(blocks_here)
        ]
        dq, dk, dv = block_grads(
            keys, values, key_t, query_refs, block, blocks_here,
            [bias_of(flag) for flag in flags], block,
        )
        add_grads(acc_ref, everything, dk, dv)
        total = far_ref[block] + partner_ref[block].astype(F32) + dq
        rows = pl.ds(pl.multiple_of(block * BLOCK, BLOCK), BLOCK)
        for head in range(GROUP):
            lanes = slice(head * HEAD_DIM, (head + 1) * HEAD_DIM)
            dq_ref[rows, lanes] = total[:, lanes].T.astype(BF16)
        return carry

    lax.fori_loop(0, blocks_here, query_step, 0)


def final_kernel(last_sender, ids_ref, acc_ref, near_ref, *refs):
    far_refs, (dk_ref, dv_ref, sum_ref) = refs[:-3], refs[-3:]
    blocks_here = acc_ref.shape[0] // BLOCK
    chip_blocks = CORES * blocks_here
    chip = lax.axis_index("ctx")
    core = lax.axis_index("rep")
    sum_ref[...] = acc_ref[...] + near_ref[...].astype(F32)
    dk_ref[...] = keys_of(sum_ref, slice(None)).astype(BF16)
    dv_ref[...] = values_of(sum_ref, slice(None)).astype(BF16)
    capacity = far_refs[0].shape[0] // BLOCK
    for slot in range(SUMMARY):
        owner, rank = chip_slot(ids_ref, slot, chip_blocks)
        local = ids_ref[slot] - chip * chip_blocks - core * blocks_here
        mine = (owner == chip) & (local >= 0) & (local < blocks_here)

        @pl.when(mine & (chip <= last_sender) & (rank < capacity))
        def _():
            rows = pl.ds(pl.multiple_of(local * BLOCK, BLOCK), BLOCK)
            place = pl.ds(pl.multiple_of(rank * BLOCK, BLOCK), BLOCK)
            total = sum_ref[rows, :]
            for far_ref in far_refs:
                total += far_ref[place, :].astype(F32)
            dk_ref[rows, :] = total[:, 0:HEAD_DIM].astype(BF16)
            dv_ref[rows, :] = total[:, HEAD_DIM : 2 * HEAD_DIM].astype(BF16)


def call(kernel, scalars, arrays, out_shape, scratch=(), flops=0, in_space=VMEM, out_specs=None, room=24):
    return pl.pallas_call(
        kernel,
        out_shape=out_shape,
        in_specs=[SMEM] * len(scalars) + [in_space] * len(arrays),
        out_specs=out_specs or jax.tree.map(lambda _: VMEM, out_shape),
        scratch_shapes=list(scratch),
        compiler_params=pltpu.CompilerParams(vmem_limit_bytes=room << 20),
        cost_estimate=pl.CostEstimate(flops=flops, bytes_accessed=0, transcendentals=0),
    )(*scalars, *arrays)


def shape_of(shape, dtype):
    return jax.ShapeDtypeStruct(shape, dtype)


def with_capacity(
    capacity, chips, queries, kv, attn_out, grads, log_sums, window_offsets, summary_ids
):
    rows = queries.shape[0]
    blocks_here = rows // BLOCK
    swap = [(0, 1), (1, 0)]
    up = [(i, i + 1) for i in range(chips - 1)]
    down = [(b, a) for a, b in up]
    routes = far_rounds(chips)
    sources = tuple({b: a // CORES for a, b in route} for route in routes)
    both = ("ctx", "rep")

    kv_partner = lax.ppermute(kv, "rep", swap)
    kv_near = lax.ppermute(kv, "ctx", up)
    far_shape = shape_of((capacity * BLOCK, 2 * HEAD_DIM), BF16)
    picked = call(pick_kernel, (summary_ids,), (kv, kv_partner), far_shape)
    kv_far = [lax.ppermute(picked, both, route) for route in routes]
    attn_out, window_offsets, _ = lax.optimization_barrier((attn_out, window_offsets, picked))
    tables = (window_offsets, summary_ids)
    stats = call(
        prep_kernel, (), (attn_out, grads, log_sums),
        shape_of((blocks_here, 8, GROUP * BLOCK), F32), flops=0,
    )
    own = (queries, grads, stats)
    every = own + tuple(lax.ppermute(x, "rep", swap) for x in own)
    acc_shape = (rows, 2 * HEAD_DIM)
    half_shape = (blocks_here, HEAD_DIM, GROUP * BLOCK)
    dq_shape = shape_of((CORES * blocks_here, *half_shape[1:]), F32)
    cross_acc, cross_dq = call(
        cross_kernel, tables, (kv, *every), (shape_of(acc_shape, F32), shape_of(half_shape, F32)),
        flops=0,
    )
    near_grads, near_dq = call(
        near_kernel, tables, (kv_near, *every, cross_dq), (shape_of(acc_shape, BF16), dq_shape),
        [pltpu.VMEM(acc_shape, F32)], flops=0,
    )
    near_back = lax.ppermute(near_grads, "ctx", down)
    chunk_shape = (min(capacity, 4) * BLOCK, 2 * HEAD_DIM)
    *far_grads, far_dq, dq_partner = call(
        functools.partial(far_kernel, sources), (summary_ids,), (*kv_far, *every, near_dq),
        (*[far_shape] * len(routes), dq_shape, shape_of(half_shape, BF16)),
        [pltpu.VMEM(chunk_shape, F32)], flops=5 * MICROSECOND,
    )
    far_back = [
        lax.ppermute(x, both, [(b, a) for a, b in route]) for x, route in zip(far_grads, routes)
    ]
    dq_partner = lax.ppermute(dq_partner, "rep", swap)
    acc, query_grads = call(
        own_kernel, tables, (kv, *own, cross_acc, far_dq, dq_partner),
        (shape_of(acc_shape, F32), shape_of(queries.shape, BF16)), flops=10 * MICROSECOND,
    )
    far_back, acc, query_grads = lax.optimization_barrier((far_back, acc, query_grads))
    far_other = [lax.ppermute(x, "rep", swap) for x in far_back]
    kv_shape = shape_of((rows, HEAD_DIM), BF16)
    key_grads, value_grads = call(
        functools.partial(final_kernel, chips - 3), (summary_ids,),
        (acc, near_back, *far_back, *far_other), (kv_shape, kv_shape),
        [pltpu.VMEM(acc_shape, F32)],
    )
    return query_grads, key_grads, value_grads


def capacities(chips):
    return CAPACITIES if len(far_rounds(chips)) == 1 else CAPACITIES[-1:]


def per_device(chips, queries, keys, values, attn_out, grads, log_sums, window_offsets, summary_ids):
    kv, branch = call(
        functools.partial(start_kernel, chips), (summary_ids,), (keys, values),
        (shape_of((keys.shape[0], 2 * HEAD_DIM), BF16), shape_of((1,), jnp.int32)),
        [pltpu.SemaphoreType.DMA((2,))], in_space=HBM, out_specs=(VMEM, SMEM), room=60,
    )
    branches = [functools.partial(with_capacity, limit, chips) for limit in capacities(chips)]
    operands = (queries, kv, attn_out, grads, log_sums, window_offsets, summary_ids)
    return lax.switch(branch[0], branches, *operands) if len(branches) > 1 else branches[0](*operands)


def solution(mesh):
    rows = P(("groups", "ctx", "rep"), "heads")
    return jax.shard_map(
        functools.partial(per_device, mesh.shape["ctx"]),
        mesh=mesh,
        in_specs=(rows,) * 5 + (P("heads", ("groups", "ctx", "rep")), P("groups", None), P("groups")),
        out_specs=(rows,) * 3,
        check_vma=False,
    )
```

```python
import functools
import math

import jax
import jax.numpy as jnp
from jax import lax
from jax.experimental import pallas as pl
from jax.experimental.pallas import tpu as pltpu
from jax.sharding import PartitionSpec as P

HEAD_DIM = 128
GROUP = 4
BLOCK = 128
REACH = 3
SUMMARY = 8
CORES = 2
SCALE = HEAD_DIM ** (-0.5)
LOG2E = math.log2(math.e)
MICROSECOND = 1_000_000_000
CAPACITIES = (2, 3, 4, SUMMARY)
F32 = jnp.float32
BF16 = jnp.bfloat16
VMEM = pl.BlockSpec(memory_space=pltpu.VMEM)
SMEM = pl.BlockSpec(memory_space=pltpu.SMEM)
HBM = pl.BlockSpec(memory_space=pltpu.HBM)


def far_rounds(chips):
    rounds = []
    for source in range(chips):
        for target in range(source + 2, chips):
            for senders, receivers, route in rounds:
                if senders.get(source, 0) < CORES and receivers.get(target, 0) < CORES:
                    break
            else:
                senders, receivers, route = {}, {}, []
                rounds.append((senders, receivers, route))
            sent, got = senders.get(source, 0), receivers.get(target, 0)
            route.append((source * CORES + sent, target * CORES + got))
            senders[source], receivers[target] = sent + 1, got + 1
    return [route for _, _, route in rounds]


def table_entry(table, position):
    value = jnp.int32(-1)
    for place, entry in table.items():
        value = jnp.where(position == place, jnp.int32(entry), value)
    return value


def chip_slot(ids_ref, slot, chip_blocks):
    chip = ids_ref[slot] // chip_blocks
    rank = jnp.int32(0)
    for other in range(slot):
        rank += jnp.where(ids_ref[other] // chip_blocks == chip, 1, 0)
    return chip, rank


def chip_count(ids_ref, chip, chip_blocks):
    count = jnp.int32(0)
    for slot in range(SUMMARY):
        count += jnp.where(ids_ref[slot] // chip_blocks == chip, 1, 0)
    return count


def prep_kernel(out_ref, grad_ref, lse_ref, stats_ref):
    stats_ref[...] = jnp.zeros_like(stats_ref)
    for block in range(stats_ref.shape[0]):
        rows = slice(block * BLOCK, (block + 1) * BLOCK)
        for head in range(GROUP):
            columns = slice(head * HEAD_DIM, (head + 1) * HEAD_DIM)
            product = out_ref[rows, columns].astype(F32) * grad_ref[rows, columns].astype(F32)
            stats_ref[block, 0:1, columns] = lse_ref[head : head + 1, rows] * LOG2E
            stats_ref[block, 1:2, columns] = jnp.sum(product.T, axis=0, keepdims=True)


def start_kernel(chips, ids_hbm, key_ref, value_ref, kv_ref, branch_ref, ids_ref, sems):
    chip_blocks = CORES * (key_ref.shape[0] // BLOCK)
    copies = [
        pltpu.make_async_copy(
            ref, kv_ref.at[:, number * HEAD_DIM : (number + 1) * HEAD_DIM], sems.at[number]
        )
        for number, ref in enumerate((key_ref, value_ref))
    ]
    ids_copy = pltpu.make_async_copy(ids_hbm, ids_ref, sems.at[2])
    ids_copy.start()
    for copy in copies:
        copy.start()
    ids_copy.wait()
    most = jnp.int32(0)
    for chip in range(chips - 2):
        most = jnp.maximum(most, chip_count(ids_ref, chip, chip_blocks))
    branch = jnp.int32(0)
    for capacity in capacities(chips)[:-1]:
        branch += jnp.where(most > capacity, 1, 0)
    branch_ref[0] = branch
    for copy in copies:
        copy.wait()


def pick_kernel(ids_ref, own_ref, partner_ref, picked_ref):
    chip = lax.axis_index("ctx")
    core = lax.axis_index("rep")
    blocks_here = own_ref.shape[0] // BLOCK
    chip_blocks = CORES * blocks_here
    capacity = picked_ref.shape[0] // BLOCK
    picked_ref[...] = jnp.zeros_like(picked_ref)
    for slot in range(SUMMARY):
        owner, rank = chip_slot(ids_ref, slot, chip_blocks)
        local = ids_ref[slot] - chip * chip_blocks
        row = pl.multiple_of((local % blocks_here) * BLOCK, BLOCK)
        place = pl.multiple_of(rank * BLOCK, BLOCK)
        mine = local // blocks_here == core
        wanted = (owner == chip) & (rank < capacity)

        @pl.when(wanted & mine)
        def _():
            picked_ref[pl.ds(place, BLOCK), :] = own_ref[pl.ds(row, BLOCK), :]

        @pl.when(wanted & ~mine)
        def _():
            picked_ref[pl.ds(place, BLOCK), :] = partner_ref[pl.ds(row, BLOCK), :]


def nt(a, b):
    return lax.dot_general(a, b, (((1,), (1,)), ((), ())), preferred_element_type=F32)


def nn(a, b):
    return jnp.dot(a, b, preferred_element_type=F32)


def block_grads(keys, values, key_t, query_refs, number, biases=None, query_at=None):
    query_ref, grad_ref, stats_ref = query_refs
    queries, grads = query_ref[number], grad_ref[number]
    log_sums, deltas = stats_ref[number, 0:1, :], stats_ref[number, 1:2, :]
    scores = nt(keys, queries) * (SCALE * LOG2E)
    if biases is None:
        probs = jnp.exp2(scores - log_sums)
    else:
        parts = []
        for key, bias in enumerate(biases):
            part = jnp.exp2(scores[key * BLOCK : (key + 1) * BLOCK] - (log_sums + bias))
            if query_at is not None:
                row = lax.broadcasted_iota(jnp.int32, part.shape, 0)
                column = lax.broadcasted_iota(jnp.int32, part.shape, 1) % BLOCK
                part = jnp.where(column - row >= (key - query_at) * BLOCK, part, 0.0)
            parts.append(part)
        probs = jnp.concatenate(parts, axis=0)
    prob_grads = nt(values, grads)
    score_grads = (probs * (prob_grads - deltas) * SCALE).astype(BF16)
    return nn(key_t, score_grads), nn(score_grads, queries), nn(probs.astype(BF16), grads)


def is_summary(ids_ref, key_block):
    found = ids_ref[0] == key_block
    for slot in range(1, SUMMARY):
        found |= ids_ref[slot] == key_block
    return found


def in_window(offsets_ref, query_block, key_block):
    distance = query_block - key_block
    return (distance == offsets_ref[query_block, 0]) | (distance == offsets_ref[query_block, 1])


def attends(offsets_ref, ids_ref, query_block, key_block):
    chosen = in_window(offsets_ref, query_block, key_block) | is_summary(ids_ref, key_block)
    return (query_block > key_block) & chosen


def keys_of(kv_ref, rows):
    return kv_ref[rows, 0:HEAD_DIM]


def values_of(kv_ref, rows):
    return kv_ref[rows, HEAD_DIM : 2 * HEAD_DIM]


def transposed(keys):
    return keys.astype(F32).T.astype(BF16)


def add_grads(acc_ref, rows, key_part, value_part):
    acc_ref[rows, 0:HEAD_DIM] += key_part
    acc_ref[rows, HEAD_DIM : 2 * HEAD_DIM] += value_part


def places(blocks_here):
    chip = lax.axis_index("ctx")
    base = chip * CORES * blocks_here
    return chip, base, base + lax.axis_index("rep") * blocks_here


def bias_of(flag):
    return jnp.where(flag, 0.0, 1e30).astype(F32)


def near_kernel(
    offsets_ref, ids_ref, kv_ref, q_ref, g_ref, s_ref, local_ref, grads_ref, dq_ref, acc_ref
):
    query_refs = (q_ref, g_ref, s_ref)
    blocks_here = kv_ref.shape[0] // BLOCK
    chip_blocks = CORES * blocks_here
    chip, base, own = places(blocks_here)
    first_key = own - chip_blocks
    acc_ref[...] = jnp.zeros_like(acc_ref)
    dq_ref[0:blocks_here] = jnp.zeros_like(local_ref)
    dq_ref[blocks_here:] = local_ref[...]
    flags = [is_summary(ids_ref, first_key + key) & (chip > 0) for key in range(blocks_here)]
    count = jnp.int32(0)
    chosen = [jnp.int32(0)] * blocks_here
    for key in range(blocks_here):
        for place in range(key + 1):
            chosen[place] = jnp.where(flags[key] & (count == place), key, chosen[place])
        count += jnp.where(flags[key], 1, 0)

    def add(number, keys, biases):
        rows = [pl.ds(pl.multiple_of(key * BLOCK, BLOCK), BLOCK) for key in keys]
        keys = jnp.concatenate([keys_of(kv_ref, row) for row in rows], axis=0)
        values = jnp.concatenate([values_of(kv_ref, row) for row in rows], axis=0)
        dq, dk, dv = block_grads(keys, values, transposed(keys), query_refs, number, biases)
        dq_ref[number] += dq
        for place, row in enumerate(rows):
            part = slice(place * BLOCK, (place + 1) * BLOCK)
            add_grads(acc_ref, row, dk[part], dv[part])

    def single_step(number, carry):
        add(number, [chosen[0]], None)
        return carry

    odd = lax.rem(count, 2)
    lax.fori_loop(0, odd * (chip_blocks // 2), lambda i, c: single_step(2 * i + 1, single_step(2 * i, c)), 0)
    pairs = (count // 2) * chip_blocks
    windows = jnp.where((chip > 0) & (lax.axis_index("rep") == CORES - 1), min(REACH, blocks_here), 0)

    def double_step(item, carry):
        summary = item < pairs
        number = jnp.where(summary, lax.rem(item, chip_blocks), item - pairs)
        query = base + number
        turn = odd + 2 * (item // chip_blocks)
        firsts, seconds = jnp.int32(0), jnp.int32(0)
        for place in range(blocks_here):
            firsts = jnp.where(turn == place, chosen[place], firsts)
            seconds = jnp.where(turn + 1 == place, chosen[place], seconds)
        keys, wanted = [], []
        for place, from_summary in enumerate((firsts, seconds)):
            key = query - offsets_ref[query, place] - first_key
            fits = (key >= 0) & (key < blocks_here)
            key = jnp.where(fits, key, 0)
            for block in range(blocks_here):
                fits &= (key != block) | ~flags[block]
            keys.append(jnp.where(summary, from_summary, key))
            wanted.append(summary | fits)
        own_number = number + jnp.where(summary, 0, blocks_here)

        @pl.when(wanted[0] | wanted[1])
        def _():
            add(own_number, keys, [bias_of(flag) for flag in wanted])

        return carry

    lax.fori_loop(0, pairs + windows, double_step, 0)
    grads_ref[...] = acc_ref[...].astype(BF16)


def far_kernel(sources, ids_ref, *refs):
    count = len(sources)
    kv_refs, query_refs, near_ref, refs = refs[:count], refs[count : count + 3], refs[count + 3], refs[count + 4 :]
    grads_refs, (dq_ref, partner_ref, acc_ref) = refs[:count], refs[count:]
    chip_blocks = near_ref.shape[0]
    blocks_here = chip_blocks // CORES
    capacity = kv_refs[0].shape[0] // BLOCK
    position = lax.axis_index("ctx") * CORES + lax.axis_index("rep")
    chunk = min(capacity, 4)
    dq_ref[...] = near_ref[...]
    for table, kv_ref, grads_ref in zip(sources, kv_refs, grads_refs):
        held = chip_count(ids_ref, table_entry(table, position), chip_blocks)
        grads_ref[...] = jnp.zeros_like(grads_ref)

        def chunk_step(turn, carry):
            rows = pl.ds(pl.multiple_of(turn * (chunk * BLOCK), BLOCK), chunk * BLOCK)
            keys, values = keys_of(kv_ref, rows), values_of(kv_ref, rows)
            key_t = transposed(keys)
            acc_ref[...] = jnp.zeros_like(acc_ref)

            def query_step(number, carry):
                dq, dk, dv = block_grads(keys, values, key_t, query_refs, number)
                dq_ref[number] += dq
                add_grads(acc_ref, slice(None), dk, dv)
                return carry

            lax.fori_loop(0, chip_blocks, query_step, 0, unroll=2)
            grads_ref[rows, :] = acc_ref[...].astype(BF16)
            return carry

        lax.fori_loop(0, (held + chunk - 1) // chunk, chunk_step, 0)
    partner_ref[...] = dq_ref[blocks_here:].astype(BF16)


def cross_kernel(
    offsets_ref, ids_ref, kv_ref, q_ref, g_ref, s_ref, pq_ref, pg_ref, ps_ref,
    acc_ref, dq_ref, all_q_ref, all_g_ref, all_s_ref,
):
    blocks_here = kv_ref.shape[0] // BLOCK
    _, base, own = places(blocks_here)
    for from_refs, to_ref in (((q_ref, pq_ref), all_q_ref), ((g_ref, pg_ref), all_g_ref)):
        for side, from_ref in enumerate(from_refs):
            for block in range(blocks_here):
                for head in range(GROUP):
                    to_ref[side * blocks_here + block, head * BLOCK : (head + 1) * BLOCK, :] = from_ref[
                        block * BLOCK : (block + 1) * BLOCK, head * HEAD_DIM : (head + 1) * HEAD_DIM
                    ]
    all_s_ref[0:blocks_here] = s_ref[...]
    all_s_ref[blocks_here:] = ps_ref[...]
    acc_ref[...] = jnp.zeros_like(acc_ref)
    dq_ref[...] = jnp.zeros_like(dq_ref)

    @pl.when(lax.axis_index("rep") == 0)
    def _():
        keys, values = keys_of(kv_ref, slice(None)), values_of(kv_ref, slice(None))
        key_t = transposed(keys)

        def query_step(block, carry):
            number = block + blocks_here
            query = base + number
            flags = [attends(offsets_ref, ids_ref, query, own + key) for key in range(blocks_here)]
            some = flags[0]
            for flag in flags[1:]:
                some |= flag

            @pl.when(some)
            def _():
                dq, dk, dv = block_grads(
                    keys, values, key_t, (all_q_ref, all_g_ref, all_s_ref), number,
                    [bias_of(flag) for flag in flags],
                )
                dq_ref[block] = dq
                add_grads(acc_ref, slice(None), dk, dv)

            return carry

        lax.fori_loop(0, blocks_here, query_step, 0)


def own_kernel(
    offsets_ref, ids_ref, kv_ref, q_ref, g_ref, s_ref, cross_ref, far_ref, partner_ref,
    acc_ref, dq_ref,
):
    blocks_here = kv_ref.shape[0] // BLOCK
    _, _, own = places(blocks_here)
    acc_ref[...] = cross_ref[...]
    keys, values = keys_of(kv_ref, slice(None)), values_of(kv_ref, slice(None))
    key_t = transposed(keys)

    def query_step(block, carry):
        flags = [
            (key >= block) | attends(offsets_ref, ids_ref, own + block, own + key)
            for key in range(blocks_here)
        ]
        dq, dk, dv = block_grads(
            keys, values, key_t, (q_ref, g_ref, s_ref), block,
            [bias_of(flag) for flag in flags], block,
        )
        add_grads(acc_ref, slice(None), dk, dv)
        total = far_ref[block] + partner_ref[block].astype(F32) + dq
        rows = pl.ds(pl.multiple_of(block * BLOCK, BLOCK), BLOCK)
        for head in range(GROUP):
            lanes = slice(head * HEAD_DIM, (head + 1) * HEAD_DIM)
            dq_ref[rows, lanes] = total[:, lanes].T.astype(BF16)
        return carry

    lax.fori_loop(0, blocks_here, query_step, 0)


def final_kernel(last_sender, ids_ref, acc_ref, near_ref, *refs):
    far_refs, (dk_ref, dv_ref, sum_ref) = refs[:-3], refs[-3:]
    blocks_here = acc_ref.shape[0] // BLOCK
    chip_blocks = CORES * blocks_here
    chip = lax.axis_index("ctx")
    core = lax.axis_index("rep")
    sum_ref[...] = acc_ref[...] + near_ref[...].astype(F32)
    dk_ref[...] = keys_of(sum_ref, slice(None)).astype(BF16)
    dv_ref[...] = values_of(sum_ref, slice(None)).astype(BF16)
    capacity = far_refs[0].shape[0] // BLOCK
    for slot in range(SUMMARY):
        owner, rank = chip_slot(ids_ref, slot, chip_blocks)
        local = ids_ref[slot] - chip * chip_blocks - core * blocks_here
        mine = (owner == chip) & (local >= 0) & (local < blocks_here)

        @pl.when(mine & (chip <= last_sender) & (rank < capacity))
        def _():
            rows = pl.ds(pl.multiple_of(local * BLOCK, BLOCK), BLOCK)
            place = pl.ds(pl.multiple_of(rank * BLOCK, BLOCK), BLOCK)
            total = sum_ref[rows, :]
            for far_ref in far_refs:
                total += far_ref[place, :].astype(F32)
            dk_ref[rows, :] = total[:, 0:HEAD_DIM].astype(BF16)
            dv_ref[rows, :] = total[:, HEAD_DIM : 2 * HEAD_DIM].astype(BF16)


def call(kernel, scalars, arrays, out_shape, scratch=(), flops=0, in_space=VMEM, out_specs=None, room=24):
    return pl.pallas_call(
        kernel,
        out_shape=out_shape,
        in_specs=[SMEM] * len(scalars) + [in_space] * len(arrays),
        out_specs=out_specs or jax.tree.map(lambda _: VMEM, out_shape),
        scratch_shapes=list(scratch),
        compiler_params=pltpu.CompilerParams(vmem_limit_bytes=room << 20),
        cost_estimate=pl.CostEstimate(flops=flops, bytes_accessed=0, transcendentals=0),
    )(*scalars, *arrays)


def shape_of(shape, dtype):
    return jax.ShapeDtypeStruct(shape, dtype)


def with_capacity(
    capacity, chips, queries, kv, attn_out, grads, log_sums, window_offsets, summary_ids
):
    rows = queries.shape[0]
    blocks_here = rows // BLOCK
    swap = [(0, 1), (1, 0)]
    up = [(i, i + 1) for i in range(chips - 1)]
    down = [(b, a) for a, b in up]
    routes = far_rounds(chips)
    sources = tuple({b: a // CORES for a, b in route} for route in routes)
    both = ("ctx", "rep")

    kv_partner = lax.ppermute(kv, "rep", swap)
    kv_near = lax.ppermute(kv, "ctx", up)
    far_shape = shape_of((capacity * BLOCK, 2 * HEAD_DIM), BF16)
    picked = call(pick_kernel, (summary_ids,), (kv, kv_partner), far_shape)
    kv_far = [lax.ppermute(picked, both, route) for route in routes]
    attn_out, window_offsets, _ = lax.optimization_barrier((attn_out, window_offsets, picked))
    tables = (window_offsets, summary_ids)
    stats = call(
        prep_kernel, (), (attn_out, grads, log_sums),
        shape_of((blocks_here, 8, GROUP * BLOCK), F32), flops=0,
    )
    own = (queries, grads, stats)
    every = own + tuple(lax.ppermute(x, "rep", swap) for x in own)
    acc_shape = (rows, 2 * HEAD_DIM)
    half_shape = (blocks_here, HEAD_DIM, GROUP * BLOCK)
    chip_blocks = CORES * blocks_here
    dq_shape = shape_of((chip_blocks, *half_shape[1:]), F32)
    stacked_shape = shape_of((chip_blocks, GROUP * BLOCK, HEAD_DIM), BF16)
    cross_acc, cross_dq, *every = call(
        cross_kernel, tables, (kv, *every),
        (
            shape_of(acc_shape, F32), shape_of(half_shape, F32), stacked_shape, stacked_shape,
            shape_of((chip_blocks, *stats.shape[1:]), F32),
        ),
    )
    near_grads, near_dq = call(
        near_kernel, tables, (kv_near, *every, cross_dq), (shape_of(acc_shape, BF16), dq_shape),
        [pltpu.VMEM(acc_shape, F32)],
    )
    near_back = lax.ppermute(near_grads, "ctx", down)
    chunk_shape = (min(capacity, 4) * BLOCK, 2 * HEAD_DIM)
    *far_grads, far_dq, dq_partner = call(
        functools.partial(far_kernel, sources), (summary_ids,), (*kv_far, *every, near_dq),
        (*[far_shape] * len(routes), dq_shape, shape_of(half_shape, BF16)),
        [pltpu.VMEM(chunk_shape, F32)], flops=5 * MICROSECOND,
    )
    far_back = [
        lax.ppermute(x, both, [(b, a) for a, b in route]) for x, route in zip(far_grads, routes)
    ]
    dq_partner = lax.ppermute(dq_partner, "rep", swap)
    acc, query_grads = call(
        own_kernel, tables, (kv, *every, cross_acc, far_dq, dq_partner),
        (shape_of(acc_shape, F32), shape_of(queries.shape, BF16)), flops=10 * MICROSECOND,
    )
    far_back, acc, query_grads = lax.optimization_barrier((far_back, acc, query_grads))
    far_other = [lax.ppermute(x, "rep", swap) for x in far_back]
    kv_shape = shape_of((rows, HEAD_DIM), BF16)
    key_grads, value_grads = call(
        functools.partial(final_kernel, chips - 3), (summary_ids,),
        (acc, near_back, *far_back, *far_other), (kv_shape, kv_shape),
        [pltpu.VMEM(acc_shape, F32)],
    )
    return query_grads, key_grads, value_grads


def capacities(chips):
    return CAPACITIES if len(far_rounds(chips)) == 1 else CAPACITIES[-1:]


def per_device(chips, queries, keys, values, attn_out, grads, log_sums, window_offsets, summary_ids):
    kv, branch = call(
        functools.partial(start_kernel, chips), (), (summary_ids, keys, values),
        (shape_of((keys.shape[0], 2 * HEAD_DIM), BF16), shape_of((1,), jnp.int32)),
        [pltpu.SMEM(summary_ids.shape, jnp.int32), pltpu.SemaphoreType.DMA((3,))], in_space=HBM, out_specs=(VMEM, SMEM), room=60,
    )
    branches = [functools.partial(with_capacity, limit, chips) for limit in capacities(chips)]
    operands = (queries, kv, attn_out, grads, log_sums, window_offsets, summary_ids)
    return lax.switch(branch[0], branches, *operands) if len(branches) > 1 else branches[0](*operands)


def solution(mesh):
    rows = P(("groups", "ctx", "rep"), "heads")
    return jax.shard_map(
        functools.partial(per_device, mesh.shape["ctx"]),
        mesh=mesh,
        in_specs=(rows,) * 5 + (P("heads", ("groups", "ctx", "rep")), P("groups", None), P("groups")),
        out_specs=(rows,) * 3,
        check_vma=False,
    )
```

```python
import functools
import math

import jax
import jax.numpy as jnp
from jax import lax
from jax.experimental import pallas as pl
from jax.experimental.pallas import tpu as pltpu
from jax.sharding import PartitionSpec as P

HEAD_DIM = 128
GROUP = 4
BLOCK = 128
REACH = 3
SUMMARY = 8
CORES = 2
SCALE = HEAD_DIM ** (-0.5)
LOG2E = math.log2(math.e)
MICROSECOND = 1_000_000_000
OWN = 10 * MICROSECOND
CAPACITIES = (2, 3, 4, 5, SUMMARY)
F32 = jnp.float32
BF16 = jnp.bfloat16
VMEM = pl.BlockSpec(memory_space=pltpu.VMEM)
SMEM = pl.BlockSpec(memory_space=pltpu.SMEM)
HBM = pl.BlockSpec(memory_space=pltpu.HBM)


def far_rounds(chips):
    rounds = []
    for source in range(chips):
        for target in range(source + 2, chips):
            for senders, receivers, route in rounds:
                if senders.get(source, 0) < CORES and receivers.get(target, 0) < CORES:
                    break
            else:
                senders, receivers, route = {}, {}, []
                rounds.append((senders, receivers, route))
            sent, got = senders.get(source, 0), receivers.get(target, 0)
            route.append((source * CORES + sent, target * CORES + got))
            senders[source], receivers[target] = sent + 1, got + 1
    return [route for _, _, route in rounds]


def table_entry(table, position):
    value = jnp.int32(-1)
    for place, entry in table.items():
        value = jnp.where(position == place, jnp.int32(entry), value)
    return value


def chip_slot(ids_ref, slot, chip_blocks):
    chip = ids_ref[slot] // chip_blocks
    rank = jnp.int32(0)
    for other in range(slot):
        rank += jnp.where(ids_ref[other] // chip_blocks == chip, 1, 0)
    return chip, rank


def chip_count(ids_ref, chip, chip_blocks):
    count = jnp.int32(0)
    for slot in range(SUMMARY):
        count += jnp.where(ids_ref[slot] // chip_blocks == chip, 1, 0)
    return count


def prep_kernel(out_ref, grad_ref, lse_ref, stats_ref):
    stats_ref[...] = jnp.zeros_like(stats_ref)
    for block in range(stats_ref.shape[0]):
        rows = slice(block * BLOCK, (block + 1) * BLOCK)
        for head in range(GROUP):
            columns = slice(head * HEAD_DIM, (head + 1) * HEAD_DIM)
            product = out_ref[rows, columns].astype(F32) * grad_ref[rows, columns].astype(F32)
            stats_ref[block, 0:1, columns] = lse_ref[head : head + 1, rows] * LOG2E
            stats_ref[block, 1:2, columns] = jnp.sum(product.T, axis=0, keepdims=True)


def start_kernel(chips, ids_hbm, key_ref, value_ref, kv_ref, branch_ref, ids_ref, sems):
    chip_blocks = CORES * (key_ref.shape[0] // BLOCK)
    copies = [
        pltpu.make_async_copy(
            ref, kv_ref.at[:, number * HEAD_DIM : (number + 1) * HEAD_DIM], sems.at[number]
        )
        for number, ref in enumerate((key_ref, value_ref))
    ]
    ids_copy = pltpu.make_async_copy(ids_hbm, ids_ref, sems.at[2])
    ids_copy.start()
    for copy in copies:
        copy.start()
    ids_copy.wait()
    most = jnp.int32(0)
    for chip in range(chips - 2):
        most = jnp.maximum(most, chip_count(ids_ref, chip, chip_blocks))
    branch = jnp.int32(0)
    for capacity in capacities(chips)[:-1]:
        branch += jnp.where(most > capacity, 1, 0)
    branch_ref[0] = branch
    for copy in copies:
        copy.wait()


def pick_kernel(ids_ref, own_ref, partner_ref, picked_ref):
    chip = lax.axis_index("ctx")
    core = lax.axis_index("rep")
    blocks_here = own_ref.shape[0] // BLOCK
    chip_blocks = CORES * blocks_here
    capacity = picked_ref.shape[0] // BLOCK
    picked_ref[...] = jnp.zeros_like(picked_ref)
    for slot in range(SUMMARY):
        owner, rank = chip_slot(ids_ref, slot, chip_blocks)
        local = ids_ref[slot] - chip * chip_blocks
        row = pl.multiple_of((local % blocks_here) * BLOCK, BLOCK)
        place = pl.multiple_of(rank * BLOCK, BLOCK)
        mine = local // blocks_here == core
        wanted = (owner == chip) & (rank < capacity)

        @pl.when(wanted & mine)
        def _():
            picked_ref[pl.ds(place, BLOCK), :] = own_ref[pl.ds(row, BLOCK), :]

        @pl.when(wanted & ~mine)
        def _():
            picked_ref[pl.ds(place, BLOCK), :] = partner_ref[pl.ds(row, BLOCK), :]


def nt(a, b):
    return lax.dot_general(a, b, (((1,), (1,)), ((), ())), preferred_element_type=F32)


def nn(a, b):
    return jnp.dot(a, b, preferred_element_type=F32)


def block_grads(keys, values, key_t, query_refs, number, biases=None, query_at=None):
    query_ref, grad_ref, stats_ref = query_refs
    queries, grads = query_ref[number], grad_ref[number]
    log_sums, deltas = stats_ref[number, 0:1, :], stats_ref[number, 1:2, :]
    scores = nt(keys, queries) * (SCALE * LOG2E)
    if biases is None:
        probs = jnp.exp2(scores - log_sums)
    else:
        parts = []
        for key, bias in enumerate(biases):
            part = jnp.exp2(scores[key * BLOCK : (key + 1) * BLOCK] - (log_sums + bias))
            if query_at is not None:
                row = lax.broadcasted_iota(jnp.int32, part.shape, 0)
                column = lax.broadcasted_iota(jnp.int32, part.shape, 1) % BLOCK
                part = jnp.where(column - row >= (key - query_at) * BLOCK, part, 0.0)
            parts.append(part)
        probs = jnp.concatenate(parts, axis=0)
    prob_grads = nt(values, grads)
    score_grads = (probs * (prob_grads - deltas) * SCALE).astype(BF16)
    return nn(key_t, score_grads), nn(score_grads, queries), nn(probs.astype(BF16), grads)


def is_summary(ids_ref, key_block):
    found = ids_ref[0] == key_block
    for slot in range(1, SUMMARY):
        found |= ids_ref[slot] == key_block
    return found


def in_window(offsets_ref, query_block, key_block):
    distance = query_block - key_block
    return (distance == offsets_ref[query_block, 0]) | (distance == offsets_ref[query_block, 1])


def attends(offsets_ref, ids_ref, query_block, key_block):
    chosen = in_window(offsets_ref, query_block, key_block) | is_summary(ids_ref, key_block)
    return (query_block > key_block) & chosen


def keys_of(kv_ref, rows):
    return kv_ref[rows, 0:HEAD_DIM]


def values_of(kv_ref, rows):
    return kv_ref[rows, HEAD_DIM : 2 * HEAD_DIM]


def transposed(keys):
    return keys.astype(F32).T.astype(BF16)


def add_grads(acc_ref, rows, key_part, value_part):
    acc_ref[rows, 0:HEAD_DIM] += key_part
    acc_ref[rows, HEAD_DIM : 2 * HEAD_DIM] += value_part


def places(blocks_here):
    chip = lax.axis_index("ctx")
    base = chip * CORES * blocks_here
    return chip, base, base + lax.axis_index("rep") * blocks_here


def bias_of(flag):
    return jnp.where(flag, 0.0, 1e30).astype(F32)


def near_kernel(
    offsets_ref, ids_ref, kv_ref, q_ref, g_ref, s_ref, local_ref, grads_ref, dq_ref, acc_ref
):
    query_refs = (q_ref, g_ref, s_ref)
    blocks_here = kv_ref.shape[0] // BLOCK
    chip_blocks = CORES * blocks_here
    chip, base, own = places(blocks_here)
    first_key = own - chip_blocks
    acc_ref[...] = jnp.zeros_like(acc_ref)
    dq_ref[0:blocks_here] = jnp.zeros_like(local_ref)
    dq_ref[blocks_here:] = local_ref[...]
    flags = [is_summary(ids_ref, first_key + key) & (chip > 0) for key in range(blocks_here)]
    count = jnp.int32(0)
    chosen = [jnp.int32(0)] * blocks_here
    for key in range(blocks_here):
        for place in range(key + 1):
            chosen[place] = jnp.where(flags[key] & (count == place), key, chosen[place])
        count += jnp.where(flags[key], 1, 0)

    def add(number, keys, biases):
        rows = [pl.ds(pl.multiple_of(key * BLOCK, BLOCK), BLOCK) for key in keys]
        keys = jnp.concatenate([keys_of(kv_ref, row) for row in rows], axis=0)
        values = jnp.concatenate([values_of(kv_ref, row) for row in rows], axis=0)
        dq, dk, dv = block_grads(keys, values, transposed(keys), query_refs, number, biases)
        dq_ref[number] += dq
        for place, row in enumerate(rows):
            part = slice(place * BLOCK, (place + 1) * BLOCK)
            add_grads(acc_ref, row, dk[part], dv[part])

    def single_step(number, carry):
        add(number, [chosen[0]], None)
        return carry

    odd = lax.rem(count, 2)
    lax.fori_loop(0, odd * (chip_blocks // 2), lambda i, c: single_step(2 * i + 1, single_step(2 * i, c)), 0)
    pairs = (count // 2) * chip_blocks
    windows = jnp.where((chip > 0) & (lax.axis_index("rep") == CORES - 1), min(REACH, blocks_here), 0)

    def double_step(item, carry):
        summary = item < pairs
        number = jnp.where(summary, lax.rem(item, chip_blocks), item - pairs)
        query = base + number
        turn = odd + 2 * (item // chip_blocks)
        firsts, seconds = jnp.int32(0), jnp.int32(0)
        for place in range(blocks_here):
            firsts = jnp.where(turn == place, chosen[place], firsts)
            seconds = jnp.where(turn + 1 == place, chosen[place], seconds)
        keys, wanted = [], []
        for place, from_summary in enumerate((firsts, seconds)):
            key = query - offsets_ref[query, place] - first_key
            fits = (key >= 0) & (key < blocks_here)
            key = jnp.where(fits, key, 0)
            for block in range(blocks_here):
                fits &= (key != block) | ~flags[block]
            keys.append(jnp.where(summary, from_summary, key))
            wanted.append(summary | fits)
        own_number = number + jnp.where(summary, 0, blocks_here)

        @pl.when(wanted[0] | wanted[1])
        def _():
            add(own_number, keys, [bias_of(flag) for flag in wanted])

        return carry

    lax.fori_loop(0, pairs + windows, double_step, 0)
    grads_ref[...] = acc_ref[...].astype(BF16)


def far_kernel(sources, ids_ref, *refs):
    count = len(sources)
    kv_refs, query_refs, near_ref, refs = refs[:count], refs[count : count + 3], refs[count + 3], refs[count + 4 :]
    grads_refs, (dq_ref, partner_ref, acc_ref) = refs[:count], refs[count:]
    chip_blocks = near_ref.shape[0]
    blocks_here = chip_blocks // CORES
    capacity = kv_refs[0].shape[0] // BLOCK
    position = lax.axis_index("ctx") * CORES + lax.axis_index("rep")
    chunk = min(capacity, 4)
    dq_ref[...] = near_ref[...]
    for table, kv_ref, grads_ref in zip(sources, kv_refs, grads_refs):
        held = chip_count(ids_ref, table_entry(table, position), chip_blocks)
        grads_ref[...] = jnp.zeros_like(grads_ref)

        def chunk_step(turn, carry):
            rows = pl.ds(pl.multiple_of(turn * (chunk * BLOCK), BLOCK), chunk * BLOCK)
            keys, values = keys_of(kv_ref, rows), values_of(kv_ref, rows)
            key_t = transposed(keys)
            acc_ref[...] = jnp.zeros_like(acc_ref)

            def query_step(number, carry):
                dq, dk, dv = block_grads(keys, values, key_t, query_refs, number)
                dq_ref[number] += dq
                add_grads(acc_ref, slice(None), dk, dv)
                return carry

            lax.fori_loop(0, chip_blocks, query_step, 0, unroll=2)
            grads_ref[rows, :] = acc_ref[...].astype(BF16)
            return carry

        lax.fori_loop(0, (held + chunk - 1) // chunk, chunk_step, 0)
    partner_ref[...] = dq_ref[blocks_here:].astype(BF16)


def cross_kernel(
    offsets_ref, ids_ref, kv_ref, q_ref, g_ref, s_ref, pq_ref, pg_ref, ps_ref,
    acc_ref, dq_ref, all_q_ref, all_g_ref, all_s_ref,
):
    blocks_here = kv_ref.shape[0] // BLOCK
    _, base, own = places(blocks_here)
    for from_refs, to_ref in (((q_ref, pq_ref), all_q_ref), ((g_ref, pg_ref), all_g_ref)):
        for side, from_ref in enumerate(from_refs):
            for block in range(blocks_here):
                for head in range(GROUP):
                    to_ref[side * blocks_here + block, head * BLOCK : (head + 1) * BLOCK, :] = from_ref[
                        block * BLOCK : (block + 1) * BLOCK, head * HEAD_DIM : (head + 1) * HEAD_DIM
                    ]
    all_s_ref[0:blocks_here] = s_ref[...]
    all_s_ref[blocks_here:] = ps_ref[...]
    acc_ref[...] = jnp.zeros_like(acc_ref)
    dq_ref[...] = jnp.zeros_like(dq_ref)

    @pl.when(lax.axis_index("rep") == 0)
    def _():
        keys, values = keys_of(kv_ref, slice(None)), values_of(kv_ref, slice(None))
        key_t = transposed(keys)

        def query_step(block, carry):
            number = block + blocks_here
            query = base + number
            flags = [attends(offsets_ref, ids_ref, query, own + key) for key in range(blocks_here)]
            some = flags[0]
            for flag in flags[1:]:
                some |= flag

            @pl.when(some)
            def _():
                dq, dk, dv = block_grads(
                    keys, values, key_t, (all_q_ref, all_g_ref, all_s_ref), number,
                    [bias_of(flag) for flag in flags],
                )
                dq_ref[block] = dq
                add_grads(acc_ref, slice(None), dk, dv)

            return carry

        lax.fori_loop(0, blocks_here, query_step, 0)


def own_kernel(
    offsets_ref, ids_ref, kv_ref, q_ref, g_ref, s_ref, cross_ref, far_ref, acc_ref, dq_ref
):
    blocks_here = kv_ref.shape[0] // BLOCK
    _, _, own = places(blocks_here)
    acc_ref[...] = cross_ref[...]
    keys, values = keys_of(kv_ref, slice(None)), values_of(kv_ref, slice(None))
    key_t = transposed(keys)

    def query_step(block, carry):
        flags = [
            (key >= block) | attends(offsets_ref, ids_ref, own + block, own + key)
            for key in range(blocks_here)
        ]
        dq, dk, dv = block_grads(
            keys, values, key_t, (q_ref, g_ref, s_ref), block,
            [bias_of(flag) for flag in flags], block,
        )
        add_grads(acc_ref, slice(None), dk, dv)
        dq_ref[block] = far_ref[block] + dq
        return carry

    lax.fori_loop(0, blocks_here, query_step, 0)


def query_kernel(own_ref, partner_ref, dq_ref):
    def block_step(block, carry):
        total = own_ref[block] + partner_ref[block].astype(F32)
        rows = pl.ds(pl.multiple_of(block * BLOCK, BLOCK), BLOCK)
        for head in range(GROUP):
            lanes = slice(head * HEAD_DIM, (head + 1) * HEAD_DIM)
            dq_ref[rows, lanes] = total[:, lanes].T.astype(BF16)
        return carry

    lax.fori_loop(0, own_ref.shape[0], block_step, 0)


def final_kernel(last_sender, ids_ref, acc_ref, near_ref, *refs):
    far_refs, (dk_ref, dv_ref, sum_ref) = refs[:-3], refs[-3:]
    blocks_here = acc_ref.shape[0] // BLOCK
    chip_blocks = CORES * blocks_here
    chip = lax.axis_index("ctx")
    core = lax.axis_index("rep")
    sum_ref[...] = acc_ref[...] + near_ref[...].astype(F32)
    dk_ref[...] = keys_of(sum_ref, slice(None)).astype(BF16)
    dv_ref[...] = values_of(sum_ref, slice(None)).astype(BF16)
    capacity = far_refs[0].shape[0] // BLOCK
    for slot in range(SUMMARY):
        owner, rank = chip_slot(ids_ref, slot, chip_blocks)
        local = ids_ref[slot] - chip * chip_blocks - core * blocks_here
        mine = (owner == chip) & (local >= 0) & (local < blocks_here)

        @pl.when(mine & (chip <= last_sender) & (rank < capacity))
        def _():
            rows = pl.ds(pl.multiple_of(local * BLOCK, BLOCK), BLOCK)
            place = pl.ds(pl.multiple_of(rank * BLOCK, BLOCK), BLOCK)
            total = sum_ref[rows, :]
            for far_ref in far_refs:
                total += far_ref[place, :].astype(F32)
            dk_ref[rows, :] = total[:, 0:HEAD_DIM].astype(BF16)
            dv_ref[rows, :] = total[:, HEAD_DIM : 2 * HEAD_DIM].astype(BF16)


def call(kernel, scalars, arrays, out_shape, scratch=(), flops=0, in_space=VMEM, out_specs=None, room=24):
    return pl.pallas_call(
        kernel,
        out_shape=out_shape,
        in_specs=[SMEM] * len(scalars) + [in_space] * len(arrays),
        out_specs=out_specs or jax.tree.map(lambda _: VMEM, out_shape),
        scratch_shapes=list(scratch),
        compiler_params=pltpu.CompilerParams(vmem_limit_bytes=room << 20),
        cost_estimate=pl.CostEstimate(flops=flops, bytes_accessed=0, transcendentals=0),
    )(*scalars, *arrays)


def shape_of(shape, dtype):
    return jax.ShapeDtypeStruct(shape, dtype)


def with_capacity(
    capacity, chips, queries, kv, attn_out, grads, log_sums, window_offsets, summary_ids
):
    rows = queries.shape[0]
    blocks_here = rows // BLOCK
    swap = [(0, 1), (1, 0)]
    up = [(i, i + 1) for i in range(chips - 1)]
    down = [(b, a) for a, b in up]
    routes = far_rounds(chips)
    sources = tuple({b: a // CORES for a, b in route} for route in routes)
    both = ("ctx", "rep")

    kv_partner = lax.ppermute(kv, "rep", swap)
    kv_near = lax.ppermute(kv, "ctx", up)
    far_shape = shape_of((capacity * BLOCK, 2 * HEAD_DIM), BF16)
    picked = call(pick_kernel, (summary_ids,), (kv, kv_partner), far_shape)
    kv_far = [lax.ppermute(picked, both, route) for route in routes]
    attn_out, window_offsets, _ = lax.optimization_barrier((attn_out, window_offsets, picked))
    tables = (window_offsets, summary_ids)
    stats = call(
        prep_kernel, (), (attn_out, grads, log_sums),
        shape_of((blocks_here, 8, GROUP * BLOCK), F32), flops=0,
    )
    own = (queries, grads, stats)
    every = own + tuple(lax.ppermute(x, "rep", swap) for x in own)
    acc_shape = (rows, 2 * HEAD_DIM)
    half_shape = (blocks_here, HEAD_DIM, GROUP * BLOCK)
    chip_blocks = CORES * blocks_here
    dq_shape = shape_of((chip_blocks, *half_shape[1:]), F32)
    stacked_shape = shape_of((chip_blocks, GROUP * BLOCK, HEAD_DIM), BF16)
    cross_acc, cross_dq, *every = call(
        cross_kernel, tables, (kv, *every),
        (
            shape_of(acc_shape, F32), shape_of(half_shape, F32), stacked_shape, stacked_shape,
            shape_of((chip_blocks, *stats.shape[1:]), F32),
        ),
    )
    near_grads, near_dq = call(
        near_kernel, tables, (kv_near, *every, cross_dq), (shape_of(acc_shape, BF16), dq_shape),
        [pltpu.VMEM(acc_shape, F32)],
    )
    near_back = lax.ppermute(near_grads, "ctx", down)
    chunk_shape = (min(capacity, 4) * BLOCK, 2 * HEAD_DIM)
    *far_grads, far_dq, dq_partner = call(
        functools.partial(far_kernel, sources), (summary_ids,), (*kv_far, *every, near_dq),
        (*[far_shape] * len(routes), dq_shape, shape_of(half_shape, BF16)),
        [pltpu.VMEM(chunk_shape, F32)], flops=5 * MICROSECOND,
    )
    far_back = [
        lax.ppermute(x, both, [(b, a) for a, b in route]) for x, route in zip(far_grads, routes)
    ]
    dq_partner = lax.ppermute(dq_partner, "rep", swap)
    acc, dq = call(
        own_kernel, tables, (kv, *every, cross_acc, far_dq),
        (shape_of(acc_shape, F32), shape_of(half_shape, F32)), flops=OWN,
    )
    query_grads = call(query_kernel, (), (dq, dq_partner), shape_of(queries.shape, BF16))
    if capacity > 4:
        acc, near_back = lax.optimization_barrier((acc, near_back))
    far_back, acc, query_grads = lax.optimization_barrier((far_back, acc, query_grads))
    far_other = [lax.ppermute(x, "rep", swap) for x in far_back]
    kv_shape = shape_of((rows, HEAD_DIM), BF16)
    key_grads, value_grads = call(
        functools.partial(final_kernel, chips - 3), (summary_ids,),
        (acc, near_back, *far_back, *far_other), (kv_shape, kv_shape),
        [pltpu.VMEM(acc_shape, F32)],
    )
    return query_grads, key_grads, value_grads


def capacities(chips):
    return CAPACITIES if len(far_rounds(chips)) == 1 else CAPACITIES[-1:]


def per_device(chips, queries, keys, values, attn_out, grads, log_sums, window_offsets, summary_ids):
    kv, branch = call(
        functools.partial(start_kernel, chips), (), (summary_ids, keys, values),
        (shape_of((keys.shape[0], 2 * HEAD_DIM), BF16), shape_of((1,), jnp.int32)),
        [pltpu.SMEM(summary_ids.shape, jnp.int32), pltpu.SemaphoreType.DMA((3,))], in_space=HBM, out_specs=(VMEM, SMEM), room=60,
    )
    branches = [functools.partial(with_capacity, limit, chips) for limit in capacities(chips)]
    operands = (queries, kv, attn_out, grads, log_sums, window_offsets, summary_ids)
    return lax.switch(branch[0], branches, *operands) if len(branches) > 1 else branches[0](*operands)


def solution(mesh):
    rows = P(("groups", "ctx", "rep"), "heads")
    return jax.shard_map(
        functools.partial(per_device, mesh.shape["ctx"]),
        mesh=mesh,
        in_specs=(rows,) * 5 + (P("heads", ("groups", "ctx", "rep")), P("groups", None), P("groups")),
        out_specs=(rows,) * 3,
        check_vma=False,
    )
```

```python
import functools
import math

import jax
import jax.numpy as jnp
from jax import lax
from jax.experimental import pallas as pl
from jax.experimental.pallas import tpu as pltpu
from jax.sharding import PartitionSpec as P

HEAD_DIM = 128
GROUP = 4
BLOCK = 128
REACH = 3
SUMMARY = 8
CORES = 2
SCALE = HEAD_DIM ** (-0.5)
LOG2E = math.log2(math.e)
MICROSECOND = 1_000_000_000
OWN = 10 * MICROSECOND
CAPACITIES = (2, 3, 4, 5, SUMMARY)
F32 = jnp.float32
BF16 = jnp.bfloat16
VMEM = pl.BlockSpec(memory_space=pltpu.VMEM)
SMEM = pl.BlockSpec(memory_space=pltpu.SMEM)
HBM = pl.BlockSpec(memory_space=pltpu.HBM)


def far_rounds(chips):
    rounds = []
    for source in range(chips):
        for target in range(source + 2, chips):
            for senders, receivers, route in rounds:
                if senders.get(source, 0) < CORES and receivers.get(target, 0) < CORES:
                    break
            else:
                senders, receivers, route = {}, {}, []
                rounds.append((senders, receivers, route))
            sent, got = senders.get(source, 0), receivers.get(target, 0)
            route.append((source * CORES + sent, target * CORES + got))
            senders[source], receivers[target] = sent + 1, got + 1
    return [route for _, _, route in rounds]


def table_entry(table, position):
    value = jnp.int32(-1)
    for place, entry in table.items():
        value = jnp.where(position == place, jnp.int32(entry), value)
    return value


def chip_slot(ids_ref, slot, chip_blocks):
    chip = ids_ref[slot] // chip_blocks
    rank = jnp.int32(0)
    for other in range(slot):
        rank += jnp.where(ids_ref[other] // chip_blocks == chip, 1, 0)
    return chip, rank


def chip_count(ids_ref, chip, chip_blocks):
    count = jnp.int32(0)
    for slot in range(SUMMARY):
        count += jnp.where(ids_ref[slot] // chip_blocks == chip, 1, 0)
    return count


def prep_kernel(out_ref, grad_ref, lse_ref, stats_ref):
    stats_ref[...] = jnp.zeros_like(stats_ref)
    for block in range(stats_ref.shape[0]):
        rows = slice(block * BLOCK, (block + 1) * BLOCK)
        for head in range(GROUP):
            columns = slice(head * HEAD_DIM, (head + 1) * HEAD_DIM)
            product = out_ref[rows, columns].astype(F32) * grad_ref[rows, columns].astype(F32)
            stats_ref[block, 0:1, columns] = lse_ref[head : head + 1, rows] * LOG2E
            stats_ref[block, 1:2, columns] = jnp.sum(product.T, axis=0, keepdims=True)


def start_kernel(chips, ids_hbm, key_ref, value_ref, kv_ref, branch_ref, ids_ref, sems):
    chip_blocks = CORES * (key_ref.shape[0] // BLOCK)
    copies = [
        pltpu.make_async_copy(
            ref, kv_ref.at[:, number * HEAD_DIM : (number + 1) * HEAD_DIM], sems.at[number]
        )
        for number, ref in enumerate((key_ref, value_ref))
    ]
    ids_copy = pltpu.make_async_copy(ids_hbm, ids_ref, sems.at[2])
    ids_copy.start()
    for copy in copies:
        copy.start()
    ids_copy.wait()
    most = jnp.int32(0)
    for chip in range(chips - 2):
        most = jnp.maximum(most, chip_count(ids_ref, chip, chip_blocks))
    branch = jnp.int32(0)
    for capacity in capacities(chips)[:-1]:
        branch += jnp.where(most > capacity, 1, 0)
    branch_ref[0] = branch
    for copy in copies:
        copy.wait()


def pick_kernel(ids_ref, own_ref, partner_ref, picked_ref):
    chip = lax.axis_index("ctx")
    core = lax.axis_index("rep")
    blocks_here = own_ref.shape[0] // BLOCK
    chip_blocks = CORES * blocks_here
    capacity = picked_ref.shape[0] // BLOCK
    picked_ref[...] = jnp.zeros_like(picked_ref)
    for slot in range(SUMMARY):
        owner, rank = chip_slot(ids_ref, slot, chip_blocks)
        local = ids_ref[slot] - chip * chip_blocks
        row = pl.multiple_of((local % blocks_here) * BLOCK, BLOCK)
        place = pl.multiple_of(rank * BLOCK, BLOCK)
        mine = local // blocks_here == core
        wanted = (owner == chip) & (rank < capacity)

        @pl.when(wanted & mine)
        def _():
            picked_ref[pl.ds(place, BLOCK), :] = own_ref[pl.ds(row, BLOCK), :]

        @pl.when(wanted & ~mine)
        def _():
            picked_ref[pl.ds(place, BLOCK), :] = partner_ref[pl.ds(row, BLOCK), :]


def nt(a, b):
    return lax.dot_general(a, b, (((1,), (1,)), ((), ())), preferred_element_type=F32)


def nn(a, b):
    return jnp.dot(a, b, preferred_element_type=F32)


def block_grads(keys, values, key_t, query_refs, number, biases=None, query_at=None):
    query_ref, grad_ref, stats_ref = query_refs
    queries, grads = query_ref[number], grad_ref[number]
    log_sums, deltas = stats_ref[number, 0:1, :], stats_ref[number, 1:2, :]
    scores = nt(keys, queries) * (SCALE * LOG2E)
    if biases is None:
        probs = jnp.exp2(scores - log_sums)
    else:
        parts = []
        for key, bias in enumerate(biases):
            part = jnp.exp2(scores[key * BLOCK : (key + 1) * BLOCK] - (log_sums + bias))
            if query_at is not None:
                row = lax.broadcasted_iota(jnp.int32, part.shape, 0)
                column = lax.broadcasted_iota(jnp.int32, part.shape, 1) % BLOCK
                part = jnp.where(column - row >= (key - query_at) * BLOCK, part, 0.0)
            parts.append(part)
        probs = jnp.concatenate(parts, axis=0)
    prob_grads = nt(values, grads)
    score_grads = (probs * (prob_grads - deltas) * SCALE).astype(BF16)
    return nn(key_t, score_grads), nn(score_grads, queries), nn(probs.astype(BF16), grads)


def is_summary(ids_ref, key_block):
    found = ids_ref[0] == key_block
    for slot in range(1, SUMMARY):
        found |= ids_ref[slot] == key_block
    return found


def in_window(offsets_ref, query_block, key_block):
    distance = query_block - key_block
    return (distance == offsets_ref[0, query_block]) | (distance == offsets_ref[1, query_block])


def attends(offsets_ref, ids_ref, query_block, key_block):
    chosen = in_window(offsets_ref, query_block, key_block) | is_summary(ids_ref, key_block)
    return (query_block > key_block) & chosen


def keys_of(kv_ref, rows):
    return kv_ref[rows, 0:HEAD_DIM]


def values_of(kv_ref, rows):
    return kv_ref[rows, HEAD_DIM : 2 * HEAD_DIM]


def transposed(keys):
    return keys.astype(F32).T.astype(BF16)


def add_grads(acc_ref, rows, key_part, value_part):
    acc_ref[rows, 0:HEAD_DIM] += key_part
    acc_ref[rows, HEAD_DIM : 2 * HEAD_DIM] += value_part


def places(blocks_here):
    chip = lax.axis_index("ctx")
    base = chip * CORES * blocks_here
    return chip, base, base + lax.axis_index("rep") * blocks_here


def bias_of(flag):
    return jnp.where(flag, 0.0, 1e30).astype(F32)


def near_kernel(
    offsets_ref, ids_ref, kv_ref, q_ref, g_ref, s_ref, local_ref, grads_ref, dq_ref, acc_ref
):
    query_refs = (q_ref, g_ref, s_ref)
    blocks_here = kv_ref.shape[0] // BLOCK
    chip_blocks = CORES * blocks_here
    chip, base, own = places(blocks_here)
    first_key = own - chip_blocks
    acc_ref[...] = jnp.zeros_like(acc_ref)
    dq_ref[0:blocks_here] = jnp.zeros_like(local_ref)
    dq_ref[blocks_here:] = local_ref[...]
    flags = [is_summary(ids_ref, first_key + key) & (chip > 0) for key in range(blocks_here)]
    count = jnp.int32(0)
    chosen = [jnp.int32(0)] * blocks_here
    for key in range(blocks_here):
        for place in range(key + 1):
            chosen[place] = jnp.where(flags[key] & (count == place), key, chosen[place])
        count += jnp.where(flags[key], 1, 0)

    def add(number, keys, biases):
        rows = [pl.ds(pl.multiple_of(key * BLOCK, BLOCK), BLOCK) for key in keys]
        keys = jnp.concatenate([keys_of(kv_ref, row) for row in rows], axis=0)
        values = jnp.concatenate([values_of(kv_ref, row) for row in rows], axis=0)
        dq, dk, dv = block_grads(keys, values, transposed(keys), query_refs, number, biases)
        dq_ref[number] += dq
        for place, row in enumerate(rows):
            part = slice(place * BLOCK, (place + 1) * BLOCK)
            add_grads(acc_ref, row, dk[part], dv[part])

    def single_step(number, carry):
        add(number, [chosen[0]], None)
        return carry

    odd = lax.rem(count, 2)
    lax.fori_loop(0, odd * (chip_blocks // 2), lambda i, c: single_step(2 * i + 1, single_step(2 * i, c)), 0)
    pairs = (count // 2) * chip_blocks
    windows = jnp.where((chip > 0) & (lax.axis_index("rep") == CORES - 1), min(REACH, blocks_here), 0)

    def double_step(item, carry):
        summary = item < pairs
        number = jnp.where(summary, lax.rem(item, chip_blocks), item - pairs)
        query = base + number
        turn = odd + 2 * (item // chip_blocks)
        firsts, seconds = jnp.int32(0), jnp.int32(0)
        for place in range(blocks_here):
            firsts = jnp.where(turn == place, chosen[place], firsts)
            seconds = jnp.where(turn + 1 == place, chosen[place], seconds)
        keys, wanted = [], []
        for place, from_summary in enumerate((firsts, seconds)):
            key = query - offsets_ref[place, query] - first_key
            fits = (key >= 0) & (key < blocks_here)
            key = jnp.where(fits, key, 0)
            for block in range(blocks_here):
                fits &= (key != block) | ~flags[block]
            keys.append(jnp.where(summary, from_summary, key))
            wanted.append(summary | fits)
        own_number = number + jnp.where(summary, 0, blocks_here)

        @pl.when(wanted[0] | wanted[1])
        def _():
            add(own_number, keys, [bias_of(flag) for flag in wanted])

        return carry

    lax.fori_loop(0, pairs + windows, double_step, 0)
    grads_ref[...] = acc_ref[...].astype(BF16)


def far_kernel(sources, ids_ref, *refs):
    count = len(sources)
    kv_refs, query_refs, near_ref, refs = refs[:count], refs[count : count + 3], refs[count + 3], refs[count + 4 :]
    grads_refs, (dq_ref, partner_ref, acc_ref) = refs[:count], refs[count:]
    chip_blocks = near_ref.shape[0]
    blocks_here = chip_blocks // CORES
    capacity = kv_refs[0].shape[0] // BLOCK
    position = lax.axis_index("ctx") * CORES + lax.axis_index("rep")
    chunk = min(capacity, 4)
    dq_ref[...] = near_ref[...]
    for table, kv_ref, grads_ref in zip(sources, kv_refs, grads_refs):
        held = chip_count(ids_ref, table_entry(table, position), chip_blocks)
        grads_ref[...] = jnp.zeros_like(grads_ref)

        def chunk_step(turn, carry):
            rows = pl.ds(pl.multiple_of(turn * (chunk * BLOCK), BLOCK), chunk * BLOCK)
            keys, values = keys_of(kv_ref, rows), values_of(kv_ref, rows)
            key_t = transposed(keys)
            acc_ref[...] = jnp.zeros_like(acc_ref)

            def query_step(number, carry):
                dq, dk, dv = block_grads(keys, values, key_t, query_refs, number)
                dq_ref[number] += dq
                add_grads(acc_ref, slice(None), dk, dv)
                return carry

            lax.fori_loop(0, chip_blocks, query_step, 0, unroll=2)
            grads_ref[rows, :] = acc_ref[...].astype(BF16)
            return carry

        lax.fori_loop(0, (held + chunk - 1) // chunk, chunk_step, 0)
    partner_ref[...] = dq_ref[blocks_here:].astype(BF16)


def cross_kernel(
    offsets_ref, ids_ref, kv_ref, q_ref, g_ref, s_ref, pq_ref, pg_ref, ps_ref,
    acc_ref, dq_ref, all_q_ref, all_g_ref, all_s_ref,
):
    blocks_here = kv_ref.shape[0] // BLOCK
    _, base, own = places(blocks_here)
    for from_refs, to_ref in (((q_ref, pq_ref), all_q_ref), ((g_ref, pg_ref), all_g_ref)):
        for side, from_ref in enumerate(from_refs):
            for block in range(blocks_here):
                for head in range(GROUP):
                    to_ref[side * blocks_here + block, head * BLOCK : (head + 1) * BLOCK, :] = from_ref[
                        block * BLOCK : (block + 1) * BLOCK, head * HEAD_DIM : (head + 1) * HEAD_DIM
                    ]
    all_s_ref[0:blocks_here] = s_ref[...]
    all_s_ref[blocks_here:] = ps_ref[...]
    acc_ref[...] = jnp.zeros_like(acc_ref)
    dq_ref[...] = jnp.zeros_like(dq_ref)

    @pl.when(lax.axis_index("rep") == 0)
    def _():
        keys, values = keys_of(kv_ref, slice(None)), values_of(kv_ref, slice(None))
        key_t = transposed(keys)

        def query_step(block, carry):
            number = block + blocks_here
            query = base + number
            flags = [attends(offsets_ref, ids_ref, query, own + key) for key in range(blocks_here)]
            some = flags[0]
            for flag in flags[1:]:
                some |= flag

            @pl.when(some)
            def _():
                dq, dk, dv = block_grads(
                    keys, values, key_t, (all_q_ref, all_g_ref, all_s_ref), number,
                    [bias_of(flag) for flag in flags],
                )
                dq_ref[block] = dq
                add_grads(acc_ref, slice(None), dk, dv)

            return carry

        lax.fori_loop(0, blocks_here, query_step, 0)


def own_kernel(
    offsets_ref, ids_ref, kv_ref, q_ref, g_ref, s_ref, cross_ref, far_ref, acc_ref, dq_ref
):
    blocks_here = kv_ref.shape[0] // BLOCK
    _, _, own = places(blocks_here)
    acc_ref[...] = cross_ref[...]
    keys, values = keys_of(kv_ref, slice(None)), values_of(kv_ref, slice(None))
    key_t = transposed(keys)

    def query_step(block, carry):
        flags = [
            (key >= block) | attends(offsets_ref, ids_ref, own + block, own + key)
            for key in range(blocks_here)
        ]
        dq, dk, dv = block_grads(
            keys, values, key_t, (q_ref, g_ref, s_ref), block,
            [bias_of(flag) for flag in flags], block,
        )
        add_grads(acc_ref, slice(None), dk, dv)
        dq_ref[block] = far_ref[block] + dq
        return carry

    lax.fori_loop(0, blocks_here, query_step, 0)


def query_kernel(own_ref, partner_ref, dq_ref):
    def block_step(block, carry):
        total = own_ref[block] + partner_ref[block].astype(F32)
        rows = pl.ds(pl.multiple_of(block * BLOCK, BLOCK), BLOCK)
        for head in range(GROUP):
            lanes = slice(head * HEAD_DIM, (head + 1) * HEAD_DIM)
            dq_ref[rows, lanes] = total[:, lanes].T.astype(BF16)
        return carry

    lax.fori_loop(0, own_ref.shape[0], block_step, 0)


def final_kernel(last_sender, ids_ref, acc_ref, near_ref, *refs):
    far_refs, (dk_ref, dv_ref, sum_ref) = refs[:-3], refs[-3:]
    blocks_here = acc_ref.shape[0] // BLOCK
    chip_blocks = CORES * blocks_here
    chip = lax.axis_index("ctx")
    core = lax.axis_index("rep")
    sum_ref[...] = acc_ref[...] + near_ref[...].astype(F32)
    dk_ref[...] = keys_of(sum_ref, slice(None)).astype(BF16)
    dv_ref[...] = values_of(sum_ref, slice(None)).astype(BF16)
    capacity = far_refs[0].shape[0] // BLOCK
    for slot in range(SUMMARY):
        owner, rank = chip_slot(ids_ref, slot, chip_blocks)
        local = ids_ref[slot] - chip * chip_blocks - core * blocks_here
        mine = (owner == chip) & (local >= 0) & (local < blocks_here)

        @pl.when(mine & (chip <= last_sender) & (rank < capacity))
        def _():
            rows = pl.ds(pl.multiple_of(local * BLOCK, BLOCK), BLOCK)
            place = pl.ds(pl.multiple_of(rank * BLOCK, BLOCK), BLOCK)
            total = sum_ref[rows, :]
            for far_ref in far_refs:
                total += far_ref[place, :].astype(F32)
            dk_ref[rows, :] = total[:, 0:HEAD_DIM].astype(BF16)
            dv_ref[rows, :] = total[:, HEAD_DIM : 2 * HEAD_DIM].astype(BF16)


def call(kernel, scalars, arrays, out_shape, scratch=(), flops=0, in_space=VMEM, out_specs=None, room=24):
    return pl.pallas_call(
        kernel,
        out_shape=out_shape,
        in_specs=[SMEM] * len(scalars) + [in_space] * len(arrays),
        out_specs=out_specs or jax.tree.map(lambda _: VMEM, out_shape),
        scratch_shapes=list(scratch),
        compiler_params=pltpu.CompilerParams(vmem_limit_bytes=room << 20),
        cost_estimate=pl.CostEstimate(flops=flops, bytes_accessed=0, transcendentals=0),
    )(*scalars, *arrays)


def shape_of(shape, dtype):
    return jax.ShapeDtypeStruct(shape, dtype)


def with_capacity(
    capacity, chips, queries, kv, attn_out, grads, log_sums, window_offsets, summary_ids
):
    rows = queries.shape[0]
    blocks_here = rows // BLOCK
    swap = [(0, 1), (1, 0)]
    up = [(i, i + 1) for i in range(chips - 1)]
    down = [(b, a) for a, b in up]
    routes = far_rounds(chips)
    sources = tuple({b: a // CORES for a, b in route} for route in routes)
    both = ("ctx", "rep")

    kv_partner = lax.ppermute(kv, "rep", swap)
    kv_near = lax.ppermute(kv, "ctx", up)
    far_shape = shape_of((capacity * BLOCK, 2 * HEAD_DIM), BF16)
    picked = call(pick_kernel, (summary_ids,), (kv, kv_partner), far_shape)
    kv_far = [lax.ppermute(picked, both, route) for route in routes]
    attn_out, window_offsets, _ = lax.optimization_barrier((attn_out, window_offsets, picked))
    tables = (window_offsets, summary_ids)
    stats = call(
        prep_kernel, (), (attn_out, grads, log_sums),
        shape_of((blocks_here, 8, GROUP * BLOCK), F32), flops=0,
    )
    own = (queries, grads, stats)
    every = own + tuple(lax.ppermute(x, "rep", swap) for x in own)
    acc_shape = (rows, 2 * HEAD_DIM)
    half_shape = (blocks_here, HEAD_DIM, GROUP * BLOCK)
    chip_blocks = CORES * blocks_here
    dq_shape = shape_of((chip_blocks, *half_shape[1:]), F32)
    stacked_shape = shape_of((chip_blocks, GROUP * BLOCK, HEAD_DIM), BF16)
    cross_acc, cross_dq, *every = call(
        cross_kernel, tables, (kv, *every),
        (
            shape_of(acc_shape, F32), shape_of(half_shape, F32), stacked_shape, stacked_shape,
            shape_of((chip_blocks, *stats.shape[1:]), F32),
        ),
    )
    near_grads, near_dq = call(
        near_kernel, tables, (kv_near, *every, cross_dq), (shape_of(acc_shape, BF16), dq_shape),
        [pltpu.VMEM(acc_shape, F32)],
    )
    chunk_shape = (min(capacity, 4) * BLOCK, 2 * HEAD_DIM)
    *far_grads, far_dq, dq_partner = call(
        functools.partial(far_kernel, sources), (summary_ids,), (*kv_far, *every, near_dq),
        (*[far_shape] * len(routes), dq_shape, shape_of(half_shape, BF16)),
        [pltpu.VMEM(chunk_shape, F32)], flops=5 * MICROSECOND,
    )
    far_back = [
        lax.ppermute(x, both, [(b, a) for a, b in route]) for x, route in zip(far_grads, routes)
    ]
    near_grads, _ = lax.optimization_barrier((near_grads, far_grads))
    near_back = lax.ppermute(near_grads, "ctx", down)
    dq_partner = lax.ppermute(dq_partner, "rep", swap)
    acc, dq = call(
        own_kernel, tables, (kv, *every, cross_acc, far_dq),
        (shape_of(acc_shape, F32), shape_of(half_shape, F32)), flops=OWN,
    )
    query_grads = call(query_kernel, (), (dq, dq_partner), shape_of(queries.shape, BF16))
    if capacity > 4:
        acc, near_back = lax.optimization_barrier((acc, near_back))
    far_back, acc, query_grads = lax.optimization_barrier((far_back, acc, query_grads))
    far_other = [lax.ppermute(x, "rep", swap) for x in far_back]
    kv_shape = shape_of((rows, HEAD_DIM), BF16)
    key_grads, value_grads = call(
        functools.partial(final_kernel, chips - 3), (summary_ids,),
        (acc, near_back, *far_back, *far_other), (kv_shape, kv_shape),
        [pltpu.VMEM(acc_shape, F32)],
    )
    return query_grads, key_grads, value_grads


def capacities(chips):
    return CAPACITIES if len(far_rounds(chips)) == 1 else CAPACITIES[-1:]


def per_device(chips, queries, keys, values, attn_out, grads, log_sums, window_offsets, summary_ids):
    kv, branch = call(
        functools.partial(start_kernel, chips), (), (summary_ids, keys, values),
        (shape_of((keys.shape[0], 2 * HEAD_DIM), BF16), shape_of((1,), jnp.int32)),
        [pltpu.SMEM(summary_ids.shape, jnp.int32), pltpu.SemaphoreType.DMA((3,))], in_space=HBM, out_specs=(VMEM, SMEM), room=60,
    )
    branches = [functools.partial(with_capacity, limit, chips) for limit in capacities(chips)]
    operands = (queries, kv, attn_out, grads, log_sums, window_offsets.T, summary_ids)
    return lax.switch(branch[0], branches, *operands) if len(branches) > 1 else branches[0](*operands)


def solution(mesh):
    rows = P(("groups", "ctx", "rep"), "heads")
    return jax.shard_map(
        functools.partial(per_device, mesh.shape["ctx"]),
        mesh=mesh,
        in_specs=(rows,) * 5 + (P("heads", ("groups", "ctx", "rep")), P("groups", None), P("groups")),
        out_specs=(rows,) * 3,
        check_vma=False,
    )
```

```python
import functools
import math

import jax
import jax.numpy as jnp
from jax import lax
from jax.experimental import pallas as pl
from jax.experimental.pallas import tpu as pltpu
from jax.sharding import PartitionSpec as P

HEAD_DIM = 128
GROUP = 4
BLOCK = 128
REACH = 3
SUMMARY = 8
CORES = 2
SCALE = HEAD_DIM ** (-0.5)
LOG2E = math.log2(math.e)
MICROSECOND = 1_000_000_000
OWN = 10 * MICROSECOND
CAPACITIES = (2, 3, 4, SUMMARY - 1)
F32 = jnp.float32
BF16 = jnp.bfloat16
VMEM = pl.BlockSpec(memory_space=pltpu.VMEM)
SMEM = pl.BlockSpec(memory_space=pltpu.SMEM)
HBM = pl.BlockSpec(memory_space=pltpu.HBM)


def far_rounds(chips):
    rounds = []
    for source in range(chips):
        for target in range(source + 2, chips):
            for senders, receivers, route in rounds:
                if senders.get(source, 0) < CORES and receivers.get(target, 0) < CORES:
                    break
            else:
                senders, receivers, route = {}, {}, []
                rounds.append((senders, receivers, route))
            sent, got = senders.get(source, 0), receivers.get(target, 0)
            route.append((source * CORES + sent, target * CORES + got))
            senders[source], receivers[target] = sent + 1, got + 1
    return [route for _, _, route in rounds]


def table_entry(table, position):
    value = jnp.int32(-1)
    for place, entry in table.items():
        value = jnp.where(position == place, jnp.int32(entry), value)
    return value


def chip_slot(ids_ref, slot, chip_blocks):
    chip = ids_ref[slot] // chip_blocks
    rank = jnp.int32(0)
    for other in range(slot):
        rank += jnp.where(ids_ref[other] // chip_blocks == chip, 1, 0)
    return chip, rank


def chip_count(ids_ref, chip, chip_blocks):
    count = jnp.int32(0)
    for slot in range(SUMMARY):
        count += jnp.where(ids_ref[slot] // chip_blocks == chip, 1, 0)
    return count


def prep_kernel(out_ref, grad_ref, lse_ref, stats_ref):
    stats_ref[...] = jnp.zeros_like(stats_ref)
    for block in range(stats_ref.shape[0]):
        rows = slice(block * BLOCK, (block + 1) * BLOCK)
        for head in range(GROUP):
            columns = slice(head * HEAD_DIM, (head + 1) * HEAD_DIM)
            product = out_ref[rows, columns].astype(F32) * grad_ref[rows, columns].astype(F32)
            stats_ref[block, 0:1, columns] = lse_ref[head : head + 1, rows] * LOG2E
            stats_ref[block, 1:2, columns] = jnp.sum(product.T, axis=0, keepdims=True)


def start_kernel(chips, ids_hbm, key_ref, value_ref, kv_ref, branch_ref, ids_ref, sems):
    chip_blocks = CORES * (key_ref.shape[0] // BLOCK)
    copies = [
        pltpu.make_async_copy(
            ref, kv_ref.at[:, number * HEAD_DIM : (number + 1) * HEAD_DIM], sems.at[number]
        )
        for number, ref in enumerate((key_ref, value_ref))
    ]
    ids_copy = pltpu.make_async_copy(ids_hbm, ids_ref, sems.at[2])
    ids_copy.start()
    for copy in copies:
        copy.start()
    ids_copy.wait()
    most = jnp.int32(0)
    for chip in range(chips - 2):
        most = jnp.maximum(most, chip_count(ids_ref, chip, chip_blocks))
    branch = jnp.int32(0)
    for capacity in capacities(chips)[:-1]:
        branch += jnp.where(most > capacity, 1, 0)
    branch_ref[0] = branch
    for copy in copies:
        copy.wait()


def pick_kernel(ids_ref, own_ref, partner_ref, picked_ref):
    chip = lax.axis_index("ctx")
    core = lax.axis_index("rep")
    blocks_here = own_ref.shape[0] // BLOCK
    chip_blocks = CORES * blocks_here
    capacity = picked_ref.shape[0] // BLOCK
    picked_ref[...] = jnp.zeros_like(picked_ref)
    for slot in range(SUMMARY):
        owner, rank = chip_slot(ids_ref, slot, chip_blocks)
        local = ids_ref[slot] - chip * chip_blocks
        row = pl.multiple_of((local % blocks_here) * BLOCK, BLOCK)
        place = pl.multiple_of(rank * BLOCK, BLOCK)
        mine = local // blocks_here == core
        wanted = (owner == chip) & (rank < capacity)

        @pl.when(wanted & mine)
        def _():
            picked_ref[pl.ds(place, BLOCK), :] = own_ref[pl.ds(row, BLOCK), :]

        @pl.when(wanted & ~mine)
        def _():
            picked_ref[pl.ds(place, BLOCK), :] = partner_ref[pl.ds(row, BLOCK), :]


def nt(a, b):
    return lax.dot_general(a, b, (((1,), (1,)), ((), ())), preferred_element_type=F32)


def nn(a, b):
    return jnp.dot(a, b, preferred_element_type=F32)


def block_grads(keys, values, key_t, query_refs, first, count=1, biases=None, query_at=None):
    query_ref, grad_ref, stats_ref = query_refs
    numbers = [first + step for step in range(count)]
    queries = jnp.concatenate([query_ref[number] for number in numbers], axis=0)
    grads = jnp.concatenate([grad_ref[number] for number in numbers], axis=0)
    log_sums = jnp.concatenate([stats_ref[number, 0:1, :] for number in numbers], axis=1)
    deltas = jnp.concatenate([stats_ref[number, 1:2, :] for number in numbers], axis=1)
    scores = nt(keys, queries) * (SCALE * LOG2E)
    if biases is None:
        probs = jnp.exp2(scores - log_sums)
    else:
        parts = []
        for key, bias in enumerate(biases):
            part = jnp.exp2(scores[key * BLOCK : (key + 1) * BLOCK] - (log_sums + bias))
            if query_at is not None:
                row = lax.broadcasted_iota(jnp.int32, part.shape, 0)
                column = lax.broadcasted_iota(jnp.int32, part.shape, 1) % BLOCK
                part = jnp.where(column - row >= (key - query_at) * BLOCK, part, 0.0)
            parts.append(part)
        probs = jnp.concatenate(parts, axis=0)
    prob_grads = nt(values, grads)
    score_grads = (probs * (prob_grads - deltas) * SCALE).astype(BF16)
    return nn(key_t, score_grads), nn(score_grads, queries), nn(probs.astype(BF16), grads)


def put_queries(to_ref, from_ref, first, dq):
    width = GROUP * BLOCK
    for step in range(dq.shape[1] // width):
        part = dq[:, step * width : (step + 1) * width]
        to_ref[first + step] = from_ref[first + step] + part


def is_summary(ids_ref, key_block):
    found = ids_ref[0] == key_block
    for slot in range(1, SUMMARY):
        found |= ids_ref[slot] == key_block
    return found


def in_window(offsets_ref, query_block, key_block):
    distance = query_block - key_block
    return (distance == offsets_ref[0, query_block]) | (distance == offsets_ref[1, query_block])


def attends(offsets_ref, ids_ref, query_block, key_block):
    chosen = in_window(offsets_ref, query_block, key_block) | is_summary(ids_ref, key_block)
    return (query_block > key_block) & chosen


def keys_of(kv_ref, rows):
    return kv_ref[rows, 0:HEAD_DIM]


def values_of(kv_ref, rows):
    return kv_ref[rows, HEAD_DIM : 2 * HEAD_DIM]


def transposed(keys):
    return keys.astype(F32).T.astype(BF16)


def add_grads(acc_ref, rows, key_part, value_part):
    acc_ref[rows, 0:HEAD_DIM] += key_part
    acc_ref[rows, HEAD_DIM : 2 * HEAD_DIM] += value_part


def places(blocks_here):
    chip = lax.axis_index("ctx")
    base = chip * CORES * blocks_here
    return chip, base, base + lax.axis_index("rep") * blocks_here


def bias_of(flag):
    return jnp.where(flag, 0.0, 1e30).astype(F32)


def near_kernel(
    offsets_ref, ids_ref, kv_ref, q_ref, g_ref, s_ref, local_ref, grads_ref, dq_ref, acc_ref
):
    query_refs = (q_ref, g_ref, s_ref)
    blocks_here = kv_ref.shape[0] // BLOCK
    chip_blocks = CORES * blocks_here
    chip, base, own = places(blocks_here)
    first_key = own - chip_blocks
    acc_ref[...] = jnp.zeros_like(acc_ref)
    dq_ref[0:blocks_here] = jnp.zeros_like(local_ref)
    dq_ref[blocks_here:] = local_ref[...]
    flags = [is_summary(ids_ref, first_key + key) & (chip > 0) for key in range(blocks_here)]
    count = jnp.int32(0)
    chosen = [jnp.int32(0)] * blocks_here
    for key in range(blocks_here):
        for place in range(key + 1):
            chosen[place] = jnp.where(flags[key] & (count == place), key, chosen[place])
        count += jnp.where(flags[key], 1, 0)

    def add(first, count, places_of_keys, biases=None):
        rows = [pl.ds(pl.multiple_of(key * BLOCK, BLOCK), BLOCK) for key in places_of_keys]
        keys = jnp.concatenate([keys_of(kv_ref, row) for row in rows], axis=0)
        values = jnp.concatenate([values_of(kv_ref, row) for row in rows], axis=0)
        dq, dk, dv = block_grads(keys, values, transposed(keys), query_refs, first, count, biases)
        put_queries(dq_ref, dq_ref, first, dq)
        for place, row in enumerate(rows):
            part = slice(place * BLOCK, (place + 1) * BLOCK)
            add_grads(acc_ref, row, dk[part], dv[part])

    def entry(place):
        key = jnp.int32(0)
        for number in range(blocks_here):
            key = jnp.where(place == number, chosen[number], key)
        return key

    odd = lax.rem(count, 2)

    def single_step(item, carry):
        add(item * 4, 4, [chosen[0]])
        return carry

    lax.fori_loop(0, odd * (chip_blocks // 4), single_step, 0)

    def double_step(item, carry):
        turn = odd + 2 * (item // (chip_blocks // 2))
        add(lax.rem(item, chip_blocks // 2) * 2, 2, [entry(turn), entry(turn + 1)])
        return carry

    lax.fori_loop(0, (count // 2) * (chip_blocks // 2), double_step, 0)

    def window_step(number, carry):
        query = base + number
        keys, wanted = [], []
        for place in range(2):
            key = query - offsets_ref[place, query] - first_key
            fits = (key >= 0) & (key < blocks_here)
            key = jnp.where(fits, key, 0)
            for block in range(blocks_here):
                fits &= (key != block) | ~flags[block]
            keys.append(key)
            wanted.append(fits)

        @pl.when(wanted[0] | wanted[1])
        def _():
            add(number + blocks_here, 1, keys, [bias_of(flag) for flag in wanted])

        return carry

    reaches = (chip > 0) & (lax.axis_index("rep") == CORES - 1)
    lax.fori_loop(0, jnp.where(reaches, min(REACH, blocks_here), 0), window_step, 0)
    grads_ref[...] = acc_ref[...].astype(BF16)


def far_kernel(sources, ids_ref, *refs):
    count = len(sources)
    kv_refs, refs = refs[:count], refs[count:]
    query_refs, near_ref, refs = refs[:3], refs[3], refs[4:]
    grads_refs, (dq_ref, partner_ref, acc_ref) = refs[:count], refs[count:]
    chip_blocks = near_ref.shape[0]
    position = lax.axis_index("ctx") * CORES + lax.axis_index("rep")
    capacity = acc_ref.shape[0] // BLOCK
    together = 4 if capacity < 4 else 2 if capacity == 4 else 1
    if count > 1:
        dq_ref[...] = near_ref[...]
        near_ref = dq_ref
    for table, kv_ref, grads_ref in zip(sources, kv_refs, grads_refs):
        held = chip_count(ids_ref, table_entry(table, position), chip_blocks)

        @pl.when(held > 0)
        def _():
            keys, values = keys_of(kv_ref, slice(None)), values_of(kv_ref, slice(None))
            key_t = transposed(keys)
            acc_ref[...] = jnp.zeros_like(acc_ref)

            def query_step(item, carry):
                first = item * together
                dq, dk, dv = block_grads(keys, values, key_t, query_refs, first, together)
                put_queries(dq_ref, near_ref, first, dq)
                add_grads(acc_ref, slice(None), dk, dv)
                return carry

            lax.fori_loop(0, chip_blocks // together, query_step, 0)
            grads_ref[...] = acc_ref[...].astype(BF16)

        @pl.when(held == 0)
        def _():
            grads_ref[...] = jnp.zeros_like(grads_ref)
            if count == 1:
                dq_ref[...] = near_ref[...]

    partner_ref[...] = dq_ref[chip_blocks // CORES :].astype(BF16)


def cross_kernel(
    offsets_ref, ids_ref, kv_ref, q_ref, g_ref, s_ref, pq_ref, pg_ref, ps_ref,
    acc_ref, dq_ref, all_q_ref, all_g_ref, all_s_ref,
):
    blocks_here = kv_ref.shape[0] // BLOCK
    _, base, own = places(blocks_here)
    for from_refs, to_ref in (((q_ref, pq_ref), all_q_ref), ((g_ref, pg_ref), all_g_ref)):
        for side, from_ref in enumerate(from_refs):
            for block in range(blocks_here):
                for head in range(GROUP):
                    to_ref[side * blocks_here + block, head * BLOCK : (head + 1) * BLOCK, :] = from_ref[
                        block * BLOCK : (block + 1) * BLOCK, head * HEAD_DIM : (head + 1) * HEAD_DIM
                    ]
    all_s_ref[0:blocks_here] = s_ref[...]
    all_s_ref[blocks_here:] = ps_ref[...]
    acc_ref[...] = jnp.zeros_like(acc_ref)
    dq_ref[...] = jnp.zeros_like(dq_ref)

    @pl.when(lax.axis_index("rep") == 0)
    def _():
        keys, values = keys_of(kv_ref, slice(None)), values_of(kv_ref, slice(None))
        key_t = transposed(keys)

        def query_step(block, carry):
            number = block + blocks_here
            query = base + number
            flags = [attends(offsets_ref, ids_ref, query, own + key) for key in range(blocks_here)]
            some = flags[0]
            for flag in flags[1:]:
                some |= flag

            @pl.when(some)
            def _():
                dq, dk, dv = block_grads(
                    keys, values, key_t, (all_q_ref, all_g_ref, all_s_ref), number, 1,
                    [bias_of(flag) for flag in flags],
                )
                dq_ref[block] = dq
                add_grads(acc_ref, slice(None), dk, dv)

            return carry

        lax.fori_loop(0, blocks_here, query_step, 0)


def own_kernel(
    offsets_ref, ids_ref, kv_ref, q_ref, g_ref, s_ref, cross_ref, far_ref, acc_ref, dq_ref
):
    blocks_here = kv_ref.shape[0] // BLOCK
    _, _, own = places(blocks_here)
    acc_ref[...] = cross_ref[...]
    keys, values = keys_of(kv_ref, slice(None)), values_of(kv_ref, slice(None))
    key_t = transposed(keys)

    def query_step(block, carry):
        flags = [
            (key >= block) | attends(offsets_ref, ids_ref, own + block, own + key)
            for key in range(blocks_here)
        ]
        dq, dk, dv = block_grads(
            keys, values, key_t, (q_ref, g_ref, s_ref), block, 1,
            [bias_of(flag) for flag in flags], block,
        )
        add_grads(acc_ref, slice(None), dk, dv)
        dq_ref[block] = far_ref[block] + dq
        return carry

    lax.fori_loop(0, blocks_here, query_step, 0)


def query_kernel(own_ref, partner_ref, dq_ref):
    def block_step(block, carry):
        total = own_ref[block] + partner_ref[block].astype(F32)
        rows = pl.ds(pl.multiple_of(block * BLOCK, BLOCK), BLOCK)
        for head in range(GROUP):
            lanes = slice(head * HEAD_DIM, (head + 1) * HEAD_DIM)
            dq_ref[rows, lanes] = total[:, lanes].T.astype(BF16)
        return carry

    lax.fori_loop(0, own_ref.shape[0], block_step, 0)


def final_kernel(last_sender, ids_ref, acc_ref, near_ref, *refs):
    far_refs, (dk_ref, dv_ref, sum_ref) = refs[:-3], refs[-3:]
    blocks_here = acc_ref.shape[0] // BLOCK
    chip_blocks = CORES * blocks_here
    chip = lax.axis_index("ctx")
    core = lax.axis_index("rep")
    sum_ref[...] = acc_ref[...] + near_ref[...].astype(F32)
    dk_ref[...] = keys_of(sum_ref, slice(None)).astype(BF16)
    dv_ref[...] = values_of(sum_ref, slice(None)).astype(BF16)
    capacity = far_refs[0].shape[0] // BLOCK
    for slot in range(SUMMARY):
        owner, rank = chip_slot(ids_ref, slot, chip_blocks)
        local = ids_ref[slot] - chip * chip_blocks - core * blocks_here
        mine = (owner == chip) & (local >= 0) & (local < blocks_here)

        @pl.when(mine & (chip <= last_sender) & (rank < capacity))
        def _():
            rows = pl.ds(pl.multiple_of(local * BLOCK, BLOCK), BLOCK)
            place = pl.ds(pl.multiple_of(rank * BLOCK, BLOCK), BLOCK)
            total = sum_ref[rows, :]
            for far_ref in far_refs:
                total += far_ref[place, :].astype(F32)
            dk_ref[rows, :] = total[:, 0:HEAD_DIM].astype(BF16)
            dv_ref[rows, :] = total[:, HEAD_DIM : 2 * HEAD_DIM].astype(BF16)


def call(kernel, scalars, arrays, out_shape, scratch=(), flops=0, in_space=VMEM, out_specs=None, room=24):
    return pl.pallas_call(
        kernel,
        out_shape=out_shape,
        in_specs=[SMEM] * len(scalars) + [in_space] * len(arrays),
        out_specs=out_specs or jax.tree.map(lambda _: VMEM, out_shape),
        scratch_shapes=list(scratch),
        compiler_params=pltpu.CompilerParams(vmem_limit_bytes=room << 20),
        cost_estimate=pl.CostEstimate(flops=flops, bytes_accessed=0, transcendentals=0),
    )(*scalars, *arrays)


def shape_of(shape, dtype):
    return jax.ShapeDtypeStruct(shape, dtype)


def with_capacity(
    capacity, chips, queries, kv, attn_out, grads, log_sums, window_offsets, summary_ids
):
    rows = queries.shape[0]
    blocks_here = rows // BLOCK
    swap = [(0, 1), (1, 0)]
    up = [(i, i + 1) for i in range(chips - 1)]
    down = [(b, a) for a, b in up]
    routes = far_rounds(chips)
    sources = tuple({b: a // CORES for a, b in route} for route in routes)
    both = ("ctx", "rep")

    kv_partner = lax.ppermute(kv, "rep", swap)
    kv_near = lax.ppermute(kv, "ctx", up)
    far_shape = shape_of((capacity * BLOCK, 2 * HEAD_DIM), BF16)
    picked = call(pick_kernel, (summary_ids,), (kv, kv_partner), far_shape)
    kv_far = [lax.ppermute(picked, both, route) for route in routes]
    attn_out, window_offsets, _ = lax.optimization_barrier((attn_out, window_offsets, picked))
    tables = (window_offsets, summary_ids)
    stats = call(
        prep_kernel, (), (attn_out, grads, log_sums),
        shape_of((blocks_here, 8, GROUP * BLOCK), F32), flops=0,
    )
    own = (queries, grads, stats)
    every = own + tuple(lax.ppermute(x, "rep", swap) for x in own)
    acc_shape = (rows, 2 * HEAD_DIM)
    half_shape = (blocks_here, HEAD_DIM, GROUP * BLOCK)
    chip_blocks = CORES * blocks_here
    dq_shape = shape_of((chip_blocks, *half_shape[1:]), F32)
    stacked_shape = shape_of((chip_blocks, GROUP * BLOCK, HEAD_DIM), BF16)
    cross_acc, cross_dq, *every = call(
        cross_kernel, tables, (kv, *every),
        (
            shape_of(acc_shape, F32), shape_of(half_shape, F32), stacked_shape, stacked_shape,
            shape_of((chip_blocks, *stats.shape[1:]), F32),
        ),
    )
    near_grads, near_dq = call(
        near_kernel, tables, (kv_near, *every, cross_dq), (shape_of(acc_shape, BF16), dq_shape),
        [pltpu.VMEM(acc_shape, F32)],
    )
    *far_grads, far_dq, dq_partner = call(
        functools.partial(far_kernel, sources), (summary_ids,), (*kv_far, *every, near_dq),
        (*[far_shape] * len(routes), dq_shape, shape_of(half_shape, BF16)),
        [pltpu.VMEM(far_shape.shape, F32)], flops=5 * MICROSECOND,
    )
    far_back = [
        lax.ppermute(x, both, [(b, a) for a, b in route]) for x, route in zip(far_grads, routes)
    ]
    near_grads, _ = lax.optimization_barrier((near_grads, far_grads))
    near_back = lax.ppermute(near_grads, "ctx", down)
    dq_partner = lax.ppermute(dq_partner, "rep", swap)
    acc, dq = call(
        own_kernel, tables, (kv, *every, cross_acc, far_dq),
        (shape_of(acc_shape, F32), shape_of(half_shape, F32)), flops=OWN,
    )
    query_grads = call(query_kernel, (), (dq, dq_partner), shape_of(queries.shape, BF16))
    if capacity > 4:
        acc, near_back = lax.optimization_barrier((acc, near_back))
    far_back, acc, query_grads = lax.optimization_barrier((far_back, acc, query_grads))
    far_other = [lax.ppermute(x, "rep", swap) for x in far_back]
    kv_shape = shape_of((rows, HEAD_DIM), BF16)
    key_grads, value_grads = call(
        functools.partial(final_kernel, chips - 3), (summary_ids,),
        (acc, near_back, *far_back, *far_other), (kv_shape, kv_shape),
        [pltpu.VMEM(acc_shape, F32)],
    )
    return query_grads, key_grads, value_grads


def capacities(chips):
    return CAPACITIES if len(far_rounds(chips)) == 1 else CAPACITIES[-1:]


def per_device(chips, queries, keys, values, attn_out, grads, log_sums, window_offsets, summary_ids):
    kv, branch = call(
        functools.partial(start_kernel, chips), (), (summary_ids, keys, values),
        (shape_of((keys.shape[0], 2 * HEAD_DIM), BF16), shape_of((1,), jnp.int32)),
        [pltpu.SMEM(summary_ids.shape, jnp.int32), pltpu.SemaphoreType.DMA((3,))], in_space=HBM, out_specs=(VMEM, SMEM), room=60,
    )
    branches = [functools.partial(with_capacity, limit, chips) for limit in capacities(chips)]
    operands = (queries, kv, attn_out, grads, log_sums, window_offsets.T, summary_ids)
    return lax.switch(branch[0], branches, *operands) if len(branches) > 1 else branches[0](*operands)


def solution(mesh):
    rows = P(("groups", "ctx", "rep"), "heads")
    return jax.shard_map(
        functools.partial(per_device, mesh.shape["ctx"]),
        mesh=mesh,
        in_specs=(rows,) * 5 + (P("heads", ("groups", "ctx", "rep")), P("groups", None), P("groups")),
        out_specs=(rows,) * 3,
        check_vma=False,
    )
```

```python
import functools
import math

import jax
import jax.numpy as jnp
from jax import lax
from jax.experimental import pallas as pl
from jax.experimental.pallas import tpu as pltpu
from jax.sharding import PartitionSpec as P

HEAD_DIM = 128
GROUP = 4
BLOCK = 128
REACH = 3
SUMMARY = 8
CORES = 2
SCALE = HEAD_DIM ** (-0.5)
LOG2E = math.log2(math.e)
MICROSECOND = 1_000_000_000
OWN = 10 * MICROSECOND
CAPACITIES = (2, 3, 4, SUMMARY - 1)
F32 = jnp.float32
BF16 = jnp.bfloat16
VMEM = pl.BlockSpec(memory_space=pltpu.VMEM)
SMEM = pl.BlockSpec(memory_space=pltpu.SMEM)
HBM = pl.BlockSpec(memory_space=pltpu.HBM)


def far_rounds(chips):
    rounds = []
    for source in range(chips):
        for target in range(source + 2, chips):
            wanted = target % CORES
            for route in rounds:
                senders = [core for core in range(CORES) if source * CORES + core not in route.values()]
                receivers = [core for core in range(CORES) if target * CORES + core not in route]
                if senders and receivers:
                    break
            else:
                senders, receivers, route = list(range(CORES)), list(range(CORES)), {}
                rounds.append(route)
            sender = wanted if wanted in senders else senders[0]
            route[target * CORES + receivers[0]] = source * CORES + sender
    return [[(a, b) for b, a in route.items()] for route in rounds]


def table_entry(table, position):
    value = jnp.int32(-1)
    for place, entry in table.items():
        value = jnp.where(position == place, jnp.int32(entry), value)
    return value


def chip_slot(ids_ref, slot, chip_blocks):
    chip = ids_ref[slot] // chip_blocks
    rank = jnp.int32(0)
    for other in range(slot):
        rank += jnp.where(ids_ref[other] // chip_blocks == chip, 1, 0)
    return chip, rank


def chip_count(ids_ref, chip, chip_blocks):
    count = jnp.int32(0)
    for slot in range(SUMMARY):
        count += jnp.where(ids_ref[slot] // chip_blocks == chip, 1, 0)
    return count


def prep_kernel(out_ref, grad_ref, lse_ref, stats_ref):
    stats_ref[...] = jnp.zeros_like(stats_ref)
    for block in range(stats_ref.shape[0]):
        rows = slice(block * BLOCK, (block + 1) * BLOCK)
        for head in range(GROUP):
            columns = slice(head * HEAD_DIM, (head + 1) * HEAD_DIM)
            product = out_ref[rows, columns].astype(F32) * grad_ref[rows, columns].astype(F32)
            stats_ref[block, 0:1, columns] = lse_ref[head : head + 1, rows] * LOG2E
            stats_ref[block, 1:2, columns] = jnp.sum(product.T, axis=0, keepdims=True)


def start_kernel(chips, ids_hbm, key_ref, value_ref, kv_ref, branch_ref, ids_ref, sems):
    chip_blocks = CORES * (key_ref.shape[0] // BLOCK)
    copies = [
        pltpu.make_async_copy(
            ref, kv_ref.at[:, number * HEAD_DIM : (number + 1) * HEAD_DIM], sems.at[number]
        )
        for number, ref in enumerate((key_ref, value_ref))
    ]
    ids_copy = pltpu.make_async_copy(ids_hbm, ids_ref, sems.at[2])
    ids_copy.start()
    for copy in copies:
        copy.start()
    ids_copy.wait()
    most = jnp.int32(0)
    for chip in range(chips - 2):
        most = jnp.maximum(most, chip_count(ids_ref, chip, chip_blocks))
    branch = jnp.int32(0)
    for capacity in capacities(chips)[:-1]:
        branch += jnp.where(most > capacity, 1, 0)
    branch_ref[0] = branch
    for copy in copies:
        copy.wait()


def pick_kernel(ids_ref, own_ref, partner_ref, picked_ref):
    chip = lax.axis_index("ctx")
    core = lax.axis_index("rep")
    blocks_here = own_ref.shape[0] // BLOCK
    chip_blocks = CORES * blocks_here
    capacity = picked_ref.shape[0] // BLOCK
    picked_ref[...] = jnp.zeros_like(picked_ref)
    for slot in range(SUMMARY):
        owner, rank = chip_slot(ids_ref, slot, chip_blocks)
        local = ids_ref[slot] - chip * chip_blocks
        row = pl.multiple_of((local % blocks_here) * BLOCK, BLOCK)
        place = pl.multiple_of(rank * BLOCK, BLOCK)
        mine = local // blocks_here == core
        wanted = (owner == chip) & (rank < capacity)

        @pl.when(wanted & mine)
        def _():
            picked_ref[pl.ds(place, BLOCK), :] = own_ref[pl.ds(row, BLOCK), :]

        @pl.when(wanted & ~mine)
        def _():
            picked_ref[pl.ds(place, BLOCK), :] = partner_ref[pl.ds(row, BLOCK), :]


def nt(a, b):
    return lax.dot_general(a, b, (((1,), (1,)), ((), ())), preferred_element_type=F32)


def nn(a, b):
    return jnp.dot(a, b, preferred_element_type=F32)


def block_grads(keys, values, key_t, query_refs, first, count=1, biases=None, query_at=None):
    query_ref, grad_ref, stats_ref = query_refs
    numbers = [first + step for step in range(count)]
    queries = jnp.concatenate([query_ref[number] for number in numbers], axis=0)
    grads = jnp.concatenate([grad_ref[number] for number in numbers], axis=0)
    log_sums = jnp.concatenate([stats_ref[number, 0:1, :] for number in numbers], axis=1)
    deltas = jnp.concatenate([stats_ref[number, 1:2, :] for number in numbers], axis=1)
    scores = nt(keys, queries) * (SCALE * LOG2E)
    if biases is None:
        probs = jnp.exp2(scores - log_sums)
    else:
        parts = []
        for key, bias in enumerate(biases):
            part = jnp.exp2(scores[key * BLOCK : (key + 1) * BLOCK] - (log_sums + bias))
            if query_at is not None:
                row = lax.broadcasted_iota(jnp.int32, part.shape, 0)
                column = lax.broadcasted_iota(jnp.int32, part.shape, 1) % BLOCK
                part = jnp.where(column - row >= (key - query_at) * BLOCK, part, 0.0)
            parts.append(part)
        probs = jnp.concatenate(parts, axis=0)
    prob_grads = nt(values, grads)
    score_grads = (probs * (prob_grads - deltas) * SCALE).astype(BF16)
    return nn(key_t, score_grads), nn(score_grads, queries), nn(probs.astype(BF16), grads)


def put_queries(to_ref, from_ref, first, dq):
    width = GROUP * BLOCK
    for step in range(dq.shape[1] // width):
        part = dq[:, step * width : (step + 1) * width]
        to_ref[first + step] = from_ref[first + step] + part


def is_summary(ids_ref, key_block):
    found = ids_ref[0] == key_block
    for slot in range(1, SUMMARY):
        found |= ids_ref[slot] == key_block
    return found


def in_window(offsets_ref, query_block, key_block):
    distance = query_block - key_block
    return (distance == offsets_ref[0, query_block]) | (distance == offsets_ref[1, query_block])


def attends(offsets_ref, ids_ref, query_block, key_block):
    chosen = in_window(offsets_ref, query_block, key_block) | is_summary(ids_ref, key_block)
    return (query_block > key_block) & chosen


def keys_of(kv_ref, rows):
    return kv_ref[rows, 0:HEAD_DIM]


def values_of(kv_ref, rows):
    return kv_ref[rows, HEAD_DIM : 2 * HEAD_DIM]


def transposed(keys):
    return keys.astype(F32).T.astype(BF16)


def add_grads(acc_ref, rows, key_part, value_part):
    acc_ref[rows, 0:HEAD_DIM] += key_part
    acc_ref[rows, HEAD_DIM : 2 * HEAD_DIM] += value_part


def places(blocks_here):
    chip = lax.axis_index("ctx")
    base = chip * CORES * blocks_here
    return chip, base, base + lax.axis_index("rep") * blocks_here


def bias_of(flag):
    return jnp.where(flag, 0.0, 1e30).astype(F32)


def near_kernel(
    offsets_ref, ids_ref, kv_ref, q_ref, g_ref, s_ref, local_ref, grads_ref, dq_ref, acc_ref
):
    query_refs = (q_ref, g_ref, s_ref)
    blocks_here = kv_ref.shape[0] // BLOCK
    chip_blocks = CORES * blocks_here
    chip, base, own = places(blocks_here)
    first_key = own - chip_blocks
    acc_ref[...] = jnp.zeros_like(acc_ref)
    dq_ref[0:blocks_here] = local_ref[...]
    dq_ref[blocks_here:] = jnp.zeros_like(local_ref)
    flags = [is_summary(ids_ref, first_key + key) & (chip > 0) for key in range(blocks_here)]
    count = jnp.int32(0)
    chosen = [jnp.int32(0)] * blocks_here
    for key in range(blocks_here):
        for place in range(key + 1):
            chosen[place] = jnp.where(flags[key] & (count == place), key, chosen[place])
        count += jnp.where(flags[key], 1, 0)

    def add(first, count, places_of_keys, biases=None):
        rows = [pl.ds(pl.multiple_of(key * BLOCK, BLOCK), BLOCK) for key in places_of_keys]
        keys = jnp.concatenate([keys_of(kv_ref, row) for row in rows], axis=0)
        values = jnp.concatenate([values_of(kv_ref, row) for row in rows], axis=0)
        dq, dk, dv = block_grads(keys, values, transposed(keys), query_refs, first, count, biases)
        put_queries(dq_ref, dq_ref, first, dq)
        for place, row in enumerate(rows):
            part = slice(place * BLOCK, (place + 1) * BLOCK)
            add_grads(acc_ref, row, dk[part], dv[part])

    def entry(place):
        key = jnp.int32(0)
        for number in range(blocks_here):
            key = jnp.where(place == number, chosen[number], key)
        return key

    odd = lax.rem(count, 2)

    def single_step(item, carry):
        add(item * 4, 4, [chosen[0]])
        return carry

    lax.fori_loop(0, odd * (chip_blocks // 4), single_step, 0)

    def double_step(item, carry):
        turn = odd + 2 * (item // (chip_blocks // 2))
        add(lax.rem(item, chip_blocks // 2) * 2, 2, [entry(turn), entry(turn + 1)])
        return carry

    lax.fori_loop(0, (count // 2) * (chip_blocks // 2), double_step, 0)

    def window_step(number, carry):
        query = base + number
        keys, wanted = [], []
        for place in range(2):
            key = query - offsets_ref[place, query] - first_key
            fits = (key >= 0) & (key < blocks_here)
            key = jnp.where(fits, key, 0)
            for block in range(blocks_here):
                fits &= (key != block) | ~flags[block]
            keys.append(key)
            wanted.append(fits)

        @pl.when(wanted[0] | wanted[1])
        def _():
            add(number + blocks_here, 1, keys, [bias_of(flag) for flag in wanted])

        return carry

    reaches = (chip > 0) & (lax.axis_index("rep") == CORES - 1)
    lax.fori_loop(0, jnp.where(reaches, min(REACH, blocks_here), 0), window_step, 0)
    grads_ref[...] = acc_ref[...].astype(BF16)


def far_kernel(sources, ids_ref, *refs):
    count = len(sources)
    kv_refs, refs = refs[:count], refs[count:]
    query_refs, (near_ref, cross_ref), refs = refs[:3], refs[3:5], refs[5:]
    grads_refs, (dq_ref, partner_ref, acc_ref) = refs[:count], refs[count:]
    chip_blocks = near_ref.shape[0]
    position = lax.axis_index("ctx") * CORES + lax.axis_index("rep")
    capacity = acc_ref.shape[0] // BLOCK
    together = 4 if capacity < 4 else 2 if capacity == 4 else 1
    if count > 1:
        dq_ref[...] = near_ref[...]
        near_ref = dq_ref
    for table, kv_ref, grads_ref in zip(sources, kv_refs, grads_refs):
        held = chip_count(ids_ref, table_entry(table, position), chip_blocks)

        @pl.when(held > 0)
        def _():
            keys, values = keys_of(kv_ref, slice(None)), values_of(kv_ref, slice(None))
            key_t = transposed(keys)
            acc_ref[...] = jnp.zeros_like(acc_ref)

            def query_step(item, carry):
                first = item * together
                dq, dk, dv = block_grads(keys, values, key_t, query_refs, first, together)
                put_queries(dq_ref, near_ref, first, dq)
                add_grads(acc_ref, slice(None), dk, dv)
                return carry

            lax.fori_loop(0, chip_blocks // together, query_step, 0)
            grads_ref[...] = acc_ref[...].astype(BF16)

        @pl.when(held == 0)
        def _():
            grads_ref[...] = jnp.zeros_like(grads_ref)
            if count == 1:
                dq_ref[...] = near_ref[...]

    partner_ref[0 : chip_blocks // CORES] = dq_ref[chip_blocks // CORES :].astype(BF16)
    partner_ref[chip_blocks // CORES :] = cross_ref[...]


def cross_kernel(
    offsets_ref, ids_ref, kv_ref, q_ref, g_ref, s_ref, pq_ref, pg_ref, ps_ref,
    grads_ref, dq_ref, all_q_ref, all_g_ref, all_s_ref, acc_ref,
):
    blocks_here = kv_ref.shape[0] // BLOCK
    _, base, own = places(blocks_here)
    for from_refs, to_ref in (((q_ref, pq_ref), all_q_ref), ((g_ref, pg_ref), all_g_ref)):
        for side, from_ref in enumerate(from_refs):
            for block in range(blocks_here):
                for head in range(GROUP):
                    to_ref[side * blocks_here + block, head * BLOCK : (head + 1) * BLOCK, :] = from_ref[
                        block * BLOCK : (block + 1) * BLOCK, head * HEAD_DIM : (head + 1) * HEAD_DIM
                    ]
    all_s_ref[0:blocks_here] = s_ref[...]
    all_s_ref[blocks_here:] = ps_ref[...]
    acc_ref[...] = jnp.zeros_like(acc_ref)
    dq_ref[...] = jnp.zeros_like(dq_ref)

    @pl.when(lax.axis_index("rep") == CORES - 1)
    def _():
        keys, values = keys_of(kv_ref, slice(None)), values_of(kv_ref, slice(None))
        key_t = transposed(keys)

        def query_step(block, carry):
            flags = [
                attends(offsets_ref, ids_ref, own + block, base + key) for key in range(blocks_here)
            ]
            some = flags[0]
            for flag in flags[1:]:
                some |= flag

            @pl.when(some)
            def _():
                dq, dk, dv = block_grads(
                    keys, values, key_t, (all_q_ref, all_g_ref, all_s_ref), block, 1,
                    [bias_of(flag) for flag in flags],
                )
                dq_ref[block] = dq
                add_grads(acc_ref, slice(None), dk, dv)

            return carry

        lax.fori_loop(0, blocks_here, query_step, 0)

    for block in range(blocks_here):
        lanes = slice((block % 2) * 2 * HEAD_DIM, (block % 2 + 1) * 2 * HEAD_DIM)
        rows = slice(block * BLOCK, (block + 1) * BLOCK)
        grads_ref[block // 2, :, lanes] = acc_ref[rows, :].astype(BF16)


def own_kernel(
    offsets_ref, ids_ref, kv_ref, q_ref, g_ref, s_ref, far_ref, acc_ref, dq_ref
):
    blocks_here = kv_ref.shape[0] // BLOCK
    _, _, own = places(blocks_here)
    acc_ref[...] = jnp.zeros_like(acc_ref)
    keys, values = keys_of(kv_ref, slice(None)), values_of(kv_ref, slice(None))
    key_t = transposed(keys)

    def query_step(block, carry):
        flags = [
            (key >= block) | attends(offsets_ref, ids_ref, own + block, own + key)
            for key in range(blocks_here)
        ]
        dq, dk, dv = block_grads(
            keys, values, key_t, (q_ref, g_ref, s_ref), block, 1,
            [bias_of(flag) for flag in flags], block,
        )
        add_grads(acc_ref, slice(None), dk, dv)
        dq_ref[block] = far_ref[block] + dq
        return carry

    lax.fori_loop(0, blocks_here, query_step, 0)


def query_kernel(own_ref, partner_ref, dq_ref):
    def block_step(block, carry):
        total = own_ref[block] + partner_ref[block].astype(F32)
        rows = pl.ds(pl.multiple_of(block * BLOCK, BLOCK), BLOCK)
        for head in range(GROUP):
            lanes = slice(head * HEAD_DIM, (head + 1) * HEAD_DIM)
            dq_ref[rows, lanes] = total[:, lanes].T.astype(BF16)
        return carry

    lax.fori_loop(0, own_ref.shape[0], block_step, 0)


def final_kernel(last_sender, ids_ref, acc_ref, near_ref, partner_ref, *refs):
    far_refs, (dk_ref, dv_ref, sum_ref) = refs[:-3], refs[-3:]
    blocks_here = acc_ref.shape[0] // BLOCK
    chip_blocks = CORES * blocks_here
    chip = lax.axis_index("ctx")
    core = lax.axis_index("rep")
    for block in range(blocks_here):
        lanes = slice((block % 2) * 2 * HEAD_DIM, (block % 2 + 1) * 2 * HEAD_DIM)
        rows = slice(block * BLOCK, (block + 1) * BLOCK)
        cross = partner_ref[blocks_here + block // 2, :, lanes].astype(F32)
        sum_ref[rows, :] = acc_ref[rows, :] + near_ref[rows, :].astype(F32) + cross
    dk_ref[...] = keys_of(sum_ref, slice(None)).astype(BF16)
    dv_ref[...] = values_of(sum_ref, slice(None)).astype(BF16)
    capacity = far_refs[0].shape[0] // BLOCK
    for slot in range(SUMMARY):
        owner, rank = chip_slot(ids_ref, slot, chip_blocks)
        local = ids_ref[slot] - chip * chip_blocks - core * blocks_here
        mine = (owner == chip) & (local >= 0) & (local < blocks_here)

        @pl.when(mine & (chip <= last_sender) & (rank < capacity))
        def _():
            rows = pl.ds(pl.multiple_of(local * BLOCK, BLOCK), BLOCK)
            place = pl.ds(pl.multiple_of(rank * BLOCK, BLOCK), BLOCK)
            total = sum_ref[rows, :]
            for far_ref in far_refs:
                total += far_ref[place, :].astype(F32)
            dk_ref[rows, :] = total[:, 0:HEAD_DIM].astype(BF16)
            dv_ref[rows, :] = total[:, HEAD_DIM : 2 * HEAD_DIM].astype(BF16)


def call(kernel, scalars, arrays, out_shape, scratch=(), flops=0, in_space=VMEM, out_specs=None, room=24):
    return pl.pallas_call(
        kernel,
        out_shape=out_shape,
        in_specs=[SMEM] * len(scalars) + [in_space] * len(arrays),
        out_specs=out_specs or jax.tree.map(lambda _: VMEM, out_shape),
        scratch_shapes=list(scratch),
        compiler_params=pltpu.CompilerParams(vmem_limit_bytes=room << 20),
        cost_estimate=pl.CostEstimate(flops=flops, bytes_accessed=0, transcendentals=0),
    )(*scalars, *arrays)


def shape_of(shape, dtype):
    return jax.ShapeDtypeStruct(shape, dtype)


def with_capacity(
    capacity, chips, queries, kv, attn_out, grads, log_sums, window_offsets, summary_ids
):
    rows = queries.shape[0]
    blocks_here = rows // BLOCK
    swap = [(0, 1), (1, 0)]
    up = [(i, i + 1) for i in range(chips - 1)]
    down = [(b, a) for a, b in up]
    routes = far_rounds(chips)
    sources = tuple({b: a // CORES for a, b in route} for route in routes)
    both = ("ctx", "rep")

    kv_partner = lax.ppermute(kv, "rep", swap)
    kv_near = lax.ppermute(kv, "ctx", up)
    far_shape = shape_of((capacity * BLOCK, 2 * HEAD_DIM), BF16)
    picked = call(pick_kernel, (summary_ids,), (kv, kv_partner), far_shape)
    kv_far = [lax.ppermute(picked, both, route) for route in routes]
    attn_out, window_offsets, _ = lax.optimization_barrier((attn_out, window_offsets, picked))
    tables = (window_offsets, summary_ids)
    stats = call(
        prep_kernel, (), (attn_out, grads, log_sums),
        shape_of((blocks_here, 8, GROUP * BLOCK), F32), flops=0,
    )
    own = (queries, grads, stats)
    every = own + tuple(lax.ppermute(x, "rep", swap) for x in own)
    acc_shape = (rows, 2 * HEAD_DIM)
    half_shape = (blocks_here, HEAD_DIM, GROUP * BLOCK)
    chip_blocks = CORES * blocks_here
    cross_shape = shape_of((blocks_here // 2, BLOCK, 4 * HEAD_DIM), BF16)
    partner_shape = shape_of((blocks_here + blocks_here // 2, *half_shape[1:]), BF16)
    dq_shape = shape_of((chip_blocks, *half_shape[1:]), F32)
    stacked_shape = shape_of((chip_blocks, GROUP * BLOCK, HEAD_DIM), BF16)
    cross_grads, cross_dq, *every = call(
        cross_kernel, tables, (kv_partner, *every),
        (
            cross_shape, shape_of(half_shape, F32), stacked_shape, stacked_shape,
            shape_of((chip_blocks, *stats.shape[1:]), F32),
        ),
        [pltpu.VMEM(acc_shape, F32)],
    )
    near_grads, near_dq = call(
        near_kernel, tables, (kv_near, *every, cross_dq), (shape_of(acc_shape, BF16), dq_shape),
        [pltpu.VMEM(acc_shape, F32)],
    )
    *far_grads, far_dq, dq_partner = call(
        functools.partial(far_kernel, sources), (summary_ids,), (*kv_far, *every, near_dq, cross_grads),
        (*[far_shape] * len(routes), dq_shape, partner_shape),
        [pltpu.VMEM(far_shape.shape, F32)], flops=5 * MICROSECOND,
    )
    far_back = [
        lax.ppermute(x, both, [(b, a) for a, b in route]) for x, route in zip(far_grads, routes)
    ]
    near_grads, _ = lax.optimization_barrier((near_grads, far_grads))
    near_back = lax.ppermute(near_grads, "ctx", down)
    dq_partner = lax.ppermute(dq_partner, "rep", swap)
    acc, dq = call(
        own_kernel, tables, (kv, *every, far_dq),
        (shape_of(acc_shape, F32), shape_of(half_shape, F32)), flops=OWN,
    )
    query_grads = call(query_kernel, (), (dq, dq_partner), shape_of(queries.shape, BF16))
    if capacity > 3:
        acc, near_back = lax.optimization_barrier((acc, near_back))
    far_back, acc, query_grads = lax.optimization_barrier((far_back, acc, query_grads))
    far_other = [lax.ppermute(x, "rep", swap) for x in far_back]
    kv_shape = shape_of((rows, HEAD_DIM), BF16)
    key_grads, value_grads = call(
        functools.partial(final_kernel, chips - 3), (summary_ids,),
        (acc, near_back, dq_partner, *far_back, *far_other), (kv_shape, kv_shape),
        [pltpu.VMEM(acc_shape, F32)],
    )
    return query_grads, key_grads, value_grads


def capacities(chips):
    return CAPACITIES if len(far_rounds(chips)) == 1 else CAPACITIES[-1:]


def per_device(chips, queries, keys, values, attn_out, grads, log_sums, window_offsets, summary_ids):
    kv, branch = call(
        functools.partial(start_kernel, chips), (), (summary_ids, keys, values),
        (shape_of((keys.shape[0], 2 * HEAD_DIM), BF16), shape_of((1,), jnp.int32)),
        [pltpu.SMEM(summary_ids.shape, jnp.int32), pltpu.SemaphoreType.DMA((3,))], in_space=HBM, out_specs=(VMEM, SMEM), room=60,
    )
    branches = [functools.partial(with_capacity, limit, chips) for limit in capacities(chips)]
    operands = (queries, kv, attn_out, grads, log_sums, window_offsets.T, summary_ids)
    return lax.switch(branch[0], branches, *operands) if len(branches) > 1 else branches[0](*operands)


def solution(mesh):
    rows = P(("groups", "ctx", "rep"), "heads")
    return jax.shard_map(
        functools.partial(per_device, mesh.shape["ctx"]),
        mesh=mesh,
        in_specs=(rows,) * 5 + (P("heads", ("groups", "ctx", "rep")), P("groups", None), P("groups")),
        out_specs=(rows,) * 3,
        check_vma=False,
    )
```

```python
import functools
import math

import jax
import jax.numpy as jnp
from jax import lax
from jax.experimental import pallas as pl
from jax.experimental.pallas import tpu as pltpu
from jax.sharding import PartitionSpec as P

HEAD_DIM = 128
GROUP = 4
BLOCK = 128
REACH = 3
SUMMARY = 8
CORES = 2
SCALE = HEAD_DIM ** (-0.5)
LOG2E = math.log2(math.e)
MICROSECOND = 1_000_000_000
OWN = 10 * MICROSECOND
CAPACITIES = (2, 3, 4, SUMMARY - 1)
F32 = jnp.float32
BF16 = jnp.bfloat16
VMEM = pl.BlockSpec(memory_space=pltpu.VMEM)
SMEM = pl.BlockSpec(memory_space=pltpu.SMEM)
HBM = pl.BlockSpec(memory_space=pltpu.HBM)


def far_rounds(chips):
    rounds = []
    for source in range(chips):
        for target in range(source + 2, chips):
            wanted = target % CORES
            for route in rounds:
                senders = [core for core in range(CORES) if source * CORES + core not in route.values()]
                receivers = [core for core in range(CORES) if target * CORES + core not in route]
                if senders and receivers:
                    break
            else:
                senders, receivers, route = list(range(CORES)), list(range(CORES)), {}
                rounds.append(route)
            sender = wanted if wanted in senders else senders[0]
            route[target * CORES + receivers[0]] = source * CORES + sender
    return [[(a, b) for b, a in route.items()] for route in rounds]


def table_entry(table, position):
    value = jnp.int32(-1)
    for place, entry in table.items():
        value = jnp.where(position == place, jnp.int32(entry), value)
    return value


def chip_slot(ids_ref, slot, chip_blocks):
    chip = ids_ref[slot] // chip_blocks
    rank = jnp.int32(0)
    for other in range(slot):
        rank += jnp.where(ids_ref[other] // chip_blocks == chip, 1, 0)
    return chip, rank


def chip_count(ids_ref, chip, chip_blocks):
    count = jnp.int32(0)
    for slot in range(SUMMARY):
        count += jnp.where(ids_ref[slot] // chip_blocks == chip, 1, 0)
    return count


def prep_kernel(out_ref, grad_ref, lse_ref, stats_ref):
    stats_ref[...] = jnp.zeros_like(stats_ref)
    for block in range(stats_ref.shape[0]):
        rows = slice(block * BLOCK, (block + 1) * BLOCK)
        for head in range(GROUP):
            columns = slice(head * HEAD_DIM, (head + 1) * HEAD_DIM)
            product = out_ref[rows, columns].astype(F32) * grad_ref[rows, columns].astype(F32)
            stats_ref[block, 0:1, columns] = lse_ref[head : head + 1, rows] * LOG2E
            stats_ref[block, 1:2, columns] = jnp.sum(product.T, axis=0, keepdims=True)


def start_kernel(chips, ids_hbm, key_ref, value_ref, kv_ref, branch_ref, ids_ref, sems):
    chip_blocks = CORES * (key_ref.shape[0] // BLOCK)
    copies = [
        pltpu.make_async_copy(
            ref, kv_ref.at[:, number * HEAD_DIM : (number + 1) * HEAD_DIM], sems.at[number]
        )
        for number, ref in enumerate((key_ref, value_ref))
    ]
    ids_copy = pltpu.make_async_copy(ids_hbm, ids_ref, sems.at[2])
    ids_copy.start()
    for copy in copies:
        copy.start()
    ids_copy.wait()
    most = jnp.int32(0)
    for chip in range(chips - 2):
        most = jnp.maximum(most, chip_count(ids_ref, chip, chip_blocks))
    branch = jnp.int32(0)
    for capacity in capacities(chips)[:-1]:
        branch += jnp.where(most > capacity, 1, 0)
    branch_ref[0] = branch
    for copy in copies:
        copy.wait()


def pick_kernel(ids_ref, own_ref, partner_ref, picked_ref):
    chip = lax.axis_index("ctx")
    core = lax.axis_index("rep")
    blocks_here = own_ref.shape[0] // BLOCK
    chip_blocks = CORES * blocks_here
    capacity = picked_ref.shape[0] // BLOCK
    picked_ref[...] = jnp.zeros_like(picked_ref)
    for slot in range(SUMMARY):
        owner, rank = chip_slot(ids_ref, slot, chip_blocks)
        local = ids_ref[slot] - chip * chip_blocks
        row = pl.multiple_of((local % blocks_here) * BLOCK, BLOCK)
        place = pl.multiple_of(rank * BLOCK, BLOCK)
        mine = local // blocks_here == core
        wanted = (owner == chip) & (rank < capacity)

        @pl.when(wanted & mine)
        def _():
            picked_ref[pl.ds(place, BLOCK), :] = own_ref[pl.ds(row, BLOCK), :]

        @pl.when(wanted & ~mine)
        def _():
            picked_ref[pl.ds(place, BLOCK), :] = partner_ref[pl.ds(row, BLOCK), :]


def nt(a, b):
    return lax.dot_general(a, b, (((1,), (1,)), ((), ())), preferred_element_type=F32)


def nn(a, b):
    return jnp.dot(a, b, preferred_element_type=F32)


def block_grads(keys, values, key_t, query_refs, first, count=1, biases=None, reach=None):
    query_ref, grad_ref, stats_ref = query_refs
    numbers = [first + step for step in range(count)]
    queries = jnp.concatenate([query_ref[number] for number in numbers], axis=0)
    grads = jnp.concatenate([grad_ref[number] for number in numbers], axis=0)
    log_sums = [stats_ref[number, 0:1, :] for number in numbers]
    deltas = jnp.concatenate([stats_ref[number, 1:2, :] for number in numbers], axis=1)
    scores = nt(keys, queries) * (SCALE * LOG2E)
    if biases is None:
        probs = jnp.exp2(scores - jnp.concatenate(log_sums, axis=1))
    else:
        if reach is not None:
            shape = (BLOCK, queries.shape[0])
            column = lax.broadcasted_iota(jnp.int32, shape, 1)
            ahead = column // (GROUP * BLOCK) * BLOCK + column % BLOCK
            ahead -= lax.broadcasted_iota(jnp.int32, shape, 0)
        parts = []
        for key, row in enumerate(biases):
            shift = jnp.concatenate([a + bias for a, bias in zip(log_sums, row)], axis=1)
            part = jnp.exp2(scores[key * BLOCK : (key + 1) * BLOCK] - shift)
            if reach is not None:
                part = jnp.where(ahead >= reach + key * BLOCK, part, 0.0)
            parts.append(part)
        probs = jnp.concatenate(parts, axis=0)
    prob_grads = nt(values, grads)
    score_grads = (probs * (prob_grads - deltas) * SCALE).astype(BF16)
    return nn(key_t, score_grads), nn(score_grads, queries), nn(probs.astype(BF16), grads)


def put_queries(to_ref, from_ref, first, dq):
    width = GROUP * BLOCK
    for step in range(dq.shape[1] // width):
        part = dq[:, step * width : (step + 1) * width]
        to_ref[first + step] = from_ref[first + step] + part


def is_summary(ids_ref, key_block):
    found = ids_ref[0] == key_block
    for slot in range(1, SUMMARY):
        found |= ids_ref[slot] == key_block
    return found


def in_window(offsets_ref, query_block, key_block):
    distance = query_block - key_block
    return (distance == offsets_ref[0, query_block]) | (distance == offsets_ref[1, query_block])


def attends(offsets_ref, ids_ref, query_block, key_block):
    chosen = in_window(offsets_ref, query_block, key_block) | is_summary(ids_ref, key_block)
    return (query_block > key_block) & chosen


def keys_of(kv_ref, rows):
    return kv_ref[rows, 0:HEAD_DIM]


def values_of(kv_ref, rows):
    return kv_ref[rows, HEAD_DIM : 2 * HEAD_DIM]


def transposed(keys):
    return keys.astype(F32).T.astype(BF16)


def add_grads(acc_ref, rows, key_part, value_part):
    acc_ref[rows, 0:HEAD_DIM] += key_part
    acc_ref[rows, HEAD_DIM : 2 * HEAD_DIM] += value_part


def places(blocks_here):
    chip = lax.axis_index("ctx")
    base = chip * CORES * blocks_here
    return chip, base, base + lax.axis_index("rep") * blocks_here


def bias_of(flag):
    return jnp.where(flag, 0.0, 1e30).astype(F32)


def near_kernel(
    offsets_ref, ids_ref, kv_ref, q_ref, g_ref, s_ref, grads_ref, dq_ref, acc_ref
):
    query_refs = (q_ref, g_ref, s_ref)
    blocks_here = kv_ref.shape[0] // BLOCK
    chip_blocks = CORES * blocks_here
    chip, base, own = places(blocks_here)
    first_key = own - chip_blocks
    acc_ref[...] = jnp.zeros_like(acc_ref)
    dq_ref[...] = jnp.zeros_like(dq_ref)
    flags = [is_summary(ids_ref, first_key + key) & (chip > 0) for key in range(blocks_here)]
    count = jnp.int32(0)
    chosen = [jnp.int32(0)] * blocks_here
    for key in range(blocks_here):
        for place in range(key + 1):
            chosen[place] = jnp.where(flags[key] & (count == place), key, chosen[place])
        count += jnp.where(flags[key], 1, 0)

    def add(first, count, places_of_keys, biases=None):
        rows = [pl.ds(pl.multiple_of(key * BLOCK, BLOCK), BLOCK) for key in places_of_keys]
        keys = jnp.concatenate([keys_of(kv_ref, row) for row in rows], axis=0)
        values = jnp.concatenate([values_of(kv_ref, row) for row in rows], axis=0)
        dq, dk, dv = block_grads(keys, values, transposed(keys), query_refs, first, count, biases)
        put_queries(dq_ref, dq_ref, first, dq)
        for place, row in enumerate(rows):
            part = slice(place * BLOCK, (place + 1) * BLOCK)
            add_grads(acc_ref, row, dk[part], dv[part])

    def entry(place):
        key = jnp.int32(0)
        for number in range(blocks_here):
            key = jnp.where(place == number, chosen[number], key)
        return key

    odd = lax.rem(count, 2)

    def single_step(item, carry):
        add(item * 4, 4, [chosen[0]])
        return carry

    lax.fori_loop(0, odd * (chip_blocks // 4), single_step, 0)

    def double_step(item, carry):
        turn = odd + 2 * (item // (chip_blocks // 2))
        add(lax.rem(item, chip_blocks // 2) * 2, 2, [entry(turn), entry(turn + 1)])
        return carry

    lax.fori_loop(0, (count // 2) * (chip_blocks // 2), double_step, 0)

    def window_step(number, carry):
        query = base + number
        keys, wanted = [], []
        for place in range(2):
            key = query - offsets_ref[place, query] - first_key
            fits = (key >= 0) & (key < blocks_here)
            key = jnp.where(fits, key, 0)
            for block in range(blocks_here):
                fits &= (key != block) | ~flags[block]
            keys.append(key)
            wanted.append(fits)

        @pl.when(wanted[0] | wanted[1])
        def _():
            add(number + blocks_here, 1, keys, [[bias_of(flag)] for flag in wanted])

        return carry

    reaches = (chip > 0) & (lax.axis_index("rep") == CORES - 1)
    lax.fori_loop(0, jnp.where(reaches, min(REACH, blocks_here), 0), window_step, 0)
    grads_ref[...] = acc_ref[...].astype(BF16)


def far_kernel(sources, ids_ref, *refs):
    count = len(sources)
    kv_refs, refs = refs[:count], refs[count:]
    query_refs, near_ref, refs = refs[:3], refs[3], refs[4:]
    grads_refs, (dq_ref, partner_ref, acc_ref) = refs[:count], refs[count:]
    chip_blocks = near_ref.shape[0]
    position = lax.axis_index("ctx") * CORES + lax.axis_index("rep")
    capacity = acc_ref.shape[0] // BLOCK
    together = 4 if capacity < 4 else 2 if capacity == 4 else 1
    if count > 1:
        dq_ref[...] = near_ref[...]
        near_ref = dq_ref
    for table, kv_ref, grads_ref in zip(sources, kv_refs, grads_refs):
        held = chip_count(ids_ref, table_entry(table, position), chip_blocks)

        @pl.when(held > 0)
        def _():
            keys, values = keys_of(kv_ref, slice(None)), values_of(kv_ref, slice(None))
            key_t = transposed(keys)
            acc_ref[...] = jnp.zeros_like(acc_ref)

            def query_step(item, carry):
                first = item * together
                dq, dk, dv = block_grads(keys, values, key_t, query_refs, first, together)
                put_queries(dq_ref, near_ref, first, dq)
                add_grads(acc_ref, slice(None), dk, dv)
                return carry

            lax.fori_loop(0, chip_blocks // together, query_step, 0)
            grads_ref[...] = acc_ref[...].astype(BF16)

        @pl.when(held == 0)
        def _():
            grads_ref[...] = jnp.zeros_like(grads_ref)
            if count == 1:
                dq_ref[...] = near_ref[...]

    partner_ref[...] = dq_ref[chip_blocks // CORES :].astype(BF16)


def layout_kernel(q_ref, g_ref, s_ref, pq_ref, pg_ref, ps_ref, all_q_ref, all_g_ref, all_s_ref):
    blocks_here = s_ref.shape[0]
    for from_refs, to_ref in (((q_ref, pq_ref), all_q_ref), ((g_ref, pg_ref), all_g_ref)):
        for side, from_ref in enumerate(from_refs):
            for block in range(blocks_here):
                rows = slice(block * BLOCK, (block + 1) * BLOCK)
                for head in range(GROUP):
                    to_rows = slice(head * BLOCK, (head + 1) * BLOCK)
                    lanes = slice(head * HEAD_DIM, (head + 1) * HEAD_DIM)
                    to_ref[side * blocks_here + block, to_rows, :] = from_ref[rows, lanes]
    all_s_ref[0:blocks_here] = s_ref[...]
    all_s_ref[blocks_here:] = ps_ref[...]


def own_kernel(
    offsets_ref, ids_ref, kv_ref, partner_ref, q_ref, g_ref, s_ref, far_ref,
    acc_ref, cross_ref, dq_ref, sum_ref,
):
    core = lax.axis_index("rep")
    blocks_here = kv_ref.shape[0] // BLOCK
    _, base, own = places(blocks_here)
    together = 2
    sum_ref[...] = jnp.zeros_like(sum_ref)
    dq_ref[...] = far_ref[0:blocks_here]

    def step(item, carry):
        side = item // (blocks_here // together)
        first = lax.rem(item, blocks_here // together) * together
        first_key = jnp.where(side == 0, own, base)
        flags = [
            [
                attends(offsets_ref, ids_ref, own + first + number, first_key + key)
                | (first_key + key == own + first + number)
                for number in range(together)
            ]
            for key in range(blocks_here)
        ]
        some = flags[0][0]
        for row in flags:
            for flag in row:
                some |= flag

        @pl.when(some)
        def _():
            kv = jnp.where(side == 0, kv_ref[...], partner_ref[...])
            keys, values = keys_of(kv, slice(None)), values_of(kv, slice(None))
            dq, dk, dv = block_grads(
                keys, values, transposed(keys), (q_ref, g_ref, s_ref), first, together,
                [[bias_of(flag) for flag in row] for row in flags],
                (first_key - own - first) * BLOCK,
            )
            put_queries(dq_ref, dq_ref, first, dq)
            add_grads(sum_ref.at[side], slice(None), dk, dv)

        return carry

    lax.fori_loop(0, (1 + core) * (blocks_here // together), step, 0)
    acc_ref[...] = sum_ref[0]
    cross_ref[...] = sum_ref[1].astype(BF16)


def query_kernel(own_ref, partner_ref, dq_ref):
    def block_step(block, carry):
        total = own_ref[block] + partner_ref[block].astype(F32)
        rows = pl.ds(pl.multiple_of(block * BLOCK, BLOCK), BLOCK)
        for head in range(GROUP):
            lanes = slice(head * HEAD_DIM, (head + 1) * HEAD_DIM)
            dq_ref[rows, lanes] = total[:, lanes].T.astype(BF16)
        return carry

    lax.fori_loop(0, own_ref.shape[0], block_step, 0)


def final_kernel(last_sender, ids_ref, acc_ref, near_ref, cross_ref, *refs):
    far_refs, (dk_ref, dv_ref, sum_ref) = refs[:-3], refs[-3:]
    blocks_here = acc_ref.shape[0] // BLOCK
    chip_blocks = CORES * blocks_here
    chip = lax.axis_index("ctx")
    core = lax.axis_index("rep")
    sum_ref[...] = acc_ref[...] + near_ref[...].astype(F32) + cross_ref[...].astype(F32)
    dk_ref[...] = keys_of(sum_ref, slice(None)).astype(BF16)
    dv_ref[...] = values_of(sum_ref, slice(None)).astype(BF16)
    capacity = far_refs[0].shape[0] // BLOCK
    for slot in range(SUMMARY):
        owner, rank = chip_slot(ids_ref, slot, chip_blocks)
        local = ids_ref[slot] - chip * chip_blocks - core * blocks_here
        mine = (owner == chip) & (local >= 0) & (local < blocks_here)

        @pl.when(mine & (chip <= last_sender) & (rank < capacity))
        def _():
            rows = pl.ds(pl.multiple_of(local * BLOCK, BLOCK), BLOCK)
            place = pl.ds(pl.multiple_of(rank * BLOCK, BLOCK), BLOCK)
            total = sum_ref[rows, :]
            for far_ref in far_refs:
                total += far_ref[place, :].astype(F32)
            dk_ref[rows, :] = total[:, 0:HEAD_DIM].astype(BF16)
            dv_ref[rows, :] = total[:, HEAD_DIM : 2 * HEAD_DIM].astype(BF16)


def call(kernel, scalars, arrays, out_shape, scratch=(), flops=0, in_space=VMEM, out_specs=None, room=24):
    return pl.pallas_call(
        kernel,
        out_shape=out_shape,
        in_specs=[SMEM] * len(scalars) + [in_space] * len(arrays),
        out_specs=out_specs or jax.tree.map(lambda _: VMEM, out_shape),
        scratch_shapes=list(scratch),
        compiler_params=pltpu.CompilerParams(vmem_limit_bytes=room << 20),
        cost_estimate=pl.CostEstimate(flops=flops, bytes_accessed=0, transcendentals=0),
    )(*scalars, *arrays)


def shape_of(shape, dtype):
    return jax.ShapeDtypeStruct(shape, dtype)


def with_capacity(
    capacity, chips, queries, kv, attn_out, grads, log_sums, window_offsets, summary_ids
):
    rows = queries.shape[0]
    blocks_here = rows // BLOCK
    swap = [(0, 1), (1, 0)]
    up = [(i, i + 1) for i in range(chips - 1)]
    down = [(b, a) for a, b in up]
    routes = far_rounds(chips)
    sources = tuple({b: a // CORES for a, b in route} for route in routes)
    both = ("ctx", "rep")

    kv_partner = lax.ppermute(kv, "rep", swap)
    kv_near = lax.ppermute(kv, "ctx", up)
    far_shape = shape_of((capacity * BLOCK, 2 * HEAD_DIM), BF16)
    picked = call(pick_kernel, (summary_ids,), (kv, kv_partner), far_shape)
    kv_far = [lax.ppermute(picked, both, route) for route in routes]
    queries, grads, attn_out, window_offsets, _ = lax.optimization_barrier(
        (queries, grads, attn_out, window_offsets, picked)
    )
    tables = (window_offsets, summary_ids)
    stats = call(
        prep_kernel, (), (attn_out, grads, log_sums),
        shape_of((blocks_here, 8, GROUP * BLOCK), F32), flops=5 * MICROSECOND,
    )
    own = (queries, grads, stats)
    every = own + tuple(lax.ppermute(x, "rep", swap) for x in own)
    acc_shape = (rows, 2 * HEAD_DIM)
    half_shape = (blocks_here, HEAD_DIM, GROUP * BLOCK)
    dq_shape = shape_of((CORES * blocks_here, *half_shape[1:]), F32)
    stacked_shape = shape_of((CORES * blocks_here, GROUP * BLOCK, HEAD_DIM), BF16)
    every = call(
        layout_kernel, (), every,
        (
            stacked_shape, stacked_shape,
            shape_of((CORES * blocks_here, *stats.shape[1:]), F32),
        ),
    )
    near_grads, near_dq = call(
        near_kernel, tables, (kv_near, *every), (shape_of(acc_shape, BF16), dq_shape),
        [pltpu.VMEM(acc_shape, F32)],
    )
    *far_grads, far_dq, dq_partner = call(
        functools.partial(far_kernel, sources), (summary_ids,), (*kv_far, *every, near_dq),
        (*[far_shape] * len(routes), dq_shape, shape_of(half_shape, BF16)),
        [pltpu.VMEM(far_shape.shape, F32)], flops=5 * MICROSECOND,
    )
    far_back = [
        lax.ppermute(x, both, [(b, a) for a, b in route]) for x, route in zip(far_grads, routes)
    ]
    near_grads, _ = lax.optimization_barrier((near_grads, far_grads))
    near_back = lax.ppermute(near_grads, "ctx", down)
    dq_partner = lax.ppermute(dq_partner, "rep", swap)
    acc, cross, dq = call(
        own_kernel, tables, (kv, kv_partner, *every, far_dq),
        (shape_of(acc_shape, F32), shape_of(acc_shape, BF16), shape_of(half_shape, F32)),
        [pltpu.VMEM((CORES, *acc_shape), F32)], flops=OWN,
    )
    cross = lax.ppermute(cross, "rep", swap)
    query_grads = call(query_kernel, (), (dq, dq_partner), shape_of(queries.shape, BF16))
    if capacity > 3:
        acc, near_back = lax.optimization_barrier((acc, near_back))
    far_back, acc, query_grads = lax.optimization_barrier((far_back, acc, query_grads))
    far_other = [lax.ppermute(x, "rep", swap) for x in far_back]
    kv_shape = shape_of((rows, HEAD_DIM), BF16)
    key_grads, value_grads = call(
        functools.partial(final_kernel, chips - 3), (summary_ids,),
        (acc, near_back, cross, *far_back, *far_other), (kv_shape, kv_shape),
        [pltpu.VMEM(acc_shape, F32)],
    )
    return query_grads, key_grads, value_grads


def capacities(chips):
    return CAPACITIES if len(far_rounds(chips)) == 1 else CAPACITIES[-1:]


def per_device(chips, queries, keys, values, attn_out, grads, log_sums, window_offsets, summary_ids):
    kv, branch = call(
        functools.partial(start_kernel, chips), (), (summary_ids, keys, values),
        (shape_of((keys.shape[0], 2 * HEAD_DIM), BF16), shape_of((1,), jnp.int32)),
        [pltpu.SMEM(summary_ids.shape, jnp.int32), pltpu.SemaphoreType.DMA((3,))], in_space=HBM, out_specs=(VMEM, SMEM), room=60,
    )
    branches = [functools.partial(with_capacity, limit, chips) for limit in capacities(chips)]
    operands = (queries, kv, attn_out, grads, log_sums, window_offsets.T, summary_ids)
    return lax.switch(branch[0], branches, *operands) if len(branches) > 1 else branches[0](*operands)


def solution(mesh):
    rows = P(("groups", "ctx", "rep"), "heads")
    return jax.shard_map(
        functools.partial(per_device, mesh.shape["ctx"]),
        mesh=mesh,
        in_specs=(rows,) * 5 + (P("heads", ("groups", "ctx", "rep")), P("groups", None), P("groups")),
        out_specs=(rows,) * 3,
        check_vma=False,
    )
```

```python
import functools
import math

import jax
import jax.numpy as jnp
from jax import lax
from jax.experimental import pallas as pl
from jax.experimental.pallas import tpu as pltpu
from jax.sharding import PartitionSpec as P

HEAD_DIM = 128
GROUP = 4
BLOCK = 128
REACH = 3
SUMMARY = 8
CORES = 2
SCALE = HEAD_DIM ** (-0.5)
LOG2E = math.log2(math.e)
MICROSECOND = 1_000_000_000
OWN = 10 * MICROSECOND
CAPACITIES = (2, 3, 4, SUMMARY - 1)
F32 = jnp.float32
BF16 = jnp.bfloat16
VMEM = pl.BlockSpec(memory_space=pltpu.VMEM)
SMEM = pl.BlockSpec(memory_space=pltpu.SMEM)
HBM = pl.BlockSpec(memory_space=pltpu.HBM)


def far_rounds(chips):
    rounds = []
    for source in range(chips):
        for target in range(source + 2, chips):
            wanted = target % CORES
            better = (source + target + 1) % CORES
            for route in rounds:
                senders = [core for core in range(CORES) if source * CORES + core not in route.values()]
                receivers = [core for core in range(CORES) if target * CORES + core not in route]
                if senders and receivers:
                    break
            else:
                senders, receivers, route = list(range(CORES)), list(range(CORES)), {}
                rounds.append(route)
            sender = wanted if wanted in senders else senders[0]
            receiver = better if better in receivers else receivers[0]
            route[target * CORES + receiver] = source * CORES + sender
    return [[(a, b) for b, a in route.items()] for route in rounds]


def table_entry(table, position):
    value = jnp.int32(-1)
    for place, entry in table.items():
        value = jnp.where(position == place, jnp.int32(entry), value)
    return value


def chip_slot(ids_ref, slot, chip_blocks):
    chip = ids_ref[slot] // chip_blocks
    rank = jnp.int32(0)
    for other in range(slot):
        rank += jnp.where(ids_ref[other] // chip_blocks == chip, 1, 0)
    return chip, rank


def chip_count(ids_ref, chip, chip_blocks):
    count = jnp.int32(0)
    for slot in range(SUMMARY):
        count += jnp.where(ids_ref[slot] // chip_blocks == chip, 1, 0)
    return count


def prep_kernel(out_ref, grad_ref, lse_ref, stats_ref):
    stats_ref[...] = jnp.zeros_like(stats_ref)
    for block in range(stats_ref.shape[0]):
        rows = slice(block * BLOCK, (block + 1) * BLOCK)
        for head in range(GROUP):
            columns = slice(head * HEAD_DIM, (head + 1) * HEAD_DIM)
            product = out_ref[rows, columns].astype(F32) * grad_ref[rows, columns].astype(F32)
            stats_ref[block, 0:1, columns] = lse_ref[head : head + 1, rows] * LOG2E
            stats_ref[block, 1:2, columns] = jnp.sum(product.T, axis=0, keepdims=True)


def start_kernel(chips, ids_hbm, key_ref, value_ref, kv_ref, branch_ref, ids_ref, sems):
    chip_blocks = CORES * (key_ref.shape[0] // BLOCK)
    copies = [
        pltpu.make_async_copy(
            ref, kv_ref.at[:, number * HEAD_DIM : (number + 1) * HEAD_DIM], sems.at[number]
        )
        for number, ref in enumerate((key_ref, value_ref))
    ]
    ids_copy = pltpu.make_async_copy(ids_hbm, ids_ref, sems.at[2])
    ids_copy.start()
    for copy in copies:
        copy.start()
    ids_copy.wait()
    most = jnp.int32(0)
    for chip in range(chips - 2):
        most = jnp.maximum(most, chip_count(ids_ref, chip, chip_blocks))
    branch = jnp.int32(0)
    for capacity in capacities(chips)[:-1]:
        branch += jnp.where(most > capacity, 1, 0)
    branch_ref[0] = branch
    for copy in copies:
        copy.wait()


def pick_kernel(ids_ref, own_ref, partner_ref, picked_ref):
    chip = lax.axis_index("ctx")
    core = lax.axis_index("rep")
    blocks_here = own_ref.shape[0] // BLOCK
    chip_blocks = CORES * blocks_here
    capacity = picked_ref.shape[0] // BLOCK
    picked_ref[...] = jnp.zeros_like(picked_ref)
    for slot in range(SUMMARY):
        owner, rank = chip_slot(ids_ref, slot, chip_blocks)
        local = ids_ref[slot] - chip * chip_blocks
        row = pl.multiple_of((local % blocks_here) * BLOCK, BLOCK)
        place = pl.multiple_of(rank * BLOCK, BLOCK)
        mine = local // blocks_here == core
        wanted = (owner == chip) & (rank < capacity)

        @pl.when(wanted & mine)
        def _():
            picked_ref[pl.ds(place, BLOCK), :] = own_ref[pl.ds(row, BLOCK), :]

        @pl.when(wanted & ~mine)
        def _():
            picked_ref[pl.ds(place, BLOCK), :] = partner_ref[pl.ds(row, BLOCK), :]


def nt(a, b):
    return lax.dot_general(a, b, (((1,), (1,)), ((), ())), preferred_element_type=F32)


def nn(a, b):
    return jnp.dot(a, b, preferred_element_type=F32)


def block_grads(keys, values, key_t, query_refs, first, count=1, biases=None, reach=None):
    query_ref, grad_ref, stats_ref = query_refs
    numbers = [first + step for step in range(count)]
    queries = jnp.concatenate([query_ref[number] for number in numbers], axis=0)
    grads = jnp.concatenate([grad_ref[number] for number in numbers], axis=0)
    log_sums = [stats_ref[number, 0:1, :] for number in numbers]
    deltas = jnp.concatenate([stats_ref[number, 1:2, :] for number in numbers], axis=1)
    scores = nt(keys, queries) * (SCALE * LOG2E)
    if biases is None:
        probs = jnp.exp2(scores - jnp.concatenate(log_sums, axis=1))
    else:
        if reach is not None:
            shape = (BLOCK, queries.shape[0])
            column = lax.broadcasted_iota(jnp.int32, shape, 1)
            ahead = column // (GROUP * BLOCK) * BLOCK + column % BLOCK
            ahead -= lax.broadcasted_iota(jnp.int32, shape, 0)
        parts = []
        for key, row in enumerate(biases):
            shift = jnp.concatenate([a + bias for a, bias in zip(log_sums, row)], axis=1)
            part = jnp.exp2(scores[key * BLOCK : (key + 1) * BLOCK] - shift)
            if reach is not None:
                part = jnp.where(ahead >= reach + key * BLOCK, part, 0.0)
            parts.append(part)
        probs = jnp.concatenate(parts, axis=0)
    prob_grads = nt(values, grads)
    score_grads = (probs * (prob_grads - deltas) * SCALE).astype(BF16)
    return nn(key_t, score_grads), nn(score_grads, queries), nn(probs.astype(BF16), grads)


def put_queries(to_ref, from_ref, first, dq):
    width = GROUP * BLOCK
    for step in range(dq.shape[1] // width):
        part = dq[:, step * width : (step + 1) * width]
        to_ref[first + step] = from_ref[first + step] + part


def is_summary(ids_ref, key_block):
    found = ids_ref[0] == key_block
    for slot in range(1, SUMMARY):
        found |= ids_ref[slot] == key_block
    return found


def in_window(offsets_ref, query_block, key_block):
    distance = query_block - key_block
    return (distance == offsets_ref[0, query_block]) | (distance == offsets_ref[1, query_block])


def attends(offsets_ref, ids_ref, query_block, key_block):
    chosen = in_window(offsets_ref, query_block, key_block) | is_summary(ids_ref, key_block)
    return (query_block > key_block) & chosen


def keys_of(kv_ref, rows):
    return kv_ref[rows, 0:HEAD_DIM]


def values_of(kv_ref, rows):
    return kv_ref[rows, HEAD_DIM : 2 * HEAD_DIM]


def transposed(keys):
    return keys.astype(F32).T.astype(BF16)


def add_grads(acc_ref, rows, key_part, value_part):
    acc_ref[rows, 0:HEAD_DIM] += key_part
    acc_ref[rows, HEAD_DIM : 2 * HEAD_DIM] += value_part


def places(blocks_here):
    chip = lax.axis_index("ctx")
    base = chip * CORES * blocks_here
    return chip, base, base + lax.axis_index("rep") * blocks_here


def bias_of(flag):
    return jnp.where(flag, 0.0, 1e30).astype(F32)


def near_kernel(
    offsets_ref, ids_ref, kv_ref, q_ref, g_ref, s_ref, cross_ref, grads_ref, dq_ref, acc_ref
):
    query_refs = (q_ref, g_ref, s_ref)
    blocks_here = kv_ref.shape[0] // BLOCK
    chip_blocks = CORES * blocks_here
    chip, base, own = places(blocks_here)
    first_key = own - chip_blocks
    acc_ref[...] = jnp.zeros_like(acc_ref)
    dq_ref[0:blocks_here] = jnp.zeros_like(cross_ref)
    dq_ref[blocks_here:] = cross_ref[...]
    flags = [is_summary(ids_ref, first_key + key) & (chip > 0) for key in range(blocks_here)]
    count = jnp.int32(0)
    chosen = [jnp.int32(0)] * blocks_here
    for key in range(blocks_here):
        for place in range(key + 1):
            chosen[place] = jnp.where(flags[key] & (count == place), key, chosen[place])
        count += jnp.where(flags[key], 1, 0)

    def add(first, count, places_of_keys, biases=None):
        rows = [pl.ds(pl.multiple_of(key * BLOCK, BLOCK), BLOCK) for key in places_of_keys]
        keys = jnp.concatenate([keys_of(kv_ref, row) for row in rows], axis=0)
        values = jnp.concatenate([values_of(kv_ref, row) for row in rows], axis=0)
        dq, dk, dv = block_grads(keys, values, transposed(keys), query_refs, first, count, biases)
        put_queries(dq_ref, dq_ref, first, dq)
        for place, row in enumerate(rows):
            part = slice(place * BLOCK, (place + 1) * BLOCK)
            add_grads(acc_ref, row, dk[part], dv[part])

    def entry(place):
        key = jnp.int32(0)
        for number in range(blocks_here):
            key = jnp.where(place == number, chosen[number], key)
        return key

    odd = lax.rem(count, 2)

    def single_step(item, carry):
        add(item * 4, 4, [chosen[0]])
        return carry

    lax.fori_loop(0, odd * (chip_blocks // 4), single_step, 0)

    def double_step(item, carry):
        turn = odd + 2 * (item // (chip_blocks // 2))
        add(lax.rem(item, chip_blocks // 2) * 2, 2, [entry(turn), entry(turn + 1)])
        return carry

    lax.fori_loop(0, (count // 2) * (chip_blocks // 2), double_step, 0)

    def window_step(number, carry):
        query = base + number
        keys, wanted = [], []
        for place in range(2):
            key = query - offsets_ref[place, query] - first_key
            fits = (key >= 0) & (key < blocks_here)
            key = jnp.where(fits, key, 0)
            for block in range(blocks_here):
                fits &= (key != block) | ~flags[block]
            keys.append(key)
            wanted.append(fits)

        @pl.when(wanted[0] | wanted[1])
        def _():
            add(number + blocks_here, 1, keys, [[bias_of(flag)] for flag in wanted])

        return carry

    reaches = (chip > 0) & (lax.axis_index("rep") == CORES - 1)
    lax.fori_loop(0, jnp.where(reaches, min(REACH, blocks_here), 0), window_step, 0)
    grads_ref[...] = acc_ref[...].astype(BF16)


def far_kernel(sources, ids_ref, *refs):
    count = len(sources)
    kv_refs, refs = refs[:count], refs[count:]
    query_refs, near_ref, refs = refs[:3], refs[3], refs[4:]
    grads_refs, (dq_ref, partner_ref, acc_ref) = refs[:count], refs[count:]
    chip_blocks = near_ref.shape[0]
    position = lax.axis_index("ctx") * CORES + lax.axis_index("rep")
    capacity = acc_ref.shape[0] // BLOCK
    together = 4 if capacity < 4 else 2 if capacity == 4 else 1
    if count > 1:
        dq_ref[...] = near_ref[...]
        near_ref = dq_ref
    for table, kv_ref, grads_ref in zip(sources, kv_refs, grads_refs):
        held = chip_count(ids_ref, table_entry(table, position), chip_blocks)

        @pl.when(held > 0)
        def _():
            keys, values = keys_of(kv_ref, slice(None)), values_of(kv_ref, slice(None))
            key_t = transposed(keys)
            acc_ref[...] = jnp.zeros_like(acc_ref)

            def query_step(item, carry):
                first = item * together
                dq, dk, dv = block_grads(keys, values, key_t, query_refs, first, together)
                put_queries(dq_ref, near_ref, first, dq)
                add_grads(acc_ref, slice(None), dk, dv)
                return carry

            lax.fori_loop(0, chip_blocks // together, query_step, 0)
            grads_ref[...] = acc_ref[...].astype(BF16)

        @pl.when(held == 0)
        def _():
            grads_ref[...] = jnp.zeros_like(grads_ref)
            if count == 1:
                dq_ref[...] = near_ref[...]

    partner_ref[...] = dq_ref[chip_blocks // CORES :].astype(BF16)


def pairs_of_blocks(
    offsets_ref, ids_ref, kv_ref, first_key, first_query, query_refs, first_number, acc_ref, dq_ref
):
    blocks_here = kv_ref.shape[0] // BLOCK
    keys, values = keys_of(kv_ref, slice(None)), values_of(kv_ref, slice(None))
    key_t = transposed(keys)

    def step(item, carry):
        first = item * 2
        flags = [
            [
                attends(offsets_ref, ids_ref, first_query + first + number, first_key + key)
                | (first_key + key == first_query + first + number)
                for number in range(2)
            ]
            for key in range(blocks_here)
        ]
        some = flags[0][0]
        for row in flags:
            for flag in row:
                some |= flag

        @pl.when(some)
        def _():
            dq, dk, dv = block_grads(
                keys, values, key_t, query_refs, first_number + first, 2,
                [[bias_of(flag) for flag in row] for row in flags],
                (first_key - first_query - first) * BLOCK if first_number == 0 else None,
            )
            put_queries(dq_ref, dq_ref, first, dq)
            add_grads(acc_ref, slice(None), dk, dv)

        return carry

    lax.fori_loop(0, blocks_here // 2, step, 0)


def cross_kernel(
    offsets_ref, ids_ref, kv_ref, q_ref, g_ref, s_ref, pq_ref, pg_ref, ps_ref,
    acc_ref, dq_ref, all_q_ref, all_g_ref, all_s_ref,
):
    blocks_here = kv_ref.shape[0] // BLOCK
    _, base, own = places(blocks_here)
    for from_refs, to_ref in (((q_ref, pq_ref), all_q_ref), ((g_ref, pg_ref), all_g_ref)):
        for side, from_ref in enumerate(from_refs):
            for block in range(blocks_here):
                rows = slice(block * BLOCK, (block + 1) * BLOCK)
                for head in range(GROUP):
                    to_rows = slice(head * BLOCK, (head + 1) * BLOCK)
                    lanes = slice(head * HEAD_DIM, (head + 1) * HEAD_DIM)
                    to_ref[side * blocks_here + block, to_rows, :] = from_ref[rows, lanes]
    all_s_ref[0:blocks_here] = s_ref[...]
    all_s_ref[blocks_here:] = ps_ref[...]
    acc_ref[...] = jnp.zeros_like(acc_ref)
    dq_ref[...] = jnp.zeros_like(dq_ref)

    @pl.when(lax.axis_index("rep") == 0)
    def _():
        pairs_of_blocks(
            offsets_ref, ids_ref, kv_ref, own, base + blocks_here,
            (all_q_ref, all_g_ref, all_s_ref), blocks_here, acc_ref, dq_ref,
        )


def own_kernel(
    offsets_ref, ids_ref, kv_ref, q_ref, g_ref, s_ref, cross_ref, far_ref, acc_ref, dq_ref
):
    blocks_here = kv_ref.shape[0] // BLOCK
    _, _, own = places(blocks_here)
    acc_ref[...] = cross_ref[...]
    dq_ref[...] = far_ref[0:blocks_here]
    pairs_of_blocks(
        offsets_ref, ids_ref, kv_ref, own, own, (q_ref, g_ref, s_ref), 0, acc_ref, dq_ref
    )


def query_kernel(own_ref, partner_ref, dq_ref):
    def block_step(block, carry):
        total = own_ref[block] + partner_ref[block].astype(F32)
        rows = pl.ds(pl.multiple_of(block * BLOCK, BLOCK), BLOCK)
        for head in range(GROUP):
            lanes = slice(head * HEAD_DIM, (head + 1) * HEAD_DIM)
            dq_ref[rows, lanes] = total[:, lanes].T.astype(BF16)
        return carry

    lax.fori_loop(0, own_ref.shape[0], block_step, 0)


def final_kernel(last_sender, ids_ref, acc_ref, near_ref, *refs):
    far_refs, (dk_ref, dv_ref, sum_ref) = refs[:-3], refs[-3:]
    blocks_here = acc_ref.shape[0] // BLOCK
    chip_blocks = CORES * blocks_here
    chip = lax.axis_index("ctx")
    core = lax.axis_index("rep")
    sum_ref[...] = acc_ref[...] + near_ref[...].astype(F32)
    dk_ref[...] = keys_of(sum_ref, slice(None)).astype(BF16)
    dv_ref[...] = values_of(sum_ref, slice(None)).astype(BF16)
    capacity = far_refs[0].shape[0] // BLOCK
    for slot in range(SUMMARY):
        owner, rank = chip_slot(ids_ref, slot, chip_blocks)
        local = ids_ref[slot] - chip * chip_blocks - core * blocks_here
        mine = (owner == chip) & (local >= 0) & (local < blocks_here)

        @pl.when(mine & (chip <= last_sender) & (rank < capacity))
        def _():
            rows = pl.ds(pl.multiple_of(local * BLOCK, BLOCK), BLOCK)
            place = pl.ds(pl.multiple_of(rank * BLOCK, BLOCK), BLOCK)
            total = sum_ref[rows, :]
            for far_ref in far_refs:
                total += far_ref[place, :].astype(F32)
            dk_ref[rows, :] = total[:, 0:HEAD_DIM].astype(BF16)
            dv_ref[rows, :] = total[:, HEAD_DIM : 2 * HEAD_DIM].astype(BF16)


def call(kernel, scalars, arrays, out_shape, scratch=(), flops=0, in_space=VMEM, out_specs=None, room=24):
    return pl.pallas_call(
        kernel,
        out_shape=out_shape,
        in_specs=[SMEM] * len(scalars) + [in_space] * len(arrays),
        out_specs=out_specs or jax.tree.map(lambda _: VMEM, out_shape),
        scratch_shapes=list(scratch),
        compiler_params=pltpu.CompilerParams(vmem_limit_bytes=room << 20),
        cost_estimate=pl.CostEstimate(flops=flops, bytes_accessed=0, transcendentals=0),
    )(*scalars, *arrays)


def shape_of(shape, dtype):
    return jax.ShapeDtypeStruct(shape, dtype)


def with_capacity(
    capacity, chips, queries, kv, attn_out, grads, log_sums, window_offsets, summary_ids
):
    rows = queries.shape[0]
    blocks_here = rows // BLOCK
    swap = [(0, 1), (1, 0)]
    up = [(i, i + 1) for i in range(chips - 1)]
    down = [(b, a) for a, b in up]
    routes = far_rounds(chips)
    sources = tuple({b: a // CORES for a, b in route} for route in routes)
    both = ("ctx", "rep")

    kv_partner = lax.ppermute(kv, "rep", swap)
    kv_near = lax.ppermute(kv, "ctx", up)
    far_shape = shape_of((capacity * BLOCK, 2 * HEAD_DIM), BF16)
    picked = call(pick_kernel, (summary_ids,), (kv, kv_partner), far_shape)
    kv_far = [lax.ppermute(picked, both, route) for route in routes]
    queries, grads, attn_out, window_offsets, _ = lax.optimization_barrier(
        (queries, grads, attn_out, window_offsets, picked)
    )
    tables = (window_offsets, summary_ids)
    stats = call(
        prep_kernel, (), (attn_out, grads, log_sums),
        shape_of((blocks_here, 8, GROUP * BLOCK), F32), flops=5 * MICROSECOND,
    )
    own = (queries, grads, stats)
    every = own + tuple(lax.ppermute(x, "rep", swap) for x in own)
    acc_shape = (rows, 2 * HEAD_DIM)
    half_shape = (blocks_here, HEAD_DIM, GROUP * BLOCK)
    dq_shape = shape_of((CORES * blocks_here, *half_shape[1:]), F32)
    stacked_shape = shape_of((CORES * blocks_here, GROUP * BLOCK, HEAD_DIM), BF16)
    cross_acc, cross_dq, *every = call(
        cross_kernel, tables, (kv, *every),
        (
            shape_of(acc_shape, F32), shape_of(half_shape, F32), stacked_shape, stacked_shape,
            shape_of((CORES * blocks_here, *stats.shape[1:]), F32),
        ),
    )
    near_grads, near_dq = call(
        near_kernel, tables, (kv_near, *every, cross_dq), (shape_of(acc_shape, BF16), dq_shape),
        [pltpu.VMEM(acc_shape, F32)],
    )
    *far_grads, far_dq, dq_partner = call(
        functools.partial(far_kernel, sources), (summary_ids,), (*kv_far, *every, near_dq),
        (*[far_shape] * len(routes), dq_shape, shape_of(half_shape, BF16)),
        [pltpu.VMEM(far_shape.shape, F32)], flops=5 * MICROSECOND,
    )
    far_back = [
        lax.ppermute(x, both, [(b, a) for a, b in route]) for x, route in zip(far_grads, routes)
    ]
    near_grads, _ = lax.optimization_barrier((near_grads, far_grads))
    near_back = lax.ppermute(near_grads, "ctx", down)
    dq_partner = lax.ppermute(dq_partner, "rep", swap)
    acc, dq = call(
        own_kernel, tables, (kv, *every, cross_acc, far_dq),
        (shape_of(acc_shape, F32), shape_of(half_shape, F32)), flops=OWN,
    )
    query_grads = call(query_kernel, (), (dq, dq_partner), shape_of(queries.shape, BF16))
    if capacity > 3:
        acc, near_back = lax.optimization_barrier((acc, near_back))
    far_back, acc, query_grads = lax.optimization_barrier((far_back, acc, query_grads))
    far_other = [lax.ppermute(x, "rep", swap) for x in far_back]
    kv_shape = shape_of((rows, HEAD_DIM), BF16)
    key_grads, value_grads = call(
        functools.partial(final_kernel, chips - 3), (summary_ids,),
        (acc, near_back, *far_back, *far_other), (kv_shape, kv_shape),
        [pltpu.VMEM(acc_shape, F32)],
    )
    return query_grads, key_grads, value_grads


def capacities(chips):
    return CAPACITIES if len(far_rounds(chips)) == 1 else CAPACITIES[-1:]


def per_device(chips, queries, keys, values, attn_out, grads, log_sums, window_offsets, summary_ids):
    kv, branch = call(
        functools.partial(start_kernel, chips), (), (summary_ids, keys, values),
        (shape_of((keys.shape[0], 2 * HEAD_DIM), BF16), shape_of((1,), jnp.int32)),
        [pltpu.SMEM(summary_ids.shape, jnp.int32), pltpu.SemaphoreType.DMA((3,))], in_space=HBM, out_specs=(VMEM, SMEM), room=60,
    )
    branches = [functools.partial(with_capacity, limit, chips) for limit in capacities(chips)]
    operands = (queries, kv, attn_out, grads, log_sums, window_offsets.T, summary_ids)
    return lax.switch(branch[0], branches, *operands) if len(branches) > 1 else branches[0](*operands)


def solution(mesh):
    rows = P(("groups", "ctx", "rep"), "heads")
    return jax.shard_map(
        functools.partial(per_device, mesh.shape["ctx"]),
        mesh=mesh,
        in_specs=(rows,) * 5 + (P("heads", ("groups", "ctx", "rep")), P("groups", None), P("groups")),
        out_specs=(rows,) * 3,
        check_vma=False,
    )
```

```python
import functools
import math

import jax
import jax.numpy as jnp
from jax import lax
from jax.experimental import pallas as pl
from jax.experimental.pallas import tpu as pltpu
from jax.sharding import PartitionSpec as P

HEAD_DIM = 128
GROUP = 4
BLOCK = 128
REACH = 3
SUMMARY = 8
CORES = 2
SCALE = HEAD_DIM ** (-0.5)
LOG2E = math.log2(math.e)
MICROSECOND = 1_000_000_000
OWN = 10 * MICROSECOND
CAPACITIES = (2, 3, 4, SUMMARY - 1)
F32 = jnp.float32
BF16 = jnp.bfloat16
VMEM = pl.BlockSpec(memory_space=pltpu.VMEM)
SMEM = pl.BlockSpec(memory_space=pltpu.SMEM)
HBM = pl.BlockSpec(memory_space=pltpu.HBM)


def far_rounds(chips):
    rounds = []
    for source in range(chips):
        for target in range(source + 2, chips):
            wanted = target % CORES
            better = (source + target + 1) % CORES
            for route in rounds:
                senders = [core for core in range(CORES) if source * CORES + core not in route.values()]
                receivers = [core for core in range(CORES) if target * CORES + core not in route]
                if senders and receivers:
                    break
            else:
                senders, receivers, route = list(range(CORES)), list(range(CORES)), {}
                rounds.append(route)
            sender = wanted if wanted in senders else senders[0]
            receiver = better if better in receivers else receivers[0]
            route[target * CORES + receiver] = source * CORES + sender
    return [[(a, b) for b, a in route.items()] for route in rounds]


def table_entry(table, position):
    value = jnp.int32(-1)
    for place, entry in table.items():
        value = jnp.where(position == place, jnp.int32(entry), value)
    return value


def chip_slot(ids_ref, slot, chip_blocks):
    chip = ids_ref[slot] // chip_blocks
    rank = jnp.int32(0)
    for other in range(slot):
        rank += jnp.where(ids_ref[other] // chip_blocks == chip, 1, 0)
    return chip, rank


def chip_count(ids_ref, chip, chip_blocks):
    count = jnp.int32(0)
    for slot in range(SUMMARY):
        count += jnp.where(ids_ref[slot] // chip_blocks == chip, 1, 0)
    return count


def prep_kernel(out_ref, grad_ref, lse_ref, stats_ref):
    stats_ref[...] = jnp.zeros_like(stats_ref)
    for block in range(stats_ref.shape[0]):
        rows = slice(block * BLOCK, (block + 1) * BLOCK)
        for head in range(GROUP):
            columns = slice(head * HEAD_DIM, (head + 1) * HEAD_DIM)
            product = out_ref[rows, columns].astype(F32) * grad_ref[rows, columns].astype(F32)
            stats_ref[block, 0:1, columns] = lse_ref[head : head + 1, rows] * LOG2E
            stats_ref[block, 1:2, columns] = jnp.sum(product.T, axis=0, keepdims=True)


def start_kernel(chips, ids_hbm, key_ref, value_ref, kv_ref, branch_ref, ids_ref, sems):
    chip_blocks = CORES * (key_ref.shape[0] // BLOCK)
    copies = [
        pltpu.make_async_copy(
            ref, kv_ref.at[:, number * HEAD_DIM : (number + 1) * HEAD_DIM], sems.at[number]
        )
        for number, ref in enumerate((key_ref, value_ref))
    ]
    ids_copy = pltpu.make_async_copy(ids_hbm, ids_ref, sems.at[2])
    ids_copy.start()
    for copy in copies:
        copy.start()
    ids_copy.wait()
    most = jnp.int32(0)
    for chip in range(chips - 2):
        most = jnp.maximum(most, chip_count(ids_ref, chip, chip_blocks))
    branch = jnp.int32(0)
    for capacity in capacities(chips)[:-1]:
        branch += jnp.where(most > capacity, 1, 0)
    branch_ref[0] = branch
    for copy in copies:
        copy.wait()


def pick_kernel(ids_ref, own_ref, partner_ref, picked_ref):
    chip = lax.axis_index("ctx")
    core = lax.axis_index("rep")
    blocks_here = own_ref.shape[0] // BLOCK
    chip_blocks = CORES * blocks_here
    capacity = picked_ref.shape[0] // BLOCK
    picked_ref[...] = jnp.zeros_like(picked_ref)
    for slot in range(SUMMARY):
        owner, rank = chip_slot(ids_ref, slot, chip_blocks)
        local = ids_ref[slot] - chip * chip_blocks
        row = pl.multiple_of((local % blocks_here) * BLOCK, BLOCK)
        place = pl.multiple_of(rank * BLOCK, BLOCK)
        mine = local // blocks_here == core
        wanted = (owner == chip) & (rank < capacity)

        @pl.when(wanted & mine)
        def _():
            picked_ref[pl.ds(place, BLOCK), :] = own_ref[pl.ds(row, BLOCK), :]

        @pl.when(wanted & ~mine)
        def _():
            picked_ref[pl.ds(place, BLOCK), :] = partner_ref[pl.ds(row, BLOCK), :]


def nt(a, b):
    return lax.dot_general(a, b, (((1,), (1,)), ((), ())), preferred_element_type=F32)


def nn(a, b):
    return jnp.dot(a, b, preferred_element_type=F32)


def block_grads(keys, values, key_t, query_refs, first, count=1, biases=None, reach=None):
    query_ref, grad_ref, stats_ref = query_refs
    numbers = [first + step for step in range(count)]
    queries = jnp.concatenate([query_ref[number] for number in numbers], axis=0)
    grads = jnp.concatenate([grad_ref[number] for number in numbers], axis=0)
    log_sums = [stats_ref[number, 0:1, :] for number in numbers]
    deltas = jnp.concatenate([stats_ref[number, 1:2, :] for number in numbers], axis=1)
    scores = nt(keys, queries) * (SCALE * LOG2E)
    if biases is None:
        probs = jnp.exp2(scores - jnp.concatenate(log_sums, axis=1))
    else:
        if reach is not None:
            shape = (BLOCK, queries.shape[0])
            column = lax.broadcasted_iota(jnp.int32, shape, 1)
            ahead = column // (GROUP * BLOCK) * BLOCK + column % BLOCK
            ahead -= lax.broadcasted_iota(jnp.int32, shape, 0)
        parts = []
        for key, row in enumerate(biases):
            shift = jnp.concatenate([a + bias for a, bias in zip(log_sums, row)], axis=1)
            part = jnp.exp2(scores[key * BLOCK : (key + 1) * BLOCK] - shift)
            if reach is not None:
                part = jnp.where(ahead >= reach + key * BLOCK, part, 0.0)
            parts.append(part)
        probs = jnp.concatenate(parts, axis=0)
    prob_grads = nt(values, grads)
    score_grads = (probs * (prob_grads - deltas) * SCALE).astype(BF16)
    return nn(key_t, score_grads), nn(score_grads, queries), nn(probs.astype(BF16), grads)


def put_queries(to_ref, from_ref, first, dq):
    width = GROUP * BLOCK
    for step in range(dq.shape[1] // width):
        part = dq[:, step * width : (step + 1) * width]
        to_ref[first + step] = from_ref[first + step] + part


def is_summary(ids_ref, key_block):
    found = ids_ref[0] == key_block
    for slot in range(1, SUMMARY):
        found |= ids_ref[slot] == key_block
    return found


def in_window(offsets_ref, query_block, key_block):
    distance = query_block - key_block
    return (distance == offsets_ref[0, query_block]) | (distance == offsets_ref[1, query_block])


def attends(offsets_ref, ids_ref, query_block, key_block):
    chosen = in_window(offsets_ref, query_block, key_block) | is_summary(ids_ref, key_block)
    return (query_block > key_block) & chosen


def keys_of(kv_ref, rows):
    return kv_ref[rows, 0:HEAD_DIM]


def values_of(kv_ref, rows):
    return kv_ref[rows, HEAD_DIM : 2 * HEAD_DIM]


def transposed(keys):
    return keys.astype(F32).T.astype(BF16)


def add_grads(acc_ref, rows, key_part, value_part):
    acc_ref[rows, 0:HEAD_DIM] += key_part
    acc_ref[rows, HEAD_DIM : 2 * HEAD_DIM] += value_part


def places(blocks_here):
    chip = lax.axis_index("ctx")
    base = chip * CORES * blocks_here
    return chip, base, base + lax.axis_index("rep") * blocks_here


def bias_of(flag):
    return jnp.where(flag, 0.0, 1e30).astype(F32)


def near_kernel(
    offsets_ref, ids_ref, kv_ref, q_ref, g_ref, s_ref, cross_ref, grads_ref, dq_ref, acc_ref
):
    query_refs = (q_ref, g_ref, s_ref)
    blocks_here = kv_ref.shape[0] // BLOCK
    chip_blocks = CORES * blocks_here
    chip, base, own = places(blocks_here)
    first_key = own - chip_blocks
    acc_ref[...] = jnp.zeros_like(acc_ref)
    dq_ref[0:blocks_here] = jnp.zeros_like(cross_ref)
    dq_ref[blocks_here:] = cross_ref[...]
    flags = [is_summary(ids_ref, first_key + key) & (chip > 0) for key in range(blocks_here)]
    count = jnp.int32(0)
    chosen = [jnp.int32(0)] * blocks_here
    for key in range(blocks_here):
        for place in range(key + 1):
            chosen[place] = jnp.where(flags[key] & (count == place), key, chosen[place])
        count += jnp.where(flags[key], 1, 0)

    def add(first, count, places_of_keys, biases=None):
        rows = [pl.ds(pl.multiple_of(key * BLOCK, BLOCK), BLOCK) for key in places_of_keys]
        keys = jnp.concatenate([keys_of(kv_ref, row) for row in rows], axis=0)
        values = jnp.concatenate([values_of(kv_ref, row) for row in rows], axis=0)
        dq, dk, dv = block_grads(keys, values, transposed(keys), query_refs, first, count, biases)
        put_queries(dq_ref, dq_ref, first, dq)
        for place, row in enumerate(rows):
            part = slice(place * BLOCK, (place + 1) * BLOCK)
            add_grads(acc_ref, row, dk[part], dv[part])

    def entry(place):
        key = jnp.int32(0)
        for number in range(blocks_here):
            key = jnp.where(place == number, chosen[number], key)
        return key

    odd = lax.rem(count, 2)

    def single_step(item, carry):
        add(item * 4, 4, [chosen[0]])
        return carry

    lax.fori_loop(0, odd * (chip_blocks // 4), single_step, 0)

    def double_step(item, carry):
        turn = odd + 2 * (item // (chip_blocks // 2))
        add(lax.rem(item, chip_blocks // 2) * 2, 2, [entry(turn), entry(turn + 1)])
        return carry

    lax.fori_loop(0, (count // 2) * (chip_blocks // 2), double_step, 0)

    def window_step(number, carry):
        query = base + number
        keys, wanted = [], []
        for place in range(2):
            key = query - offsets_ref[place, query] - first_key
            fits = (key >= 0) & (key < blocks_here)
            key = jnp.where(fits, key, 0)
            for block in range(blocks_here):
                fits &= (key != block) | ~flags[block]
            keys.append(key)
            wanted.append(fits)

        @pl.when(wanted[0] | wanted[1])
        def _():
            add(number + blocks_here, 1, keys, [[bias_of(flag)] for flag in wanted])

        return carry

    reaches = (chip > 0) & (lax.axis_index("rep") == CORES - 1)
    lax.fori_loop(0, jnp.where(reaches, min(REACH, blocks_here), 0), window_step, 0)
    grads_ref[...] = acc_ref[...].astype(BF16)


def far_kernel(sources, ids_ref, *refs):
    count = len(sources)
    kv_refs, refs = refs[:count], refs[count:]
    query_refs, near_ref, refs = refs[:3], refs[3], refs[4:]
    grads_refs, (dq_ref, partner_ref, acc_ref) = refs[:count], refs[count:]
    chip_blocks = near_ref.shape[0]
    position = lax.axis_index("ctx") * CORES + lax.axis_index("rep")
    capacity = acc_ref.shape[0] // BLOCK
    together = 4 if capacity < 4 else 2 if capacity == 4 else 1
    if count > 1:
        dq_ref[...] = near_ref[...]
        near_ref = dq_ref
    for table, kv_ref, grads_ref in zip(sources, kv_refs, grads_refs):
        held = chip_count(ids_ref, table_entry(table, position), chip_blocks)

        @pl.when(held > 0)
        def _():
            keys, values = keys_of(kv_ref, slice(None)), values_of(kv_ref, slice(None))
            key_t = transposed(keys)
            acc_ref[...] = jnp.zeros_like(acc_ref)

            def query_step(item, carry):
                first = item * together
                dq, dk, dv = block_grads(keys, values, key_t, query_refs, first, together)
                put_queries(dq_ref, near_ref, first, dq)
                add_grads(acc_ref, slice(None), dk, dv)
                return carry

            lax.fori_loop(0, chip_blocks // together, query_step, 0)
            grads_ref[...] = acc_ref[...].astype(BF16)

        @pl.when(held == 0)
        def _():
            grads_ref[...] = jnp.zeros_like(grads_ref)
            if count == 1:
                dq_ref[...] = near_ref[...]

    partner_ref[...] = dq_ref[chip_blocks // CORES :].astype(BF16)


def pairs_of_blocks(
    offsets_ref, ids_ref, kv_ref, first_key, first_query, query_refs, first_number, acc_ref, dq_ref
):
    blocks_here = kv_ref.shape[0] // BLOCK
    keys, values = keys_of(kv_ref, slice(None)), values_of(kv_ref, slice(None))
    key_t = transposed(keys)

    def step(number, carry):
        query = first_query + number
        flags = [
            attends(offsets_ref, ids_ref, query, first_key + key) | (first_key + key == query)
            for key in range(blocks_here)
        ]
        some = flags[0]
        for flag in flags[1:]:
            some |= flag

        @pl.when(some)
        def _():
            dq, dk, dv = block_grads(
                keys, values, key_t, query_refs, first_number + number, 1,
                [[bias_of(flag)] for flag in flags],
                (first_key - query) * BLOCK if first_number == 0 else None,
            )
            put_queries(dq_ref, dq_ref, number, dq)
            add_grads(acc_ref, slice(None), dk, dv)

        return carry

    lax.fori_loop(0, blocks_here, step, 0)


def cross_kernel(
    offsets_ref, ids_ref, kv_ref, q_ref, g_ref, s_ref, pq_ref, pg_ref, ps_ref,
    acc_ref, dq_ref, all_q_ref, all_g_ref, all_s_ref,
):
    blocks_here = kv_ref.shape[0] // BLOCK
    _, base, own = places(blocks_here)
    for from_refs, to_ref in (((q_ref, pq_ref), all_q_ref), ((g_ref, pg_ref), all_g_ref)):
        for side, from_ref in enumerate(from_refs):
            for block in range(blocks_here):
                rows = slice(block * BLOCK, (block + 1) * BLOCK)
                for head in range(GROUP):
                    to_rows = slice(head * BLOCK, (head + 1) * BLOCK)
                    lanes = slice(head * HEAD_DIM, (head + 1) * HEAD_DIM)
                    to_ref[side * blocks_here + block, to_rows, :] = from_ref[rows, lanes]
    all_s_ref[0:blocks_here] = s_ref[...]
    all_s_ref[blocks_here:] = ps_ref[...]
    acc_ref[...] = jnp.zeros_like(acc_ref)
    dq_ref[...] = jnp.zeros_like(dq_ref)

    @pl.when(lax.axis_index("rep") == 0)
    def _():
        pairs_of_blocks(
            offsets_ref, ids_ref, kv_ref, own, base + blocks_here,
            (all_q_ref, all_g_ref, all_s_ref), blocks_here, acc_ref, dq_ref,
        )


def own_kernel(
    offsets_ref, ids_ref, kv_ref, q_ref, g_ref, s_ref, cross_ref, far_ref, acc_ref, dq_ref
):
    blocks_here = kv_ref.shape[0] // BLOCK
    _, _, own = places(blocks_here)
    acc_ref[...] = cross_ref[...]
    dq_ref[...] = far_ref[0:blocks_here]
    pairs_of_blocks(
        offsets_ref, ids_ref, kv_ref, own, own, (q_ref, g_ref, s_ref), 0, acc_ref, dq_ref
    )


def query_kernel(own_ref, partner_ref, dq_ref):
    def block_step(block, carry):
        total = own_ref[block] + partner_ref[block].astype(F32)
        rows = pl.ds(pl.multiple_of(block * BLOCK, BLOCK), BLOCK)
        for head in range(GROUP):
            lanes = slice(head * HEAD_DIM, (head + 1) * HEAD_DIM)
            dq_ref[rows, lanes] = total[:, lanes].T.astype(BF16)
        return carry

    lax.fori_loop(0, own_ref.shape[0], block_step, 0)


def final_kernel(last_sender, ids_ref, acc_ref, near_ref, *refs):
    far_refs, (dk_ref, dv_ref, sum_ref) = refs[:-3], refs[-3:]
    blocks_here = acc_ref.shape[0] // BLOCK
    chip_blocks = CORES * blocks_here
    chip = lax.axis_index("ctx")
    core = lax.axis_index("rep")
    sum_ref[...] = acc_ref[...] + near_ref[...].astype(F32)
    dk_ref[...] = keys_of(sum_ref, slice(None)).astype(BF16)
    dv_ref[...] = values_of(sum_ref, slice(None)).astype(BF16)
    capacity = far_refs[0].shape[0] // BLOCK
    for slot in range(SUMMARY):
        owner, rank = chip_slot(ids_ref, slot, chip_blocks)
        local = ids_ref[slot] - chip * chip_blocks - core * blocks_here
        mine = (owner == chip) & (local >= 0) & (local < blocks_here)

        @pl.when(mine & (chip <= last_sender) & (rank < capacity))
        def _():
            rows = pl.ds(pl.multiple_of(local * BLOCK, BLOCK), BLOCK)
            place = pl.ds(pl.multiple_of(rank * BLOCK, BLOCK), BLOCK)
            total = sum_ref[rows, :]
            for far_ref in far_refs:
                total += far_ref[place, :].astype(F32)
            dk_ref[rows, :] = total[:, 0:HEAD_DIM].astype(BF16)
            dv_ref[rows, :] = total[:, HEAD_DIM : 2 * HEAD_DIM].astype(BF16)


def call(kernel, scalars, arrays, out_shape, scratch=(), flops=0, in_space=VMEM, out_specs=None, room=24):
    return pl.pallas_call(
        kernel,
        out_shape=out_shape,
        in_specs=[SMEM] * len(scalars) + [in_space] * len(arrays),
        out_specs=out_specs or jax.tree.map(lambda _: VMEM, out_shape),
        scratch_shapes=list(scratch),
        compiler_params=pltpu.CompilerParams(vmem_limit_bytes=room << 20),
        cost_estimate=pl.CostEstimate(flops=flops, bytes_accessed=0, transcendentals=0),
    )(*scalars, *arrays)


def shape_of(shape, dtype):
    return jax.ShapeDtypeStruct(shape, dtype)


def with_capacity(
    capacity, chips, queries, kv, attn_out, grads, log_sums, window_offsets, summary_ids
):
    rows = queries.shape[0]
    blocks_here = rows // BLOCK
    swap = [(0, 1), (1, 0)]
    up = [(i, i + 1) for i in range(chips - 1)]
    down = [(b, a) for a, b in up]
    routes = far_rounds(chips)
    sources = tuple({b: a // CORES for a, b in route} for route in routes)
    both = ("ctx", "rep")

    kv_partner = lax.ppermute(kv, "rep", swap)
    kv_near = lax.ppermute(kv, "ctx", up)
    far_shape = shape_of((capacity * BLOCK, 2 * HEAD_DIM), BF16)
    picked = call(pick_kernel, (summary_ids,), (kv, kv_partner), far_shape)
    kv_far = [lax.ppermute(picked, both, route) for route in routes]
    queries, grads, attn_out, window_offsets, _ = lax.optimization_barrier(
        (queries, grads, attn_out, window_offsets, picked)
    )
    tables = (window_offsets, summary_ids)
    stats = call(
        prep_kernel, (), (attn_out, grads, log_sums),
        shape_of((blocks_here, 8, GROUP * BLOCK), F32), flops=5 * MICROSECOND,
    )
    own = (queries, grads, stats)
    every = own + tuple(lax.ppermute(x, "rep", swap) for x in own)
    acc_shape = (rows, 2 * HEAD_DIM)
    half_shape = (blocks_here, HEAD_DIM, GROUP * BLOCK)
    dq_shape = shape_of((CORES * blocks_here, *half_shape[1:]), F32)
    stacked_shape = shape_of((CORES * blocks_here, GROUP * BLOCK, HEAD_DIM), BF16)
    cross_acc, cross_dq, *every = call(
        cross_kernel, tables, (kv, *every),
        (
            shape_of(acc_shape, F32), shape_of(half_shape, F32), stacked_shape, stacked_shape,
            shape_of((CORES * blocks_here, *stats.shape[1:]), F32),
        ),
    )
    near_grads, near_dq = call(
        near_kernel, tables, (kv_near, *every, cross_dq), (shape_of(acc_shape, BF16), dq_shape),
        [pltpu.VMEM(acc_shape, F32)],
    )
    *far_grads, far_dq, dq_partner = call(
        functools.partial(far_kernel, sources), (summary_ids,), (*kv_far, *every, near_dq),
        (*[far_shape] * len(routes), dq_shape, shape_of(half_shape, BF16)),
        [pltpu.VMEM(far_shape.shape, F32)], flops=5 * MICROSECOND,
    )
    far_back = [
        lax.ppermute(x, both, [(b, a) for a, b in route]) for x, route in zip(far_grads, routes)
    ]
    near_back = lax.ppermute(near_grads, "ctx", down)
    dq_partner = lax.ppermute(dq_partner, "rep", swap)
    acc, dq = call(
        own_kernel, tables, (kv, *every, cross_acc, far_dq),
        (shape_of(acc_shape, F32), shape_of(half_shape, F32)), flops=OWN,
    )
    query_grads = call(query_kernel, (), (dq, dq_partner), shape_of(queries.shape, BF16))
    if capacity > 3:
        acc, near_back = lax.optimization_barrier((acc, near_back))
    far_back, acc, query_grads = lax.optimization_barrier((far_back, acc, query_grads))
    far_other = [lax.ppermute(x, "rep", swap) for x in far_back]
    kv_shape = shape_of((rows, HEAD_DIM), BF16)
    key_grads, value_grads = call(
        functools.partial(final_kernel, chips - 3), (summary_ids,),
        (acc, near_back, *far_back, *far_other), (kv_shape, kv_shape),
        [pltpu.VMEM(acc_shape, F32)],
    )
    return query_grads, key_grads, value_grads


def capacities(chips):
    return CAPACITIES if len(far_rounds(chips)) == 1 else CAPACITIES[-1:]


def per_device(chips, queries, keys, values, attn_out, grads, log_sums, window_offsets, summary_ids):
    kv, branch = call(
        functools.partial(start_kernel, chips), (), (summary_ids, keys, values),
        (shape_of((keys.shape[0], 2 * HEAD_DIM), BF16), shape_of((1,), jnp.int32)),
        [pltpu.SMEM(summary_ids.shape, jnp.int32), pltpu.SemaphoreType.DMA((3,))], in_space=HBM, out_specs=(VMEM, SMEM), room=60,
    )
    branches = [functools.partial(with_capacity, limit, chips) for limit in capacities(chips)]
    operands = (queries, kv, attn_out, grads, log_sums, window_offsets.T, summary_ids)
    return lax.switch(branch[0], branches, *operands) if len(branches) > 1 else branches[0](*operands)


def solution(mesh):
    rows = P(("groups", "ctx", "rep"), "heads")
    return jax.shard_map(
        functools.partial(per_device, mesh.shape["ctx"]),
        mesh=mesh,
        in_specs=(rows,) * 5 + (P("heads", ("groups", "ctx", "rep")), P("groups", None), P("groups")),
        out_specs=(rows,) * 3,
        check_vma=False,
    )
```

```python
import functools
import math

import jax
import jax.numpy as jnp
from jax import lax
from jax.experimental import pallas as pl
from jax.experimental.pallas import tpu as pltpu
from jax.sharding import PartitionSpec as P

HEAD_DIM = 128
GROUP = 4
BLOCK = 128
REACH = 3
SUMMARY = 8
CORES = 2
SCALE = HEAD_DIM ** (-0.5)
LOG2E = math.log2(math.e)
MICROSECOND = 1_000_000_000
OWN = 10 * MICROSECOND
CAPACITIES = ((2, 2), (3, 2), (4, 3), (SUMMARY - 1, 4))
F32 = jnp.float32
BF16 = jnp.bfloat16
VMEM = pl.BlockSpec(memory_space=pltpu.VMEM)
SMEM = pl.BlockSpec(memory_space=pltpu.SMEM)
HBM = pl.BlockSpec(memory_space=pltpu.HBM)


def far_rounds(chips):
    rounds = []
    for source in range(chips):
        for target in range(source + 2, chips):
            wanted = target % CORES
            better = (source + target + 1) % CORES
            for route in rounds:
                senders = [core for core in range(CORES) if source * CORES + core not in route.values()]
                receivers = [core for core in range(CORES) if target * CORES + core not in route]
                if senders and receivers:
                    break
            else:
                senders, receivers, route = list(range(CORES)), list(range(CORES)), {}
                rounds.append(route)
            sender = wanted if wanted in senders else senders[0]
            receiver = better if better in receivers else receivers[0]
            route[target * CORES + receiver] = source * CORES + sender
    return [[(a, b) for b, a in route.items()] for route in rounds]


def table_entry(table, position):
    value = jnp.int32(-1)
    for place, entry in table.items():
        value = jnp.where(position == place, jnp.int32(entry), value)
    return value


def summary_count(ids_ref, first, blocks):
    count = jnp.int32(0)
    for slot in range(SUMMARY):
        count += jnp.where((ids_ref[slot] >= first) & (ids_ref[slot] < first + blocks), 1, 0)
    return count


def prep_kernel(out_ref, grad_ref, lse_ref, stats_ref):
    stats_ref[...] = jnp.zeros_like(stats_ref)
    for block in range(stats_ref.shape[0]):
        rows = slice(block * BLOCK, (block + 1) * BLOCK)
        for head in range(GROUP):
            columns = slice(head * HEAD_DIM, (head + 1) * HEAD_DIM)
            product = out_ref[rows, columns].astype(F32) * grad_ref[rows, columns].astype(F32)
            stats_ref[block, 0:1, columns] = lse_ref[head : head + 1, rows] * LOG2E
            stats_ref[block, 1:2, columns] = jnp.sum(product.T, axis=0, keepdims=True)


def start_kernel(chips, ids_hbm, key_ref, value_ref, kv_ref, branch_ref, ids_ref, sems):
    chip_blocks = CORES * (key_ref.shape[0] // BLOCK)
    copies = [
        pltpu.make_async_copy(
            ref, kv_ref.at[:, number * HEAD_DIM : (number + 1) * HEAD_DIM], sems.at[number]
        )
        for number, ref in enumerate((key_ref, value_ref))
    ]
    ids_copy = pltpu.make_async_copy(ids_hbm, ids_ref, sems.at[2])
    ids_copy.start()
    for copy in copies:
        copy.start()
    ids_copy.wait()
    far_most = near_most = jnp.int32(0)
    for chip in range(chips - 1):
        first = chip * chip_blocks
        near_most = jnp.maximum(near_most, summary_count(ids_ref, first, chip_blocks // CORES))
        if chip < chips - 2:
            far_most = jnp.maximum(far_most, summary_count(ids_ref, first, chip_blocks))
    branch = jnp.int32(0)
    for far_slots, near_slots in capacities(chips)[:-1]:
        branch += jnp.where((far_most > far_slots) | (near_most > near_slots), 1, 0)
    branch_ref[0] = branch
    for copy in copies:
        copy.wait()


def core_slot(ids_ref, slot, first, blocks):
    def inside(other):
        return (ids_ref[other] >= first) & (ids_ref[other] < first + blocks)

    rank = jnp.int32(0)
    for other in range(SUMMARY):
        rank += jnp.where(inside(other) & (other < slot), 1, 0)
    return inside(slot), rank


def block_rows(number):
    return pl.ds(pl.multiple_of(number * BLOCK, BLOCK), BLOCK)


def pick_kernel(ids_ref, own_ref, partner_ref, far_ref, near_ref):
    blocks_here = own_ref.shape[0] // BLOCK
    _, base, own = places(blocks_here)
    far_ref[...] = jnp.zeros_like(far_ref)
    near_ref[...] = jnp.zeros_like(near_ref)

    def slot_step(slot, carry):
        of_chip, chip_rank = core_slot(ids_ref, slot, base, CORES * blocks_here)
        of_core, core_rank = core_slot(ids_ref, slot, own, blocks_here)
        row = block_rows(lax.rem(ids_ref[slot], blocks_here))

        @pl.when(of_chip & (chip_rank < far_ref.shape[0] // BLOCK))
        def _():
            far_ref[block_rows(chip_rank), :] = jnp.where(
                of_core, own_ref[row, :], partner_ref[row, :]
            )

        @pl.when(of_core & (core_rank < near_ref.shape[0] // BLOCK))
        def _():
            near_ref[block_rows(core_rank), :] = own_ref[row, :]

        return carry

    lax.fori_loop(0, SUMMARY, slot_step, 0)


def nt(a, b):
    return lax.dot_general(a, b, (((1,), (1,)), ((), ())), preferred_element_type=F32)


def nn(a, b):
    return jnp.dot(a, b, preferred_element_type=F32)


def block_grads(keys, values, key_t, query_refs, first, count=1, biases=None, reach=None):
    query_ref, grad_ref, stats_ref = query_refs
    numbers = [first + step for step in range(count)]
    queries = jnp.concatenate([query_ref[number] for number in numbers], axis=0)
    grads = jnp.concatenate([grad_ref[number] for number in numbers], axis=0)
    log_sums = [stats_ref[number, 0:1, :] for number in numbers]
    deltas = jnp.concatenate([stats_ref[number, 1:2, :] for number in numbers], axis=1)
    scores = nt(keys, queries) * (SCALE * LOG2E)
    if biases is None:
        probs = jnp.exp2(scores - jnp.concatenate(log_sums, axis=1))
    else:
        if reach is not None:
            shape = (BLOCK, queries.shape[0])
            column = lax.broadcasted_iota(jnp.int32, shape, 1)
            ahead = column // (GROUP * BLOCK) * BLOCK + column % BLOCK
            ahead -= lax.broadcasted_iota(jnp.int32, shape, 0)
        parts = []
        for key, row in enumerate(biases):
            shift = jnp.concatenate([a + bias for a, bias in zip(log_sums, row)], axis=1)
            part = jnp.exp2(scores[key * BLOCK : (key + 1) * BLOCK] - shift)
            if reach is not None:
                part = jnp.where(ahead >= reach + key * BLOCK, part, 0.0)
            parts.append(part)
        probs = jnp.concatenate(parts, axis=0)
    prob_grads = nt(values, grads)
    score_grads = (probs * (prob_grads - deltas) * SCALE).astype(BF16)
    return nn(key_t, score_grads), nn(score_grads, queries), nn(probs.astype(BF16), grads)


def put_queries(to_ref, from_ref, first, dq):
    width = GROUP * BLOCK
    for step in range(dq.shape[1] // width):
        part = dq[:, step * width : (step + 1) * width]
        to_ref[first + step] = from_ref[first + step] + part


def is_summary(ids_ref, key_block):
    found = ids_ref[0] == key_block
    for slot in range(1, SUMMARY):
        found |= ids_ref[slot] == key_block
    return found


def in_window(offsets_ref, query_block, key_block):
    distance = query_block - key_block
    return (distance == offsets_ref[0, query_block]) | (distance == offsets_ref[1, query_block])


def attends(offsets_ref, ids_ref, query_block, key_block):
    chosen = in_window(offsets_ref, query_block, key_block) | is_summary(ids_ref, key_block)
    return (query_block > key_block) & chosen


def keys_of(kv_ref, rows):
    return kv_ref[rows, 0:HEAD_DIM]


def values_of(kv_ref, rows):
    return kv_ref[rows, HEAD_DIM : 2 * HEAD_DIM]


def transposed(keys):
    return keys.astype(F32).T.astype(BF16)


def add_grads(acc_ref, rows, key_part, value_part):
    acc_ref[rows, 0:HEAD_DIM] += key_part
    acc_ref[rows, HEAD_DIM : 2 * HEAD_DIM] += value_part


def places(blocks_here):
    chip = lax.axis_index("ctx")
    base = chip * CORES * blocks_here
    return chip, base, base + lax.axis_index("rep") * blocks_here


def bias_of(flag):
    return jnp.where(flag, 0.0, 1e30).astype(F32)


def near_kernel(
    offsets_ref, ids_ref, blocks_ref, slots_ref, q_ref, g_ref, s_ref, cross_ref,
    block_grads_ref, slot_grads_ref, dq_ref, acc_ref, kv_ref,
):
    query_refs = (q_ref, g_ref, s_ref)
    blocks_here = blocks_ref.shape[0] // BLOCK
    chip_blocks = CORES * blocks_here
    chip, base, own = places(blocks_here)
    last_core = lax.axis_index("rep") == CORES - 1
    first_key = own - chip_blocks
    acc_ref[...] = jnp.zeros_like(acc_ref)
    dq_ref[0:blocks_here] = jnp.zeros_like(cross_ref)
    dq_ref[blocks_here:] = cross_ref[...]

    @pl.when(last_core)
    def _():
        kv_ref[...] = blocks_ref[...]

    @pl.when(~last_core)
    def _():
        kv_ref[0 : slots_ref.shape[0], :] = slots_ref[...]

    flags = [is_summary(ids_ref, first_key + key) & (chip > 0) for key in range(blocks_here)]
    count = jnp.int32(0)
    chosen = [jnp.int32(0)] * blocks_here
    for key in range(blocks_here):
        for place in range(key + 1):
            chosen[place] = jnp.where(flags[key] & (count == place), key, chosen[place])
        count += jnp.where(flags[key], 1, 0)
    chosen = [jnp.where(last_core, key, place) for place, key in enumerate(chosen)]

    def add(first, count, places_of_keys, biases=None):
        rows = [pl.ds(pl.multiple_of(key * BLOCK, BLOCK), BLOCK) for key in places_of_keys]
        keys = jnp.concatenate([keys_of(kv_ref, row) for row in rows], axis=0)
        values = jnp.concatenate([values_of(kv_ref, row) for row in rows], axis=0)
        dq, dk, dv = block_grads(keys, values, transposed(keys), query_refs, first, count, biases)
        put_queries(dq_ref, dq_ref, first, dq)
        for place, row in enumerate(rows):
            part = slice(place * BLOCK, (place + 1) * BLOCK)
            add_grads(acc_ref, row, dk[part], dv[part])

    def entry(place):
        key = jnp.int32(0)
        for number in range(blocks_here):
            key = jnp.where(place == number, chosen[number], key)
        return key

    odd = lax.rem(count, 2)

    def single_step(item, carry):
        add(item * 4, 4, [chosen[0]])
        return carry

    lax.fori_loop(0, odd * (chip_blocks // 4), single_step, 0)

    def double_step(item, carry):
        turn = odd + 2 * (item // (chip_blocks // 2))
        add(lax.rem(item, chip_blocks // 2) * 2, 2, [entry(turn), entry(turn + 1)])
        return carry

    lax.fori_loop(0, (count // 2) * (chip_blocks // 2), double_step, 0)

    def window_step(number, carry):
        query = base + number
        keys, wanted = [], []
        for place in range(2):
            key = query - offsets_ref[place, query] - first_key
            fits = (key >= 0) & (key < blocks_here)
            key = jnp.where(fits, key, 0)
            for block in range(blocks_here):
                fits &= (key != block) | ~flags[block]
            keys.append(key)
            wanted.append(fits)

        @pl.when(wanted[0] | wanted[1])
        def _():
            add(number + blocks_here, 1, keys, [[bias_of(flag)] for flag in wanted])

        return carry

    reaches = (chip > 0) & last_core
    lax.fori_loop(0, jnp.where(reaches, min(REACH, blocks_here), 0), window_step, 0)
    block_grads_ref[...] = acc_ref[...].astype(BF16)
    slot_grads_ref[...] = acc_ref[0 : slot_grads_ref.shape[0], :].astype(BF16)


def far_kernel(sources, ids_ref, *refs):
    count = len(sources)
    kv_refs, refs = refs[:count], refs[count:]
    query_refs, near_ref, refs = refs[:3], refs[3], refs[4:]
    grads_refs, (dq_ref, partner_ref, acc_ref) = refs[:count], refs[count:]
    chip_blocks = near_ref.shape[0]
    position = lax.axis_index("ctx") * CORES + lax.axis_index("rep")
    capacity = acc_ref.shape[0] // BLOCK
    together = 4 if capacity < 4 else 2 if capacity == 4 else 1
    if count > 1:
        dq_ref[...] = near_ref[...]
        near_ref = dq_ref
    for table, kv_ref, grads_ref in zip(sources, kv_refs, grads_refs):
        first = table_entry(table, position) * chip_blocks
        held = summary_count(ids_ref, first, chip_blocks)

        @pl.when(held > 0)
        def _():
            keys, values = keys_of(kv_ref, slice(None)), values_of(kv_ref, slice(None))
            key_t = transposed(keys)
            acc_ref[...] = jnp.zeros_like(acc_ref)

            def query_step(item, carry):
                first = item * together
                dq, dk, dv = block_grads(keys, values, key_t, query_refs, first, together)
                put_queries(dq_ref, near_ref, first, dq)
                add_grads(acc_ref, slice(None), dk, dv)
                return carry

            lax.fori_loop(0, chip_blocks // together, query_step, 0)
            grads_ref[...] = acc_ref[...].astype(BF16)

        @pl.when(held == 0)
        def _():
            grads_ref[...] = jnp.zeros_like(grads_ref)
            if count == 1:
                dq_ref[...] = near_ref[...]

    partner_ref[...] = dq_ref[chip_blocks // CORES :].astype(BF16)


def pairs_of_blocks(
    offsets_ref, ids_ref, kv_ref, first_key, first_query, query_refs, first_number, acc_ref, dq_ref
):
    blocks_here = kv_ref.shape[0] // BLOCK
    keys, values = keys_of(kv_ref, slice(None)), values_of(kv_ref, slice(None))
    key_t = transposed(keys)

    def step(number, carry):
        query = first_query + number
        flags = [
            attends(offsets_ref, ids_ref, query, first_key + key) | (first_key + key == query)
            for key in range(blocks_here)
        ]
        some = flags[0]
        for flag in flags[1:]:
            some |= flag

        @pl.when(some)
        def _():
            dq, dk, dv = block_grads(
                keys, values, key_t, query_refs, first_number + number, 1,
                [[bias_of(flag)] for flag in flags],
                (first_key - query) * BLOCK if first_number == 0 else None,
            )
            put_queries(dq_ref, dq_ref, number, dq)
            add_grads(acc_ref, slice(None), dk, dv)

        return carry

    lax.fori_loop(0, blocks_here, step, 0)


def cross_kernel(
    offsets_ref, ids_ref, kv_ref, q_ref, g_ref, s_ref, pq_ref, pg_ref, ps_ref,
    acc_ref, dq_ref, all_q_ref, all_g_ref, all_s_ref,
):
    blocks_here = kv_ref.shape[0] // BLOCK
    _, base, own = places(blocks_here)
    for from_refs, to_ref in (((q_ref, pq_ref), all_q_ref), ((g_ref, pg_ref), all_g_ref)):
        for side, from_ref in enumerate(from_refs):
            for block in range(blocks_here):
                rows = slice(block * BLOCK, (block + 1) * BLOCK)
                for head in range(GROUP):
                    to_rows = slice(head * BLOCK, (head + 1) * BLOCK)
                    lanes = slice(head * HEAD_DIM, (head + 1) * HEAD_DIM)
                    to_ref[side * blocks_here + block, to_rows, :] = from_ref[rows, lanes]
    all_s_ref[0:blocks_here] = s_ref[...]
    all_s_ref[blocks_here:] = ps_ref[...]
    acc_ref[...] = jnp.zeros_like(acc_ref)
    dq_ref[...] = jnp.zeros_like(dq_ref)

    @pl.when(lax.axis_index("rep") == 0)
    def _():
        pairs_of_blocks(
            offsets_ref, ids_ref, kv_ref, own, base + blocks_here,
            (all_q_ref, all_g_ref, all_s_ref), blocks_here, acc_ref, dq_ref,
        )


def own_kernel(
    offsets_ref, ids_ref, kv_ref, q_ref, g_ref, s_ref, cross_ref, far_ref, acc_ref, dq_ref
):
    blocks_here = kv_ref.shape[0] // BLOCK
    _, _, own = places(blocks_here)
    acc_ref[...] = cross_ref[...]
    dq_ref[...] = far_ref[0:blocks_here]
    pairs_of_blocks(
        offsets_ref, ids_ref, kv_ref, own, own, (q_ref, g_ref, s_ref), 0, acc_ref, dq_ref
    )


def query_kernel(own_ref, partner_ref, dq_ref):
    def block_step(block, carry):
        total = own_ref[block] + partner_ref[block].astype(F32)
        rows = pl.ds(pl.multiple_of(block * BLOCK, BLOCK), BLOCK)
        for head in range(GROUP):
            lanes = slice(head * HEAD_DIM, (head + 1) * HEAD_DIM)
            dq_ref[rows, lanes] = total[:, lanes].T.astype(BF16)
        return carry

    lax.fori_loop(0, own_ref.shape[0], block_step, 0)


def final_kernel(last_sender, ids_ref, acc_ref, blocks_ref, slots_ref, *refs):
    far_refs, (dk_ref, dv_ref, sum_ref) = refs[:-3], refs[-3:]
    blocks_here = acc_ref.shape[0] // BLOCK
    chip, base, own = places(blocks_here)
    sum_ref[...] = acc_ref[...] + blocks_ref[...].astype(F32)
    first_core = lax.axis_index("rep") == 0

    def slot_step(slot, carry):
        _, chip_rank = core_slot(ids_ref, slot, base, CORES * blocks_here)
        of_core, core_rank = core_slot(ids_ref, slot, own, blocks_here)
        rows = block_rows(lax.rem(ids_ref[slot], blocks_here))

        @pl.when(of_core & first_core & (core_rank < slots_ref.shape[0] // BLOCK))
        def _():
            sum_ref[rows, :] += slots_ref[block_rows(core_rank), :].astype(F32)

        @pl.when(of_core & (chip <= last_sender) & (chip_rank < far_refs[0].shape[0] // BLOCK))
        def _():
            for far_ref in far_refs:
                sum_ref[rows, :] += far_ref[block_rows(chip_rank), :].astype(F32)

        return carry

    lax.fori_loop(0, SUMMARY, slot_step, 0)
    dk_ref[...] = keys_of(sum_ref, slice(None)).astype(BF16)
    dv_ref[...] = values_of(sum_ref, slice(None)).astype(BF16)


def call(kernel, scalars, arrays, out_shape, scratch=(), flops=0, in_space=VMEM, out_specs=None, room=24):
    return pl.pallas_call(
        kernel,
        out_shape=out_shape,
        in_specs=[SMEM] * len(scalars) + [in_space] * len(arrays),
        out_specs=out_specs or jax.tree.map(lambda _: VMEM, out_shape),
        scratch_shapes=list(scratch),
        compiler_params=pltpu.CompilerParams(vmem_limit_bytes=room << 20),
        cost_estimate=pl.CostEstimate(flops=flops, bytes_accessed=0, transcendentals=0),
    )(*scalars, *arrays)


def shape_of(shape, dtype):
    return jax.ShapeDtypeStruct(shape, dtype)


def with_capacity(
    slots, chips, queries, kv, attn_out, grads, log_sums, window_offsets, summary_ids
):
    rows = queries.shape[0]
    blocks_here = rows // BLOCK
    swap = [(0, 1), (1, 0)]
    up_first, up_last = (
        [(i * CORES + core, (i + 1) * CORES + core) for i in range(chips - 1)]
        for core in (0, CORES - 1)
    )
    down_first, down_last = ([(b, a) for a, b in route] for route in (up_first, up_last))
    routes = far_rounds(chips)
    sources = tuple({b: a // CORES for a, b in route} for route in routes)
    both = ("ctx", "rep")

    kv_partner = lax.ppermute(kv, "rep", swap)
    near_blocks = lax.ppermute(kv, both, up_last)
    far_shape, slots_shape = (shape_of((slot * BLOCK, 2 * HEAD_DIM), BF16) for slot in slots)
    picked, near_slots = call(
        pick_kernel, (summary_ids,), (kv, kv_partner), (far_shape, slots_shape)
    )
    near_slots = lax.ppermute(near_slots, both, up_first)
    kv_far = [lax.ppermute(picked, both, route) for route in routes]
    queries, grads, attn_out, window_offsets, _ = lax.optimization_barrier(
        (queries, grads, attn_out, window_offsets, picked)
    )
    tables = (window_offsets, summary_ids)
    stats = call(
        prep_kernel, (), (attn_out, grads, log_sums),
        shape_of((blocks_here, 8, GROUP * BLOCK), F32), flops=10 * MICROSECOND,
    )
    partner_queries, partner_grads = (lax.ppermute(x, "rep", swap) for x in (queries, grads))
    stats, partner_queries, partner_grads = lax.optimization_barrier(
        (stats, partner_queries, partner_grads)
    )
    every = (queries, grads, stats, partner_queries, partner_grads, lax.ppermute(stats, "rep", swap))
    acc_shape = (rows, 2 * HEAD_DIM)
    half_shape = (blocks_here, HEAD_DIM, GROUP * BLOCK)
    dq_shape = shape_of((CORES * blocks_here, *half_shape[1:]), F32)
    stacked_shape = shape_of((CORES * blocks_here, GROUP * BLOCK, HEAD_DIM), BF16)
    cross_acc, cross_dq, *every = call(
        cross_kernel, tables, (kv, *every),
        (
            shape_of(acc_shape, F32), shape_of(half_shape, F32), stacked_shape, stacked_shape,
            shape_of((CORES * blocks_here, *stats.shape[1:]), F32),
        ),
    )
    block_part, slot_part, near_dq = call(
        near_kernel, tables, (near_blocks, near_slots, *every, cross_dq),
        (shape_of(acc_shape, BF16), slots_shape, dq_shape),
        [pltpu.VMEM(acc_shape, F32), pltpu.VMEM(acc_shape, BF16)],
    )
    *far_grads, far_dq, dq_partner = call(
        functools.partial(far_kernel, sources), (summary_ids,), (*kv_far, *every, near_dq),
        (*[far_shape] * len(routes), dq_shape, shape_of(half_shape, BF16)),
        [pltpu.VMEM(far_shape.shape, F32)], flops=5 * MICROSECOND,
    )
    far_back = [
        lax.ppermute(x, both, [(b, a) for a, b in route]) for x, route in zip(far_grads, routes)
    ]
    block_part, slot_part, _ = lax.optimization_barrier((block_part, slot_part, far_grads))
    block_part = lax.ppermute(block_part, both, down_last)
    slot_part = lax.ppermute(slot_part, both, down_first)
    dq_partner = lax.ppermute(dq_partner, "rep", swap)
    acc, dq = call(
        own_kernel, tables, (kv, *every, cross_acc, far_dq),
        (shape_of(acc_shape, F32), shape_of(half_shape, F32)), flops=OWN,
    )
    query_grads = call(query_kernel, (), (dq, dq_partner), shape_of(queries.shape, BF16))
    if slots[0] > 2:
        acc, slot_part = lax.optimization_barrier((acc, slot_part))
    if slots[0] > 3:
        acc, block_part = lax.optimization_barrier((acc, block_part))
    far_back, acc, query_grads = lax.optimization_barrier((far_back, acc, query_grads))
    far_other = [lax.ppermute(x, "rep", swap) for x in far_back]
    kv_shape = shape_of((rows, HEAD_DIM), BF16)
    key_grads, value_grads = call(
        functools.partial(final_kernel, chips - 3), (summary_ids,),
        (acc, block_part, slot_part, *far_back, *far_other), (kv_shape, kv_shape),
        [pltpu.VMEM(acc_shape, F32)],
    )
    return query_grads, key_grads, value_grads


def capacities(chips):
    return CAPACITIES if len(far_rounds(chips)) == 1 else CAPACITIES[-1:]


def per_device(chips, queries, keys, values, attn_out, grads, log_sums, window_offsets, summary_ids):
    kv, branch = call(
        functools.partial(start_kernel, chips), (), (summary_ids, keys, values),
        (shape_of((keys.shape[0], 2 * HEAD_DIM), BF16), shape_of((1,), jnp.int32)),
        [pltpu.SMEM(summary_ids.shape, jnp.int32), pltpu.SemaphoreType.DMA((3,))], in_space=HBM, out_specs=(VMEM, SMEM), room=60,
    )
    branches = [functools.partial(with_capacity, limit, chips) for limit in capacities(chips)]
    operands = (queries, kv, attn_out, grads, log_sums, window_offsets.T, summary_ids)
    return lax.switch(branch[0], branches, *operands) if len(branches) > 1 else branches[0](*operands)


def solution(mesh):
    rows = P(("groups", "ctx", "rep"), "heads")
    return jax.shard_map(
        functools.partial(per_device, mesh.shape["ctx"]),
        mesh=mesh,
        in_specs=(rows,) * 5 + (P("heads", ("groups", "ctx", "rep")), P("groups", None), P("groups")),
        out_specs=(rows,) * 3,
        check_vma=False,
    )
```

```python
import functools
import math

import jax
import jax.numpy as jnp
from jax import lax
from jax.experimental import pallas as pl
from jax.experimental.pallas import tpu as pltpu
from jax.sharding import PartitionSpec as P

HEAD_DIM = 128
GROUP = 4
BLOCK = 128
REACH = 3
SUMMARY = 8
CORES = 2
SCALE = HEAD_DIM ** (-0.5)
LOG2E = math.log2(math.e)
MICROSECOND = 1_000_000_000
OWN = 10 * MICROSECOND
CROSS = 10 * MICROSECOND
CAPACITIES = ((2, 2), (3, 2), (4, 3), (SUMMARY - 1, 4))
F32 = jnp.float32
BF16 = jnp.bfloat16
VMEM = pl.BlockSpec(memory_space=pltpu.VMEM)
SMEM = pl.BlockSpec(memory_space=pltpu.SMEM)
HBM = pl.BlockSpec(memory_space=pltpu.HBM)


def far_rounds(chips):
    rounds = []
    for source in range(chips):
        for target in range(source + 2, chips):
            wanted = (target - source) % CORES
            better = (target - source) % CORES
            for route in rounds:
                senders = [core for core in range(CORES) if source * CORES + core not in route.values()]
                receivers = [core for core in range(CORES) if target * CORES + core not in route]
                if senders and receivers:
                    break
            else:
                senders, receivers, route = list(range(CORES)), list(range(CORES)), {}
                rounds.append(route)
            sender = wanted if wanted in senders else senders[0]
            receiver = better if better in receivers else receivers[0]
            route[target * CORES + receiver] = source * CORES + sender
    return [[(a, b) for b, a in route.items()] for route in rounds]


def table_entry(table, position):
    value = jnp.int32(-1)
    for place, entry in table.items():
        value = jnp.where(position == place, jnp.int32(entry), value)
    return value


def summary_count(ids_ref, first, blocks):
    count = jnp.int32(0)
    for slot in range(SUMMARY):
        count += jnp.where((ids_ref[slot] >= first) & (ids_ref[slot] < first + blocks), 1, 0)
    return count


def prep_kernel(out_ref, grad_ref, lse_ref, stats_ref):
    stats_ref[...] = jnp.zeros_like(stats_ref)
    for block in range(stats_ref.shape[0]):
        rows = slice(block * BLOCK, (block + 1) * BLOCK)
        for head in range(GROUP):
            columns = slice(head * HEAD_DIM, (head + 1) * HEAD_DIM)
            product = out_ref[rows, columns].astype(F32) * grad_ref[rows, columns].astype(F32)
            stats_ref[block, 0:1, columns] = lse_ref[head : head + 1, rows] * LOG2E
            stats_ref[block, 1:2, columns] = jnp.sum(product.T, axis=0, keepdims=True)


def start_kernel(chips, ids_hbm, key_ref, value_ref, kv_ref, branch_ref, ids_ref, sems):
    chip_blocks = CORES * (key_ref.shape[0] // BLOCK)
    copies = [
        pltpu.make_async_copy(
            ref, kv_ref.at[:, number * HEAD_DIM : (number + 1) * HEAD_DIM], sems.at[number]
        )
        for number, ref in enumerate((key_ref, value_ref))
    ]
    ids_copy = pltpu.make_async_copy(ids_hbm, ids_ref, sems.at[2])
    ids_copy.start()
    for copy in copies:
        copy.start()
    ids_copy.wait()
    far_most = near_most = jnp.int32(0)
    for chip in range(chips - 1):
        first = chip * chip_blocks
        near_most = jnp.maximum(near_most, summary_count(ids_ref, first, chip_blocks // CORES))
        if chip < chips - 2:
            far_most = jnp.maximum(far_most, summary_count(ids_ref, first, chip_blocks))
    branch = jnp.int32(0)
    for far_slots, near_slots in capacities(chips)[:-1]:
        branch += jnp.where((far_most > far_slots) | (near_most > near_slots), 1, 0)
    branch_ref[0] = branch
    for copy in copies:
        copy.wait()


def core_slot(ids_ref, slot, first, blocks):
    def inside(other):
        return (ids_ref[other] >= first) & (ids_ref[other] < first + blocks)

    rank = jnp.int32(0)
    for other in range(SUMMARY):
        rank += jnp.where(inside(other) & (other < slot), 1, 0)
    return inside(slot), rank


def block_rows(number):
    return pl.ds(pl.multiple_of(number * BLOCK, BLOCK), BLOCK)


def pick_kernel(ids_ref, own_ref, partner_ref, far_ref, near_ref):
    blocks_here = own_ref.shape[0] // BLOCK
    _, base, own = places(blocks_here)
    far_ref[...] = jnp.zeros_like(far_ref)
    near_ref[...] = jnp.zeros_like(near_ref)

    def slot_step(slot, carry):
        of_chip, chip_rank = core_slot(ids_ref, slot, base, CORES * blocks_here)
        of_core, core_rank = core_slot(ids_ref, slot, own, blocks_here)
        row = block_rows(lax.rem(ids_ref[slot], blocks_here))

        @pl.when(of_chip & (chip_rank < far_ref.shape[0] // BLOCK))
        def _():
            far_ref[block_rows(chip_rank), :] = jnp.where(
                of_core, own_ref[row, :], partner_ref[row, :]
            )

        @pl.when(of_core & (core_rank < near_ref.shape[0] // BLOCK))
        def _():
            near_ref[block_rows(core_rank), :] = own_ref[row, :]

        return carry

    lax.fori_loop(0, SUMMARY, slot_step, 0)


def nt(a, b):
    return lax.dot_general(a, b, (((1,), (1,)), ((), ())), preferred_element_type=F32)


def nn(a, b):
    return jnp.dot(a, b, preferred_element_type=F32)


def block_grads(keys, values, key_t, query_refs, first, count=1, biases=None, reach=None):
    query_ref, grad_ref, stats_ref = query_refs
    numbers = [first + step for step in range(count)]
    queries = jnp.concatenate([query_ref[number] for number in numbers], axis=0)
    grads = jnp.concatenate([grad_ref[number] for number in numbers], axis=0)
    log_sums = [stats_ref[number, 0:1, :] for number in numbers]
    deltas = jnp.concatenate([stats_ref[number, 1:2, :] for number in numbers], axis=1)
    scores = nt(keys, queries) * (SCALE * LOG2E)
    if biases is None:
        probs = jnp.exp2(scores - jnp.concatenate(log_sums, axis=1))
    else:
        if reach is not None:
            shape = (BLOCK, queries.shape[0])
            column = lax.broadcasted_iota(jnp.int32, shape, 1)
            ahead = column // (GROUP * BLOCK) * BLOCK + column % BLOCK
            ahead -= lax.broadcasted_iota(jnp.int32, shape, 0)
        parts = []
        for key, row in enumerate(biases):
            shift = jnp.concatenate([a + bias for a, bias in zip(log_sums, row)], axis=1)
            part = jnp.exp2(scores[key * BLOCK : (key + 1) * BLOCK] - shift)
            if reach is not None:
                part = jnp.where(ahead >= reach + key * BLOCK, part, 0.0)
            parts.append(part)
        probs = jnp.concatenate(parts, axis=0)
    prob_grads = nt(values, grads)
    score_grads = (probs * (prob_grads - deltas) * SCALE).astype(BF16)
    return nn(key_t, score_grads), nn(score_grads, queries), nn(probs.astype(BF16), grads)


def put_queries(to_ref, from_ref, first, dq):
    width = GROUP * BLOCK
    for step in range(dq.shape[1] // width):
        part = dq[:, step * width : (step + 1) * width]
        to_ref[first + step] = from_ref[first + step] + part


def is_summary(ids_ref, key_block):
    found = ids_ref[0] == key_block
    for slot in range(1, SUMMARY):
        found |= ids_ref[slot] == key_block
    return found


def in_window(offsets_ref, query_block, key_block):
    distance = query_block - key_block
    return (distance == offsets_ref[0, query_block]) | (distance == offsets_ref[1, query_block])


def attends(offsets_ref, ids_ref, query_block, key_block):
    chosen = in_window(offsets_ref, query_block, key_block) | is_summary(ids_ref, key_block)
    return (query_block > key_block) & chosen


def keys_of(kv_ref, rows):
    return kv_ref[rows, 0:HEAD_DIM]


def values_of(kv_ref, rows):
    return kv_ref[rows, HEAD_DIM : 2 * HEAD_DIM]


def transposed(keys):
    return keys.astype(F32).T.astype(BF16)


def add_grads(acc_ref, rows, key_part, value_part):
    acc_ref[rows, 0:HEAD_DIM] += key_part
    acc_ref[rows, HEAD_DIM : 2 * HEAD_DIM] += value_part


def places(blocks_here):
    chip = lax.axis_index("ctx")
    base = chip * CORES * blocks_here
    return chip, base, base + lax.axis_index("rep") * blocks_here


def bias_of(flag):
    return jnp.where(flag, 0.0, 1e30).astype(F32)


def near_kernel(
    offsets_ref, ids_ref, blocks_ref, slots_ref, q_ref, g_ref, s_ref,
    block_grads_ref, slot_grads_ref, dq_ref, acc_ref, kv_ref,
):
    query_refs = (q_ref, g_ref, s_ref)
    blocks_here = blocks_ref.shape[0] // BLOCK
    chip_blocks = CORES * blocks_here
    chip, base, own = places(blocks_here)
    last_core = lax.axis_index("rep") == CORES - 1
    first_key = own - chip_blocks
    acc_ref[...] = jnp.zeros_like(acc_ref)
    dq_ref[...] = jnp.zeros_like(dq_ref)

    @pl.when(last_core)
    def _():
        kv_ref[...] = blocks_ref[...]

    @pl.when(~last_core)
    def _():
        kv_ref[0 : slots_ref.shape[0], :] = slots_ref[...]

    flags = [is_summary(ids_ref, first_key + key) & (chip > 0) for key in range(blocks_here)]
    count = jnp.int32(0)
    chosen = [jnp.int32(0)] * blocks_here
    for key in range(blocks_here):
        for place in range(key + 1):
            chosen[place] = jnp.where(flags[key] & (count == place), key, chosen[place])
        count += jnp.where(flags[key], 1, 0)
    chosen = [jnp.where(last_core, key, place) for place, key in enumerate(chosen)]

    def add(first, count, places_of_keys, biases=None):
        rows = [pl.ds(pl.multiple_of(key * BLOCK, BLOCK), BLOCK) for key in places_of_keys]
        keys = jnp.concatenate([keys_of(kv_ref, row) for row in rows], axis=0)
        values = jnp.concatenate([values_of(kv_ref, row) for row in rows], axis=0)
        dq, dk, dv = block_grads(keys, values, transposed(keys), query_refs, first, count, biases)
        put_queries(dq_ref, dq_ref, first, dq)
        for place, row in enumerate(rows):
            part = slice(place * BLOCK, (place + 1) * BLOCK)
            add_grads(acc_ref, row, dk[part], dv[part])

    def entry(place):
        key = jnp.int32(0)
        for number in range(blocks_here):
            key = jnp.where(place == number, chosen[number], key)
        return key

    odd = lax.rem(count, 2)

    def single_step(item, carry):
        add(item * 4, 4, [chosen[0]])
        return carry

    lax.fori_loop(0, odd * (chip_blocks // 4), single_step, 0)

    def double_step(item, carry):
        turn = odd + 2 * (item // (chip_blocks // 2))
        add(lax.rem(item, chip_blocks // 2) * 2, 2, [entry(turn), entry(turn + 1)])
        return carry

    lax.fori_loop(0, (count // 2) * (chip_blocks // 2), double_step, 0)

    def window_step(number, carry):
        query = base + number
        keys, wanted = [], []
        for place in range(2):
            key = query - offsets_ref[place, query] - first_key
            fits = (key >= 0) & (key < blocks_here)
            key = jnp.where(fits, key, 0)
            for block in range(blocks_here):
                fits &= (key != block) | ~flags[block]
            keys.append(key)
            wanted.append(fits)

        @pl.when(wanted[0] | wanted[1])
        def _():
            add(number + blocks_here, 1, keys, [[bias_of(flag)] for flag in wanted])

        return carry

    reaches = (chip > 0) & last_core
    lax.fori_loop(0, jnp.where(reaches, min(REACH, blocks_here), 0), window_step, 0)
    block_grads_ref[...] = acc_ref[...].astype(BF16)
    slot_grads_ref[...] = acc_ref[0 : slot_grads_ref.shape[0], :].astype(BF16)


def far_kernel(sources, ids_ref, *refs):
    count = len(sources)
    kv_refs, refs = refs[:count], refs[count:]
    query_refs, near_ref, refs = refs[:3], refs[3], refs[4:]
    grads_refs, (dq_ref, acc_ref) = refs[:count], refs[count:]
    chip_blocks = near_ref.shape[0]
    position = lax.axis_index("ctx") * CORES + lax.axis_index("rep")
    capacity = acc_ref.shape[0] // BLOCK
    together = 4 if capacity < 4 else 2 if capacity == 4 else 1
    if count > 1:
        dq_ref[...] = near_ref[...]
        near_ref = dq_ref
    for table, kv_ref, grads_ref in zip(sources, kv_refs, grads_refs):
        first = table_entry(table, position) * chip_blocks
        held = summary_count(ids_ref, first, chip_blocks)

        @pl.when(held > 0)
        def _():
            keys, values = keys_of(kv_ref, slice(None)), values_of(kv_ref, slice(None))
            key_t = transposed(keys)
            acc_ref[...] = jnp.zeros_like(acc_ref)

            def query_step(item, carry):
                first = item * together
                dq, dk, dv = block_grads(keys, values, key_t, query_refs, first, together)
                put_queries(dq_ref, near_ref, first, dq)
                add_grads(acc_ref, slice(None), dk, dv)
                return carry

            lax.fori_loop(0, chip_blocks // together, query_step, 0)
            grads_ref[...] = acc_ref[...].astype(BF16)

        @pl.when(held == 0)
        def _():
            grads_ref[...] = jnp.zeros_like(grads_ref)
            if count == 1:
                dq_ref[...] = near_ref[...]


def pairs_of_blocks(
    offsets_ref, ids_ref, kv_ref, first_key, first_query, query_refs, first_number, acc_ref, dq_ref
):
    blocks_here = kv_ref.shape[0] // BLOCK
    keys, values = keys_of(kv_ref, slice(None)), values_of(kv_ref, slice(None))
    key_t = transposed(keys)

    def step(number, carry):
        query = first_query + number
        flags = [
            attends(offsets_ref, ids_ref, query, first_key + key) | (first_key + key == query)
            for key in range(blocks_here)
        ]
        some = flags[0]
        for flag in flags[1:]:
            some |= flag

        @pl.when(some)
        def _():
            dq, dk, dv = block_grads(
                keys, values, key_t, query_refs, first_number + number, 1,
                [[bias_of(flag)] for flag in flags],
                (first_key - query) * BLOCK if first_number == 0 else None,
            )
            put_queries(dq_ref, dq_ref, number, dq)
            add_grads(acc_ref, slice(None), dk, dv)

        return carry

    lax.fori_loop(0, blocks_here, step, 0)


def layout_kernel(q_ref, g_ref, s_ref, pq_ref, pg_ref, ps_ref, all_q_ref, all_g_ref, all_s_ref):
    blocks_here = s_ref.shape[0]
    for from_refs, to_ref in (((q_ref, pq_ref), all_q_ref), ((g_ref, pg_ref), all_g_ref)):
        for side, from_ref in enumerate(from_refs):
            for block in range(blocks_here):
                rows = slice(block * BLOCK, (block + 1) * BLOCK)
                for head in range(GROUP):
                    to_rows = slice(head * BLOCK, (head + 1) * BLOCK)
                    lanes = slice(head * HEAD_DIM, (head + 1) * HEAD_DIM)
                    to_ref[side * blocks_here + block, to_rows, :] = from_ref[rows, lanes]
    all_s_ref[0:blocks_here] = s_ref[...]
    all_s_ref[blocks_here:] = ps_ref[...]


def cross_kernel(
    offsets_ref, ids_ref, kv_ref, q_ref, g_ref, s_ref, far_ref, acc_ref, dq_ref, sum_ref
):
    blocks_here = kv_ref.shape[0] // BLOCK
    _, base, own = places(blocks_here)
    acc_ref[...] = jnp.zeros_like(acc_ref)
    sum_ref[...] = far_ref[blocks_here:]

    @pl.when(lax.axis_index("rep") == 0)
    def _():
        pairs_of_blocks(
            offsets_ref, ids_ref, kv_ref, own, base + blocks_here, (q_ref, g_ref, s_ref),
            blocks_here, acc_ref, sum_ref,
        )

    dq_ref[...] = sum_ref[...].astype(BF16)


def own_kernel(
    offsets_ref, ids_ref, kv_ref, q_ref, g_ref, s_ref, cross_ref, far_ref, acc_ref, dq_ref
):
    blocks_here = kv_ref.shape[0] // BLOCK
    _, _, own = places(blocks_here)
    acc_ref[...] = cross_ref[...]
    dq_ref[...] = far_ref[0:blocks_here]
    pairs_of_blocks(
        offsets_ref, ids_ref, kv_ref, own, own, (q_ref, g_ref, s_ref), 0, acc_ref, dq_ref
    )


def query_kernel(own_ref, partner_ref, dq_ref):
    def block_step(block, carry):
        total = own_ref[block] + partner_ref[block].astype(F32)
        rows = pl.ds(pl.multiple_of(block * BLOCK, BLOCK), BLOCK)
        for head in range(GROUP):
            lanes = slice(head * HEAD_DIM, (head + 1) * HEAD_DIM)
            dq_ref[rows, lanes] = total[:, lanes].T.astype(BF16)
        return carry

    lax.fori_loop(0, own_ref.shape[0], block_step, 0)


def final_kernel(last_sender, ids_ref, acc_ref, blocks_ref, slots_ref, *refs):
    far_refs, (dk_ref, dv_ref, sum_ref) = refs[:-3], refs[-3:]
    blocks_here = acc_ref.shape[0] // BLOCK
    chip, base, own = places(blocks_here)
    sum_ref[...] = acc_ref[...] + blocks_ref[...].astype(F32)
    first_core = lax.axis_index("rep") == 0

    def slot_step(slot, carry):
        _, chip_rank = core_slot(ids_ref, slot, base, CORES * blocks_here)
        of_core, core_rank = core_slot(ids_ref, slot, own, blocks_here)
        rows = block_rows(lax.rem(ids_ref[slot], blocks_here))

        @pl.when(of_core & first_core & (core_rank < slots_ref.shape[0] // BLOCK))
        def _():
            sum_ref[rows, :] += slots_ref[block_rows(core_rank), :].astype(F32)

        @pl.when(of_core & (chip <= last_sender) & (chip_rank < far_refs[0].shape[0] // BLOCK))
        def _():
            for far_ref in far_refs:
                sum_ref[rows, :] += far_ref[block_rows(chip_rank), :].astype(F32)

        return carry

    lax.fori_loop(0, SUMMARY, slot_step, 0)
    dk_ref[...] = keys_of(sum_ref, slice(None)).astype(BF16)
    dv_ref[...] = values_of(sum_ref, slice(None)).astype(BF16)


def call(kernel, scalars, arrays, out_shape, scratch=(), flops=0, in_space=VMEM, out_specs=None, room=24):
    return pl.pallas_call(
        kernel,
        out_shape=out_shape,
        in_specs=[SMEM] * len(scalars) + [in_space] * len(arrays),
        out_specs=out_specs or jax.tree.map(lambda _: VMEM, out_shape),
        scratch_shapes=list(scratch),
        compiler_params=pltpu.CompilerParams(vmem_limit_bytes=room << 20),
        cost_estimate=pl.CostEstimate(flops=flops, bytes_accessed=0, transcendentals=0),
    )(*scalars, *arrays)


def shape_of(shape, dtype):
    return jax.ShapeDtypeStruct(shape, dtype)


def with_capacity(
    slots, chips, queries, kv, attn_out, grads, log_sums, window_offsets, summary_ids
):
    rows = queries.shape[0]
    blocks_here = rows // BLOCK
    swap = [(0, 1), (1, 0)]
    up_first, up_last = (
        [(i * CORES + core, (i + 1) * CORES + core) for i in range(chips - 1)]
        for core in (0, CORES - 1)
    )
    down_first, down_last = ([(b, a) for a, b in route] for route in (up_first, up_last))
    routes = far_rounds(chips)
    sources = tuple({b: a // CORES for a, b in route} for route in routes)
    both = ("ctx", "rep")

    kv_partner = lax.ppermute(kv, "rep", swap)
    near_blocks = lax.ppermute(kv, both, up_last)
    far_shape, slots_shape = (shape_of((slot * BLOCK, 2 * HEAD_DIM), BF16) for slot in slots)
    picked, near_slots = call(
        pick_kernel, (summary_ids,), (kv, kv_partner), (far_shape, slots_shape)
    )
    near_slots = lax.ppermute(near_slots, both, up_first)
    kv_far = [lax.ppermute(picked, both, route) for route in routes]
    queries, grads, attn_out, window_offsets, _ = lax.optimization_barrier(
        (queries, grads, attn_out, window_offsets, picked)
    )
    tables = (window_offsets, summary_ids)
    stats = call(
        prep_kernel, (), (attn_out, grads, log_sums),
        shape_of((blocks_here, 8, GROUP * BLOCK), F32), flops=10 * MICROSECOND,
    )
    partner_queries, partner_grads = (lax.ppermute(x, "rep", swap) for x in (queries, grads))
    stats, partner_queries, partner_grads = lax.optimization_barrier(
        (stats, partner_queries, partner_grads)
    )
    every = (queries, grads, stats, partner_queries, partner_grads, lax.ppermute(stats, "rep", swap))
    acc_shape = (rows, 2 * HEAD_DIM)
    half_shape = (blocks_here, HEAD_DIM, GROUP * BLOCK)
    dq_shape = shape_of((CORES * blocks_here, *half_shape[1:]), F32)
    stacked_shape = shape_of((CORES * blocks_here, GROUP * BLOCK, HEAD_DIM), BF16)
    every = call(
        layout_kernel, (), every,
        (
            stacked_shape, stacked_shape,
            shape_of((CORES * blocks_here, *stats.shape[1:]), F32),
        ),
    )
    block_part, slot_part, near_dq = call(
        near_kernel, tables, (near_blocks, near_slots, *every),
        (shape_of(acc_shape, BF16), slots_shape, dq_shape),
        [pltpu.VMEM(acc_shape, F32), pltpu.VMEM(acc_shape, BF16)],
    )
    *far_grads, far_dq = call(
        functools.partial(far_kernel, sources), (summary_ids,), (*kv_far, *every, near_dq),
        (*[far_shape] * len(routes), dq_shape),
        [pltpu.VMEM(far_shape.shape, F32)], flops=5 * MICROSECOND,
    )
    far_back = [
        lax.ppermute(x, both, [(b, a) for a, b in route]) for x, route in zip(far_grads, routes)
    ]
    block_part, slot_part, _ = lax.optimization_barrier((block_part, slot_part, far_grads))
    block_part = lax.ppermute(block_part, both, down_last)
    slot_part = lax.ppermute(slot_part, both, down_first)
    cross_acc, dq_partner = call(
        cross_kernel, tables, (kv, *every, far_dq),
        (shape_of(acc_shape, F32), shape_of(half_shape, BF16)),
        [pltpu.VMEM(half_shape, F32)], flops=CROSS,
    )
    dq_partner = lax.ppermute(dq_partner, "rep", swap)
    acc, dq = call(
        own_kernel, tables, (kv, *every, cross_acc, far_dq),
        (shape_of(acc_shape, F32), shape_of(half_shape, F32)), flops=OWN,
    )
    query_grads = call(
        query_kernel, (), (dq, dq_partner), shape_of(queries.shape, BF16), flops=2 * MICROSECOND
    )
    if slots[0] > 2:
        acc, slot_part = lax.optimization_barrier((acc, slot_part))
    if slots[0] > 3:
        acc, block_part = lax.optimization_barrier((acc, block_part))
    far_back, acc = lax.optimization_barrier((far_back, acc))
    far_other = [lax.ppermute(x, "rep", swap) for x in far_back]
    acc, query_grads = lax.optimization_barrier((acc, query_grads))
    kv_shape = shape_of((rows, HEAD_DIM), BF16)
    key_grads, value_grads = call(
        functools.partial(final_kernel, chips - 3), (summary_ids,),
        (acc, block_part, slot_part, *far_back, *far_other), (kv_shape, kv_shape),
        [pltpu.VMEM(acc_shape, F32)],
    )
    return query_grads, key_grads, value_grads


def capacities(chips):
    return CAPACITIES if len(far_rounds(chips)) == 1 else CAPACITIES[-1:]


def per_device(chips, queries, keys, values, attn_out, grads, log_sums, window_offsets, summary_ids):
    kv, branch = call(
        functools.partial(start_kernel, chips), (), (summary_ids, keys, values),
        (shape_of((keys.shape[0], 2 * HEAD_DIM), BF16), shape_of((1,), jnp.int32)),
        [pltpu.SMEM(summary_ids.shape, jnp.int32), pltpu.SemaphoreType.DMA((3,))], in_space=HBM, out_specs=(VMEM, SMEM), room=60,
    )
    branches = [functools.partial(with_capacity, limit, chips) for limit in capacities(chips)]
    operands = (queries, kv, attn_out, grads, log_sums, window_offsets.T, summary_ids)
    return lax.switch(branch[0], branches, *operands) if len(branches) > 1 else branches[0](*operands)


def solution(mesh):
    rows = P(("groups", "ctx", "rep"), "heads")
    return jax.shard_map(
        functools.partial(per_device, mesh.shape["ctx"]),
        mesh=mesh,
        in_specs=(rows,) * 5 + (P("heads", ("groups", "ctx", "rep")), P("groups", None), P("groups")),
        out_specs=(rows,) * 3,
        check_vma=False,
    )
```

```python
import functools
import math

import jax
import jax.numpy as jnp
from jax import lax
from jax.experimental import pallas as pl
from jax.experimental.pallas import tpu as pltpu
from jax.sharding import PartitionSpec as P

HEAD_DIM = 128
GROUP = 4
BLOCK = 128
REACH = 3
SUMMARY = 8
CORES = 2
SCALE = HEAD_DIM ** (-0.5)
LOG2E = math.log2(math.e)
MICROSECOND = 1_000_000_000
TAIL = 20 * MICROSECOND
PIECES = 2
CAPACITIES = ((2, 2), (3, 2), (4, 3), (SUMMARY - 1, 4))
F32 = jnp.float32
BF16 = jnp.bfloat16
VMEM = pl.BlockSpec(memory_space=pltpu.VMEM)
SMEM = pl.BlockSpec(memory_space=pltpu.SMEM)
HBM = pl.BlockSpec(memory_space=pltpu.HBM)


def far_rounds(chips):
    rounds = []
    for source in range(chips):
        for target in range(source + 2, chips):
            wanted = (target - source) % CORES
            better = (target - source) % CORES
            for route in rounds:
                senders = [core for core in range(CORES) if source * CORES + core not in route.values()]
                receivers = [core for core in range(CORES) if target * CORES + core not in route]
                if senders and receivers:
                    break
            else:
                senders, receivers, route = list(range(CORES)), list(range(CORES)), {}
                rounds.append(route)
            sender = wanted if wanted in senders else senders[0]
            receiver = better if better in receivers else receivers[0]
            route[target * CORES + receiver] = source * CORES + sender
    return [[(a, b) for b, a in route.items()] for route in rounds]


def table_entry(table, position):
    value = jnp.int32(-1)
    for place, entry in table.items():
        value = jnp.where(position == place, jnp.int32(entry), value)
    return value


def summary_count(ids_ref, first, blocks):
    count = jnp.int32(0)
    for slot in range(SUMMARY):
        count += jnp.where((ids_ref[slot] >= first) & (ids_ref[slot] < first + blocks), 1, 0)
    return count


def prep_kernel(out_ref, grad_ref, lse_ref, stats_ref):
    stats_ref[...] = jnp.zeros_like(stats_ref)
    for block in range(stats_ref.shape[0]):
        rows = slice(block * BLOCK, (block + 1) * BLOCK)
        for head in range(GROUP):
            columns = slice(head * HEAD_DIM, (head + 1) * HEAD_DIM)
            product = out_ref[rows, columns].astype(F32) * grad_ref[rows, columns].astype(F32)
            stats_ref[block, 0:1, columns] = lse_ref[head : head + 1, rows] * LOG2E
            stats_ref[block, 1:2, columns] = jnp.sum(product.T, axis=0, keepdims=True)


def start_kernel(chips, ids_hbm, key_ref, value_ref, kv_ref, branch_ref, ids_ref, sems):
    chip_blocks = CORES * (key_ref.shape[0] // BLOCK)
    copies = [
        pltpu.make_async_copy(
            ref, kv_ref.at[:, number * HEAD_DIM : (number + 1) * HEAD_DIM], sems.at[number]
        )
        for number, ref in enumerate((key_ref, value_ref))
    ]
    ids_copy = pltpu.make_async_copy(ids_hbm, ids_ref, sems.at[2])
    ids_copy.start()
    for copy in copies:
        copy.start()
    ids_copy.wait()
    far_most = near_most = jnp.int32(0)
    for chip in range(chips - 1):
        first = chip * chip_blocks
        near_most = jnp.maximum(near_most, summary_count(ids_ref, first, chip_blocks // CORES))
        if chip < chips - 2:
            far_most = jnp.maximum(far_most, summary_count(ids_ref, first, chip_blocks))
    branch = jnp.int32(0)
    for far_slots, near_slots in capacities(chips)[:-1]:
        branch += jnp.where((far_most > far_slots) | (near_most > near_slots), 1, 0)
    branch_ref[0] = branch
    for copy in copies:
        copy.wait()


def core_slot(ids_ref, slot, first, blocks):
    def inside(other):
        return (ids_ref[other] >= first) & (ids_ref[other] < first + blocks)

    rank = jnp.int32(0)
    for other in range(SUMMARY):
        rank += jnp.where(inside(other) & (other < slot), 1, 0)
    return inside(slot), rank


def block_rows(number):
    return pl.ds(pl.multiple_of(number * BLOCK, BLOCK), BLOCK)


def pick_kernel(ids_ref, own_ref, partner_ref, far_ref, near_ref):
    blocks_here = own_ref.shape[0] // BLOCK
    _, base, own = places(blocks_here)
    far_ref[...] = jnp.zeros_like(far_ref)
    near_ref[...] = jnp.zeros_like(near_ref)

    def slot_step(slot, carry):
        of_chip, chip_rank = core_slot(ids_ref, slot, base, CORES * blocks_here)
        of_core, core_rank = core_slot(ids_ref, slot, own, blocks_here)
        row = block_rows(lax.rem(ids_ref[slot], blocks_here))

        @pl.when(of_chip & (chip_rank < far_ref.shape[0] // BLOCK))
        def _():
            far_ref[block_rows(chip_rank), :] = jnp.where(
                of_core, own_ref[row, :], partner_ref[row, :]
            )

        @pl.when(of_core & (core_rank < near_ref.shape[0] // BLOCK))
        def _():
            near_ref[block_rows(core_rank), :] = own_ref[row, :]

        return carry

    lax.fori_loop(0, SUMMARY, slot_step, 0)


def nt(a, b):
    return lax.dot_general(a, b, (((1,), (1,)), ((), ())), preferred_element_type=F32)


def nn(a, b):
    return jnp.dot(a, b, preferred_element_type=F32)


def block_grads(keys, values, key_t, query_refs, first, count=1, biases=None, reach=None):
    query_ref, grad_ref, stats_ref = query_refs
    numbers = [first + step for step in range(count)]
    queries = jnp.concatenate([query_ref[number] for number in numbers], axis=0)
    grads = jnp.concatenate([grad_ref[number] for number in numbers], axis=0)
    log_sums = [stats_ref[number, 0:1, :] for number in numbers]
    deltas = jnp.concatenate([stats_ref[number, 1:2, :] for number in numbers], axis=1)
    scores = nt(keys, queries) * (SCALE * LOG2E)
    if biases is None:
        probs = jnp.exp2(scores - jnp.concatenate(log_sums, axis=1))
    else:
        if reach is not None:
            shape = (BLOCK, queries.shape[0])
            column = lax.broadcasted_iota(jnp.int32, shape, 1)
            ahead = (column & (BLOCK - 1)) - lax.broadcasted_iota(jnp.int32, shape, 0)
        parts = []
        for key, row in enumerate(biases):
            shift = jnp.concatenate([a + bias for a, bias in zip(log_sums, row)], axis=1)
            part = jnp.exp2(scores[key * BLOCK : (key + 1) * BLOCK] - shift)
            if reach is not None:
                part = jnp.where(ahead >= reach + key * BLOCK, part, 0.0)
            parts.append(part)
        probs = jnp.concatenate(parts, axis=0)
    prob_grads = nt(values, grads)
    score_grads = (probs * (prob_grads - deltas) * SCALE).astype(BF16)
    return nn(key_t, score_grads), nn(score_grads, queries), nn(probs.astype(BF16), grads)


def put_queries(to_ref, from_ref, first, dq):
    width = GROUP * BLOCK
    for step in range(dq.shape[1] // width):
        part = dq[:, step * width : (step + 1) * width]
        to_ref[first + step] = from_ref[first + step] + part


def is_summary(ids_ref, key_block):
    found = ids_ref[0] == key_block
    for slot in range(1, SUMMARY):
        found |= ids_ref[slot] == key_block
    return found


def in_window(offsets_ref, query_block, key_block):
    distance = query_block - key_block
    return (distance == offsets_ref[0, query_block]) | (distance == offsets_ref[1, query_block])


def attends(offsets_ref, ids_ref, query_block, key_block):
    chosen = in_window(offsets_ref, query_block, key_block) | is_summary(ids_ref, key_block)
    return (query_block > key_block) & chosen


def keys_of(kv_ref, rows):
    return kv_ref[rows, 0:HEAD_DIM]


def values_of(kv_ref, rows):
    return kv_ref[rows, HEAD_DIM : 2 * HEAD_DIM]


def transposed(keys):
    return keys.astype(F32).T.astype(BF16)


def add_grads(acc_ref, rows, key_part, value_part):
    acc_ref[rows, 0:HEAD_DIM] += key_part
    acc_ref[rows, HEAD_DIM : 2 * HEAD_DIM] += value_part


def places(blocks_here):
    chip = lax.axis_index("ctx")
    base = chip * CORES * blocks_here
    return chip, base, base + lax.axis_index("rep") * blocks_here


def bias_of(flag):
    return jnp.where(flag, 0.0, 1e30).astype(F32)


def near_kernel(
    offsets_ref, ids_ref, blocks_ref, slots_ref, q_ref, g_ref, s_ref,
    block_grads_ref, slot_grads_ref, dq_ref, acc_ref, kv_ref,
):
    query_refs = (q_ref, g_ref, s_ref)
    blocks_here = blocks_ref.shape[0] // BLOCK
    chip_blocks = CORES * blocks_here
    chip, base, own = places(blocks_here)
    last_core = lax.axis_index("rep") == CORES - 1
    first_key = own - chip_blocks
    acc_ref[...] = jnp.zeros_like(acc_ref)
    dq_ref[...] = jnp.zeros_like(dq_ref)

    @pl.when(last_core)
    def _():
        kv_ref[...] = blocks_ref[...]

    @pl.when(~last_core)
    def _():
        kv_ref[0 : slots_ref.shape[0], :] = slots_ref[...]

    flags = [is_summary(ids_ref, first_key + key) & (chip > 0) for key in range(blocks_here)]
    count = jnp.int32(0)
    chosen = [jnp.int32(0)] * blocks_here
    for key in range(blocks_here):
        for place in range(key + 1):
            chosen[place] = jnp.where(flags[key] & (count == place), key, chosen[place])
        count += jnp.where(flags[key], 1, 0)
    chosen = [jnp.where(last_core, key, place) for place, key in enumerate(chosen)]

    def add(first, count, places_of_keys, biases=None):
        rows = [pl.ds(pl.multiple_of(key * BLOCK, BLOCK), BLOCK) for key in places_of_keys]
        keys = jnp.concatenate([keys_of(kv_ref, row) for row in rows], axis=0)
        values = jnp.concatenate([values_of(kv_ref, row) for row in rows], axis=0)
        dq, dk, dv = block_grads(keys, values, transposed(keys), query_refs, first, count, biases)
        put_queries(dq_ref, dq_ref, first, dq)
        for place, row in enumerate(rows):
            part = slice(place * BLOCK, (place + 1) * BLOCK)
            add_grads(acc_ref, row, dk[part], dv[part])

    def entry(place):
        key = jnp.int32(0)
        for number in range(blocks_here):
            key = jnp.where(place == number, chosen[number], key)
        return key

    odd = lax.rem(count, 2)

    def single_step(item, carry):
        add(item * 4, 4, [chosen[0]])
        return carry

    lax.fori_loop(0, odd * (chip_blocks // 4), single_step, 0)

    def double_step(item, carry):
        turn = odd + 2 * (item // (chip_blocks // 2))
        add(lax.rem(item, chip_blocks // 2) * 2, 2, [entry(turn), entry(turn + 1)])
        return carry

    lax.fori_loop(0, (count // 2) * (chip_blocks // 2), double_step, 0)

    def window_step(number, carry):
        query = base + number
        keys, wanted = [], []
        for place in range(2):
            key = query - offsets_ref[place, query] - first_key
            fits = (key >= 0) & (key < blocks_here)
            key = jnp.where(fits, key, 0)
            for block in range(blocks_here):
                fits &= (key != block) | ~flags[block]
            keys.append(key)
            wanted.append(fits)

        @pl.when(wanted[0] | wanted[1])
        def _():
            add(number + blocks_here, 1, keys, [[bias_of(flag)] for flag in wanted])

        return carry

    reaches = (chip > 0) & last_core
    lax.fori_loop(0, jnp.where(reaches, min(REACH, blocks_here), 0), window_step, 0)
    block_grads_ref[...] = acc_ref[...].astype(BF16)
    slot_grads_ref[...] = acc_ref[0 : slot_grads_ref.shape[0], :].astype(BF16)


def far_kernel(sources, ids_ref, *refs):
    count = len(sources)
    kv_refs, refs = refs[:count], refs[count:]
    query_refs, near_ref, refs = refs[:3], refs[3], refs[4:]
    grads_refs, (dq_ref, acc_ref) = refs[:count], refs[count:]
    chip_blocks = near_ref.shape[0]
    position = lax.axis_index("ctx") * CORES + lax.axis_index("rep")
    capacity = acc_ref.shape[0] // BLOCK
    together = 4 if capacity < 4 else 2 if capacity == 4 else 1
    if count > 1:
        dq_ref[...] = near_ref[...]
        near_ref = dq_ref
    for table, kv_ref, grads_ref in zip(sources, kv_refs, grads_refs):
        first = table_entry(table, position) * chip_blocks
        held = summary_count(ids_ref, first, chip_blocks)

        @pl.when(held > 0)
        def _():
            keys, values = keys_of(kv_ref, slice(None)), values_of(kv_ref, slice(None))
            key_t = transposed(keys)
            acc_ref[...] = jnp.zeros_like(acc_ref)

            def query_step(item, carry):
                first = item * together
                dq, dk, dv = block_grads(keys, values, key_t, query_refs, first, together)
                put_queries(dq_ref, near_ref, first, dq)
                add_grads(acc_ref, slice(None), dk, dv)
                return carry

            lax.fori_loop(0, chip_blocks // together, query_step, 0)
            grads_ref[...] = acc_ref[...].astype(BF16)

        @pl.when(held == 0)
        def _():
            grads_ref[...] = jnp.zeros_like(grads_ref)
            if count == 1:
                dq_ref[...] = near_ref[...]


def pairs_of_blocks(offsets_ref, ids_ref, kv_ref, query_refs, low, high, acc_ref, dq_ref):
    blocks_here = kv_ref.shape[0] // BLOCK
    _, base, own = places(blocks_here)
    keys, values = keys_of(kv_ref, slice(None)), values_of(kv_ref, slice(None))
    key_t = transposed(keys)

    def step(number, carry):
        query = jnp.where(number < blocks_here, own, base) + number
        flags = [
            attends(offsets_ref, ids_ref, query, own + key) | (own + key == query)
            for key in range(blocks_here)
        ]
        some = flags[0]
        for flag in flags[1:]:
            some |= flag

        @pl.when(some)
        def _():
            dq, dk, dv = block_grads(
                keys, values, key_t, query_refs, number, 1, [[bias_of(flag)] for flag in flags],
                (own - query) * BLOCK,
            )
            put_queries(dq_ref, dq_ref, number, dq)
            add_grads(acc_ref, slice(None), dk, dv)

        return carry

    lax.fori_loop(low, high, step, 0)


def is_early(chips):
    return (lax.axis_index("rep") == 0) & (lax.axis_index("ctx") >= (chips + 1) // 2)


def layout_kernel(
    chips, offsets_ref, ids_ref, kv_ref, q_ref, g_ref, s_ref, pq_ref, pg_ref, ps_ref,
    all_q_ref, all_g_ref, all_s_ref, acc_ref, dq_ref,
):
    blocks_here = s_ref.shape[0]
    for from_refs, to_ref in (((q_ref, pq_ref), all_q_ref), ((g_ref, pg_ref), all_g_ref)):
        for side, from_ref in enumerate(from_refs):
            for block in range(blocks_here):
                rows = slice(block * BLOCK, (block + 1) * BLOCK)
                for head in range(GROUP):
                    to_rows = slice(head * BLOCK, (head + 1) * BLOCK)
                    lanes = slice(head * HEAD_DIM, (head + 1) * HEAD_DIM)
                    to_ref[side * blocks_here + block, to_rows, :] = from_ref[rows, lanes]
    all_s_ref[0:blocks_here] = s_ref[...]
    all_s_ref[blocks_here:] = ps_ref[...]
    acc_ref[...] = jnp.zeros_like(acc_ref)
    dq_ref[...] = jnp.zeros_like(dq_ref)

    @pl.when(is_early(chips))
    def _():
        pairs_of_blocks(
            offsets_ref, ids_ref, kv_ref, (all_q_ref, all_g_ref, all_s_ref), 0, blocks_here,
            acc_ref, dq_ref,
        )


def tail_kernel(
    chips, offsets_ref, ids_ref, kv_ref, q_ref, g_ref, s_ref, early_acc_ref, early_dq_ref, far_ref,
    acc_ref, own_ref, *refs
):
    blocks_here = kv_ref.shape[0] // BLOCK
    core = lax.axis_index("rep")
    partner_refs, dq_ref = refs[:-1], refs[-1]
    acc_ref[...] = early_acc_ref[...]
    dq_ref[0:blocks_here] = far_ref[0:blocks_here] + early_dq_ref[...]
    dq_ref[blocks_here:] = far_ref[blocks_here:]
    low = jnp.where(is_early(chips), blocks_here, 0)
    high = jnp.where(core == 0, CORES * blocks_here, blocks_here)
    pairs_of_blocks(
        offsets_ref, ids_ref, kv_ref, (q_ref, g_ref, s_ref), low, high, acc_ref, dq_ref
    )
    own_ref[...] = dq_ref[0:blocks_here]
    for piece, partner_ref in enumerate(partner_refs):
        first = blocks_here + piece * partner_ref.shape[0]
        partner_ref[...] = dq_ref[first : first + partner_ref.shape[0]].astype(BF16)


def final_kernel(
    last_sender, ids_ref, acc_ref, own_dq_ref, blocks_ref, slots_ref, *refs
):
    piece_refs, refs = refs[:PIECES], refs[PIECES:]
    far_refs, (dq_ref, dk_ref, dv_ref, sum_ref) = refs[:-4], refs[-4:]
    blocks_here = acc_ref.shape[0] // BLOCK
    chip, base, own = places(blocks_here)
    sum_ref[...] = acc_ref[...] + blocks_ref[...].astype(F32)
    first_core = lax.axis_index("rep") == 0

    def slot_step(slot, carry):
        _, chip_rank = core_slot(ids_ref, slot, base, CORES * blocks_here)
        of_core, core_rank = core_slot(ids_ref, slot, own, blocks_here)
        rows = block_rows(lax.rem(ids_ref[slot], blocks_here))

        @pl.when(of_core & first_core & (core_rank < slots_ref.shape[0] // BLOCK))
        def _():
            sum_ref[rows, :] += slots_ref[block_rows(core_rank), :].astype(F32)

        @pl.when(of_core & (chip <= last_sender) & (chip_rank < far_refs[0].shape[0] // BLOCK))
        def _():
            for far_ref in far_refs:
                sum_ref[rows, :] += far_ref[block_rows(chip_rank), :].astype(F32)

        return carry

    lax.fori_loop(0, SUMMARY, slot_step, 0)
    dk_ref[...] = keys_of(sum_ref, slice(None)).astype(BF16)
    dv_ref[...] = values_of(sum_ref, slice(None)).astype(BF16)

    each = blocks_here // PIECES
    for piece, piece_ref in enumerate(piece_refs):

        def query_step(number, carry):
            block = piece * each + number
            total = own_dq_ref[block] + piece_ref[number].astype(F32)
            for head in range(GROUP):
                lanes = slice(head * HEAD_DIM, (head + 1) * HEAD_DIM)
                dq_ref[block_rows(block), lanes] = total[:, lanes].T.astype(BF16)
            return carry

        lax.fori_loop(0, each, query_step, 0)


def call(kernel, scalars, arrays, out_shape, scratch=(), flops=0, in_space=VMEM, out_specs=None, room=24):
    return pl.pallas_call(
        kernel,
        out_shape=out_shape,
        in_specs=[SMEM] * len(scalars) + [in_space] * len(arrays),
        out_specs=out_specs or jax.tree.map(lambda _: VMEM, out_shape),
        scratch_shapes=list(scratch),
        compiler_params=pltpu.CompilerParams(vmem_limit_bytes=room << 20),
        cost_estimate=pl.CostEstimate(flops=flops, bytes_accessed=0, transcendentals=0),
    )(*scalars, *arrays)


def shape_of(shape, dtype):
    return jax.ShapeDtypeStruct(shape, dtype)


def with_capacity(
    slots, chips, queries, kv, attn_out, grads, log_sums, window_offsets, summary_ids
):
    rows = queries.shape[0]
    blocks_here = rows // BLOCK
    swap = [(0, 1), (1, 0)]
    up_first, up_last = (
        [(i * CORES + core, (i + 1) * CORES + core) for i in range(chips - 1)]
        for core in (0, CORES - 1)
    )
    down_first, down_last = ([(b, a) for a, b in route] for route in (up_first, up_last))
    routes = far_rounds(chips)
    sources = tuple({b: a // CORES for a, b in route} for route in routes)
    both = ("ctx", "rep")

    kv_partner = lax.ppermute(kv, "rep", swap)
    near_blocks = lax.ppermute(kv, both, up_last)
    far_shape, slots_shape = (shape_of((slot * BLOCK, 2 * HEAD_DIM), BF16) for slot in slots)
    picked, near_slots = call(
        pick_kernel, (summary_ids,), (kv, kv_partner), (far_shape, slots_shape)
    )
    near_slots = lax.ppermute(near_slots, both, up_first)
    kv_far = [lax.ppermute(picked, both, route) for route in routes]
    queries, grads, attn_out, window_offsets, _ = lax.optimization_barrier(
        (queries, grads, attn_out, window_offsets, picked)
    )
    tables = (window_offsets, summary_ids)
    stats = call(
        prep_kernel, (), (attn_out, grads, log_sums),
        shape_of((blocks_here, 8, GROUP * BLOCK), F32), flops=10 * MICROSECOND,
    )
    partner_queries, partner_grads = (lax.ppermute(x, "rep", swap) for x in (queries, grads))
    stats, partner_queries, partner_grads = lax.optimization_barrier(
        (stats, partner_queries, partner_grads)
    )
    every = (queries, grads, stats, partner_queries, partner_grads, lax.ppermute(stats, "rep", swap))
    acc_shape = (rows, 2 * HEAD_DIM)
    half_shape = (blocks_here, HEAD_DIM, GROUP * BLOCK)
    dq_shape = shape_of((CORES * blocks_here, *half_shape[1:]), F32)
    stacked_shape = shape_of((CORES * blocks_here, GROUP * BLOCK, HEAD_DIM), BF16)
    *every, early_acc, early_dq = call(
        functools.partial(layout_kernel, chips), tables, (kv, *every),
        (
            stacked_shape, stacked_shape,
            shape_of((CORES * blocks_here, *stats.shape[1:]), F32),
            shape_of(acc_shape, F32), shape_of(half_shape, F32),
        ),
    )
    block_part, slot_part, near_dq = call(
        near_kernel, tables, (near_blocks, near_slots, *every),
        (shape_of(acc_shape, BF16), slots_shape, dq_shape),
        [pltpu.VMEM(acc_shape, F32), pltpu.VMEM(acc_shape, BF16)],
    )
    *far_grads, far_dq = call(
        functools.partial(far_kernel, sources), (summary_ids,), (*kv_far, *every, near_dq),
        (*[far_shape] * len(routes), dq_shape),
        [pltpu.VMEM(far_shape.shape, F32)], flops=5 * MICROSECOND,
    )
    far_back = [
        lax.ppermute(x, both, [(b, a) for a, b in route]) for x, route in zip(far_grads, routes)
    ]
    block_part, slot_part, _ = lax.optimization_barrier((block_part, slot_part, far_grads))
    block_part = lax.ppermute(block_part, both, down_last)
    slot_part = lax.ppermute(slot_part, both, down_first)
    piece_shape = shape_of((blocks_here // PIECES, *half_shape[1:]), BF16)
    acc, dq_own, *dq_partner = call(
        functools.partial(tail_kernel, chips), tables,
        (kv, *every, early_acc, early_dq, far_dq),
        (shape_of(acc_shape, F32), shape_of(half_shape, F32), *[piece_shape] * PIECES),
        [pltpu.VMEM(dq_shape.shape, F32)], flops=TAIL,
    )
    dq_partner = [lax.ppermute(x, "rep", swap) for x in dq_partner]
    acc, slot_part = lax.optimization_barrier((acc, slot_part))
    if slots[0] > 3:
        acc, block_part = lax.optimization_barrier((acc, block_part))
    far_back, acc = lax.optimization_barrier((far_back, acc))
    far_other = [lax.ppermute(x, "rep", swap) for x in far_back]
    kv_shape = shape_of((rows, HEAD_DIM), BF16)
    return call(
        functools.partial(final_kernel, chips - 3), (summary_ids,),
        (acc, dq_own, block_part, slot_part, *dq_partner, *far_back, *far_other),
        (shape_of(queries.shape, BF16), kv_shape, kv_shape), [pltpu.VMEM(acc_shape, F32)],
    )


def capacities(chips):
    return CAPACITIES if len(far_rounds(chips)) == 1 else CAPACITIES[-1:]


def per_device(chips, queries, keys, values, attn_out, grads, log_sums, window_offsets, summary_ids):
    kv, branch = call(
        functools.partial(start_kernel, chips), (), (summary_ids, keys, values),
        (shape_of((keys.shape[0], 2 * HEAD_DIM), BF16), shape_of((1,), jnp.int32)),
        [pltpu.SMEM(summary_ids.shape, jnp.int32), pltpu.SemaphoreType.DMA((3,))], in_space=HBM, out_specs=(VMEM, SMEM), room=60,
    )
    branches = [functools.partial(with_capacity, limit, chips) for limit in capacities(chips)]
    operands = (queries, kv, attn_out, grads, log_sums, window_offsets.T, summary_ids)
    return lax.switch(branch[0], branches, *operands) if len(branches) > 1 else branches[0](*operands)


def solution(mesh):
    rows = P(("groups", "ctx", "rep"), "heads")
    return jax.shard_map(
        functools.partial(per_device, mesh.shape["ctx"]),
        mesh=mesh,
        in_specs=(rows,) * 5 + (P("heads", ("groups", "ctx", "rep")), P("groups", None), P("groups")),
        out_specs=(rows,) * 3,
        check_vma=False,
    )
```

```python
import functools
import math

import jax
import jax.numpy as jnp
from jax import lax
from jax.experimental import pallas as pl
from jax.experimental.pallas import tpu as pltpu
from jax.sharding import PartitionSpec as P

HEAD_DIM = 128
GROUP = 4
BLOCK = 128
REACH = 3
SUMMARY = 8
CORES = 2
SCALE = HEAD_DIM ** (-0.5)
LOG2E = math.log2(math.e)
MICROSECOND = 1_000_000_000
OWN = 10 * MICROSECOND
CAPACITIES = ((2, 2), (3, 2), (4, 3), (SUMMARY - 1, 4))
F32 = jnp.float32
BF16 = jnp.bfloat16
VMEM = pl.BlockSpec(memory_space=pltpu.VMEM)
SMEM = pl.BlockSpec(memory_space=pltpu.SMEM)
HBM = pl.BlockSpec(memory_space=pltpu.HBM)


def far_rounds(chips):
    rounds = []
    for source in range(chips):
        for target in range(source + 2, chips):
            wanted = target % CORES
            better = (source + target + 1) % CORES
            for route in rounds:
                senders = [core for core in range(CORES) if source * CORES + core not in route.values()]
                receivers = [core for core in range(CORES) if target * CORES + core not in route]
                if senders and receivers:
                    break
            else:
                senders, receivers, route = list(range(CORES)), list(range(CORES)), {}
                rounds.append(route)
            sender = wanted if wanted in senders else senders[0]
            receiver = better if better in receivers else receivers[0]
            route[target * CORES + receiver] = source * CORES + sender
    return [[(a, b) for b, a in route.items()] for route in rounds]


def table_entry(table, position):
    value = jnp.int32(-1)
    for place, entry in table.items():
        value = jnp.where(position == place, jnp.int32(entry), value)
    return value


def summary_count(ids_ref, first, blocks):
    count = jnp.int32(0)
    for slot in range(SUMMARY):
        count += jnp.where((ids_ref[slot] >= first) & (ids_ref[slot] < first + blocks), 1, 0)
    return count


def prep_kernel(out_ref, grad_ref, lse_ref, stats_ref):
    stats_ref[...] = jnp.zeros_like(stats_ref)
    for block in range(stats_ref.shape[0]):
        rows = slice(block * BLOCK, (block + 1) * BLOCK)
        for head in range(GROUP):
            columns = slice(head * HEAD_DIM, (head + 1) * HEAD_DIM)
            product = out_ref[rows, columns].astype(F32) * grad_ref[rows, columns].astype(F32)
            stats_ref[block, 0:1, columns] = lse_ref[head : head + 1, rows] * LOG2E
            stats_ref[block, 1:2, columns] = jnp.sum(product.T, axis=0, keepdims=True)


def start_kernel(chips, ids_hbm, key_ref, value_ref, kv_ref, branch_ref, ids_ref, sems):
    chip_blocks = CORES * (key_ref.shape[0] // BLOCK)
    copies = [
        pltpu.make_async_copy(
            ref, kv_ref.at[:, number * HEAD_DIM : (number + 1) * HEAD_DIM], sems.at[number]
        )
        for number, ref in enumerate((key_ref, value_ref))
    ]
    ids_copy = pltpu.make_async_copy(ids_hbm, ids_ref, sems.at[2])
    ids_copy.start()
    for copy in copies:
        copy.start()
    ids_copy.wait()
    far_most = near_most = jnp.int32(0)
    for chip in range(chips - 1):
        first = chip * chip_blocks
        near_most = jnp.maximum(near_most, summary_count(ids_ref, first, chip_blocks // CORES))
        if chip < chips - 2:
            far_most = jnp.maximum(far_most, summary_count(ids_ref, first, chip_blocks))
    branch = jnp.int32(0)
    for far_slots, near_slots in capacities(chips)[:-1]:
        branch += jnp.where((far_most > far_slots) | (near_most > near_slots), 1, 0)
    branch_ref[0] = branch
    for copy in copies:
        copy.wait()


def core_slot(ids_ref, slot, first, blocks):
    def inside(other):
        return (ids_ref[other] >= first) & (ids_ref[other] < first + blocks)

    rank = jnp.int32(0)
    for other in range(SUMMARY):
        rank += jnp.where(inside(other) & (other < slot), 1, 0)
    return inside(slot), rank


def block_rows(number):
    return pl.ds(pl.multiple_of(number * BLOCK, BLOCK), BLOCK)


def pick_kernel(ids_ref, own_ref, partner_ref, far_ref):
    blocks_here = own_ref.shape[0] // BLOCK
    _, base, own = places(blocks_here)
    far_ref[...] = jnp.zeros_like(far_ref)

    def slot_step(slot, carry):
        of_chip, chip_rank = core_slot(ids_ref, slot, base, CORES * blocks_here)
        of_core, _ = core_slot(ids_ref, slot, own, blocks_here)
        row = block_rows(lax.rem(ids_ref[slot], blocks_here))

        @pl.when(of_chip & (chip_rank < far_ref.shape[0] // BLOCK))
        def _():
            far_ref[block_rows(chip_rank), :] = jnp.where(
                of_core, own_ref[row, :], partner_ref[row, :]
            )

        return carry

    lax.fori_loop(0, SUMMARY, slot_step, 0)


def nt(a, b):
    return lax.dot_general(a, b, (((1,), (1,)), ((), ())), preferred_element_type=F32)


def nn(a, b):
    return jnp.dot(a, b, preferred_element_type=F32)


def block_grads(keys, values, key_t, query_refs, first, count=1, biases=None, reach=None):
    query_ref, grad_ref, stats_ref = query_refs
    numbers = [first + step for step in range(count)]
    queries = jnp.concatenate([query_ref[number] for number in numbers], axis=0)
    grads = jnp.concatenate([grad_ref[number] for number in numbers], axis=0)
    log_sums = [stats_ref[number, 0:1, :] for number in numbers]
    deltas = jnp.concatenate([stats_ref[number, 1:2, :] for number in numbers], axis=1)
    scores = nt(keys, queries) * (SCALE * LOG2E)
    if biases is None:
        probs = jnp.exp2(scores - jnp.concatenate(log_sums, axis=1))
    else:
        if reach is not None:
            shape = (BLOCK, queries.shape[0])
            column = lax.broadcasted_iota(jnp.int32, shape, 1)
            ahead = column // (GROUP * BLOCK) * BLOCK + column % BLOCK
            ahead -= lax.broadcasted_iota(jnp.int32, shape, 0)
        parts = []
        for key, row in enumerate(biases):
            shift = jnp.concatenate([a + bias for a, bias in zip(log_sums, row)], axis=1)
            part = jnp.exp2(scores[key * BLOCK : (key + 1) * BLOCK] - shift)
            if reach is not None:
                part = jnp.where(ahead >= reach + key * BLOCK, part, 0.0)
            parts.append(part)
        probs = jnp.concatenate(parts, axis=0)
    prob_grads = nt(values, grads)
    score_grads = (probs * (prob_grads - deltas) * SCALE).astype(BF16)
    return nn(key_t, score_grads), nn(score_grads, queries), nn(probs.astype(BF16), grads)


def put_queries(to_ref, from_ref, first, dq):
    width = GROUP * BLOCK
    for step in range(dq.shape[1] // width):
        part = dq[:, step * width : (step + 1) * width]
        to_ref[first + step] = from_ref[first + step] + part


def is_summary(ids_ref, key_block):
    found = ids_ref[0] == key_block
    for slot in range(1, SUMMARY):
        found |= ids_ref[slot] == key_block
    return found


def in_window(offsets_ref, query_block, key_block):
    distance = query_block - key_block
    return (distance == offsets_ref[0, query_block]) | (distance == offsets_ref[1, query_block])


def attends(offsets_ref, ids_ref, query_block, key_block):
    chosen = in_window(offsets_ref, query_block, key_block) | is_summary(ids_ref, key_block)
    return (query_block > key_block) & chosen


def keys_of(kv_ref, rows):
    return kv_ref[rows, 0:HEAD_DIM]


def values_of(kv_ref, rows):
    return kv_ref[rows, HEAD_DIM : 2 * HEAD_DIM]


def transposed(keys):
    return keys.astype(F32).T.astype(BF16)


def add_grads(acc_ref, rows, key_part, value_part):
    acc_ref[rows, 0:HEAD_DIM] += key_part
    acc_ref[rows, HEAD_DIM : 2 * HEAD_DIM] += value_part


def places(blocks_here):
    chip = lax.axis_index("ctx")
    base = chip * CORES * blocks_here
    return chip, base, base + lax.axis_index("rep") * blocks_here


def bias_of(flag):
    return jnp.where(flag, 0.0, 1e30).astype(F32)


def near_kernel(
    offsets_ref, ids_ref, kv_ref, q_ref, g_ref, s_ref, cross_ref,
    block_grads_ref, slot_grads_ref, dq_ref, acc_ref,
):
    query_refs = (q_ref, g_ref, s_ref)
    blocks_here = kv_ref.shape[0] // BLOCK
    chip_blocks = CORES * blocks_here
    chip, base, own = places(blocks_here)
    first_key = own - chip_blocks
    acc_ref[...] = jnp.zeros_like(acc_ref)
    dq_ref[0:blocks_here] = jnp.zeros_like(cross_ref)
    dq_ref[blocks_here:] = cross_ref[...]
    flags = [is_summary(ids_ref, first_key + key) & (chip > 0) for key in range(blocks_here)]
    count = jnp.int32(0)
    chosen = [jnp.int32(0)] * blocks_here
    for key in range(blocks_here):
        for place in range(key + 1):
            chosen[place] = jnp.where(flags[key] & (count == place), key, chosen[place])
        count += jnp.where(flags[key], 1, 0)

    def add(first, count, places_of_keys, biases=None):
        rows = [pl.ds(pl.multiple_of(key * BLOCK, BLOCK), BLOCK) for key in places_of_keys]
        keys = jnp.concatenate([keys_of(kv_ref, row) for row in rows], axis=0)
        values = jnp.concatenate([values_of(kv_ref, row) for row in rows], axis=0)
        dq, dk, dv = block_grads(keys, values, transposed(keys), query_refs, first, count, biases)
        put_queries(dq_ref, dq_ref, first, dq)
        for place, row in enumerate(rows):
            part = slice(place * BLOCK, (place + 1) * BLOCK)
            add_grads(acc_ref, row, dk[part], dv[part])

    def entry(place):
        key = jnp.int32(0)
        for number in range(blocks_here):
            key = jnp.where(place == number, chosen[number], key)
        return key

    odd = lax.rem(count, 2)

    def single_step(item, carry):
        add(item * 4, 4, [chosen[0]])
        return carry

    lax.fori_loop(0, odd * (chip_blocks // 4), single_step, 0)

    def double_step(item, carry):
        turn = odd + 2 * (item // (chip_blocks // 2))
        add(lax.rem(item, chip_blocks // 2) * 2, 2, [entry(turn), entry(turn + 1)])
        return carry

    lax.fori_loop(0, (count // 2) * (chip_blocks // 2), double_step, 0)

    def window_step(number, carry):
        query = base + number
        keys, wanted = [], []
        for place in range(2):
            key = query - offsets_ref[place, query] - first_key
            fits = (key >= 0) & (key < blocks_here)
            key = jnp.where(fits, key, 0)
            for block in range(blocks_here):
                fits &= (key != block) | ~flags[block]
            keys.append(key)
            wanted.append(fits)

        @pl.when(wanted[0] | wanted[1])
        def _():
            add(number + blocks_here, 1, keys, [[bias_of(flag)] for flag in wanted])

        return carry

    reaches = (chip > 0) & (lax.axis_index("rep") == CORES - 1)
    lax.fori_loop(0, jnp.where(reaches, min(REACH, blocks_here), 0), window_step, 0)
    block_grads_ref[...] = acc_ref[...].astype(BF16)
    slot_grads_ref[...] = jnp.zeros_like(slot_grads_ref)

    def slot_step(slot, carry):
        inside, rank = core_slot(ids_ref, slot, first_key, blocks_here)

        @pl.when(inside & (rank < slot_grads_ref.shape[0] // BLOCK))
        def _():
            rows = block_rows(lax.rem(ids_ref[slot], blocks_here))
            slot_grads_ref[block_rows(rank), :] = acc_ref[rows, :].astype(BF16)

        return carry

    lax.fori_loop(0, SUMMARY, slot_step, 0)


def far_kernel(sources, ids_ref, *refs):
    count = len(sources)
    kv_refs, refs = refs[:count], refs[count:]
    query_refs, near_ref, refs = refs[:3], refs[3], refs[4:]
    grads_refs, (dq_ref, partner_ref, acc_ref) = refs[:count], refs[count:]
    chip_blocks = near_ref.shape[0]
    position = lax.axis_index("ctx") * CORES + lax.axis_index("rep")
    capacity = acc_ref.shape[0] // BLOCK
    together = 4 if capacity < 4 else 2 if capacity == 4 else 1
    if count > 1:
        dq_ref[...] = near_ref[...]
        near_ref = dq_ref
    for table, kv_ref, grads_ref in zip(sources, kv_refs, grads_refs):
        first = table_entry(table, position) * chip_blocks
        held = summary_count(ids_ref, first, chip_blocks)

        @pl.when(held > 0)
        def _():
            keys, values = keys_of(kv_ref, slice(None)), values_of(kv_ref, slice(None))
            key_t = transposed(keys)
            acc_ref[...] = jnp.zeros_like(acc_ref)

            def query_step(item, carry):
                first = item * together
                dq, dk, dv = block_grads(keys, values, key_t, query_refs, first, together)
                put_queries(dq_ref, near_ref, first, dq)
                add_grads(acc_ref, slice(None), dk, dv)
                return carry

            lax.fori_loop(0, chip_blocks // together, query_step, 0)
            grads_ref[...] = acc_ref[...].astype(BF16)

        @pl.when(held == 0)
        def _():
            grads_ref[...] = jnp.zeros_like(grads_ref)
            if count == 1:
                dq_ref[...] = near_ref[...]

    partner_ref[...] = dq_ref[chip_blocks // CORES :].astype(BF16)


def pairs_of_blocks(
    offsets_ref, ids_ref, kv_ref, first_key, first_query, query_refs, first_number, acc_ref, dq_ref
):
    blocks_here = kv_ref.shape[0] // BLOCK
    keys, values = keys_of(kv_ref, slice(None)), values_of(kv_ref, slice(None))
    key_t = transposed(keys)

    def step(number, carry):
        query = first_query + number
        flags = [
            attends(offsets_ref, ids_ref, query, first_key + key) | (first_key + key == query)
            for key in range(blocks_here)
        ]
        some = flags[0]
        for flag in flags[1:]:
            some |= flag

        @pl.when(some)
        def _():
            dq, dk, dv = block_grads(
                keys, values, key_t, query_refs, first_number + number, 1,
                [[bias_of(flag)] for flag in flags],
                (first_key - query) * BLOCK if first_number == 0 else None,
            )
            put_queries(dq_ref, dq_ref, number, dq)
            add_grads(acc_ref, slice(None), dk, dv)

        return carry

    lax.fori_loop(0, blocks_here, step, 0)


def cross_kernel(
    offsets_ref, ids_ref, kv_ref, q_ref, g_ref, s_ref, pq_ref, pg_ref, ps_ref,
    acc_ref, dq_ref, all_q_ref, all_g_ref, all_s_ref,
):
    blocks_here = kv_ref.shape[0] // BLOCK
    _, base, own = places(blocks_here)
    for from_refs, to_ref in (((q_ref, pq_ref), all_q_ref), ((g_ref, pg_ref), all_g_ref)):
        for side, from_ref in enumerate(from_refs):
            for block in range(blocks_here):
                rows = slice(block * BLOCK, (block + 1) * BLOCK)
                for head in range(GROUP):
                    to_rows = slice(head * BLOCK, (head + 1) * BLOCK)
                    lanes = slice(head * HEAD_DIM, (head + 1) * HEAD_DIM)
                    to_ref[side * blocks_here + block, to_rows, :] = from_ref[rows, lanes]
    all_s_ref[0:blocks_here] = s_ref[...]
    all_s_ref[blocks_here:] = ps_ref[...]
    acc_ref[...] = jnp.zeros_like(acc_ref)
    dq_ref[...] = jnp.zeros_like(dq_ref)

    @pl.when(lax.axis_index("rep") == 0)
    def _():
        pairs_of_blocks(
            offsets_ref, ids_ref, kv_ref, own, base + blocks_here,
            (all_q_ref, all_g_ref, all_s_ref), blocks_here, acc_ref, dq_ref,
        )


def own_kernel(
    offsets_ref, ids_ref, kv_ref, q_ref, g_ref, s_ref, cross_ref, far_ref, acc_ref, dq_ref
):
    blocks_here = kv_ref.shape[0] // BLOCK
    _, _, own = places(blocks_here)
    acc_ref[...] = cross_ref[...]
    dq_ref[...] = far_ref[0:blocks_here]
    pairs_of_blocks(
        offsets_ref, ids_ref, kv_ref, own, own, (q_ref, g_ref, s_ref), 0, acc_ref, dq_ref
    )


def query_kernel(own_ref, partner_ref, dq_ref):
    def block_step(block, carry):
        total = own_ref[block] + partner_ref[block].astype(F32)
        rows = pl.ds(pl.multiple_of(block * BLOCK, BLOCK), BLOCK)
        for head in range(GROUP):
            lanes = slice(head * HEAD_DIM, (head + 1) * HEAD_DIM)
            dq_ref[rows, lanes] = total[:, lanes].T.astype(BF16)
        return carry

    lax.fori_loop(0, own_ref.shape[0], block_step, 0)


def final_kernel(last_sender, ids_ref, acc_ref, blocks_ref, slots_ref, *refs):
    far_refs, (dk_ref, dv_ref, sum_ref) = refs[:-3], refs[-3:]
    blocks_here = acc_ref.shape[0] // BLOCK
    chip, base, own = places(blocks_here)
    sum_ref[...] = acc_ref[...] + blocks_ref[...].astype(F32)
    first_core = lax.axis_index("rep") == 0

    def slot_step(slot, carry):
        _, chip_rank = core_slot(ids_ref, slot, base, CORES * blocks_here)
        of_core, core_rank = core_slot(ids_ref, slot, own, blocks_here)
        rows = block_rows(lax.rem(ids_ref[slot], blocks_here))

        @pl.when(of_core & first_core & (core_rank < slots_ref.shape[0] // BLOCK))
        def _():
            sum_ref[rows, :] += slots_ref[block_rows(core_rank), :].astype(F32)

        @pl.when(of_core & (chip <= last_sender) & (chip_rank < far_refs[0].shape[0] // BLOCK))
        def _():
            for far_ref in far_refs:
                sum_ref[rows, :] += far_ref[block_rows(chip_rank), :].astype(F32)

        return carry

    lax.fori_loop(0, SUMMARY, slot_step, 0)
    dk_ref[...] = keys_of(sum_ref, slice(None)).astype(BF16)
    dv_ref[...] = values_of(sum_ref, slice(None)).astype(BF16)


def call(kernel, scalars, arrays, out_shape, scratch=(), flops=0, in_space=VMEM, out_specs=None, room=24):
    return pl.pallas_call(
        kernel,
        out_shape=out_shape,
        in_specs=[SMEM] * len(scalars) + [in_space] * len(arrays),
        out_specs=out_specs or jax.tree.map(lambda _: VMEM, out_shape),
        scratch_shapes=list(scratch),
        compiler_params=pltpu.CompilerParams(vmem_limit_bytes=room << 20),
        cost_estimate=pl.CostEstimate(flops=flops, bytes_accessed=0, transcendentals=0),
    )(*scalars, *arrays)


def shape_of(shape, dtype):
    return jax.ShapeDtypeStruct(shape, dtype)


def with_capacity(
    slots, chips, queries, kv, attn_out, grads, log_sums, window_offsets, summary_ids
):
    rows = queries.shape[0]
    blocks_here = rows // BLOCK
    swap = [(0, 1), (1, 0)]
    up = [(i, i + 1) for i in range(chips - 1)]
    down_first, down_last = (
        [(b * CORES + core, a * CORES + core) for a, b in up] for core in (0, CORES - 1)
    )
    routes = far_rounds(chips)
    sources = tuple({b: a // CORES for a, b in route} for route in routes)
    both = ("ctx", "rep")

    kv_partner = lax.ppermute(kv, "rep", swap)
    kv_near = lax.ppermute(kv, "ctx", up)
    far_shape, slots_shape = (shape_of((slot * BLOCK, 2 * HEAD_DIM), BF16) for slot in slots)
    picked = call(pick_kernel, (summary_ids,), (kv, kv_partner), far_shape)
    kv_far = [lax.ppermute(picked, both, route) for route in routes]
    queries, grads, attn_out, window_offsets, _ = lax.optimization_barrier(
        (queries, grads, attn_out, window_offsets, picked)
    )
    tables = (window_offsets, summary_ids)
    stats = call(
        prep_kernel, (), (attn_out, grads, log_sums),
        shape_of((blocks_here, 8, GROUP * BLOCK), F32), flops=5 * MICROSECOND,
    )
    own = (queries, grads, stats)
    every = own + tuple(lax.ppermute(x, "rep", swap) for x in own)
    acc_shape = (rows, 2 * HEAD_DIM)
    half_shape = (blocks_here, HEAD_DIM, GROUP * BLOCK)
    dq_shape = shape_of((CORES * blocks_here, *half_shape[1:]), F32)
    stacked_shape = shape_of((CORES * blocks_here, GROUP * BLOCK, HEAD_DIM), BF16)
    cross_acc, cross_dq, *every = call(
        cross_kernel, tables, (kv, *every),
        (
            shape_of(acc_shape, F32), shape_of(half_shape, F32), stacked_shape, stacked_shape,
            shape_of((CORES * blocks_here, *stats.shape[1:]), F32),
        ),
    )
    block_part, slot_part, near_dq = call(
        near_kernel, tables, (kv_near, *every, cross_dq),
        (shape_of(acc_shape, BF16), slots_shape, dq_shape),
        [pltpu.VMEM(acc_shape, F32)],
    )
    *far_grads, far_dq, dq_partner = call(
        functools.partial(far_kernel, sources), (summary_ids,), (*kv_far, *every, near_dq),
        (*[far_shape] * len(routes), dq_shape, shape_of(half_shape, BF16)),
        [pltpu.VMEM(far_shape.shape, F32)], flops=5 * MICROSECOND,
    )
    far_back = [
        lax.ppermute(x, both, [(b, a) for a, b in route]) for x, route in zip(far_grads, routes)
    ]
    block_part, slot_part, _ = lax.optimization_barrier((block_part, slot_part, far_grads))
    block_part = lax.ppermute(block_part, both, down_last)
    slot_part = lax.ppermute(slot_part, both, down_first)
    dq_partner = lax.ppermute(dq_partner, "rep", swap)
    acc, dq = call(
        own_kernel, tables, (kv, *every, cross_acc, far_dq),
        (shape_of(acc_shape, F32), shape_of(half_shape, F32)), flops=OWN,
    )
    query_grads = call(query_kernel, (), (dq, dq_partner), shape_of(queries.shape, BF16))
    acc, slot_part = lax.optimization_barrier((acc, slot_part))
    if slots[0] > 3:
        acc, block_part = lax.optimization_barrier((acc, block_part))
    far_back, acc, query_grads = lax.optimization_barrier((far_back, acc, query_grads))
    far_other = [lax.ppermute(x, "rep", swap) for x in far_back]
    kv_shape = shape_of((rows, HEAD_DIM), BF16)
    key_grads, value_grads = call(
        functools.partial(final_kernel, chips - 3), (summary_ids,),
        (acc, block_part, slot_part, *far_back, *far_other), (kv_shape, kv_shape),
        [pltpu.VMEM(acc_shape, F32)],
    )
    return query_grads, key_grads, value_grads


def capacities(chips):
    return CAPACITIES if len(far_rounds(chips)) == 1 else CAPACITIES[-1:]


def per_device(chips, queries, keys, values, attn_out, grads, log_sums, window_offsets, summary_ids):
    kv, branch = call(
        functools.partial(start_kernel, chips), (), (summary_ids, keys, values),
        (shape_of((keys.shape[0], 2 * HEAD_DIM), BF16), shape_of((1,), jnp.int32)),
        [pltpu.SMEM(summary_ids.shape, jnp.int32), pltpu.SemaphoreType.DMA((3,))], in_space=HBM, out_specs=(VMEM, SMEM), room=60,
    )
    branches = [functools.partial(with_capacity, limit, chips) for limit in capacities(chips)]
    operands = (queries, kv, attn_out, grads, log_sums, window_offsets.T, summary_ids)
    return lax.switch(branch[0], branches, *operands) if len(branches) > 1 else branches[0](*operands)


def solution(mesh):
    rows = P(("groups", "ctx", "rep"), "heads")
    return jax.shard_map(
        functools.partial(per_device, mesh.shape["ctx"]),
        mesh=mesh,
        in_specs=(rows,) * 5 + (P("heads", ("groups", "ctx", "rep")), P("groups", None), P("groups")),
        out_specs=(rows,) * 3,
        check_vma=False,
    )
```

```python
import functools
import math

import jax
import jax.numpy as jnp
from jax import lax
from jax.experimental import pallas as pl
from jax.experimental.pallas import tpu as pltpu
from jax.sharding import PartitionSpec as P

HEAD_DIM = 128
GROUP = 4
BLOCK = 128
REACH = 3
SUMMARY = 8
CORES = 2
SCALE = HEAD_DIM ** (-0.5)
LOG2E = math.log2(math.e)
MICROSECOND = 1_000_000_000
OWN = 10 * MICROSECOND
CAPACITIES = ((2, 2), (3, 2), (4, 3), (SUMMARY - 1, 4))
F32 = jnp.float32
BF16 = jnp.bfloat16
VMEM = pl.BlockSpec(memory_space=pltpu.VMEM)
SMEM = pl.BlockSpec(memory_space=pltpu.SMEM)
HBM = pl.BlockSpec(memory_space=pltpu.HBM)


def far_rounds(chips):
    rounds = []
    for source in range(chips):
        for target in range(source + 2, chips):
            wanted = target % CORES
            better = (source + target + 1) % CORES
            for route in rounds:
                senders = [core for core in range(CORES) if source * CORES + core not in route.values()]
                receivers = [core for core in range(CORES) if target * CORES + core not in route]
                if senders and receivers:
                    break
            else:
                senders, receivers, route = list(range(CORES)), list(range(CORES)), {}
                rounds.append(route)
            sender = wanted if wanted in senders else senders[0]
            receiver = better if better in receivers else receivers[0]
            route[target * CORES + receiver] = source * CORES + sender
    return [[(a, b) for b, a in route.items()] for route in rounds]


def table_entry(table, position):
    value = jnp.int32(-1)
    for place, entry in table.items():
        value = jnp.where(position == place, jnp.int32(entry), value)
    return value


def summary_count(ids_ref, first, blocks):
    count = jnp.int32(0)
    for slot in range(SUMMARY):
        count += jnp.where((ids_ref[slot] >= first) & (ids_ref[slot] < first + blocks), 1, 0)
    return count


def prep_kernel(out_ref, grad_ref, lse_ref, stats_ref):
    stats_ref[...] = jnp.zeros_like(stats_ref)
    for block in range(stats_ref.shape[0]):
        rows = slice(block * BLOCK, (block + 1) * BLOCK)
        for head in range(GROUP):
            columns = slice(head * HEAD_DIM, (head + 1) * HEAD_DIM)
            product = out_ref[rows, columns].astype(F32) * grad_ref[rows, columns].astype(F32)
            stats_ref[block, 0:1, columns] = lse_ref[head : head + 1, rows] * LOG2E
            stats_ref[block, 1:2, columns] = jnp.sum(product.T, axis=0, keepdims=True)


def start_kernel(chips, ids_hbm, key_ref, value_ref, kv_ref, branch_ref, ids_ref, sems):
    chip_blocks = CORES * (key_ref.shape[0] // BLOCK)
    copies = [
        pltpu.make_async_copy(
            ref, kv_ref.at[:, number * HEAD_DIM : (number + 1) * HEAD_DIM], sems.at[number]
        )
        for number, ref in enumerate((key_ref, value_ref))
    ]
    ids_copy = pltpu.make_async_copy(ids_hbm, ids_ref, sems.at[2])
    ids_copy.start()
    for copy in copies:
        copy.start()
    ids_copy.wait()
    far_most = near_most = jnp.int32(0)
    for chip in range(chips - 1):
        first = chip * chip_blocks
        near_most = jnp.maximum(near_most, summary_count(ids_ref, first, chip_blocks // CORES))
        if chip < chips - 2:
            far_most = jnp.maximum(far_most, summary_count(ids_ref, first, chip_blocks))
    branch = jnp.int32(0)
    for far_slots, near_slots in capacities(chips)[:-1]:
        branch += jnp.where((far_most > far_slots) | (near_most > near_slots), 1, 0)
    branch_ref[0] = branch
    for copy in copies:
        copy.wait()


def core_slot(ids_ref, slot, first, blocks):
    def inside(other):
        return (ids_ref[other] >= first) & (ids_ref[other] < first + blocks)

    rank = jnp.int32(0)
    for other in range(SUMMARY):
        rank += jnp.where(inside(other) & (other < slot), 1, 0)
    return inside(slot), rank


def block_rows(number):
    return pl.ds(pl.multiple_of(number * BLOCK, BLOCK), BLOCK)


def pick_kernel(ids_ref, own_ref, partner_ref, far_ref):
    blocks_here = own_ref.shape[0] // BLOCK
    _, base, own = places(blocks_here)
    far_ref[...] = jnp.zeros_like(far_ref)

    def slot_step(slot, carry):
        of_chip, chip_rank = core_slot(ids_ref, slot, base, CORES * blocks_here)
        of_core, _ = core_slot(ids_ref, slot, own, blocks_here)
        row = block_rows(lax.rem(ids_ref[slot], blocks_here))

        @pl.when(of_chip & (chip_rank < far_ref.shape[0] // BLOCK))
        def _():
            far_ref[block_rows(chip_rank), :] = jnp.where(
                of_core, own_ref[row, :], partner_ref[row, :]
            )

        return carry

    lax.fori_loop(0, SUMMARY, slot_step, 0)


def nt(a, b):
    return lax.dot_general(a, b, (((1,), (1,)), ((), ())), preferred_element_type=F32)


def nn(a, b):
    return jnp.dot(a, b, preferred_element_type=F32)


def block_grads(keys, values, key_t, query_refs, first, count=1, biases=None, reach=None):
    query_ref, grad_ref, stats_ref = query_refs
    numbers = [first + step for step in range(count)]
    queries = jnp.concatenate([query_ref[number] for number in numbers], axis=0)
    grads = jnp.concatenate([grad_ref[number] for number in numbers], axis=0)
    log_sums = [stats_ref[number, 0:1, :] for number in numbers]
    deltas = jnp.concatenate([stats_ref[number, 1:2, :] for number in numbers], axis=1)
    scores = nt(keys, queries) * (SCALE * LOG2E)
    if biases is None:
        probs = jnp.exp2(scores - jnp.concatenate(log_sums, axis=1))
    else:
        if reach is not None:
            shape = (BLOCK, queries.shape[0])
            column = lax.broadcasted_iota(jnp.int32, shape, 1)
            ahead = column // (GROUP * BLOCK) * BLOCK + column % BLOCK
            ahead -= lax.broadcasted_iota(jnp.int32, shape, 0)
        parts = []
        for key, row in enumerate(biases):
            shift = jnp.concatenate([a + bias for a, bias in zip(log_sums, row)], axis=1)
            part = jnp.exp2(scores[key * BLOCK : (key + 1) * BLOCK] - shift)
            if reach is not None:
                part = jnp.where(ahead >= reach + key * BLOCK, part, 0.0)
            parts.append(part)
        probs = jnp.concatenate(parts, axis=0)
    prob_grads = nt(values, grads)
    score_grads = (probs * (prob_grads - deltas) * SCALE).astype(BF16)
    return nn(key_t, score_grads), nn(score_grads, queries), nn(probs.astype(BF16), grads)


def put_queries(to_ref, from_ref, first, dq):
    width = GROUP * BLOCK
    for step in range(dq.shape[1] // width):
        part = dq[:, step * width : (step + 1) * width]
        to_ref[first + step] = from_ref[first + step] + part


def is_summary(ids_ref, key_block):
    found = ids_ref[0] == key_block
    for slot in range(1, SUMMARY):
        found |= ids_ref[slot] == key_block
    return found


def in_window(offsets_ref, query_block, key_block):
    distance = query_block - key_block
    return (distance == offsets_ref[0, query_block]) | (distance == offsets_ref[1, query_block])


def attends(offsets_ref, ids_ref, query_block, key_block):
    chosen = in_window(offsets_ref, query_block, key_block) | is_summary(ids_ref, key_block)
    return (query_block > key_block) & chosen


def keys_of(kv_ref, rows):
    return kv_ref[rows, 0:HEAD_DIM]


def values_of(kv_ref, rows):
    return kv_ref[rows, HEAD_DIM : 2 * HEAD_DIM]


def transposed(keys):
    return keys.astype(F32).T.astype(BF16)


def add_grads(acc_ref, rows, key_part, value_part):
    acc_ref[rows, 0:HEAD_DIM] += key_part
    acc_ref[rows, HEAD_DIM : 2 * HEAD_DIM] += value_part


def places(blocks_here):
    chip = lax.axis_index("ctx")
    base = chip * CORES * blocks_here
    return chip, base, base + lax.axis_index("rep") * blocks_here


def bias_of(flag):
    return jnp.where(flag, 0.0, 1e30).astype(F32)


def near_kernel(
    offsets_ref, ids_ref, kv_ref, q_ref, g_ref, s_ref, cross_ref,
    block_grads_ref, slot_grads_ref, dq_ref, acc_ref,
):
    query_refs = (q_ref, g_ref, s_ref)
    blocks_here = kv_ref.shape[0] // BLOCK
    chip_blocks = CORES * blocks_here
    chip, base, own = places(blocks_here)
    first_key = own - chip_blocks
    acc_ref[...] = jnp.zeros_like(acc_ref)
    dq_ref[0:blocks_here] = jnp.zeros_like(cross_ref)
    dq_ref[blocks_here:] = cross_ref[...]
    flags = [is_summary(ids_ref, first_key + key) & (chip > 0) for key in range(blocks_here)]
    count = jnp.int32(0)
    chosen = [jnp.int32(0)] * blocks_here
    for key in range(blocks_here):
        for place in range(key + 1):
            chosen[place] = jnp.where(flags[key] & (count == place), key, chosen[place])
        count += jnp.where(flags[key], 1, 0)

    def add(first, count, places_of_keys, biases=None):
        rows = [pl.ds(pl.multiple_of(key * BLOCK, BLOCK), BLOCK) for key in places_of_keys]
        keys = jnp.concatenate([keys_of(kv_ref, row) for row in rows], axis=0)
        values = jnp.concatenate([values_of(kv_ref, row) for row in rows], axis=0)
        dq, dk, dv = block_grads(keys, values, transposed(keys), query_refs, first, count, biases)
        put_queries(dq_ref, dq_ref, first, dq)
        for place, row in enumerate(rows):
            part = slice(place * BLOCK, (place + 1) * BLOCK)
            add_grads(acc_ref, row, dk[part], dv[part])

    def entry(place):
        key = jnp.int32(0)
        for number in range(blocks_here):
            key = jnp.where(place == number, chosen[number], key)
        return key

    odd = lax.rem(count, 2)

    def single_step(item, carry):
        add(item * 4, 4, [chosen[0]])
        return carry

    lax.fori_loop(0, odd * (chip_blocks // 4), single_step, 0)

    def double_step(item, carry):
        turn = odd + 2 * (item // (chip_blocks // 2))
        add(lax.rem(item, chip_blocks // 2) * 2, 2, [entry(turn), entry(turn + 1)])
        return carry

    lax.fori_loop(0, (count // 2) * (chip_blocks // 2), double_step, 0)

    def window_step(number, carry):
        query = base + number
        keys, wanted = [], []
        for place in range(2):
            key = query - offsets_ref[place, query] - first_key
            fits = (key >= 0) & (key < blocks_here)
            key = jnp.where(fits, key, 0)
            for block in range(blocks_here):
                fits &= (key != block) | ~flags[block]
            keys.append(key)
            wanted.append(fits)

        @pl.when(wanted[0] | wanted[1])
        def _():
            add(number + blocks_here, 1, keys, [[bias_of(flag)] for flag in wanted])

        return carry

    reaches = (chip > 0) & (lax.axis_index("rep") == CORES - 1)
    lax.fori_loop(0, jnp.where(reaches, min(REACH, blocks_here), 0), window_step, 0)
    block_grads_ref[...] = acc_ref[...].astype(BF16)
    slot_grads_ref[...] = jnp.zeros_like(slot_grads_ref)

    def slot_step(slot, carry):
        inside, rank = core_slot(ids_ref, slot, first_key, blocks_here)

        @pl.when(inside & (rank < slot_grads_ref.shape[0] // BLOCK))
        def _():
            rows = block_rows(lax.rem(ids_ref[slot], blocks_here))
            slot_grads_ref[block_rows(rank), :] = acc_ref[rows, :].astype(BF16)

        return carry

    lax.fori_loop(0, SUMMARY, slot_step, 0)


def far_kernel(sources, ids_ref, *refs):
    count = len(sources)
    kv_refs, refs = refs[:count], refs[count:]
    query_refs, near_ref, refs = refs[:3], refs[3], refs[4:]
    grads_refs, (dq_ref, partner_ref, acc_ref) = refs[:count], refs[count:]
    chip_blocks = near_ref.shape[0]
    position = lax.axis_index("ctx") * CORES + lax.axis_index("rep")
    capacity = acc_ref.shape[0] // BLOCK
    together = 4 if capacity < 4 else 2 if capacity == 4 else 1
    if count > 1:
        dq_ref[...] = near_ref[...]
        near_ref = dq_ref
    for table, kv_ref, grads_ref in zip(sources, kv_refs, grads_refs):
        first = table_entry(table, position) * chip_blocks
        held = summary_count(ids_ref, first, chip_blocks)

        @pl.when(held > 0)
        def _():
            keys, values = keys_of(kv_ref, slice(None)), values_of(kv_ref, slice(None))
            key_t = transposed(keys)
            acc_ref[...] = jnp.zeros_like(acc_ref)

            def query_step(item, carry):
                first = item * together
                dq, dk, dv = block_grads(keys, values, key_t, query_refs, first, together)
                put_queries(dq_ref, near_ref, first, dq)
                add_grads(acc_ref, slice(None), dk, dv)
                return carry

            lax.fori_loop(0, chip_blocks // together, query_step, 0)
            grads_ref[...] = acc_ref[...].astype(BF16)

        @pl.when(held == 0)
        def _():
            grads_ref[...] = jnp.zeros_like(grads_ref)
            if count == 1:
                dq_ref[...] = near_ref[...]

    partner_ref[...] = dq_ref[chip_blocks // CORES :].astype(BF16)


def pairs_of_blocks(
    offsets_ref, ids_ref, kv_ref, first_key, first_query, query_refs, first_number, acc_ref, dq_ref
):
    blocks_here = kv_ref.shape[0] // BLOCK
    keys, values = keys_of(kv_ref, slice(None)), values_of(kv_ref, slice(None))
    key_t = transposed(keys)

    def step(number, carry):
        query = first_query + number
        flags = [
            attends(offsets_ref, ids_ref, query, first_key + key) | (first_key + key == query)
            for key in range(blocks_here)
        ]
        some = flags[0]
        for flag in flags[1:]:
            some |= flag

        @pl.when(some)
        def _():
            dq, dk, dv = block_grads(
                keys, values, key_t, query_refs, first_number + number, 1,
                [[bias_of(flag)] for flag in flags],
                (first_key - query) * BLOCK if first_number == 0 else None,
            )
            put_queries(dq_ref, dq_ref, number, dq)
            add_grads(acc_ref, slice(None), dk, dv)

        return carry

    lax.fori_loop(0, blocks_here, step, 0)


def cross_kernel(
    offsets_ref, ids_ref, kv_ref, q_ref, g_ref, s_ref, pq_ref, pg_ref, ps_ref,
    acc_ref, dq_ref, all_q_ref, all_g_ref, all_s_ref,
):
    blocks_here = kv_ref.shape[0] // BLOCK
    _, base, own = places(blocks_here)
    for from_refs, to_ref in (((q_ref, pq_ref), all_q_ref), ((g_ref, pg_ref), all_g_ref)):
        for side, from_ref in enumerate(from_refs):
            for block in range(blocks_here):
                rows = slice(block * BLOCK, (block + 1) * BLOCK)
                for head in range(GROUP):
                    to_rows = slice(head * BLOCK, (head + 1) * BLOCK)
                    lanes = slice(head * HEAD_DIM, (head + 1) * HEAD_DIM)
                    to_ref[side * blocks_here + block, to_rows, :] = from_ref[rows, lanes]
    all_s_ref[0:blocks_here] = s_ref[...]
    all_s_ref[blocks_here:] = ps_ref[...]
    acc_ref[...] = jnp.zeros_like(acc_ref)
    dq_ref[...] = jnp.zeros_like(dq_ref)

    @pl.when(lax.axis_index("rep") == 0)
    def _():
        pairs_of_blocks(
            offsets_ref, ids_ref, kv_ref, own, base + blocks_here,
            (all_q_ref, all_g_ref, all_s_ref), blocks_here, acc_ref, dq_ref,
        )


def own_kernel(
    offsets_ref, ids_ref, kv_ref, q_ref, g_ref, s_ref, cross_ref, far_ref, acc_ref, dq_ref
):
    blocks_here = kv_ref.shape[0] // BLOCK
    _, _, own = places(blocks_here)
    acc_ref[...] = cross_ref[...]
    dq_ref[...] = far_ref[0:blocks_here]
    pairs_of_blocks(
        offsets_ref, ids_ref, kv_ref, own, own, (q_ref, g_ref, s_ref), 0, acc_ref, dq_ref
    )


def query_kernel(own_ref, partner_ref, dq_ref):
    def block_step(block, carry):
        total = own_ref[block] + partner_ref[block].astype(F32)
        rows = pl.ds(pl.multiple_of(block * BLOCK, BLOCK), BLOCK)
        for head in range(GROUP):
            lanes = slice(head * HEAD_DIM, (head + 1) * HEAD_DIM)
            dq_ref[rows, lanes] = total[:, lanes].T.astype(BF16)
        return carry

    lax.fori_loop(0, own_ref.shape[0], block_step, 0)


def final_kernel(last_sender, ids_ref, acc_ref, blocks_ref, slots_ref, *refs):
    far_refs, (dk_ref, dv_ref, sum_ref) = refs[:-3], refs[-3:]
    blocks_here = acc_ref.shape[0] // BLOCK
    chip, base, own = places(blocks_here)
    sum_ref[...] = acc_ref[...] + blocks_ref[...].astype(F32)
    first_core = lax.axis_index("rep") == 0

    def slot_step(slot, carry):
        _, chip_rank = core_slot(ids_ref, slot, base, CORES * blocks_here)
        of_core, core_rank = core_slot(ids_ref, slot, own, blocks_here)
        rows = block_rows(lax.rem(ids_ref[slot], blocks_here))

        @pl.when(of_core & first_core & (core_rank < slots_ref.shape[0] // BLOCK))
        def _():
            sum_ref[rows, :] += slots_ref[block_rows(core_rank), :].astype(F32)

        @pl.when(of_core & (chip <= last_sender) & (chip_rank < far_refs[0].shape[0] // BLOCK))
        def _():
            for far_ref in far_refs:
                sum_ref[rows, :] += far_ref[block_rows(chip_rank), :].astype(F32)

        return carry

    lax.fori_loop(0, SUMMARY, slot_step, 0)
    dk_ref[...] = keys_of(sum_ref, slice(None)).astype(BF16)
    dv_ref[...] = values_of(sum_ref, slice(None)).astype(BF16)


def call(kernel, scalars, arrays, out_shape, scratch=(), flops=0, in_space=VMEM, out_specs=None, room=24):
    return pl.pallas_call(
        kernel,
        out_shape=out_shape,
        in_specs=[SMEM] * len(scalars) + [in_space] * len(arrays),
        out_specs=out_specs or jax.tree.map(lambda _: VMEM, out_shape),
        scratch_shapes=list(scratch),
        compiler_params=pltpu.CompilerParams(vmem_limit_bytes=room << 20),
        cost_estimate=pl.CostEstimate(flops=flops, bytes_accessed=0, transcendentals=0),
    )(*scalars, *arrays)


def shape_of(shape, dtype):
    return jax.ShapeDtypeStruct(shape, dtype)


def with_capacity(
    slots, chips, queries, kv, attn_out, grads, log_sums, window_offsets, summary_ids
):
    rows = queries.shape[0]
    blocks_here = rows // BLOCK
    swap = [(0, 1), (1, 0)]
    up = [(i, i + 1) for i in range(chips - 1)]
    down_first, down_last = (
        [(b * CORES + core, a * CORES + core) for a, b in up] for core in (0, CORES - 1)
    )
    routes = far_rounds(chips)
    sources = tuple({b: a // CORES for a, b in route} for route in routes)
    both = ("ctx", "rep")

    kv_partner = lax.ppermute(kv, "rep", swap)
    kv_near = lax.ppermute(kv, "ctx", up)
    far_shape, slots_shape = (shape_of((slot * BLOCK, 2 * HEAD_DIM), BF16) for slot in slots)
    picked = call(pick_kernel, (summary_ids,), (kv, kv_partner), far_shape)
    kv_far = [lax.ppermute(picked, both, route) for route in routes]
    queries, grads, attn_out, window_offsets, _ = lax.optimization_barrier(
        (queries, grads, attn_out, window_offsets, picked)
    )
    tables = (window_offsets, summary_ids)
    stats = call(
        prep_kernel, (), (attn_out, grads, log_sums),
        shape_of((blocks_here, 8, GROUP * BLOCK), F32), flops=5 * MICROSECOND,
    )
    own = (queries, grads, stats)
    every = own + tuple(lax.ppermute(x, "rep", swap) for x in own)
    acc_shape = (rows, 2 * HEAD_DIM)
    half_shape = (blocks_here, HEAD_DIM, GROUP * BLOCK)
    dq_shape = shape_of((CORES * blocks_here, *half_shape[1:]), F32)
    stacked_shape = shape_of((CORES * blocks_here, GROUP * BLOCK, HEAD_DIM), BF16)
    cross_acc, cross_dq, *every = call(
        cross_kernel, tables, (kv, *every),
        (
            shape_of(acc_shape, F32), shape_of(half_shape, F32), stacked_shape, stacked_shape,
            shape_of((CORES * blocks_here, *stats.shape[1:]), F32),
        ),
    )
    block_part, slot_part, near_dq = call(
        near_kernel, tables, (kv_near, *every, cross_dq),
        (shape_of(acc_shape, BF16), slots_shape, dq_shape),
        [pltpu.VMEM(acc_shape, F32)],
    )
    *far_grads, far_dq, dq_partner = call(
        functools.partial(far_kernel, sources), (summary_ids,), (*kv_far, *every, near_dq),
        (*[far_shape] * len(routes), dq_shape, shape_of(half_shape, BF16)),
        [pltpu.VMEM(far_shape.shape, F32)], flops=5 * MICROSECOND,
    )
    far_back = [
        lax.ppermute(x, both, [(b, a) for a, b in route]) for x, route in zip(far_grads, routes)
    ]
    block_part, slot_part, _ = lax.optimization_barrier((block_part, slot_part, far_grads))
    block_part = lax.ppermute(block_part, both, down_last)
    slot_part = lax.ppermute(slot_part, both, down_first)
    dq_partner = lax.ppermute(dq_partner, "rep", swap)
    acc, dq = call(
        own_kernel, tables, (kv, *every, cross_acc, far_dq),
        (shape_of(acc_shape, F32), shape_of(half_shape, F32)), flops=OWN,
    )
    query_grads = call(query_kernel, (), (dq, dq_partner), shape_of(queries.shape, BF16))
    if slots[0] > 4:
        slot_part, block_part = lax.optimization_barrier((slot_part, block_part))
    far_back, acc, query_grads, slot_part = lax.optimization_barrier(
        (far_back, acc, query_grads, slot_part)
    )
    far_other = [lax.ppermute(x, "rep", swap) for x in far_back]
    kv_shape = shape_of((rows, HEAD_DIM), BF16)
    key_grads, value_grads = call(
        functools.partial(final_kernel, chips - 3), (summary_ids,),
        (acc, block_part, slot_part, *far_back, *far_other), (kv_shape, kv_shape),
        [pltpu.VMEM(acc_shape, F32)],
    )
    return query_grads, key_grads, value_grads


def capacities(chips):
    return CAPACITIES if len(far_rounds(chips)) == 1 else CAPACITIES[-1:]


def per_device(chips, queries, keys, values, attn_out, grads, log_sums, window_offsets, summary_ids):
    kv, branch = call(
        functools.partial(start_kernel, chips), (), (summary_ids, keys, values),
        (shape_of((keys.shape[0], 2 * HEAD_DIM), BF16), shape_of((1,), jnp.int32)),
        [pltpu.SMEM(summary_ids.shape, jnp.int32), pltpu.SemaphoreType.DMA((3,))], in_space=HBM, out_specs=(VMEM, SMEM), room=60,
    )
    branches = [functools.partial(with_capacity, limit, chips) for limit in capacities(chips)]
    operands = (queries, kv, attn_out, grads, log_sums, window_offsets.T, summary_ids)
    return lax.switch(branch[0], branches, *operands) if len(branches) > 1 else branches[0](*operands)


def solution(mesh):
    rows = P(("groups", "ctx", "rep"), "heads")
    return jax.shard_map(
        functools.partial(per_device, mesh.shape["ctx"]),
        mesh=mesh,
        in_specs=(rows,) * 5 + (P("heads", ("groups", "ctx", "rep")), P("groups", None), P("groups")),
        out_specs=(rows,) * 3,
        check_vma=False,
    )
```
